32 devices in a mesh: rep: 4 (over z), ep: 8 (over y, x, core).
Axes of the slice: x: 2, y: 2, z: 4, core: 2. Of those that a mesh axis runs over, the one named last changes fastest.
Arguments:
- tokens: bfloat16 [4096, 2048], P(('rep', 'ep')), may hold values from -6 to 6
- cotangent: bfloat16 [4096, 2048], P(('rep', 'ep')), may hold values from -6 to 6
- query_weight: bfloat16 [2048, 2048], P(('rep', 'ep')), may hold values from -0.125 to 0.125
- key_weight: bfloat16 [2048, 2048], P(('rep', 'ep')), may hold values from -0.125 to 0.125
- value_weight: bfloat16 [2048, 2048], P(('rep', 'ep')), may hold values from -0.125 to 0.125
- output_weight: bfloat16 [2048, 2048], P(('rep', 'ep')), may hold values from -0.5 to 0.5
- router_weight: bfloat16 [2048, 24], P(('rep', 'ep')), may hold values from -0.06591797 to 0.06591797
- gains: bfloat16 [4352], P(('rep', 'ep')), may hold values from 0.5 to 1.5
- expert_gate: bfloat16 [24, 2048, 1024], P('ep'), may hold values from -0.125 to 0.125
- expert_up: bfloat16 [24, 2048, 1024], P('ep'), may hold values from -0.125 to 0.125
- expert_down: bfloat16 [24, 1024, 2048], P('ep'), may hold values from -0.5 to 0.5
- lengths: int32 [4, 3], P('rep'), may hold values from 1 to 768, 1024 in all within a row
- deal: int32 [4096], P(('rep', 'ep')), may hold values from 0 to 1023, as said below
- routes: int32 [4096, 8], P(('rep', 'ep')), may hold values from 0 to 23, all different within a row; in each aligned block of 128 rows (0 to 127, 128 to 255, ...) at most 64 rows name the same one
- priority: int32 [4096], P(('rep', 'ep')), may hold values from 0 to 1023, as said below
Outputs:
- block_out: bfloat16 [4096, 2048], P(('rep', 'ep'))
- input_grad: float32 [4096, 2048], P(('rep', 'ep'))
- query_grad: float32 [2048, 2048], P(('rep', 'ep'))
- key_grad: float32 [2048, 2048], P(('rep', 'ep'))
- value_grad: float32 [2048, 2048], P(('rep', 'ep'))
- output_grad: float32 [2048, 2048], P(('rep', 'ep'))
- router_grad: float32 [2048, 24], P(('rep', 'ep'))
- gains_grad: float32 [4352], P(('rep', 'ep'))
- gate_grad: float32 [24, 2048, 1024], P('ep', 'rep')
- up_grad: float32 [24, 2048, 1024], P('ep', 'rep')
- down_grad: float32 [24, 1024, 2048], P('ep', 'rep')
The draws below stay inside these ranges and needn't reach their ends.
Inputs may be any that keep to these rules, and one draw needn't show every extreme that they name: `deal`: within each group's 1024 rows, every packed position appears once. `priority`: within each group's 1024 rows, every rank appears once. `routes`: a token's 8 experts are different; the rows of one device name each expert at most 64 times, and some expert exactly that often. Each group's lengths sum to 1024; the longest is 768.
All inputs are finite; a program needn't handle non-finite values.
Results may differ from the reference program's by a relative error of at most 0.02.
Values may be sent and summed in bfloat16 or wider, within the bound.
A program may use at most 384 MiB of HBM per device.

```python
import math
import jax
import jax.numpy as jnp
import numpy as np
from jax import lax

D = 2048
H = 16
HD = 128
FF = 1024
TOP = 8
TOK_DEV = 128
SEQS = 3
REPS = 4
GROUP = 1024
TOKENS = 4096
EXPERTS = 24
LONGEST = 768
SEND_MOST = 64
CAP = 426


def draw_deal(key, part):
    key = jax.random.fold_in(key, 11)
    ep_count = GROUP // TOK_DEV
    order_key, shuffle_key = jax.random.split(key)
    order_keys = jax.random.split(order_key, REPS * TOK_DEV)
    orders = jax.vmap(lambda sub_key: jax.random.permutation(sub_key, ep_count))(order_keys).reshape(REPS, TOK_DEV, ep_count)
    blocks = jnp.arange(TOK_DEV, dtype=jnp.int32)[None, :, None] * ep_count
    held = jnp.transpose(blocks + orders.astype(jnp.int32), (0, 2, 1))
    shuffle_keys = jax.random.split(shuffle_key, REPS * ep_count)
    shuffles = jax.vmap(lambda sub_key: jax.random.permutation(sub_key, TOK_DEV))(shuffle_keys).reshape(REPS, ep_count, TOK_DEV)
    dealt = jnp.take_along_axis(held, shuffles.astype(jnp.int32), axis=2)
    return dealt.reshape(-1).astype(jnp.int32)


def draw_priority(key, part):
    key = jax.random.fold_in(key, 13)
    group_keys = jax.random.split(key, REPS)
    ranks = jax.vmap(lambda sub_key: jax.random.permutation(sub_key, GROUP))(group_keys)
    return ranks.reshape(-1).astype(jnp.int32)


def with_spikes(values, own_key, source, target, blocks, factor):
    def block_of(axis_at):
        return (jnp.arange(values.shape[axis_at]) // (values.shape[axis_at] // blocks)).reshape((-1,) + (1,) * (values.ndim - 1 - axis_at))

    first = jax.random.permutation(own_key, blocks)[block_of(target)]
    other_side = (block_of(target) + blocks // 2) % blocks
    return jnp.where((block_of(source) == first) | (block_of(source) == other_side), factor * values, values)


def block_levels(own_key, extent, cuts, smallest, top_value):
    level, own = 1.0, jax.random.fold_in(own_key, 6)
    for axis_at, blocks in cuts:
        steps = jnp.exp(jax.random.uniform(jax.random.fold_in(own, axis_at), (blocks,), jnp.float32, smallest / len(cuts), top_value / len(cuts)))
        level = level * jnp.repeat(steps, extent[axis_at] // blocks).reshape([-1 if axis == axis_at else 1 for axis in range(len(extent))])
    return level


def length_profile(number_of, total, limit, slope):
    loads = [(1 << 20) // math.isqrt(standing ** slope) + 1 for standing in range(2, number_of + 1)]
    spare, given = total - limit - (number_of - 1), [1] * (number_of - 1)
    while spare > 0:
        movable = [i for i in range(number_of - 1) if given[i] < limit]
        whole, budget = sum([loads[i] for i in movable]), spare
        for i in movable:
            more = min(limit - given[i], max(1, budget * loads[i] // whole), spare)
            given[i] = given[i] + more
            spare = spare - more
    return np.array([limit] + given)


def uneven(own_key, count, total, bound, slope):
    if count == 2:
        one = jax.random.randint(own_key, (), max(1, total - bound), min(bound, total - 1) + 1)
        return jnp.stack([one, total - one])
    sizes = jnp.asarray(length_profile(count, total, bound, slope), jnp.int32)
    twos = (count - 1) // 2
    source_of, taker = sizes[1:1 + 2 * twos:2], sizes[2:2 + 2 * twos:2]
    margin = jnp.minimum(source_of - 1, bound - taker)
    passed = jax.random.randint(jax.random.fold_in(own_key, 1), (twos,), 0, 1 << 20) % (margin + 1)
    sizes = sizes.at[1:1 + 2 * twos:2].set(source_of - passed).at[2:2 + 2 * twos:2].set(taker + passed)
    return sizes[jax.random.permutation(jax.random.fold_in(own_key, 2), count)]


def shared_out(stream_key, own, number, rows, number_of, top, most, lean):
    ranking = jax.random.permutation(stream_key, number_of)
    crowded, common = shares(number_of, rows * top, most, lean, True), shares(number_of, rows * top, most, lean, False)
    places = jnp.arange(number_of)

    def named(sizes, turn):
        used = int((sizes > 0).sum())
        fixed = max(1, used // 4)
        moved = fixed + (places - fixed + turn * (used - fixed)) % max(1, number_of - fixed)
        return jnp.zeros((number_of,), jnp.int32).at[ranking[jnp.where(places < fixed, places, moved)]].set(jnp.asarray(sizes, jnp.int32))

    sizes = jnp.where(number % 4 == 0, named(crowded, number // 4), named(common, number - number // 4 - 1))
    mixed = jax.random.permutation(jax.random.fold_in(own, 3), number_of)
    source_of, taker = mixed[0:number_of // 2 * 2:2], mixed[1:number_of // 2 * 2:2]
    room = jnp.minimum(sizes[source_of] - 1, most - sizes[taker]) // 2
    room = jnp.where((source_of == ranking[0]) | (taker == ranking[0]) | (sizes[taker] == 0), 0, jnp.maximum(room, 0))
    moved = jax.random.randint(jax.random.fold_in(own, 4), (number_of // 2,), 0, 1 << 20) % (room + 1)
    sizes = sizes.at[source_of].add(-moved).at[taker].add(moved)
    items = jnp.searchsorted(jnp.cumsum(sizes), jnp.arange(rows * top), side="right").astype(jnp.int32)
    listing = items.reshape(top, rows).T
    listing = listing[jax.random.permutation(jax.random.fold_in(own, 1), rows)]
    turn = jax.random.randint(jax.random.fold_in(own, 2), (rows, 1), 0, top)
    return jnp.take_along_axis(listing, (jnp.arange(top)[None, :] + turn) % top, axis=1)


def shares(count, total, reach, slope, full):
    portions = [(1 << 20) // math.isqrt(grade ** slope) + 1 for grade in range(1, count + 1)]
    largest = reach if full else min(reach, max(-(-total // count), total * portions[0] // sum(portions)))
    least = 1 if total - largest >= count - 1 else 0
    holding, spare = [largest] + [least] * (count - 1), total - largest - least * (count - 1)
    while spare > 0:
        candidates = [i for i in range(1, count) if holding[i] < largest] or [i for i in range(1, count) if holding[i] < reach]
        pool, remaining = sum([portions[i] for i in candidates]), spare
        for i in candidates:
            addition = min(reach - holding[i], max(1, remaining * portions[i] // pool), spare)
            holding[i] = holding[i] + addition
            spare = spare - addition
    return np.array(holding)


def gaussian(key, dims, width, limit, cuts=(), kind=jnp.bfloat16):
    factor_of = block_levels(key, dims, cuts, -0.22, 0.18) if cuts else 1.0
    values = jax.random.normal(key, dims, jnp.float32) * width * factor_of
    return jnp.minimum(jnp.maximum(values, -limit), limit).astype(kind)


def bell_draw_with(key, dims, spread, reach, cuts, heavy, kind=jnp.bfloat16):
    drawn = spread * jax.random.normal(key, dims, jnp.float32)
    if cuts:
        drawn = drawn * block_levels(key, dims, cuts, -0.22, 0.18)
    return jnp.clip(with_spikes(drawn, jax.random.fold_in(key, 3), *heavy), -reach, reach).astype(kind)


def setup_inputs(seed: int = 0) -> dict:
    key_of = jax.random.split(jax.random.key(seed), 16)
    tokens = bell_draw_with(key_of[0], (TOKENS, D), 1.0, 6.0, ((0, 32),), (0, 1, 32, 2.75))
    cotangent = gaussian(key_of[1], (TOKENS, D), 1.0, 6.0, ((0, 32),))
    query_weight = gaussian(key_of[2], (D, D), D ** -0.5, 0.125, ((0, 32),))
    key_weight = gaussian(key_of[3], (D, D), D ** -0.5, 0.125, ((0, 32),))
    value_weight = gaussian(key_of[4], (D, D), D ** -0.5, 0.125, ((0, 32),))
    output_weight = gaussian(key_of[5], (D, D), (D // 16) ** -0.5, 0.5, ((0, 32),))
    router_weight = gaussian(key_of[6], (D, EXPERTS), (0.5 * D ** -0.5), 0.06591797, ((0, 32),))
    gains = jnp.clip(1.0 + 0.1 * jax.random.normal(key_of[7], (2 * D + 2 * HD,), jnp.float32), 0.5, 1.5).astype(jnp.bfloat16)
    expert_gate = gaussian(key_of[8], (EXPERTS, D, FF), D ** -0.5, 0.125, ((0, 8),))
    expert_up = gaussian(key_of[9], (EXPERTS, D, FF), D ** -0.5, 0.125, ((0, 8),))
    expert_down = gaussian(key_of[10], (EXPERTS, FF, D), (FF // 8) ** -0.5, 0.5, ((0, 8),))
    lengths = jax.vmap(lambda own: uneven(own, SEQS, GROUP, LONGEST, 1))(jax.random.split(key_of[11], REPS)).reshape((REPS, SEQS)).astype(jnp.int32)
    deal = draw_deal(jax.random.fold_in(key_of[15], 71), 0)
    routes_keys = jax.random.split(jax.random.fold_in(key_of[13], 1), TOKENS // TOK_DEV)
    routes_turns = jax.random.permutation(jax.random.fold_in(key_of[13], 3), TOKENS // TOK_DEV)
    routes = jax.vmap(lambda own, number: shared_out(jax.random.fold_in(key_of[13], 2), own, number, TOK_DEV, EXPERTS, TOP, SEND_MOST, 1))(routes_keys, routes_turns).reshape((TOKENS, TOP))
    priority = draw_priority(jax.random.fold_in(key_of[15], 71), 0)
    return {"tokens": tokens, "cotangent": cotangent, "query_weight": query_weight, "key_weight": key_weight, "value_weight": value_weight, "output_weight": output_weight, "router_weight": router_weight, "gains": gains, "expert_gate": expert_gate, "expert_up": expert_up, "expert_down": expert_down, "lengths": lengths, "deal": deal, "routes": routes, "priority": priority}


@jax.custom_vjp
def low(v):
    return lax.optimization_barrier(v.astype(jnp.bfloat16)).astype(jnp.float32)

@jax.custom_vjp
def low_back(v):
    return v

def low_keep(v):
    return (low(v), None)

def low_pass(kept, grad):
    return (grad,)

def back_keep(v):
    return (v, None)

def back_low(kept, grad):
    return (low(grad),)
low.defvjp(low_keep, low_pass)
low_back.defvjp(back_keep, back_low)
norm_eps = 1e-06
rope_base = 10000.0
masked_score = -1e+30
highest = lax.Precision.HIGHEST

def rms_scale(values, gain_vec):
    return values * lax.rsqrt(lax.optimization_barrier(jnp.mean(values * values, axis=-1, keepdims=True)) + norm_eps) * gain_vec

def rotate(values, positions):
    half_width = values.shape[-1] // 2
    frequency = rope_base ** (-2.0 * jnp.arange(half_width, dtype=jnp.float32) / values.shape[-1])
    angles = positions.astype(jnp.float32)[:, None] * frequency[None, :]
    cosine = jnp.cos(angles)[:, None, :]
    sine_part = jnp.sin(angles)[:, None, :]
    low_half = values[..., :half_width]
    high_half = values[..., half_width:]
    return jnp.concatenate([low_half * cosine - high_half * sine_part, high_half * cosine + low_half * sine_part], axis=-1)

def placement(deal_rows, lengths_row):
    seq_ends = jnp.cumsum(lengths_row).astype(jnp.int32)
    is_after = (seq_ends[None, :] <= deal_rows[:, None]).astype(jnp.int32)
    segment = lax.optimization_barrier(jnp.sum(is_after, axis=1)).astype(jnp.int32)
    seq_start = lax.optimization_barrier(jnp.sum(is_after * lengths_row[None, :], axis=1)).astype(jnp.int32)
    return (segment, (deal_rows - seq_start).astype(jnp.int32))

def group_forward(params, tokens_g, deal_g, lengths_g, routes_g, priority_g):
    query_weight, key_weight, value_weight, output_weight, router_weight, gains, expert_gate, expert_up, expert_down = params
    row_count = tokens_g.shape[0]
    gain_in = gains[:D]
    gain_mid = gains[D:2 * D]
    gain_query = gains[2 * D:2 * D + HD]
    gain_key = gains[2 * D + HD:]
    segment, position = placement(deal_g, lengths_g)
    normed = low(rms_scale(tokens_g, gain_in))
    query_pre = low_back(jnp.dot(normed, query_weight, precision=highest)).reshape(row_count, H, HD)
    key_pre = low_back(jnp.dot(normed, key_weight, precision=highest)).reshape(row_count, H, HD)
    value_all = low(low_back(jnp.dot(normed, value_weight, precision=highest))).reshape(row_count, H, HD)
    query_all = low(rotate(rms_scale(query_pre, gain_query), position))
    key_all = low(rotate(rms_scale(key_pre, gain_key), position))
    same_seq = segment[:, None] == segment[None, :]

    def head_attention(parts):
        head_query, head_key, head_value = parts
        scores = jnp.dot(head_query, head_key.T, precision=highest) * HD ** (-0.5)
        scores = low_back(jnp.where(same_seq, scores, masked_score))
        prob_low = low(jax.nn.softmax(scores, axis=-1))
        return jnp.dot(prob_low, head_value, precision=highest)
    heads_out = lax.map(jax.checkpoint(head_attention), (query_all.transpose(1, 0, 2), key_all.transpose(1, 0, 2), value_all.transpose(1, 0, 2)))
    mixed_out = low(low_back(heads_out.transpose(1, 0, 2).reshape(row_count, D)))
    after_attn = tokens_g + low_back(jnp.dot(mixed_out, output_weight, precision=highest))
    mid_norm = low(rms_scale(after_attn, gain_mid))
    logits = low_back(jnp.dot(mid_norm, router_weight, precision=highest))
    gate_prob = jax.nn.softmax(jnp.take_along_axis(logits, routes_g, axis=1), axis=-1)
    expert_ids = jnp.arange(EXPERTS, dtype=jnp.int32)
    member = (routes_g[:, :, None] == expert_ids[None, None, :]).astype(jnp.float32)
    onehot = lax.optimization_barrier(jnp.sum(member, axis=1))
    earlier = (priority_g[None, :] < priority_g[:, None]).astype(jnp.float32)
    slot_count = jnp.take_along_axis(jnp.dot(earlier, onehot, precision=highest), routes_g, axis=1)
    kept = (slot_count < CAP).astype(jnp.float32)
    combine = jnp.einsum('tk,tke->et', gate_prob * kept, member, precision=highest)

    def expert_step(total_sum, parts):
        weight_gate, weight_up, weight_down, column = parts
        rows_in = low_back(mid_norm)
        gate_part = low_back(jnp.dot(rows_in, weight_gate, precision=highest))
        up_part = low_back(jnp.dot(rows_in, weight_up, precision=highest))
        hidden = low(jax.nn.silu(gate_part) * up_part)
        result = low_back(low(jnp.dot(hidden, weight_down, precision=highest)))
        return (total_sum + column[:, None] * result, None)
    moe_out, _ = lax.scan(jax.checkpoint(expert_step), jnp.zeros_like(tokens_g), (expert_gate, expert_up, expert_down, combine))
    return after_attn + moe_out

def reference(tokens, cotangent, query_weight, key_weight, value_weight, output_weight, router_weight, gains, expert_gate, expert_up, expert_down, lengths, deal, routes, priority):
    params = tuple((weight.astype(jnp.float32) for weight in (query_weight, key_weight, value_weight, output_weight, router_weight, gains, expert_gate, expert_up, expert_down)))
    tokens_all = tokens.astype(jnp.float32).reshape(REPS, GROUP, D)
    cot_all = cotangent.astype(jnp.float32).reshape(REPS, GROUP, D)

    def group_step(totals, items):
        tok_one, cot_one, deal_one, length_one, route_one, prio_one = items

        def closed(param_set, tok_in):
            return group_forward(param_set, tok_in, deal_one, length_one, route_one, prio_one)
        out_one, pull = jax.vjp(closed, params, tok_one)
        param_grads, tok_grad = pull(cot_one)
        return (jax.tree.map(jnp.add, totals, param_grads), (out_one.astype(jnp.bfloat16), tok_grad))
    start_totals = jax.tree.map(jnp.zeros_like, params)
    totals, (outs_all, grads_all) = lax.scan(group_step, start_totals, (tokens_all, cot_all, deal.reshape(REPS, GROUP), lengths, routes.reshape(REPS, GROUP, TOP), priority.reshape(REPS, GROUP)))
    return (outs_all.reshape(TOKENS, D), grads_all.reshape(TOKENS, D), totals[0], totals[1], totals[2], totals[3], totals[4], totals[5], totals[6], totals[7], totals[8])
```

```python
from functools import partial

import jax
import jax.numpy as jnp
from jax import lax
from jax.sharding import PartitionSpec as P

HD = 128


norm_eps = 1e-06
rope_base = 10000.0
masked_score = -1e30
highest = lax.Precision.HIGHEST


def rms_scale(values, gain_vec):
    return (
        values * lax.rsqrt(jnp.mean(values * values, axis=-1, keepdims=True) + norm_eps) * gain_vec
    )


def rotate(values, positions):
    half_width = values.shape[-1] // 2
    frequency = rope_base ** (-2.0 * jnp.arange(half_width, dtype=jnp.float32) / values.shape[-1])
    angles = positions.astype(jnp.float32)[:, None] * frequency[None, :]
    cosine = jnp.cos(angles)[:, None, :]
    sine_part = jnp.sin(angles)[:, None, :]
    low_half = values[..., :half_width]
    high_half = values[..., half_width:]
    return jnp.concatenate(
        [low_half * cosine - high_half * sine_part, high_half * cosine + low_half * sine_part],
        axis=-1,
    )


def placement(deal_rows, lengths_row):
    seq_ends = jnp.cumsum(lengths_row)
    is_after = (seq_ends[None, :] <= deal_rows[:, None]).astype(jnp.int32)
    segment = jnp.sum(is_after, axis=1)
    seq_start = jnp.sum(is_after * lengths_row[None, :], axis=1)
    return (segment, deal_rows - seq_start)


def rope_norm(projected, gain_vec, positions):
    return rotate(rms_scale(projected, gain_vec), positions)


def attend_forward(parts, same_seq, score_scale):
    head_query, head_key, head_value = parts
    scores = (
        jnp.einsum("thd,shd->hts", head_query, head_key, preferred_element_type=jnp.float32)
        * score_scale
    )
    scores = jnp.where(same_seq[None], scores, masked_score)
    top_score = jnp.max(scores, axis=-1, keepdims=True)
    lifted = jnp.exp(scores - top_score)
    total_sum = jnp.sum(lifted, axis=-1, keepdims=True)
    prob_low = (lifted / total_sum).astype(jnp.bfloat16)
    mixed_out = jnp.einsum("hts,shd->thd", prob_low, head_value, preferred_element_type=jnp.float32)
    return (mixed_out, top_score, total_sum)


def attend_backward(parts, same_seq, score_scale):
    head_query, head_key, head_value, head_grad, top_score, total_sum = parts
    scores = (
        jnp.einsum("thd,shd->hts", head_query, head_key, preferred_element_type=jnp.float32)
        * score_scale
    )
    scores = jnp.where(same_seq[None], scores, masked_score)
    prob_full = jnp.exp(scores - top_score) / total_sum
    prob_low = prob_full.astype(jnp.bfloat16)
    prob_grad = jnp.einsum(
        "thd,shd->hts", head_grad, head_value, preferred_element_type=jnp.float32
    )
    row_dot = jnp.sum(prob_full * prob_grad, axis=-1, keepdims=True)
    score_grad = (prob_full * (prob_grad - row_dot)).astype(jnp.bfloat16)
    query_grad = (
        jnp.einsum("hts,shd->thd", score_grad, head_key, preferred_element_type=jnp.float32)
        * score_scale
    )
    key_grad = (
        jnp.einsum("hts,thd->shd", score_grad, head_query, preferred_element_type=jnp.float32)
        * score_scale
    )
    value_grad = jnp.einsum("hts,thd->shd", prob_low, head_grad, preferred_element_type=jnp.float32)
    return (query_grad, key_grad, value_grad)


def on_device_general(
    tokens,
    cotangent,
    query_weight,
    key_weight,
    value_weight,
    output_weight,
    router_weight,
    gains,
    expert_gate,
    expert_up,
    expert_down,
    lengths,
    deal,
    routes,
    priority,
):
    tok_dev, width = tokens.shape
    ep_count = lax.axis_size("ep")
    ep_index = lax.axis_index("ep")
    exp_dev = expert_gate.shape[0]
    top_count = routes.shape[1]
    experts_all = exp_dev * ep_count
    group_rows = tok_dev * ep_count
    send_most = min(tok_dev, 3 * tok_dev * top_count // (2 * experts_all))
    capacity = 5 * tok_dev * top_count // (4 * exp_dev)
    head_dim = HD
    head_count = width // head_dim
    per_group = min(head_count, 4)
    group_count = head_count // per_group
    score_scale = head_dim ** (-0.5)
    query_full, key_full, value_full, output_full, router_full, gains_full = (
        lax.all_gather(query_weight, ("rep", "ep"), axis=0, tiled=True),
        lax.all_gather(key_weight, ("rep", "ep"), axis=0, tiled=True),
        lax.all_gather(value_weight, ("rep", "ep"), axis=0, tiled=True),
        lax.all_gather(output_weight, ("rep", "ep"), axis=0, tiled=True),
        lax.all_gather(router_weight, ("rep", "ep"), axis=0, tiled=True),
        lax.all_gather(gains, ("rep", "ep"), axis=0, tiled=True),
    )
    gains_float = gains_full.astype(jnp.float32)
    gain_in = gains_float[:width]
    gain_mid = gains_float[width : 2 * width]
    gain_query = gains_float[2 * width : 2 * width + head_dim]
    gain_key = gains_float[2 * width + head_dim :]
    deal_all, priority_all, routes_all = (
        lax.all_gather(deal, "ep", axis=0, tiled=True),
        lax.all_gather(priority, "ep", axis=0, tiled=True),
        lax.all_gather(routes, "ep", axis=0, tiled=True),
    )
    segment_all, position_all = placement(deal_all, lengths[0])
    segment_own = lax.dynamic_slice_in_dim(segment_all, ep_index * tok_dev, tok_dev)
    position_own = lax.dynamic_slice_in_dim(position_all, ep_index * tok_dev, tok_dev)
    residual = tokens.astype(jnp.float32)
    normed_low = rms_scale(residual, gain_in).astype(jnp.bfloat16)
    query_pre = jnp.dot(normed_low, query_full, preferred_element_type=jnp.float32).reshape(
        tok_dev, head_count, head_dim
    )
    key_pre = jnp.dot(normed_low, key_full, preferred_element_type=jnp.float32).reshape(
        tok_dev, head_count, head_dim
    )
    value_low = jnp.dot(normed_low, value_full, preferred_element_type=jnp.float32).astype(
        jnp.bfloat16
    )
    query_low = rope_norm(query_pre, gain_query, position_own).astype(jnp.bfloat16)
    key_low = (
        rope_norm(key_pre, gain_key, position_own).astype(jnp.bfloat16).reshape(tok_dev, width)
    )
    key_group, value_group = (
        lax.all_gather(key_low, "ep", axis=0, tiled=True),
        lax.all_gather(value_low, "ep", axis=0, tiled=True),
    )
    same_seq = segment_own[:, None] == segment_all[None, :]
    query_heads = query_low.reshape(tok_dev, group_count, per_group, head_dim).transpose(1, 0, 2, 3)
    key_heads = key_group.reshape(group_rows, group_count, per_group, head_dim).transpose(
        1, 0, 2, 3
    )
    value_heads = value_group.reshape(group_rows, group_count, per_group, head_dim).transpose(
        1, 0, 2, 3
    )
    mixed_heads, top_heads, total_heads = lax.map(
        partial(attend_forward, same_seq=same_seq, score_scale=score_scale),
        (query_heads, key_heads, value_heads),
    )
    mixed_low = mixed_heads.transpose(1, 0, 2, 3).reshape(tok_dev, width).astype(jnp.bfloat16)
    after_attn = residual + jnp.dot(mixed_low, output_full, preferred_element_type=jnp.float32)
    mid_low = rms_scale(after_attn, gain_mid).astype(jnp.bfloat16)
    logits = jnp.dot(mid_low, router_full, preferred_element_type=jnp.float32)
    chosen = jnp.take_along_axis(logits, routes, axis=1)
    gate_prob = jax.nn.softmax(chosen, axis=-1)
    expert_ids = jnp.arange(experts_all, dtype=jnp.int32)
    onehot_all = jnp.sum(
        (routes_all[:, :, None] == expert_ids[None, None, :]).astype(jnp.float32), axis=1
    )
    earlier = (priority_all[None, :] < priority_all[:, None]).astype(jnp.float32)
    slot_all = jnp.take_along_axis(
        jnp.dot(earlier, onehot_all, precision=highest), routes_all, axis=1
    ).astype(jnp.int32)
    row_ids = jnp.arange(tok_dev, dtype=jnp.int32)
    lower_tri = (row_ids[:, None] > row_ids[None, :]).astype(jnp.float32)
    before = jnp.einsum(
        "ij,dje->die",
        lower_tri,
        onehot_all.reshape(ep_count, tok_dev, experts_all),
        precision=highest,
    ).reshape(group_rows, experts_all)
    place_all = jnp.take_along_axis(before, routes_all, axis=1).astype(jnp.int32)
    kept_all = slot_all < capacity
    kept_own = lax.dynamic_slice_in_dim(kept_all, ep_index * tok_dev, tok_dev)
    place_own = lax.dynamic_slice_in_dim(place_all, ep_index * tok_dev, tok_dev)
    buffer_index = (routes * send_most + place_own).reshape(-1)
    rows_out = jnp.where(
        kept_own[:, :, None], mid_low[:, None, :], jnp.zeros((), jnp.bfloat16)
    ).reshape(tok_dev * top_count, width)
    send_rows = (
        jnp.zeros((experts_all * send_most, width), jnp.bfloat16)
        .at[buffer_index]
        .set(rows_out)
        .reshape(experts_all, send_most, width)
    )
    received = lax.all_to_all(send_rows, "ep", split_axis=0, concat_axis=1, tiled=True)
    gate_part = jnp.einsum(
        "erd,edf->erf", received, expert_gate, preferred_element_type=jnp.float32
    )
    up_part = jnp.einsum("erd,edf->erf", received, expert_up, preferred_element_type=jnp.float32)
    hidden = (jax.nn.silu(gate_part) * up_part).astype(jnp.bfloat16)
    result = jnp.einsum(
        "erf,efd->erd", hidden, expert_down, preferred_element_type=jnp.float32
    ).astype(jnp.bfloat16)
    returned = lax.all_to_all(result, "ep", split_axis=1, concat_axis=0, tiled=True)
    pair_out = returned.reshape(experts_all * send_most, width)[buffer_index].reshape(
        tok_dev, top_count, width
    )
    pair_weight = gate_prob * kept_own.astype(jnp.float32)
    moe_out = jnp.einsum("tk,tkd->td", pair_weight, pair_out, preferred_element_type=jnp.float32)
    block_out = (after_attn + moe_out).astype(jnp.bfloat16)
    out_grad = cotangent.astype(jnp.float32)
    pair_gate_grad = kept_own.astype(jnp.float32) * jnp.einsum(
        "tkd,td->tk", pair_out, out_grad, preferred_element_type=jnp.float32
    )
    pair_grad = (
        (pair_weight[:, :, None] * out_grad[:, None, :])
        .astype(jnp.bfloat16)
        .reshape(tok_dev * top_count, width)
    )
    grad_send = (
        jnp.zeros((experts_all * send_most, width), jnp.bfloat16)
        .at[buffer_index]
        .set(pair_grad)
        .reshape(experts_all, send_most, width)
    )
    grad_received = lax.all_to_all(grad_send, "ep", split_axis=0, concat_axis=1, tiled=True)
    hidden_grad = jnp.einsum(
        "erd,efd->erf", grad_received, expert_down, preferred_element_type=jnp.float32
    )
    _, silu_pull = jax.vjp(lambda gate_in, up_in: jax.nn.silu(gate_in) * up_in, gate_part, up_part)
    gate_part_grad, up_part_grad = silu_pull(hidden_grad)
    gate_low_grad = gate_part_grad.astype(jnp.bfloat16)
    up_low_grad = up_part_grad.astype(jnp.bfloat16)
    down_term = jnp.einsum(
        "erf,erd->efd", hidden, grad_received, preferred_element_type=jnp.float32
    )
    gate_term = jnp.einsum(
        "erd,erf->edf", received, gate_low_grad, preferred_element_type=jnp.float32
    )
    up_term = jnp.einsum("erd,erf->edf", received, up_low_grad, preferred_element_type=jnp.float32)
    rows_grad = (
        jnp.einsum("erf,edf->erd", gate_low_grad, expert_gate, preferred_element_type=jnp.float32)
        + jnp.einsum("erf,edf->erd", up_low_grad, expert_up, preferred_element_type=jnp.float32)
    ).astype(jnp.bfloat16)
    back_rows = lax.all_to_all(rows_grad, "ep", split_axis=1, concat_axis=0, tiled=True)
    mid_grad = jnp.sum(
        back_rows.reshape(experts_all * send_most, width)[buffer_index]
        .reshape(tok_dev, top_count, width)
        .astype(jnp.float32),
        axis=1,
    )
    gate_w_grad, up_w_grad, down_w_grad = (
        lax.psum_scatter(
            gate_term.astype(jnp.bfloat16), "rep", scatter_dimension=1, tiled=True
        ).astype(jnp.float32),
        lax.psum_scatter(
            up_term.astype(jnp.bfloat16), "rep", scatter_dimension=1, tiled=True
        ).astype(jnp.float32),
        lax.psum_scatter(
            down_term.astype(jnp.bfloat16), "rep", scatter_dimension=1, tiled=True
        ).astype(jnp.float32),
    )
    _, soft_pull = jax.vjp(lambda values: jax.nn.softmax(values, axis=-1), chosen)
    (chosen_grad,) = soft_pull(pair_gate_grad)
    onehot_own = (routes[:, :, None] == expert_ids[None, None, :]).astype(jnp.float32)
    logit_grad = jnp.einsum("tk,tke->te", chosen_grad, onehot_own).astype(jnp.bfloat16)
    mid_grad = mid_grad + jnp.dot(logit_grad, router_full.T, preferred_element_type=jnp.float32)
    router_term = jnp.dot(mid_low.T, logit_grad, preferred_element_type=jnp.float32)
    _, mid_pull = jax.vjp(rms_scale, after_attn, gain_mid)
    after_extra, gain_mid_grad = mid_pull(mid_grad)
    after_grad = out_grad + after_extra
    attn_low_grad = after_grad.astype(jnp.bfloat16)
    output_term = jnp.dot(mixed_low.T, attn_low_grad, preferred_element_type=jnp.float32)
    mixed_grad = jnp.dot(attn_low_grad, output_full.T, preferred_element_type=jnp.float32).astype(
        jnp.bfloat16
    )
    mixed_grad_heads = mixed_grad.reshape(tok_dev, group_count, per_group, head_dim).transpose(
        1, 0, 2, 3
    )
    query_grad_h, key_grad_h, value_grad_h = lax.map(
        partial(attend_backward, same_seq=same_seq, score_scale=score_scale),
        (query_heads, key_heads, value_heads, mixed_grad_heads, top_heads, total_heads),
    )
    query_grad_own = query_grad_h.transpose(1, 0, 2, 3).reshape(tok_dev, head_count, head_dim)
    key_grad_group = key_grad_h.transpose(1, 0, 2, 3).reshape(group_rows, width)
    value_grad_group = value_grad_h.transpose(1, 0, 2, 3).reshape(group_rows, width)
    key_sum, value_sum = (
        lax.psum_scatter(
            key_grad_group.astype(jnp.bfloat16), "ep", scatter_dimension=0, tiled=True
        ).astype(jnp.float32),
        lax.psum_scatter(
            value_grad_group.astype(jnp.bfloat16), "ep", scatter_dimension=0, tiled=True
        ).astype(jnp.float32),
    )
    value_low_grad = value_sum.astype(jnp.bfloat16)
    _, query_pull = jax.vjp(
        lambda projected, gain_vec: rope_norm(projected, gain_vec, position_own),
        query_pre,
        gain_query,
    )
    query_pre_grad, gain_query_grad = query_pull(query_grad_own)
    _, key_pull = jax.vjp(
        lambda projected, gain_vec: rope_norm(projected, gain_vec, position_own), key_pre, gain_key
    )
    key_pre_grad, gain_key_grad = key_pull(key_sum.reshape(tok_dev, head_count, head_dim))
    query_low_grad = query_pre_grad.reshape(tok_dev, width).astype(jnp.bfloat16)
    key_low_grad = key_pre_grad.reshape(tok_dev, width).astype(jnp.bfloat16)
    normed_grad = jnp.dot(query_low_grad, query_full.T, preferred_element_type=jnp.float32)
    normed_grad = normed_grad + jnp.dot(
        key_low_grad, key_full.T, preferred_element_type=jnp.float32
    )
    normed_grad = normed_grad + jnp.dot(
        value_low_grad, value_full.T, preferred_element_type=jnp.float32
    )
    query_term = jnp.dot(normed_low.T, query_low_grad, preferred_element_type=jnp.float32)
    key_term = jnp.dot(normed_low.T, key_low_grad, preferred_element_type=jnp.float32)
    value_term = jnp.dot(normed_low.T, value_low_grad, preferred_element_type=jnp.float32)
    _, input_pull = jax.vjp(rms_scale, residual, gain_in)
    input_extra, gain_in_grad = input_pull(normed_grad)
    input_grad = after_grad + input_extra
    gains_term = jnp.concatenate([gain_in_grad, gain_mid_grad, gain_query_grad, gain_key_grad])
    query_sum, key_total, value_total, output_sum, router_sum, gains_sum = (
        lax.psum_scatter(query_term, ("rep", "ep"), scatter_dimension=0, tiled=True),
        lax.psum_scatter(key_term, ("rep", "ep"), scatter_dimension=0, tiled=True),
        lax.psum_scatter(value_term, ("rep", "ep"), scatter_dimension=0, tiled=True),
        lax.psum_scatter(output_term, ("rep", "ep"), scatter_dimension=0, tiled=True),
        lax.psum_scatter(router_term, ("rep", "ep"), scatter_dimension=0, tiled=True),
        lax.psum_scatter(gains_term, ("rep", "ep"), scatter_dimension=0, tiled=True),
    )
    return (
        block_out,
        input_grad,
        query_sum,
        key_total,
        value_total,
        output_sum,
        router_sum,
        gains_sum,
        gate_w_grad,
        up_w_grad,
        down_w_grad,
    )


def gather_block(block, axes):
    return lax.all_gather(block, axes, axis=0, tiled=True)


def scatter_sum(partial_sums, axes):
    return lax.psum_scatter(partial_sums, axes, scatter_dimension=0, tiled=True)


def on_device_split(
    tokens,
    cotangent,
    query_weight,
    key_weight,
    value_weight,
    output_weight,
    router_weight,
    gains,
    expert_gate,
    expert_up,
    expert_down,
    lengths,
    deal,
    routes,
    priority,
):
    bf16, f32 = jnp.bfloat16, jnp.float32
    tok_dev, width = tokens.shape
    ep_count, rep_count = lax.axis_size("ep"), lax.axis_size("rep")
    ep_index, rep_index = lax.axis_index("ep"), lax.axis_index("rep")
    exp_dev, _, ff_width = expert_gate.shape
    top_count = routes.shape[1]
    experts_all = exp_dev * ep_count
    group_rows = tok_dev * ep_count
    capacity = 5 * tok_dev * top_count // (4 * exp_dev)
    head_dim = HD
    heads_dev = width // head_dim // ep_count
    slice_width = heads_dev * head_dim
    rows_dev = query_weight.shape[0]
    ff_slice = ff_width // rep_count
    score_scale = head_dim ** (-0.5)
    core = ep_index % 2
    every = ("rep", "ep")

    gains_dev = gains.shape[0]
    packed = jnp.concatenate(
        [gains, router_weight.reshape(-1), jnp.zeros((2048 - gains_dev - router_weight.size,), bf16)]
    ).reshape(16, 128)
    packed_all = gather_block(packed, every).reshape(rep_count * ep_count, 2048)
    gains_float = packed_all[:, :gains_dev].reshape(-1).astype(f32)
    router_full = packed_all[:, gains_dev : gains_dev + router_weight.size].reshape(width, experts_all)
    gain_in = gains_float[:width]
    gain_mid = gains_float[width : 2 * width]
    gain_query = gains_float[2 * width : 2 * width + head_dim]
    gain_key = gains_float[2 * width + head_dim :]
    numbers = jnp.concatenate([deal, priority, routes.T.reshape(-1)]).reshape(-1, 128)
    numbers_all = gather_block(numbers, "ep").reshape(ep_count, -1, tok_dev)
    deal_all = numbers_all[:, 0].reshape(-1)
    priority_all = numbers_all[:, 1].reshape(-1)
    routes_all = numbers_all[:, 2:].transpose(0, 2, 1).reshape(group_rows, top_count)
    segment_all, position_all = placement(deal_all, lengths[0])

    chips = ep_count // 2
    def columns_of(weight):
        parts = weight.reshape(rows_dev, 2, heads_dev, chips, head_dim).transpose(3, 1, 0, 2, 4)
        parts = parts.reshape(ep_count, rows_dev, slice_width)
        return lax.all_to_all(parts, "ep", split_axis=0, concat_axis=0, tiled=True)

    qkv_rows = jnp.concatenate(
        [columns_of(query_weight), columns_of(key_weight), columns_of(value_weight)], axis=2
    ).reshape(ep_count * rows_dev, 3 * slice_width)
    qkv_slice = gather_block(qkv_rows, "rep")
    out_rows = gather_block(output_weight, "rep").reshape(2, heads_dev, rows_dev, width)
    out_own = lax.dynamic_index_in_dim(out_rows, core, 0, keepdims=False)
    out_other = lax.ppermute(
        lax.dynamic_index_in_dim(out_rows, 1 - core, 0, keepdims=False),
        "ep",
        [(i, i + 1 - 2 * (i % 2)) for i in range(ep_count)],
    )
    out_slice = jnp.where(
        core == 0,
        jnp.concatenate([out_own, out_other], axis=1),
        jnp.concatenate([out_other, out_own], axis=1),
    ).reshape(slice_width, width)

    cot_all = gather_block(cotangent, every)
    tokens_group = gather_block(tokens, "ep").astype(f32)
    normed_group = rms_scale(tokens_group, gain_in).astype(bf16)
    projected = jnp.dot(normed_group, qkv_slice, preferred_element_type=f32)
    query_pre = projected[:, :slice_width].reshape(group_rows, heads_dev, head_dim)
    key_pre = projected[:, slice_width : 2 * slice_width].reshape(group_rows, heads_dev, head_dim)
    value_low = projected[:, 2 * slice_width :].astype(bf16).reshape(group_rows, heads_dev, head_dim)
    query_low = rope_norm(query_pre, gain_query, position_all).astype(bf16)
    key_low = rope_norm(key_pre, gain_key, position_all).astype(bf16)
    same_seq = segment_all[:, None] == segment_all[None, :]
    mixed, top_score, total_sum = attend_forward(
        (query_low, key_low, value_low), same_seq, score_scale
    )
    mixed_low = mixed.reshape(group_rows, slice_width).astype(bf16)
    attn_part = jnp.dot(mixed_low, out_slice, preferred_element_type=f32).astype(bf16)
    residual = tokens.astype(f32)
    after_attn = residual + scatter_sum(attn_part, "ep").astype(f32)
    mid_low = rms_scale(after_attn, gain_mid).astype(bf16)

    logits = jnp.dot(mid_low, router_full, preferred_element_type=f32)
    expert_ids = jnp.arange(experts_all, dtype=jnp.int32)
    member = (routes[:, :, None] == expert_ids[None, None, :]).astype(f32)
    named = jnp.sum(member, axis=1)
    lifted = jnp.where(named > 0, logits, masked_score)
    lifted = jnp.exp(lifted - jnp.max(lifted, axis=-1, keepdims=True)) * named
    gate_dense = lifted / jnp.sum(lifted, axis=-1, keepdims=True)
    onehot_all = jnp.sum(
        (routes_all[:, :, None] == expert_ids[None, None, :]).astype(bf16), axis=1
    )
    earlier = (priority_all[None, :] < priority[:, None]).astype(bf16)
    slots = jnp.dot(earlier, onehot_all, preferred_element_type=f32)
    kept_dense = named * (slots < capacity).astype(f32)
    pair_weight = gate_dense * kept_dense

    weight_high = pair_weight.astype(bf16)
    weight_low = (pair_weight - weight_high.astype(f32)).astype(bf16)
    side = jnp.concatenate(
        [weight_high, weight_low, jnp.zeros((tok_dev, 128 - 2 * experts_all), bf16)], axis=1
    )
    sent = gather_block(jnp.concatenate([mid_low, side], axis=1), every)
    mid_all = sent[:, :width]
    side_all = sent[:, width:]
    weight_own = lax.dynamic_slice_in_dim(side_all, ep_index * exp_dev, exp_dev, axis=1).astype(
        f32
    ) + lax.dynamic_slice_in_dim(
        side_all, experts_all + ep_index * exp_dev, exp_dev, axis=1
    ).astype(f32)
    gate_slice = lax.dynamic_slice_in_dim(expert_gate, rep_index * ff_slice, ff_slice, axis=2)
    up_slice = lax.dynamic_slice_in_dim(expert_up, rep_index * ff_slice, ff_slice, axis=2)
    down_slice = lax.dynamic_slice_in_dim(expert_down, rep_index * ff_slice, ff_slice, axis=1)
    gate_flat = gate_slice.transpose(1, 0, 2).reshape(width, exp_dev * ff_slice)
    up_flat = up_slice.transpose(1, 0, 2).reshape(width, exp_dev * ff_slice)
    down_flat = down_slice.reshape(exp_dev * ff_slice, width)
    gate_part = jnp.dot(mid_all, gate_flat, preferred_element_type=f32)
    up_part = jnp.dot(mid_all, up_flat, preferred_element_type=f32)
    down_cot = jnp.dot(cot_all, down_flat.T, preferred_element_type=f32)
    weight_wide = jnp.repeat(weight_own, ff_slice, axis=1)
    sigma = jax.nn.sigmoid(gate_part)
    silu = gate_part * sigma
    hidden = (silu * up_part).astype(bf16).astype(f32)
    hidden_weighted = (hidden * weight_wide).astype(bf16)
    hidden_cot = weight_wide * down_cot
    a_cot = (hidden_cot * up_part * (sigma * (1 + gate_part * (1 - sigma)))).astype(bf16)
    b_cot = (hidden_cot * silu).astype(bf16)
    row_part = (
        jnp.dot(a_cot, gate_flat.T, preferred_element_type=f32)
        + jnp.dot(b_cot, up_flat.T, preferred_element_type=f32)
    ).astype(bf16)
    gate_cot_own = jnp.sum((hidden * down_cot).reshape(-1, exp_dev, ff_slice), axis=2)
    gate_cot_part = lax.dynamic_update_slice_in_dim(
        jnp.zeros((gate_cot_own.shape[0], 128), bf16),
        gate_cot_own.astype(bf16),
        ep_index * exp_dev,
        axis=1,
    )
    row_sum = scatter_sum(jnp.concatenate([row_part, gate_cot_part], axis=1), every)
    moe_part = jnp.dot(hidden_weighted, down_flat, preferred_element_type=f32).astype(bf16)
    moe_out = scatter_sum(moe_part, every).astype(f32)
    block_out = (after_attn + moe_out).astype(bf16)
    gate_term = jnp.dot(mid_all.T, a_cot, preferred_element_type=f32)
    up_term = jnp.dot(mid_all.T, b_cot, preferred_element_type=f32)
    down_w_grad = jnp.dot(hidden_weighted.T, cot_all, preferred_element_type=f32).reshape(
        exp_dev, ff_slice, width
    )

    def rows_of(term):
        parts = term.astype(bf16).reshape(rep_count, width // rep_count, exp_dev, ff_slice)
        parts = parts.transpose(0, 2, 1, 3)
        got = lax.all_to_all(parts, "rep", split_axis=0, concat_axis=0, tiled=True)
        return got.transpose(1, 2, 0, 3).reshape(exp_dev, width // rep_count, ff_width).astype(f32)

    gate_w_grad = rows_of(gate_term)
    up_w_grad = rows_of(up_term)

    out_grad = cotangent.astype(f32)
    gate_cot = row_sum[:, width : width + experts_all].astype(f32) * kept_dense
    chosen_cot = gate_dense * (gate_cot - jnp.sum(gate_dense * gate_cot, axis=-1, keepdims=True))
    logit_cot = chosen_cot.astype(bf16)
    mid_cot = row_sum[:, :width].astype(f32) + jnp.dot(
        logit_cot, router_full.T, preferred_element_type=f32
    )
    router_term = jnp.dot(mid_low.T, logit_cot, preferred_element_type=f32)
    _, mid_pull = jax.vjp(rms_scale, after_attn, gain_mid)
    after_extra, gain_mid_cot = mid_pull(mid_cot)
    after_cot = out_grad + after_extra
    attn_cot_group = gather_block(after_cot.astype(bf16), "ep")

    mixed_cot = jnp.dot(attn_cot_group, out_slice.T, preferred_element_type=f32).astype(bf16)
    output_term = jnp.dot(mixed_low.T, attn_cot_group, preferred_element_type=f32)
    query_cot, key_cot, value_cot = attend_backward(
        (
            query_low,
            key_low,
            value_low,
            mixed_cot.reshape(group_rows, heads_dev, head_dim),
            top_score,
            total_sum,
        ),
        same_seq,
        score_scale,
    )
    _, query_pull = jax.vjp(
        lambda pre, gain_vec: rope_norm(pre, gain_vec, position_all), query_pre, gain_query
    )
    query_pre_cot, gain_query_cot = query_pull(query_cot)
    _, key_pull = jax.vjp(
        lambda pre, gain_vec: rope_norm(pre, gain_vec, position_all), key_pre, gain_key
    )
    key_pre_cot, gain_key_cot = key_pull(key_cot)
    pre_cot = jnp.concatenate(
        [
            part.reshape(group_rows, slice_width).astype(bf16)
            for part in (query_pre_cot, key_pre_cot, value_cot)
        ],
        axis=1,
    )
    normed_part = jnp.dot(pre_cot, qkv_slice.T, preferred_element_type=f32).astype(bf16)
    normed_cot = scatter_sum(normed_part, "ep").astype(f32)
    _, input_pull = jax.vjp(rms_scale, residual, gain_in)
    input_extra, gain_in_cot = input_pull(normed_cot)
    input_grad = after_cot + input_extra
    qkv_term = jnp.dot(normed_group.T, pre_cot, preferred_element_type=f32)

    qkv_sum = scatter_sum(qkv_term.astype(bf16), "rep").reshape(ep_count, rows_dev, 3, slice_width)

    def whole_rows(part):
        got = lax.all_to_all(part, "ep", split_axis=0, concat_axis=0, tiled=True)
        got = got.reshape(chips, 2, rows_dev, heads_dev, head_dim).transpose(2, 1, 3, 0, 4)
        return got.reshape(rows_dev, width).astype(f32)

    query_sum, key_sum, value_sum = (whole_rows(qkv_sum[:, :, i]) for i in range(3))
    out_halves = output_term.astype(bf16).reshape(heads_dev, 2, rows_dev, width)
    out_keep = lax.dynamic_index_in_dim(out_halves, core, 1, keepdims=False)
    out_pass = lax.ppermute(
        lax.dynamic_index_in_dim(out_halves, 1 - core, 1, keepdims=False),
        "ep",
        [(i, i + 1 - 2 * (i % 2)) for i in range(ep_count)],
    )
    out_parts = jnp.where(
        core == 0, jnp.stack([out_keep, out_pass]), jnp.stack([out_pass, out_keep])
    ).reshape(2 * heads_dev * rows_dev, width)
    output_sum = scatter_sum(out_parts, "rep").astype(f32)
    gains_term = jnp.concatenate([gain_in_cot, gain_mid_cot, gain_query_cot, gain_key_cot])
    small_term = jnp.concatenate(
        [
            gains_term.reshape(rep_count * ep_count, gains_dev),
            router_term.reshape(rep_count * ep_count, router_weight.size),
            jnp.zeros((rep_count * ep_count, 2048 - gains_dev - router_weight.size), f32),
        ],
        axis=1,
    ).reshape(rep_count * ep_count * 16, 128)
    small_sum = scatter_sum(small_term, every).reshape(-1)
    gains_sum = small_sum[:gains_dev]
    router_sum = small_sum[gains_dev : gains_dev + router_weight.size].reshape(
        rows_dev, experts_all
    )
    return (
        block_out,
        input_grad,
        query_sum,
        key_sum,
        value_sum,
        output_sum,
        router_sum,
        gains_sum,
        gate_w_grad,
        up_w_grad,
        down_w_grad,
    )


def solution(mesh):
    placed = (
        P(("rep", "ep"), None),
        P(("rep", "ep"), None),
        P(("rep", "ep"), None),
        P(("rep", "ep"), None),
        P(("rep", "ep"), None),
        P(("rep", "ep"), None),
        P(("rep", "ep"), None),
        P(("rep", "ep")),
        P("ep", None, None),
        P("ep", None, None),
        P("ep", None, None),
        P("rep", None),
        P(("rep", "ep")),
        P(("rep", "ep"), None),
        P(("rep", "ep")),
    )
    return jax.shard_map(
        on_device_split if mesh.shape["rep"] == 4 else on_device_general,
        mesh=mesh,
        in_specs=placed,
        out_specs=(
            P(("rep", "ep"), None),
            P(("rep", "ep"), None),
            P(("rep", "ep"), None),
            P(("rep", "ep"), None),
            P(("rep", "ep"), None),
            P(("rep", "ep"), None),
            P(("rep", "ep"), None),
            P(("rep", "ep")),
            P("ep", "rep", None),
            P("ep", "rep", None),
            P("ep", "rep", None),
        ),
        check_vma=False,
    )
```

```python
from functools import partial

import jax
import jax.numpy as jnp
from jax import lax
from jax.experimental import pallas as pl
from jax.experimental.pallas import tpu as pltpu
from jax.sharding import PartitionSpec as P

HD = 128


norm_eps = 1e-06
rope_base = 10000.0
masked_score = -1e30
highest = lax.Precision.HIGHEST


def rms_scale(values, gain_vec):
    return (
        values * lax.rsqrt(jnp.mean(values * values, axis=-1, keepdims=True) + norm_eps) * gain_vec
    )


def rotate(values, positions):
    half_width = values.shape[-1] // 2
    frequency = rope_base ** (-2.0 * jnp.arange(half_width, dtype=jnp.float32) / values.shape[-1])
    angles = positions.astype(jnp.float32)[:, None] * frequency[None, :]
    cosine = jnp.cos(angles)[:, None, :]
    sine_part = jnp.sin(angles)[:, None, :]
    low_half = values[..., :half_width]
    high_half = values[..., half_width:]
    return jnp.concatenate(
        [low_half * cosine - high_half * sine_part, high_half * cosine + low_half * sine_part],
        axis=-1,
    )


def placement(deal_rows, lengths_row):
    seq_ends = jnp.cumsum(lengths_row)
    is_after = (seq_ends[None, :] <= deal_rows[:, None]).astype(jnp.int32)
    segment = jnp.sum(is_after, axis=1)
    seq_start = jnp.sum(is_after * lengths_row[None, :], axis=1)
    return (segment, deal_rows - seq_start)


def rope_norm(projected, gain_vec, positions):
    return rotate(rms_scale(projected, gain_vec), positions)


def attend_forward(parts, same_seq, score_scale):
    head_query, head_key, head_value = parts
    scores = (
        jnp.einsum("thd,shd->hts", head_query, head_key, preferred_element_type=jnp.float32)
        * score_scale
    )
    scores = jnp.where(same_seq[None], scores, masked_score)
    top_score = jnp.max(scores, axis=-1, keepdims=True)
    lifted = jnp.exp(scores - top_score)
    total_sum = jnp.sum(lifted, axis=-1, keepdims=True)
    prob_low = (lifted / total_sum).astype(jnp.bfloat16)
    mixed_out = jnp.einsum("hts,shd->thd", prob_low, head_value, preferred_element_type=jnp.float32)
    return (mixed_out, top_score, total_sum)


def attend_backward(parts, same_seq, score_scale):
    head_query, head_key, head_value, head_grad, top_score, total_sum = parts
    scores = (
        jnp.einsum("thd,shd->hts", head_query, head_key, preferred_element_type=jnp.float32)
        * score_scale
    )
    scores = jnp.where(same_seq[None], scores, masked_score)
    prob_full = jnp.exp(scores - top_score) / total_sum
    prob_low = prob_full.astype(jnp.bfloat16)
    prob_grad = jnp.einsum(
        "thd,shd->hts", head_grad, head_value, preferred_element_type=jnp.float32
    )
    row_dot = jnp.sum(prob_full * prob_grad, axis=-1, keepdims=True)
    score_grad = (prob_full * (prob_grad - row_dot)).astype(jnp.bfloat16)
    query_grad = (
        jnp.einsum("hts,shd->thd", score_grad, head_key, preferred_element_type=jnp.float32)
        * score_scale
    )
    key_grad = (
        jnp.einsum("hts,thd->shd", score_grad, head_query, preferred_element_type=jnp.float32)
        * score_scale
    )
    value_grad = jnp.einsum("hts,thd->shd", prob_low, head_grad, preferred_element_type=jnp.float32)
    return (query_grad, key_grad, value_grad)


def on_device_general(
    tokens,
    cotangent,
    query_weight,
    key_weight,
    value_weight,
    output_weight,
    router_weight,
    gains,
    expert_gate,
    expert_up,
    expert_down,
    lengths,
    deal,
    routes,
    priority,
):
    tok_dev, width = tokens.shape
    ep_count = lax.axis_size("ep")
    ep_index = lax.axis_index("ep")
    exp_dev = expert_gate.shape[0]
    top_count = routes.shape[1]
    experts_all = exp_dev * ep_count
    group_rows = tok_dev * ep_count
    send_most = min(tok_dev, 3 * tok_dev * top_count // (2 * experts_all))
    capacity = 5 * tok_dev * top_count // (4 * exp_dev)
    head_dim = HD
    head_count = width // head_dim
    per_group = min(head_count, 4)
    group_count = head_count // per_group
    score_scale = head_dim ** (-0.5)
    query_full, key_full, value_full, output_full, router_full, gains_full = (
        lax.all_gather(query_weight, ("rep", "ep"), axis=0, tiled=True),
        lax.all_gather(key_weight, ("rep", "ep"), axis=0, tiled=True),
        lax.all_gather(value_weight, ("rep", "ep"), axis=0, tiled=True),
        lax.all_gather(output_weight, ("rep", "ep"), axis=0, tiled=True),
        lax.all_gather(router_weight, ("rep", "ep"), axis=0, tiled=True),
        lax.all_gather(gains, ("rep", "ep"), axis=0, tiled=True),
    )
    gains_float = gains_full.astype(jnp.float32)
    gain_in = gains_float[:width]
    gain_mid = gains_float[width : 2 * width]
    gain_query = gains_float[2 * width : 2 * width + head_dim]
    gain_key = gains_float[2 * width + head_dim :]
    deal_all, priority_all, routes_all = (
        lax.all_gather(deal, "ep", axis=0, tiled=True),
        lax.all_gather(priority, "ep", axis=0, tiled=True),
        lax.all_gather(routes, "ep", axis=0, tiled=True),
    )
    segment_all, position_all = placement(deal_all, lengths[0])
    segment_own = lax.dynamic_slice_in_dim(segment_all, ep_index * tok_dev, tok_dev)
    position_own = lax.dynamic_slice_in_dim(position_all, ep_index * tok_dev, tok_dev)
    residual = tokens.astype(jnp.float32)
    normed_low = rms_scale(residual, gain_in).astype(jnp.bfloat16)
    query_pre = jnp.dot(normed_low, query_full, preferred_element_type=jnp.float32).reshape(
        tok_dev, head_count, head_dim
    )
    key_pre = jnp.dot(normed_low, key_full, preferred_element_type=jnp.float32).reshape(
        tok_dev, head_count, head_dim
    )
    value_low = jnp.dot(normed_low, value_full, preferred_element_type=jnp.float32).astype(
        jnp.bfloat16
    )
    query_low = rope_norm(query_pre, gain_query, position_own).astype(jnp.bfloat16)
    key_low = (
        rope_norm(key_pre, gain_key, position_own).astype(jnp.bfloat16).reshape(tok_dev, width)
    )
    key_group, value_group = (
        lax.all_gather(key_low, "ep", axis=0, tiled=True),
        lax.all_gather(value_low, "ep", axis=0, tiled=True),
    )
    same_seq = segment_own[:, None] == segment_all[None, :]
    query_heads = query_low.reshape(tok_dev, group_count, per_group, head_dim).transpose(1, 0, 2, 3)
    key_heads = key_group.reshape(group_rows, group_count, per_group, head_dim).transpose(
        1, 0, 2, 3
    )
    value_heads = value_group.reshape(group_rows, group_count, per_group, head_dim).transpose(
        1, 0, 2, 3
    )
    mixed_heads, top_heads, total_heads = lax.map(
        partial(attend_forward, same_seq=same_seq, score_scale=score_scale),
        (query_heads, key_heads, value_heads),
    )
    mixed_low = mixed_heads.transpose(1, 0, 2, 3).reshape(tok_dev, width).astype(jnp.bfloat16)
    after_attn = residual + jnp.dot(mixed_low, output_full, preferred_element_type=jnp.float32)
    mid_low = rms_scale(after_attn, gain_mid).astype(jnp.bfloat16)
    logits = jnp.dot(mid_low, router_full, preferred_element_type=jnp.float32)
    chosen = jnp.take_along_axis(logits, routes, axis=1)
    gate_prob = jax.nn.softmax(chosen, axis=-1)
    expert_ids = jnp.arange(experts_all, dtype=jnp.int32)
    onehot_all = jnp.sum(
        (routes_all[:, :, None] == expert_ids[None, None, :]).astype(jnp.float32), axis=1
    )
    earlier = (priority_all[None, :] < priority_all[:, None]).astype(jnp.float32)
    slot_all = jnp.take_along_axis(
        jnp.dot(earlier, onehot_all, precision=highest), routes_all, axis=1
    ).astype(jnp.int32)
    row_ids = jnp.arange(tok_dev, dtype=jnp.int32)
    lower_tri = (row_ids[:, None] > row_ids[None, :]).astype(jnp.float32)
    before = jnp.einsum(
        "ij,dje->die",
        lower_tri,
        onehot_all.reshape(ep_count, tok_dev, experts_all),
        precision=highest,
    ).reshape(group_rows, experts_all)
    place_all = jnp.take_along_axis(before, routes_all, axis=1).astype(jnp.int32)
    kept_all = slot_all < capacity
    kept_own = lax.dynamic_slice_in_dim(kept_all, ep_index * tok_dev, tok_dev)
    place_own = lax.dynamic_slice_in_dim(place_all, ep_index * tok_dev, tok_dev)
    buffer_index = (routes * send_most + place_own).reshape(-1)
    rows_out = jnp.where(
        kept_own[:, :, None], mid_low[:, None, :], jnp.zeros((), jnp.bfloat16)
    ).reshape(tok_dev * top_count, width)
    send_rows = (
        jnp.zeros((experts_all * send_most, width), jnp.bfloat16)
        .at[buffer_index]
        .set(rows_out)
        .reshape(experts_all, send_most, width)
    )
    received = lax.all_to_all(send_rows, "ep", split_axis=0, concat_axis=1, tiled=True)
    gate_part = jnp.einsum(
        "erd,edf->erf", received, expert_gate, preferred_element_type=jnp.float32
    )
    up_part = jnp.einsum("erd,edf->erf", received, expert_up, preferred_element_type=jnp.float32)
    hidden = (jax.nn.silu(gate_part) * up_part).astype(jnp.bfloat16)
    result = jnp.einsum(
        "erf,efd->erd", hidden, expert_down, preferred_element_type=jnp.float32
    ).astype(jnp.bfloat16)
    returned = lax.all_to_all(result, "ep", split_axis=1, concat_axis=0, tiled=True)
    pair_out = returned.reshape(experts_all * send_most, width)[buffer_index].reshape(
        tok_dev, top_count, width
    )
    pair_weight = gate_prob * kept_own.astype(jnp.float32)
    moe_out = jnp.einsum("tk,tkd->td", pair_weight, pair_out, preferred_element_type=jnp.float32)
    block_out = (after_attn + moe_out).astype(jnp.bfloat16)
    out_grad = cotangent.astype(jnp.float32)
    pair_gate_grad = kept_own.astype(jnp.float32) * jnp.einsum(
        "tkd,td->tk", pair_out, out_grad, preferred_element_type=jnp.float32
    )
    pair_grad = (
        (pair_weight[:, :, None] * out_grad[:, None, :])
        .astype(jnp.bfloat16)
        .reshape(tok_dev * top_count, width)
    )
    grad_send = (
        jnp.zeros((experts_all * send_most, width), jnp.bfloat16)
        .at[buffer_index]
        .set(pair_grad)
        .reshape(experts_all, send_most, width)
    )
    grad_received = lax.all_to_all(grad_send, "ep", split_axis=0, concat_axis=1, tiled=True)
    hidden_grad = jnp.einsum(
        "erd,efd->erf", grad_received, expert_down, preferred_element_type=jnp.float32
    )
    _, silu_pull = jax.vjp(lambda gate_in, up_in: jax.nn.silu(gate_in) * up_in, gate_part, up_part)
    gate_part_grad, up_part_grad = silu_pull(hidden_grad)
    gate_low_grad = gate_part_grad.astype(jnp.bfloat16)
    up_low_grad = up_part_grad.astype(jnp.bfloat16)
    down_term = jnp.einsum(
        "erf,erd->efd", hidden, grad_received, preferred_element_type=jnp.float32
    )
    gate_term = jnp.einsum(
        "erd,erf->edf", received, gate_low_grad, preferred_element_type=jnp.float32
    )
    up_term = jnp.einsum("erd,erf->edf", received, up_low_grad, preferred_element_type=jnp.float32)
    rows_grad = (
        jnp.einsum("erf,edf->erd", gate_low_grad, expert_gate, preferred_element_type=jnp.float32)
        + jnp.einsum("erf,edf->erd", up_low_grad, expert_up, preferred_element_type=jnp.float32)
    ).astype(jnp.bfloat16)
    back_rows = lax.all_to_all(rows_grad, "ep", split_axis=1, concat_axis=0, tiled=True)
    mid_grad = jnp.sum(
        back_rows.reshape(experts_all * send_most, width)[buffer_index]
        .reshape(tok_dev, top_count, width)
        .astype(jnp.float32),
        axis=1,
    )
    gate_w_grad, up_w_grad, down_w_grad = (
        lax.psum_scatter(
            gate_term.astype(jnp.bfloat16), "rep", scatter_dimension=1, tiled=True
        ).astype(jnp.float32),
        lax.psum_scatter(
            up_term.astype(jnp.bfloat16), "rep", scatter_dimension=1, tiled=True
        ).astype(jnp.float32),
        lax.psum_scatter(
            down_term.astype(jnp.bfloat16), "rep", scatter_dimension=1, tiled=True
        ).astype(jnp.float32),
    )
    _, soft_pull = jax.vjp(lambda values: jax.nn.softmax(values, axis=-1), chosen)
    (chosen_grad,) = soft_pull(pair_gate_grad)
    onehot_own = (routes[:, :, None] == expert_ids[None, None, :]).astype(jnp.float32)
    logit_grad = jnp.einsum("tk,tke->te", chosen_grad, onehot_own).astype(jnp.bfloat16)
    mid_grad = mid_grad + jnp.dot(logit_grad, router_full.T, preferred_element_type=jnp.float32)
    router_term = jnp.dot(mid_low.T, logit_grad, preferred_element_type=jnp.float32)
    _, mid_pull = jax.vjp(rms_scale, after_attn, gain_mid)
    after_extra, gain_mid_grad = mid_pull(mid_grad)
    after_grad = out_grad + after_extra
    attn_low_grad = after_grad.astype(jnp.bfloat16)
    output_term = jnp.dot(mixed_low.T, attn_low_grad, preferred_element_type=jnp.float32)
    mixed_grad = jnp.dot(attn_low_grad, output_full.T, preferred_element_type=jnp.float32).astype(
        jnp.bfloat16
    )
    mixed_grad_heads = mixed_grad.reshape(tok_dev, group_count, per_group, head_dim).transpose(
        1, 0, 2, 3
    )
    query_grad_h, key_grad_h, value_grad_h = lax.map(
        partial(attend_backward, same_seq=same_seq, score_scale=score_scale),
        (query_heads, key_heads, value_heads, mixed_grad_heads, top_heads, total_heads),
    )
    query_grad_own = query_grad_h.transpose(1, 0, 2, 3).reshape(tok_dev, head_count, head_dim)
    key_grad_group = key_grad_h.transpose(1, 0, 2, 3).reshape(group_rows, width)
    value_grad_group = value_grad_h.transpose(1, 0, 2, 3).reshape(group_rows, width)
    key_sum, value_sum = (
        lax.psum_scatter(
            key_grad_group.astype(jnp.bfloat16), "ep", scatter_dimension=0, tiled=True
        ).astype(jnp.float32),
        lax.psum_scatter(
            value_grad_group.astype(jnp.bfloat16), "ep", scatter_dimension=0, tiled=True
        ).astype(jnp.float32),
    )
    value_low_grad = value_sum.astype(jnp.bfloat16)
    _, query_pull = jax.vjp(
        lambda projected, gain_vec: rope_norm(projected, gain_vec, position_own),
        query_pre,
        gain_query,
    )
    query_pre_grad, gain_query_grad = query_pull(query_grad_own)
    _, key_pull = jax.vjp(
        lambda projected, gain_vec: rope_norm(projected, gain_vec, position_own), key_pre, gain_key
    )
    key_pre_grad, gain_key_grad = key_pull(key_sum.reshape(tok_dev, head_count, head_dim))
    query_low_grad = query_pre_grad.reshape(tok_dev, width).astype(jnp.bfloat16)
    key_low_grad = key_pre_grad.reshape(tok_dev, width).astype(jnp.bfloat16)
    normed_grad = jnp.dot(query_low_grad, query_full.T, preferred_element_type=jnp.float32)
    normed_grad = normed_grad + jnp.dot(
        key_low_grad, key_full.T, preferred_element_type=jnp.float32
    )
    normed_grad = normed_grad + jnp.dot(
        value_low_grad, value_full.T, preferred_element_type=jnp.float32
    )
    query_term = jnp.dot(normed_low.T, query_low_grad, preferred_element_type=jnp.float32)
    key_term = jnp.dot(normed_low.T, key_low_grad, preferred_element_type=jnp.float32)
    value_term = jnp.dot(normed_low.T, value_low_grad, preferred_element_type=jnp.float32)
    _, input_pull = jax.vjp(rms_scale, residual, gain_in)
    input_extra, gain_in_grad = input_pull(normed_grad)
    input_grad = after_grad + input_extra
    gains_term = jnp.concatenate([gain_in_grad, gain_mid_grad, gain_query_grad, gain_key_grad])
    query_sum, key_total, value_total, output_sum, router_sum, gains_sum = (
        lax.psum_scatter(query_term, ("rep", "ep"), scatter_dimension=0, tiled=True),
        lax.psum_scatter(key_term, ("rep", "ep"), scatter_dimension=0, tiled=True),
        lax.psum_scatter(value_term, ("rep", "ep"), scatter_dimension=0, tiled=True),
        lax.psum_scatter(output_term, ("rep", "ep"), scatter_dimension=0, tiled=True),
        lax.psum_scatter(router_term, ("rep", "ep"), scatter_dimension=0, tiled=True),
        lax.psum_scatter(gains_term, ("rep", "ep"), scatter_dimension=0, tiled=True),
    )
    return (
        block_out,
        input_grad,
        query_sum,
        key_total,
        value_total,
        output_sum,
        router_sum,
        gains_sum,
        gate_w_grad,
        up_w_grad,
        down_w_grad,
    )


MESH = pl.DeviceIdType.MESH


def partners(e):
    sib = e + 1 - 2 * (e % 2)
    xn = e + 2 - 4 * ((e // 2) % 2)
    yn = e + 4 - 8 * ((e // 4) % 2)
    dg = xn + 4 - 8 * ((e // 4) % 2)
    return sib, (xn, yn, dg)


def greet(z, e, reps, across):
    barrier = pltpu.get_barrier_semaphore()
    sib, chips = partners(e)
    for other in (sib, *chips):
        pl.semaphore_signal(barrier, inc=1, device_id={"rep": z, "ep": other}, device_id_type=MESH)
    if across:
        @pl.when(z > 0)
        def _():
            pl.semaphore_signal(barrier, inc=1, device_id={"rep": z - 1, "ep": e}, device_id_type=MESH)
        @pl.when(z < reps - 1)
        def _():
            pl.semaphore_signal(barrier, inc=1, device_id={"rep": z + 1, "ep": e}, device_id_type=MESH)
    peers = 4
    if across:
        peers = peers + jnp.where(z > 0, 1, 0) + jnp.where(z < reps - 1, 1, 0)
    pl.semaphore_wait(barrier, peers)


def ag_kernel(reps, across, x_ref, out_ref, own_sem, zs, zr, ps, pr, cs, cr):
    z = lax.axis_index("rep")
    e = lax.axis_index("ep")
    sib, chips = partners(e)
    greet(z, e, reps, across)
    own = z if across else 0
    groups = reps if across else 1
    half = x_ref.shape[0] // 2
    local = pltpu.make_async_copy(x_ref, out_ref.at[own, e], own_sem)
    local.start()

    def zcopy(src, g, up):
        d = 0 if up else 1
        return pltpu.make_async_remote_copy(
            src_ref=src, dst_ref=out_ref.at[g, e], send_sem=zs.at[d, g], recv_sem=zr.at[g],
            device_id={"rep": z + 1 if up else z - 1, "ep": e}, device_id_type=MESH)

    def pcopy(src, g, j):
        return pltpu.make_async_remote_copy(
            src_ref=src, dst_ref=out_ref.at[g, e], send_sem=ps.at[g, j], recv_sem=pr.at[g, j],
            device_id={"rep": z, "ep": chips[j]}, device_id_type=MESH)

    def relay(g, j):
        rows = pl.ds(half * j, half)
        part = out_ref.at[g, chips[j], rows]
        return pltpu.make_async_remote_copy(
            src_ref=part, dst_ref=part, send_sem=ps.at[g, 2 + j], recv_sem=pr.at[g, 2 + j],
            device_id={"rep": z, "ep": chips[1 - j]}, device_id_type=MESH)

    def relayed(g, j):
        part = out_ref.at[g, chips[2], pl.ds(half * j, half)]
        return pltpu.make_async_remote_copy(
            src_ref=part, dst_ref=part, send_sem=ps.at[g, 2 + j], recv_sem=pr.at[g, 2 + j],
            device_id={"rep": z, "ep": chips[1 - j]}, device_id_type=MESH)

    def ccopy(src, g, j):
        who = e if j == 0 else chips[j - 1]
        return pltpu.make_async_remote_copy(
            src_ref=src, dst_ref=out_ref.at[g, who], send_sem=cs.at[g, j], recv_sem=cr.at[g, j],
            device_id={"rep": z, "ep": sib}, device_id_type=MESH)

    def spread(src, g):
        pcopy(src, g, 0).start()
        pcopy(src, g, 1).start()
        ccopy(src, g, 0).start()

    def pass_on(g):
        for j in range(2):
            pcopy(x_ref, g, j).wait_recv()
            relay(g, j).start()
            ccopy(out_ref.at[g, chips[j]], g, j + 1).start()

    def finish(g):
        for j in range(2):
            relayed(g, j).wait_recv()
        ccopy(out_ref.at[g, chips[2]], g, 3).start()

    def at(k, fn):
        if k == 0:
            fn(own)
            return
        @pl.when(z - k >= 0)
        def _():
            fn(z - k)
        @pl.when(z + k < reps)
        def _():
            fn(z + k)

    if across:
        @pl.when(z < reps - 1)
        def _():
            zcopy(x_ref, z, True).start()
        @pl.when(z > 0)
        def _():
            zcopy(x_ref, z, False).start()
    spread(x_ref, own)
    for k in range(1, groups):
        @pl.when(z - k >= 0)
        def _():
            g = z - k
            zcopy(x_ref, g, True).wait_recv()
            @pl.when(z < reps - 1)
            def _():
                zcopy(out_ref.at[g, e], g, True).start()
            spread(out_ref.at[g, e], g)
        @pl.when(z + k < reps)
        def _():
            g = z + k
            zcopy(x_ref, g, False).wait_recv()
            @pl.when(z > 0)
            def _():
                zcopy(out_ref.at[g, e], g, False).start()
            spread(out_ref.at[g, e], g)
        at(k - 1, pass_on)
        if k >= 2:
            at(k - 2, finish)
    at(groups - 1, pass_on)
    if groups >= 2:
        at(groups - 2, finish)
    at(groups - 1, finish)
    local.wait()
    for g in range(groups):
        for j in range(4):
            ccopy(x_ref, g, j).wait()
        for j in range(2):
            pcopy(x_ref, g, j).wait_send()
            relay(g, j).wait_send()
        if across:
            @pl.when((z < reps - 1) & (z >= g))
            def _():
                zcopy(x_ref, g, True).wait_send()
            @pl.when((z > 0) & (z <= g))
            def _():
                zcopy(x_ref, g, False).wait_send()


def all_gather(x, reps, eps, across, cid):
    groups = reps if across else 1
    D = pltpu.SemaphoreType.DMA
    out = pl.pallas_call(
        partial(ag_kernel, reps, across),
        out_shape=jax.ShapeDtypeStruct((groups, eps, *x.shape), x.dtype),
        in_specs=[pl.BlockSpec(memory_space=pl.ANY)],
        out_specs=pl.BlockSpec(memory_space=pl.ANY),
        scratch_shapes=[D, D((2, reps)), D((reps,)), D((groups, 4)), D((groups, 4)), D((groups, 4)), D((groups, 4))],
        compiler_params=pltpu.CompilerParams(collective_id=cid, has_side_effects=True),
    )(x)
    return out


def rs_kernel(reps, across, p_ref, out_ref, own, sib_in, chip_in, up_in, down_in, res,
              own_sem, ss, sr, ps, pr, us, ur, ds, dr):
    z = lax.axis_index("rep")
    e = lax.axis_index("ep")
    core = e % 2
    chip = e // 2
    sib, chips = partners(e)
    groups = reps if across else 1
    greet(z, e, reps, across)
    rows, W = res.shape[1], res.shape[2]
    half = reps // 2

    def order(s):
        if not across:
            return 0
        t = reps - 1 - s
        down = jnp.where(t > z, t, t - 1)
        upw = jnp.where(s < z, s, s + 1)
        g = jnp.where(z < half, down, upw)
        return z if s == reps - 1 else g

    def sibcopy(g):
        return pltpu.make_async_remote_copy(
            src_ref=p_ref.at[g, :, 1 - core], dst_ref=sib_in.at[g], send_sem=ss.at[g], recv_sem=sr.at[g],
            device_id={"rep": z, "ep": sib}, device_id_type=MESH)

    def load(g):
        return pltpu.make_async_copy(p_ref.at[g, :, core], own.at[g], own_sem.at[g])

    def pcopy(g, j):
        return pltpu.make_async_remote_copy(
            src_ref=own.at[g, chips[j] // 2], dst_ref=chip_in.at[g, j], send_sem=ps.at[g, j], recv_sem=pr.at[g, j],
            device_id={"rep": z, "ep": chips[j]}, device_id_type=MESH)

    def zcopy(g, up):
        if up:
            return pltpu.make_async_remote_copy(
                src_ref=res.at[g], dst_ref=up_in.at[g], send_sem=us.at[g], recv_sem=ur.at[g],
                device_id={"rep": z + 1, "ep": e}, device_id_type=MESH)
        return pltpu.make_async_remote_copy(
            src_ref=res.at[g], dst_ref=down_in.at[g], send_sem=ds.at[g], recv_sem=dr.at[g],
            device_id={"rep": z - 1, "ep": e}, device_id_type=MESH)

    for s in range(groups):
        g = order(s)
        sibcopy(g).start()
        load(g).start()
    step = 16

    def add_in(g, q):
        @pl.loop(0, rows // step)
        def _(i):
            r = pl.ds(pl.multiple_of(i * step, step), step)
            own[g, q, r, :] = (own[g, q, r, :].astype(jnp.float32) + sib_in[g, q, r, :].astype(jnp.float32)).astype(own.dtype)

    def stage1(g):
        load(g).wait()
        sibcopy(g).wait_recv()
        for j in (2, 0, 1):
            add_in(g, chips[j] // 2)
            pcopy(g, j).start()

    def stage2(g):
        for j in range(3):
            pcopy(g, j).wait_recv()
        @pl.loop(0, rows // step)
        def _(i):
            r = pl.ds(pl.multiple_of(i * step, step), step)
            t = own[g, chip, r, :].astype(jnp.float32) + sib_in[g, chip, r, :].astype(jnp.float32)
            for j in range(3):
                t = t + chip_in[g, j, r, :].astype(jnp.float32)
            res[g, r, :] = t.astype(res.dtype)

    def plus(g, ref):
        @pl.loop(0, rows // step)
        def _(i):
            r = pl.ds(pl.multiple_of(i * step, step), step)
            res[g, r, :] = (res[g, r, :].astype(jnp.float32) + ref[g, r, :].astype(jnp.float32)).astype(res.dtype)

    def stage3(g):
        @pl.when(g > z)
        def _():
            @pl.when(z > 0)
            def _():
                zcopy(g, True).wait_recv()
                plus(g, up_in)
            zcopy(g, True).start()
        @pl.when(g < z)
        def _():
            @pl.when(z < reps - 1)
            def _():
                zcopy(g, False).wait_recv()
                plus(g, down_in)
            zcopy(g, False).start()

    stage1(order(0))
    for s in range(1, groups):
        stage1(order(s))
        stage2(order(s - 1))
        if s >= 2:
            stage3(order(s - 2))
    stage2(order(groups - 1))
    if across:
        stage3(order(groups - 2))
        @pl.when(z > 0)
        def _():
            zcopy(z, True).wait_recv()
            plus(z, up_in)
        @pl.when(z < reps - 1)
        def _():
            zcopy(z, False).wait_recv()
            plus(z, down_in)
    fin = res.at[z if across else 0]
    out = pltpu.make_async_copy(fin, out_ref, own_sem.at[0])
    out.start()
    out.wait()
    for g in range(groups):
        sibcopy(g).wait_send()
        for j in range(3):
            pcopy(g, j).wait_send()
        if across:
            @pl.when(g > z)
            def _():
                zcopy(g, True).wait_send()
            @pl.when(g < z)
            def _():
                zcopy(g, False).wait_send()


def reduce_scatter(p, reps, eps, across, cid):
    groups = reps if across else 1
    W = p.shape[1]
    rows = p.shape[0] // groups // eps
    p = p.reshape(groups, eps // 2, 2, rows, W)
    D = pltpu.SemaphoreType.DMA
    V = pltpu.VMEM
    q = eps // 2
    return pl.pallas_call(
        partial(rs_kernel, reps, across),
        out_shape=jax.ShapeDtypeStruct((rows, W), p.dtype),
        in_specs=[pl.BlockSpec(memory_space=pl.ANY)],
        out_specs=pl.BlockSpec(memory_space=pl.ANY),
        scratch_shapes=[V((groups, q, rows, W), p.dtype), V((groups, q, rows, W), p.dtype), V((groups, 3, rows, W), p.dtype),
                        V((groups, rows, W), p.dtype), V((groups, rows, W), p.dtype), V((groups, rows, W), p.dtype),
                        D((groups,)), D((groups,)), D((groups,)), D((groups, 3)), D((groups, 3)),
                        D((groups,)), D((groups,)), D((groups,)), D((groups,))],
        compiler_params=pltpu.CompilerParams(collective_id=cid, has_side_effects=True, vmem_limit_bytes=56 * 2**20),
    )(p)

def gather_block(block, axes):
    return lax.all_gather(block, axes, axis=0, tiled=True)


def scatter_sum(partial_sums, axes):
    return lax.psum_scatter(partial_sums, axes, scatter_dimension=0, tiled=True)


def on_device_split(
    tokens,
    cotangent,
    query_weight,
    key_weight,
    value_weight,
    output_weight,
    router_weight,
    gains,
    expert_gate,
    expert_up,
    expert_down,
    lengths,
    deal,
    routes,
    priority,
):
    bf16, f32 = jnp.bfloat16, jnp.float32
    tok_dev, width = tokens.shape
    ep_count, rep_count = lax.axis_size("ep"), lax.axis_size("rep")
    ep_index, rep_index = lax.axis_index("ep"), lax.axis_index("rep")
    exp_dev, _, ff_width = expert_gate.shape
    top_count = routes.shape[1]
    experts_all = exp_dev * ep_count
    group_rows = tok_dev * ep_count
    capacity = 5 * tok_dev * top_count // (4 * exp_dev)
    head_dim = HD
    heads_dev = width // head_dim // ep_count
    slice_width = heads_dev * head_dim
    rows_dev = query_weight.shape[0]
    ff_slice = ff_width // rep_count
    score_scale = head_dim ** (-0.5)
    core = ep_index % 2
    every = ("rep", "ep")

    gains_dev = gains.shape[0]
    packed = jnp.concatenate(
        [gains, router_weight.reshape(-1), jnp.zeros((2048 - gains_dev - router_weight.size,), bf16)]
    ).reshape(16, 128)
    packed_all = gather_block(packed, every).reshape(rep_count * ep_count, 2048)
    gains_float = packed_all[:, :gains_dev].reshape(-1).astype(f32)
    router_full = packed_all[:, gains_dev : gains_dev + router_weight.size].reshape(width, experts_all)
    gain_in = gains_float[:width]
    gain_mid = gains_float[width : 2 * width]
    gain_query = gains_float[2 * width : 2 * width + head_dim]
    gain_key = gains_float[2 * width + head_dim :]
    numbers = jnp.concatenate([deal, priority, routes.T.reshape(-1)]).reshape(-1, 128)
    numbers_all = gather_block(numbers, "ep").reshape(ep_count, -1, tok_dev)
    deal_all = numbers_all[:, 0].reshape(-1)
    priority_all = numbers_all[:, 1].reshape(-1)
    routes_all = numbers_all[:, 2:].transpose(0, 2, 1).reshape(group_rows, top_count)
    segment_all, position_all = placement(deal_all, lengths[0])

    chips = ep_count // 2
    def columns_of(weight):
        parts = weight.reshape(rows_dev, 2, heads_dev, chips, head_dim).transpose(3, 1, 0, 2, 4)
        parts = parts.reshape(ep_count, rows_dev, slice_width)
        return lax.all_to_all(parts, "ep", split_axis=0, concat_axis=0, tiled=True)

    qkv_rows = jnp.concatenate(
        [columns_of(query_weight), columns_of(key_weight), columns_of(value_weight)], axis=2
    ).reshape(ep_count * rows_dev, 3 * slice_width)
    qkv_slice = gather_block(qkv_rows, "rep")
    out_rows = gather_block(output_weight, "rep").reshape(2, heads_dev, rows_dev, width)
    out_own = lax.dynamic_index_in_dim(out_rows, core, 0, keepdims=False)
    out_other = lax.ppermute(
        lax.dynamic_index_in_dim(out_rows, 1 - core, 0, keepdims=False),
        "ep",
        [(i, i + 1 - 2 * (i % 2)) for i in range(ep_count)],
    )
    out_slice = jnp.where(
        core == 0,
        jnp.concatenate([out_own, out_other], axis=1),
        jnp.concatenate([out_other, out_own], axis=1),
    ).reshape(slice_width, width)

    cot_all = all_gather(cotangent, rep_count, ep_count, True, 0).reshape(-1, width)
    tokens_group = (
        all_gather(tokens, rep_count, ep_count, False, 1).reshape(group_rows, width).astype(f32)
    )
    normed_group = rms_scale(tokens_group, gain_in).astype(bf16)
    projected = jnp.dot(normed_group, qkv_slice, preferred_element_type=f32)
    query_pre = projected[:, :slice_width].reshape(group_rows, heads_dev, head_dim)
    key_pre = projected[:, slice_width : 2 * slice_width].reshape(group_rows, heads_dev, head_dim)
    value_low = projected[:, 2 * slice_width :].astype(bf16).reshape(group_rows, heads_dev, head_dim)
    query_low = rope_norm(query_pre, gain_query, position_all).astype(bf16)
    key_low = rope_norm(key_pre, gain_key, position_all).astype(bf16)
    same_seq = segment_all[:, None] == segment_all[None, :]
    mixed, top_score, total_sum = attend_forward(
        (query_low, key_low, value_low), same_seq, score_scale
    )
    mixed_low = mixed.reshape(group_rows, slice_width).astype(bf16)
    attn_part = jnp.dot(mixed_low, out_slice, preferred_element_type=f32).astype(bf16)
    residual = tokens.astype(f32)
    after_attn = residual + reduce_scatter(attn_part, rep_count, ep_count, False, 2).astype(f32)
    mid_low = rms_scale(after_attn, gain_mid).astype(bf16)

    logits = jnp.dot(mid_low, router_full, preferred_element_type=f32)
    expert_ids = jnp.arange(experts_all, dtype=jnp.int32)
    member = (routes[:, :, None] == expert_ids[None, None, :]).astype(f32)
    named = jnp.sum(member, axis=1)
    lifted = jnp.where(named > 0, logits, masked_score)
    lifted = jnp.exp(lifted - jnp.max(lifted, axis=-1, keepdims=True)) * named
    gate_dense = lifted / jnp.sum(lifted, axis=-1, keepdims=True)
    onehot_all = jnp.sum(
        (routes_all[:, :, None] == expert_ids[None, None, :]).astype(bf16), axis=1
    )
    earlier = (priority_all[None, :] < priority[:, None]).astype(bf16)
    slots = jnp.dot(earlier, onehot_all, preferred_element_type=f32)
    kept_dense = named * (slots < capacity).astype(f32)
    pair_weight = gate_dense * kept_dense

    weight_high = pair_weight.astype(bf16)
    weight_low = (pair_weight - weight_high.astype(f32)).astype(bf16)
    side = jnp.concatenate(
        [weight_high, weight_low, jnp.zeros((tok_dev, 128 - 2 * experts_all), bf16)], axis=1
    )
    sent = all_gather(
        jnp.concatenate([mid_low, side], axis=1), rep_count, ep_count, True, 3
    ).reshape(-1, width + 128)
    mid_all = sent[:, :width]
    side_all = sent[:, width:]
    weight_own = lax.dynamic_slice_in_dim(side_all, ep_index * exp_dev, exp_dev, axis=1).astype(
        f32
    ) + lax.dynamic_slice_in_dim(
        side_all, experts_all + ep_index * exp_dev, exp_dev, axis=1
    ).astype(f32)
    gate_slice = lax.dynamic_slice_in_dim(expert_gate, rep_index * ff_slice, ff_slice, axis=2)
    up_slice = lax.dynamic_slice_in_dim(expert_up, rep_index * ff_slice, ff_slice, axis=2)
    down_slice = lax.dynamic_slice_in_dim(expert_down, rep_index * ff_slice, ff_slice, axis=1)
    gate_flat = gate_slice.transpose(1, 0, 2).reshape(width, exp_dev * ff_slice)
    up_flat = up_slice.transpose(1, 0, 2).reshape(width, exp_dev * ff_slice)
    down_flat = down_slice.reshape(exp_dev * ff_slice, width)
    gate_part = jnp.dot(mid_all, gate_flat, preferred_element_type=f32)
    up_part = jnp.dot(mid_all, up_flat, preferred_element_type=f32)
    down_cot = jnp.dot(cot_all, down_flat.T, preferred_element_type=f32)
    weight_wide = jnp.repeat(weight_own, ff_slice, axis=1)
    sigma = jax.nn.sigmoid(gate_part)
    silu = gate_part * sigma
    hidden = (silu * up_part).astype(bf16).astype(f32)
    hidden_weighted = (hidden * weight_wide).astype(bf16)
    hidden_cot = weight_wide * down_cot
    a_cot = (hidden_cot * up_part * (sigma * (1 + gate_part * (1 - sigma)))).astype(bf16)
    b_cot = (hidden_cot * silu).astype(bf16)
    row_part = (
        jnp.dot(a_cot, gate_flat.T, preferred_element_type=f32)
        + jnp.dot(b_cot, up_flat.T, preferred_element_type=f32)
    ).astype(bf16)
    gate_cot_own = jnp.sum((hidden * down_cot).reshape(-1, exp_dev, ff_slice), axis=2)
    gate_cot_part = lax.dynamic_update_slice_in_dim(
        jnp.zeros((gate_cot_own.shape[0], 128), bf16),
        gate_cot_own.astype(bf16),
        ep_index * exp_dev,
        axis=1,
    )
    row_sum = reduce_scatter(
        jnp.concatenate([row_part, gate_cot_part], axis=1), rep_count, ep_count, True, 4
    )
    moe_part = jnp.dot(hidden_weighted, down_flat, preferred_element_type=f32).astype(bf16)
    moe_out = reduce_scatter(moe_part, rep_count, ep_count, True, 5).astype(f32)
    block_out = (after_attn + moe_out).astype(bf16)
    gate_term = jnp.dot(mid_all.T, a_cot, preferred_element_type=f32)
    up_term = jnp.dot(mid_all.T, b_cot, preferred_element_type=f32)
    down_w_grad = jnp.dot(hidden_weighted.T, cot_all, preferred_element_type=f32).reshape(
        exp_dev, ff_slice, width
    )

    def rows_of(term):
        parts = term.astype(bf16).reshape(rep_count, width // rep_count, exp_dev, ff_slice)
        parts = parts.transpose(0, 2, 1, 3)
        got = lax.all_to_all(parts, "rep", split_axis=0, concat_axis=0, tiled=True)
        return got.transpose(1, 2, 0, 3).reshape(exp_dev, width // rep_count, ff_width).astype(f32)

    gate_w_grad = rows_of(gate_term)
    up_w_grad = rows_of(up_term)

    out_grad = cotangent.astype(f32)
    gate_cot = row_sum[:, width : width + experts_all].astype(f32) * kept_dense
    chosen_cot = gate_dense * (gate_cot - jnp.sum(gate_dense * gate_cot, axis=-1, keepdims=True))
    logit_cot = chosen_cot.astype(bf16)
    mid_cot = row_sum[:, :width].astype(f32) + jnp.dot(
        logit_cot, router_full.T, preferred_element_type=f32
    )
    router_term = jnp.dot(mid_low.T, logit_cot, preferred_element_type=f32)
    _, mid_pull = jax.vjp(rms_scale, after_attn, gain_mid)
    after_extra, gain_mid_cot = mid_pull(mid_cot)
    after_cot = out_grad + after_extra
    attn_cot_group = all_gather(
        after_cot.astype(bf16), rep_count, ep_count, False, 6
    ).reshape(group_rows, width)

    mixed_cot = jnp.dot(attn_cot_group, out_slice.T, preferred_element_type=f32).astype(bf16)
    output_term = jnp.dot(mixed_low.T, attn_cot_group, preferred_element_type=f32)
    query_cot, key_cot, value_cot = attend_backward(
        (
            query_low,
            key_low,
            value_low,
            mixed_cot.reshape(group_rows, heads_dev, head_dim),
            top_score,
            total_sum,
        ),
        same_seq,
        score_scale,
    )
    _, query_pull = jax.vjp(
        lambda pre, gain_vec: rope_norm(pre, gain_vec, position_all), query_pre, gain_query
    )
    query_pre_cot, gain_query_cot = query_pull(query_cot)
    _, key_pull = jax.vjp(
        lambda pre, gain_vec: rope_norm(pre, gain_vec, position_all), key_pre, gain_key
    )
    key_pre_cot, gain_key_cot = key_pull(key_cot)
    pre_cot = jnp.concatenate(
        [
            part.reshape(group_rows, slice_width).astype(bf16)
            for part in (query_pre_cot, key_pre_cot, value_cot)
        ],
        axis=1,
    )
    normed_part = jnp.dot(pre_cot, qkv_slice.T, preferred_element_type=f32).astype(bf16)
    normed_cot = reduce_scatter(normed_part, rep_count, ep_count, False, 7).astype(f32)
    _, input_pull = jax.vjp(rms_scale, residual, gain_in)
    input_extra, gain_in_cot = input_pull(normed_cot)
    input_grad = after_cot + input_extra
    qkv_term = jnp.dot(normed_group.T, pre_cot, preferred_element_type=f32)

    qkv_sum = scatter_sum(qkv_term.astype(bf16), "rep").reshape(ep_count, rows_dev, 3, slice_width)

    def whole_rows(part):
        got = lax.all_to_all(part, "ep", split_axis=0, concat_axis=0, tiled=True)
        got = got.reshape(chips, 2, rows_dev, heads_dev, head_dim).transpose(2, 1, 3, 0, 4)
        return got.reshape(rows_dev, width).astype(f32)

    query_sum, key_sum, value_sum = (whole_rows(qkv_sum[:, :, i]) for i in range(3))
    out_halves = output_term.astype(bf16).reshape(heads_dev, 2, rows_dev, width)
    out_keep = lax.dynamic_index_in_dim(out_halves, core, 1, keepdims=False)
    out_pass = lax.ppermute(
        lax.dynamic_index_in_dim(out_halves, 1 - core, 1, keepdims=False),
        "ep",
        [(i, i + 1 - 2 * (i % 2)) for i in range(ep_count)],
    )
    out_parts = jnp.where(
        core == 0, jnp.stack([out_keep, out_pass]), jnp.stack([out_pass, out_keep])
    ).reshape(2 * heads_dev * rows_dev, width)
    output_sum = scatter_sum(out_parts, "rep").astype(f32)
    gains_term = jnp.concatenate([gain_in_cot, gain_mid_cot, gain_query_cot, gain_key_cot])
    small_term = jnp.concatenate(
        [
            gains_term.reshape(rep_count * ep_count, gains_dev),
            router_term.reshape(rep_count * ep_count, router_weight.size),
            jnp.zeros((rep_count * ep_count, 2048 - gains_dev - router_weight.size), f32),
        ],
        axis=1,
    ).reshape(rep_count * ep_count * 16, 128)
    small_sum = scatter_sum(small_term, every).reshape(-1)
    gains_sum = small_sum[:gains_dev]
    router_sum = small_sum[gains_dev : gains_dev + router_weight.size].reshape(
        rows_dev, experts_all
    )
    return (
        block_out,
        input_grad,
        query_sum,
        key_sum,
        value_sum,
        output_sum,
        router_sum,
        gains_sum,
        gate_w_grad,
        up_w_grad,
        down_w_grad,
    )


def solution(mesh):
    placed = (
        P(("rep", "ep"), None),
        P(("rep", "ep"), None),
        P(("rep", "ep"), None),
        P(("rep", "ep"), None),
        P(("rep", "ep"), None),
        P(("rep", "ep"), None),
        P(("rep", "ep"), None),
        P(("rep", "ep")),
        P("ep", None, None),
        P("ep", None, None),
        P("ep", None, None),
        P("rep", None),
        P(("rep", "ep")),
        P(("rep", "ep"), None),
        P(("rep", "ep")),
    )
    return jax.shard_map(
        on_device_split if mesh.shape["rep"] == 4 else on_device_general,
        mesh=mesh,
        in_specs=placed,
        out_specs=(
            P(("rep", "ep"), None),
            P(("rep", "ep"), None),
            P(("rep", "ep"), None),
            P(("rep", "ep"), None),
            P(("rep", "ep"), None),
            P(("rep", "ep"), None),
            P(("rep", "ep"), None),
            P(("rep", "ep")),
            P("ep", "rep", None),
            P("ep", "rep", None),
            P("ep", "rep", None),
        ),
        check_vma=False,
    )
```

```python
from functools import partial

import jax
import jax.numpy as jnp
from jax import lax
from jax.experimental import pallas as pl
from jax.experimental.pallas import tpu as pltpu
from jax.sharding import PartitionSpec as P

HD = 128


norm_eps = 1e-06
rope_base = 10000.0
masked_score = -1e30
highest = lax.Precision.HIGHEST


def rms_scale(values, gain_vec):
    return (
        values * lax.rsqrt(jnp.mean(values * values, axis=-1, keepdims=True) + norm_eps) * gain_vec
    )


def rotate(values, positions):
    half_width = values.shape[-1] // 2
    frequency = rope_base ** (-2.0 * jnp.arange(half_width, dtype=jnp.float32) / values.shape[-1])
    angles = positions.astype(jnp.float32)[:, None] * frequency[None, :]
    cosine = jnp.cos(angles)[:, None, :]
    sine_part = jnp.sin(angles)[:, None, :]
    low_half = values[..., :half_width]
    high_half = values[..., half_width:]
    return jnp.concatenate(
        [low_half * cosine - high_half * sine_part, high_half * cosine + low_half * sine_part],
        axis=-1,
    )


def placement(deal_rows, lengths_row):
    seq_ends = jnp.cumsum(lengths_row)
    is_after = (seq_ends[None, :] <= deal_rows[:, None]).astype(jnp.int32)
    segment = jnp.sum(is_after, axis=1)
    seq_start = jnp.sum(is_after * lengths_row[None, :], axis=1)
    return (segment, deal_rows - seq_start)


def rope_norm(projected, gain_vec, positions):
    return rotate(rms_scale(projected, gain_vec), positions)


def attend_forward(parts, same_seq, score_scale):
    head_query, head_key, head_value = parts
    scores = (
        jnp.einsum("thd,shd->hts", head_query, head_key, preferred_element_type=jnp.float32)
        * score_scale
    )
    scores = jnp.where(same_seq[None], scores, masked_score)
    top_score = jnp.max(scores, axis=-1, keepdims=True)
    lifted = jnp.exp(scores - top_score)
    total_sum = jnp.sum(lifted, axis=-1, keepdims=True)
    prob_low = (lifted / total_sum).astype(jnp.bfloat16)
    mixed_out = jnp.einsum("hts,shd->thd", prob_low, head_value, preferred_element_type=jnp.float32)
    return (mixed_out, top_score, total_sum)


def attend_backward(parts, same_seq, score_scale):
    head_query, head_key, head_value, head_grad, top_score, total_sum = parts
    scores = (
        jnp.einsum("thd,shd->hts", head_query, head_key, preferred_element_type=jnp.float32)
        * score_scale
    )
    scores = jnp.where(same_seq[None], scores, masked_score)
    prob_full = jnp.exp(scores - top_score) / total_sum
    prob_low = prob_full.astype(jnp.bfloat16)
    prob_grad = jnp.einsum(
        "thd,shd->hts", head_grad, head_value, preferred_element_type=jnp.float32
    )
    row_dot = jnp.sum(prob_full * prob_grad, axis=-1, keepdims=True)
    score_grad = (prob_full * (prob_grad - row_dot)).astype(jnp.bfloat16)
    query_grad = (
        jnp.einsum("hts,shd->thd", score_grad, head_key, preferred_element_type=jnp.float32)
        * score_scale
    )
    key_grad = (
        jnp.einsum("hts,thd->shd", score_grad, head_query, preferred_element_type=jnp.float32)
        * score_scale
    )
    value_grad = jnp.einsum("hts,thd->shd", prob_low, head_grad, preferred_element_type=jnp.float32)
    return (query_grad, key_grad, value_grad)


def on_device_general(
    tokens,
    cotangent,
    query_weight,
    key_weight,
    value_weight,
    output_weight,
    router_weight,
    gains,
    expert_gate,
    expert_up,
    expert_down,
    lengths,
    deal,
    routes,
    priority,
):
    tok_dev, width = tokens.shape
    ep_count = lax.axis_size("ep")
    ep_index = lax.axis_index("ep")
    exp_dev = expert_gate.shape[0]
    top_count = routes.shape[1]
    experts_all = exp_dev * ep_count
    group_rows = tok_dev * ep_count
    send_most = min(tok_dev, 3 * tok_dev * top_count // (2 * experts_all))
    capacity = 5 * tok_dev * top_count // (4 * exp_dev)
    head_dim = HD
    head_count = width // head_dim
    per_group = min(head_count, 4)
    group_count = head_count // per_group
    score_scale = head_dim ** (-0.5)
    query_full, key_full, value_full, output_full, router_full, gains_full = (
        lax.all_gather(query_weight, ("rep", "ep"), axis=0, tiled=True),
        lax.all_gather(key_weight, ("rep", "ep"), axis=0, tiled=True),
        lax.all_gather(value_weight, ("rep", "ep"), axis=0, tiled=True),
        lax.all_gather(output_weight, ("rep", "ep"), axis=0, tiled=True),
        lax.all_gather(router_weight, ("rep", "ep"), axis=0, tiled=True),
        lax.all_gather(gains, ("rep", "ep"), axis=0, tiled=True),
    )
    gains_float = gains_full.astype(jnp.float32)
    gain_in = gains_float[:width]
    gain_mid = gains_float[width : 2 * width]
    gain_query = gains_float[2 * width : 2 * width + head_dim]
    gain_key = gains_float[2 * width + head_dim :]
    deal_all, priority_all, routes_all = (
        lax.all_gather(deal, "ep", axis=0, tiled=True),
        lax.all_gather(priority, "ep", axis=0, tiled=True),
        lax.all_gather(routes, "ep", axis=0, tiled=True),
    )
    segment_all, position_all = placement(deal_all, lengths[0])
    segment_own = lax.dynamic_slice_in_dim(segment_all, ep_index * tok_dev, tok_dev)
    position_own = lax.dynamic_slice_in_dim(position_all, ep_index * tok_dev, tok_dev)
    residual = tokens.astype(jnp.float32)
    normed_low = rms_scale(residual, gain_in).astype(jnp.bfloat16)
    query_pre = jnp.dot(normed_low, query_full, preferred_element_type=jnp.float32).reshape(
        tok_dev, head_count, head_dim
    )
    key_pre = jnp.dot(normed_low, key_full, preferred_element_type=jnp.float32).reshape(
        tok_dev, head_count, head_dim
    )
    value_low = jnp.dot(normed_low, value_full, preferred_element_type=jnp.float32).astype(
        jnp.bfloat16
    )
    query_low = rope_norm(query_pre, gain_query, position_own).astype(jnp.bfloat16)
    key_low = (
        rope_norm(key_pre, gain_key, position_own).astype(jnp.bfloat16).reshape(tok_dev, width)
    )
    key_group, value_group = (
        lax.all_gather(key_low, "ep", axis=0, tiled=True),
        lax.all_gather(value_low, "ep", axis=0, tiled=True),
    )
    same_seq = segment_own[:, None] == segment_all[None, :]
    query_heads = query_low.reshape(tok_dev, group_count, per_group, head_dim).transpose(1, 0, 2, 3)
    key_heads = key_group.reshape(group_rows, group_count, per_group, head_dim).transpose(
        1, 0, 2, 3
    )
    value_heads = value_group.reshape(group_rows, group_count, per_group, head_dim).transpose(
        1, 0, 2, 3
    )
    mixed_heads, top_heads, total_heads = lax.map(
        partial(attend_forward, same_seq=same_seq, score_scale=score_scale),
        (query_heads, key_heads, value_heads),
    )
    mixed_low = mixed_heads.transpose(1, 0, 2, 3).reshape(tok_dev, width).astype(jnp.bfloat16)
    after_attn = residual + jnp.dot(mixed_low, output_full, preferred_element_type=jnp.float32)
    mid_low = rms_scale(after_attn, gain_mid).astype(jnp.bfloat16)
    logits = jnp.dot(mid_low, router_full, preferred_element_type=jnp.float32)
    chosen = jnp.take_along_axis(logits, routes, axis=1)
    gate_prob = jax.nn.softmax(chosen, axis=-1)
    expert_ids = jnp.arange(experts_all, dtype=jnp.int32)
    onehot_all = jnp.sum(
        (routes_all[:, :, None] == expert_ids[None, None, :]).astype(jnp.float32), axis=1
    )
    earlier = (priority_all[None, :] < priority_all[:, None]).astype(jnp.float32)
    slot_all = jnp.take_along_axis(
        jnp.dot(earlier, onehot_all, precision=highest), routes_all, axis=1
    ).astype(jnp.int32)
    row_ids = jnp.arange(tok_dev, dtype=jnp.int32)
    lower_tri = (row_ids[:, None] > row_ids[None, :]).astype(jnp.float32)
    before = jnp.einsum(
        "ij,dje->die",
        lower_tri,
        onehot_all.reshape(ep_count, tok_dev, experts_all),
        precision=highest,
    ).reshape(group_rows, experts_all)
    place_all = jnp.take_along_axis(before, routes_all, axis=1).astype(jnp.int32)
    kept_all = slot_all < capacity
    kept_own = lax.dynamic_slice_in_dim(kept_all, ep_index * tok_dev, tok_dev)
    place_own = lax.dynamic_slice_in_dim(place_all, ep_index * tok_dev, tok_dev)
    buffer_index = (routes * send_most + place_own).reshape(-1)
    rows_out = jnp.where(
        kept_own[:, :, None], mid_low[:, None, :], jnp.zeros((), jnp.bfloat16)
    ).reshape(tok_dev * top_count, width)
    send_rows = (
        jnp.zeros((experts_all * send_most, width), jnp.bfloat16)
        .at[buffer_index]
        .set(rows_out)
        .reshape(experts_all, send_most, width)
    )
    received = lax.all_to_all(send_rows, "ep", split_axis=0, concat_axis=1, tiled=True)
    gate_part = jnp.einsum(
        "erd,edf->erf", received, expert_gate, preferred_element_type=jnp.float32
    )
    up_part = jnp.einsum("erd,edf->erf", received, expert_up, preferred_element_type=jnp.float32)
    hidden = (jax.nn.silu(gate_part) * up_part).astype(jnp.bfloat16)
    result = jnp.einsum(
        "erf,efd->erd", hidden, expert_down, preferred_element_type=jnp.float32
    ).astype(jnp.bfloat16)
    returned = lax.all_to_all(result, "ep", split_axis=1, concat_axis=0, tiled=True)
    pair_out = returned.reshape(experts_all * send_most, width)[buffer_index].reshape(
        tok_dev, top_count, width
    )
    pair_weight = gate_prob * kept_own.astype(jnp.float32)
    moe_out = jnp.einsum("tk,tkd->td", pair_weight, pair_out, preferred_element_type=jnp.float32)
    block_out = (after_attn + moe_out).astype(jnp.bfloat16)
    out_grad = cotangent.astype(jnp.float32)
    pair_gate_grad = kept_own.astype(jnp.float32) * jnp.einsum(
        "tkd,td->tk", pair_out, out_grad, preferred_element_type=jnp.float32
    )
    pair_grad = (
        (pair_weight[:, :, None] * out_grad[:, None, :])
        .astype(jnp.bfloat16)
        .reshape(tok_dev * top_count, width)
    )
    grad_send = (
        jnp.zeros((experts_all * send_most, width), jnp.bfloat16)
        .at[buffer_index]
        .set(pair_grad)
        .reshape(experts_all, send_most, width)
    )
    grad_received = lax.all_to_all(grad_send, "ep", split_axis=0, concat_axis=1, tiled=True)
    hidden_grad = jnp.einsum(
        "erd,efd->erf", grad_received, expert_down, preferred_element_type=jnp.float32
    )
    _, silu_pull = jax.vjp(lambda gate_in, up_in: jax.nn.silu(gate_in) * up_in, gate_part, up_part)
    gate_part_grad, up_part_grad = silu_pull(hidden_grad)
    gate_low_grad = gate_part_grad.astype(jnp.bfloat16)
    up_low_grad = up_part_grad.astype(jnp.bfloat16)
    down_term = jnp.einsum(
        "erf,erd->efd", hidden, grad_received, preferred_element_type=jnp.float32
    )
    gate_term = jnp.einsum(
        "erd,erf->edf", received, gate_low_grad, preferred_element_type=jnp.float32
    )
    up_term = jnp.einsum("erd,erf->edf", received, up_low_grad, preferred_element_type=jnp.float32)
    rows_grad = (
        jnp.einsum("erf,edf->erd", gate_low_grad, expert_gate, preferred_element_type=jnp.float32)
        + jnp.einsum("erf,edf->erd", up_low_grad, expert_up, preferred_element_type=jnp.float32)
    ).astype(jnp.bfloat16)
    back_rows = lax.all_to_all(rows_grad, "ep", split_axis=1, concat_axis=0, tiled=True)
    mid_grad = jnp.sum(
        back_rows.reshape(experts_all * send_most, width)[buffer_index]
        .reshape(tok_dev, top_count, width)
        .astype(jnp.float32),
        axis=1,
    )
    gate_w_grad, up_w_grad, down_w_grad = (
        lax.psum_scatter(
            gate_term.astype(jnp.bfloat16), "rep", scatter_dimension=1, tiled=True
        ).astype(jnp.float32),
        lax.psum_scatter(
            up_term.astype(jnp.bfloat16), "rep", scatter_dimension=1, tiled=True
        ).astype(jnp.float32),
        lax.psum_scatter(
            down_term.astype(jnp.bfloat16), "rep", scatter_dimension=1, tiled=True
        ).astype(jnp.float32),
    )
    _, soft_pull = jax.vjp(lambda values: jax.nn.softmax(values, axis=-1), chosen)
    (chosen_grad,) = soft_pull(pair_gate_grad)
    onehot_own = (routes[:, :, None] == expert_ids[None, None, :]).astype(jnp.float32)
    logit_grad = jnp.einsum("tk,tke->te", chosen_grad, onehot_own).astype(jnp.bfloat16)
    mid_grad = mid_grad + jnp.dot(logit_grad, router_full.T, preferred_element_type=jnp.float32)
    router_term = jnp.dot(mid_low.T, logit_grad, preferred_element_type=jnp.float32)
    _, mid_pull = jax.vjp(rms_scale, after_attn, gain_mid)
    after_extra, gain_mid_grad = mid_pull(mid_grad)
    after_grad = out_grad + after_extra
    attn_low_grad = after_grad.astype(jnp.bfloat16)
    output_term = jnp.dot(mixed_low.T, attn_low_grad, preferred_element_type=jnp.float32)
    mixed_grad = jnp.dot(attn_low_grad, output_full.T, preferred_element_type=jnp.float32).astype(
        jnp.bfloat16
    )
    mixed_grad_heads = mixed_grad.reshape(tok_dev, group_count, per_group, head_dim).transpose(
        1, 0, 2, 3
    )
    query_grad_h, key_grad_h, value_grad_h = lax.map(
        partial(attend_backward, same_seq=same_seq, score_scale=score_scale),
        (query_heads, key_heads, value_heads, mixed_grad_heads, top_heads, total_heads),
    )
    query_grad_own = query_grad_h.transpose(1, 0, 2, 3).reshape(tok_dev, head_count, head_dim)
    key_grad_group = key_grad_h.transpose(1, 0, 2, 3).reshape(group_rows, width)
    value_grad_group = value_grad_h.transpose(1, 0, 2, 3).reshape(group_rows, width)
    key_sum, value_sum = (
        lax.psum_scatter(
            key_grad_group.astype(jnp.bfloat16), "ep", scatter_dimension=0, tiled=True
        ).astype(jnp.float32),
        lax.psum_scatter(
            value_grad_group.astype(jnp.bfloat16), "ep", scatter_dimension=0, tiled=True
        ).astype(jnp.float32),
    )
    value_low_grad = value_sum.astype(jnp.bfloat16)
    _, query_pull = jax.vjp(
        lambda projected, gain_vec: rope_norm(projected, gain_vec, position_own),
        query_pre,
        gain_query,
    )
    query_pre_grad, gain_query_grad = query_pull(query_grad_own)
    _, key_pull = jax.vjp(
        lambda projected, gain_vec: rope_norm(projected, gain_vec, position_own), key_pre, gain_key
    )
    key_pre_grad, gain_key_grad = key_pull(key_sum.reshape(tok_dev, head_count, head_dim))
    query_low_grad = query_pre_grad.reshape(tok_dev, width).astype(jnp.bfloat16)
    key_low_grad = key_pre_grad.reshape(tok_dev, width).astype(jnp.bfloat16)
    normed_grad = jnp.dot(query_low_grad, query_full.T, preferred_element_type=jnp.float32)
    normed_grad = normed_grad + jnp.dot(
        key_low_grad, key_full.T, preferred_element_type=jnp.float32
    )
    normed_grad = normed_grad + jnp.dot(
        value_low_grad, value_full.T, preferred_element_type=jnp.float32
    )
    query_term = jnp.dot(normed_low.T, query_low_grad, preferred_element_type=jnp.float32)
    key_term = jnp.dot(normed_low.T, key_low_grad, preferred_element_type=jnp.float32)
    value_term = jnp.dot(normed_low.T, value_low_grad, preferred_element_type=jnp.float32)
    _, input_pull = jax.vjp(rms_scale, residual, gain_in)
    input_extra, gain_in_grad = input_pull(normed_grad)
    input_grad = after_grad + input_extra
    gains_term = jnp.concatenate([gain_in_grad, gain_mid_grad, gain_query_grad, gain_key_grad])
    query_sum, key_total, value_total, output_sum, router_sum, gains_sum = (
        lax.psum_scatter(query_term, ("rep", "ep"), scatter_dimension=0, tiled=True),
        lax.psum_scatter(key_term, ("rep", "ep"), scatter_dimension=0, tiled=True),
        lax.psum_scatter(value_term, ("rep", "ep"), scatter_dimension=0, tiled=True),
        lax.psum_scatter(output_term, ("rep", "ep"), scatter_dimension=0, tiled=True),
        lax.psum_scatter(router_term, ("rep", "ep"), scatter_dimension=0, tiled=True),
        lax.psum_scatter(gains_term, ("rep", "ep"), scatter_dimension=0, tiled=True),
    )
    return (
        block_out,
        input_grad,
        query_sum,
        key_total,
        value_total,
        output_sum,
        router_sum,
        gains_sum,
        gate_w_grad,
        up_w_grad,
        down_w_grad,
    )


MESH = pl.DeviceIdType.MESH


def partners(e):
    sib = e + 1 - 2 * (e % 2)
    xn = e + 2 - 4 * ((e // 2) % 2)
    yn = e + 4 - 8 * ((e // 4) % 2)
    dg = xn + 4 - 8 * ((e // 4) % 2)
    return sib, (xn, yn, dg)


def greet(z, e, reps, across):
    barrier = pltpu.get_barrier_semaphore()
    sib, chips = partners(e)
    for other in (sib, *chips):
        pl.semaphore_signal(barrier, inc=1, device_id={"rep": z, "ep": other}, device_id_type=MESH)
    if across:
        @pl.when(z > 0)
        def _():
            pl.semaphore_signal(barrier, inc=1, device_id={"rep": z - 1, "ep": e}, device_id_type=MESH)
        @pl.when(z < reps - 1)
        def _():
            pl.semaphore_signal(barrier, inc=1, device_id={"rep": z + 1, "ep": e}, device_id_type=MESH)
    peers = 4
    if across:
        peers = peers + jnp.where(z > 0, 1, 0) + jnp.where(z < reps - 1, 1, 0)
    pl.semaphore_wait(barrier, peers)


def ag_kernel(reps, across, x_ref, out_ref, own_sem, zs, zr, ps, pr, cs, cr):
    z = lax.axis_index("rep")
    e = lax.axis_index("ep")
    sib, chips = partners(e)
    greet(z, e, reps, across)
    own = z if across else 0
    groups = reps if across else 1
    half = x_ref.shape[0] // 2
    local = pltpu.make_async_copy(x_ref, out_ref.at[own, e], own_sem)
    local.start()

    def zcopy(src, g, up):
        d = 0 if up else 1
        return pltpu.make_async_remote_copy(
            src_ref=src, dst_ref=out_ref.at[g, e], send_sem=zs.at[d, g], recv_sem=zr.at[g],
            device_id={"rep": z + 1 if up else z - 1, "ep": e}, device_id_type=MESH)

    def pcopy(src, g, j):
        return pltpu.make_async_remote_copy(
            src_ref=src, dst_ref=out_ref.at[g, e], send_sem=ps.at[g, j], recv_sem=pr.at[g, j],
            device_id={"rep": z, "ep": chips[j]}, device_id_type=MESH)

    def relay(g, j):
        rows = pl.ds(half * j, half)
        part = out_ref.at[g, chips[j], rows]
        return pltpu.make_async_remote_copy(
            src_ref=part, dst_ref=part, send_sem=ps.at[g, 2 + j], recv_sem=pr.at[g, 2 + j],
            device_id={"rep": z, "ep": chips[1 - j]}, device_id_type=MESH)

    def relayed(g, j):
        part = out_ref.at[g, chips[2], pl.ds(half * j, half)]
        return pltpu.make_async_remote_copy(
            src_ref=part, dst_ref=part, send_sem=ps.at[g, 2 + j], recv_sem=pr.at[g, 2 + j],
            device_id={"rep": z, "ep": chips[1 - j]}, device_id_type=MESH)

    def ccopy(src, g, j):
        who = e if j == 0 else chips[j - 1]
        return pltpu.make_async_remote_copy(
            src_ref=src, dst_ref=out_ref.at[g, who], send_sem=cs.at[g, j], recv_sem=cr.at[g, j],
            device_id={"rep": z, "ep": sib}, device_id_type=MESH)

    def spread(src, g):
        pcopy(src, g, 0).start()
        pcopy(src, g, 1).start()
        ccopy(src, g, 0).start()

    def pass_on(g):
        for j in range(2):
            pcopy(x_ref, g, j).wait_recv()
            relay(g, j).start()
            ccopy(out_ref.at[g, chips[j]], g, j + 1).start()

    def finish(g):
        for j in range(2):
            relayed(g, j).wait_recv()
        ccopy(out_ref.at[g, chips[2]], g, 3).start()

    def at(k, fn):
        if k == 0:
            fn(own)
            return
        @pl.when(z - k >= 0)
        def _():
            fn(z - k)
        @pl.when(z + k < reps)
        def _():
            fn(z + k)

    if across:
        @pl.when(z < reps - 1)
        def _():
            zcopy(x_ref, z, True).start()
        @pl.when(z > 0)
        def _():
            zcopy(x_ref, z, False).start()
    spread(x_ref, own)
    for k in range(1, groups):
        @pl.when(z - k >= 0)
        def _():
            g = z - k
            zcopy(x_ref, g, True).wait_recv()
            @pl.when(z < reps - 1)
            def _():
                zcopy(out_ref.at[g, e], g, True).start()
            spread(out_ref.at[g, e], g)
        @pl.when(z + k < reps)
        def _():
            g = z + k
            zcopy(x_ref, g, False).wait_recv()
            @pl.when(z > 0)
            def _():
                zcopy(out_ref.at[g, e], g, False).start()
            spread(out_ref.at[g, e], g)
        at(k - 1, pass_on)
        if k >= 2:
            at(k - 2, finish)
    at(groups - 1, pass_on)
    if groups >= 2:
        at(groups - 2, finish)
    at(groups - 1, finish)
    local.wait()
    for g in range(groups):
        for j in range(4):
            ccopy(x_ref, g, j).wait()
        for j in range(2):
            pcopy(x_ref, g, j).wait_send()
            relay(g, j).wait_send()
        if across:
            @pl.when((z < reps - 1) & (z >= g))
            def _():
                zcopy(x_ref, g, True).wait_send()
            @pl.when((z > 0) & (z <= g))
            def _():
                zcopy(x_ref, g, False).wait_send()


def all_gather(x, reps, eps, across, cid):
    groups = reps if across else 1
    D = pltpu.SemaphoreType.DMA
    out = pl.pallas_call(
        partial(ag_kernel, reps, across),
        out_shape=jax.ShapeDtypeStruct((groups, eps, *x.shape), x.dtype),
        in_specs=[pl.BlockSpec(memory_space=pl.ANY)],
        out_specs=pl.BlockSpec(memory_space=pl.ANY),
        scratch_shapes=[D, D((2, reps)), D((reps,)), D((groups, 4)), D((groups, 4)), D((groups, 4)), D((groups, 4))],
        compiler_params=pltpu.CompilerParams(collective_id=cid, has_side_effects=True),
    )(x)
    return out


def rs_kernel(reps, across, p_ref, out_ref, own, sib_in, chip_in, up_in, down_in, res,
              own_sem, ss, sr, ps, pr, us, ur, ds, dr):
    z = lax.axis_index("rep")
    e = lax.axis_index("ep")
    core = e % 2
    chip = e // 2
    sib, chips = partners(e)
    groups = reps if across else 1
    greet(z, e, reps, across)
    rows, W = res.shape[1], res.shape[2]
    half = reps // 2

    def order(s):
        if not across:
            return 0
        t = reps - 1 - s
        down = jnp.where(t > z, t, t - 1)
        upw = jnp.where(s < z, s, s + 1)
        g = jnp.where(z < half, down, upw)
        return z if s == reps - 1 else g

    def sibcopy(g):
        return pltpu.make_async_remote_copy(
            src_ref=p_ref.at[g, :, 1 - core], dst_ref=sib_in.at[g], send_sem=ss.at[g], recv_sem=sr.at[g],
            device_id={"rep": z, "ep": sib}, device_id_type=MESH)

    def load(g):
        return pltpu.make_async_copy(p_ref.at[g, :, core], own.at[g], own_sem.at[g])

    def pcopy(g, j):
        return pltpu.make_async_remote_copy(
            src_ref=own.at[g, chips[j] // 2], dst_ref=chip_in.at[g, j], send_sem=ps.at[g, j], recv_sem=pr.at[g, j],
            device_id={"rep": z, "ep": chips[j]}, device_id_type=MESH)

    def zcopy(g, up):
        if up:
            return pltpu.make_async_remote_copy(
                src_ref=res.at[g], dst_ref=up_in.at[g], send_sem=us.at[g], recv_sem=ur.at[g],
                device_id={"rep": z + 1, "ep": e}, device_id_type=MESH)
        return pltpu.make_async_remote_copy(
            src_ref=res.at[g], dst_ref=down_in.at[g], send_sem=ds.at[g], recv_sem=dr.at[g],
            device_id={"rep": z - 1, "ep": e}, device_id_type=MESH)

    for s in range(groups):
        g = order(s)
        sibcopy(g).start()
        load(g).start()
    step = 16

    def add_in(g, q):
        @pl.loop(0, rows // step)
        def _(i):
            r = pl.ds(pl.multiple_of(i * step, step), step)
            own[g, q, r, :] = (own[g, q, r, :].astype(jnp.float32) + sib_in[g, q, r, :].astype(jnp.float32)).astype(own.dtype)

    def stage1(g):
        load(g).wait()
        sibcopy(g).wait_recv()
        for j in (2, 0, 1):
            add_in(g, chips[j] // 2)
            pcopy(g, j).start()

    def stage2(g):
        for j in range(3):
            pcopy(g, j).wait_recv()
        @pl.loop(0, rows // step)
        def _(i):
            r = pl.ds(pl.multiple_of(i * step, step), step)
            t = own[g, chip, r, :].astype(jnp.float32) + sib_in[g, chip, r, :].astype(jnp.float32)
            for j in range(3):
                t = t + chip_in[g, j, r, :].astype(jnp.float32)
            res[g, r, :] = t.astype(res.dtype)

    def plus(g, ref):
        @pl.loop(0, rows // step)
        def _(i):
            r = pl.ds(pl.multiple_of(i * step, step), step)
            res[g, r, :] = (res[g, r, :].astype(jnp.float32) + ref[g, r, :].astype(jnp.float32)).astype(res.dtype)

    def stage3(g):
        @pl.when(g > z)
        def _():
            @pl.when(z > 0)
            def _():
                zcopy(g, True).wait_recv()
                plus(g, up_in)
            zcopy(g, True).start()
        @pl.when(g < z)
        def _():
            @pl.when(z < reps - 1)
            def _():
                zcopy(g, False).wait_recv()
                plus(g, down_in)
            zcopy(g, False).start()

    stage1(order(0))
    for s in range(1, groups):
        stage1(order(s))
        stage2(order(s - 1))
        if s >= 2:
            stage3(order(s - 2))
    stage2(order(groups - 1))
    if across:
        stage3(order(groups - 2))
        @pl.when(z > 0)
        def _():
            zcopy(z, True).wait_recv()
            plus(z, up_in)
        @pl.when(z < reps - 1)
        def _():
            zcopy(z, False).wait_recv()
            plus(z, down_in)
    fin = res.at[z if across else 0]
    out = pltpu.make_async_copy(fin, out_ref, own_sem.at[0])
    out.start()
    out.wait()
    for g in range(groups):
        sibcopy(g).wait_send()
        for j in range(3):
            pcopy(g, j).wait_send()
        if across:
            @pl.when(g > z)
            def _():
                zcopy(g, True).wait_send()
            @pl.when(g < z)
            def _():
                zcopy(g, False).wait_send()


def reduce_scatter(p, reps, eps, across, cid):
    groups = reps if across else 1
    W = p.shape[1]
    rows = p.shape[0] // groups // eps
    p = p.reshape(groups, eps // 2, 2, rows, W)
    D = pltpu.SemaphoreType.DMA
    V = pltpu.VMEM
    q = eps // 2
    return pl.pallas_call(
        partial(rs_kernel, reps, across),
        out_shape=jax.ShapeDtypeStruct((rows, W), p.dtype),
        in_specs=[pl.BlockSpec(memory_space=pl.ANY)],
        out_specs=pl.BlockSpec(memory_space=pl.ANY),
        scratch_shapes=[V((groups, q, rows, W), p.dtype), V((groups, q, rows, W), p.dtype), V((groups, 3, rows, W), p.dtype),
                        V((groups, rows, W), p.dtype), V((groups, rows, W), p.dtype), V((groups, rows, W), p.dtype),
                        D((groups,)), D((groups,)), D((groups,)), D((groups, 3)), D((groups, 3)),
                        D((groups,)), D((groups,)), D((groups,)), D((groups,))],
        compiler_params=pltpu.CompilerParams(collective_id=cid, has_side_effects=True, vmem_limit_bytes=56 * 2**20),
    )(p)

NT = (((1,), (1,)), ((), ()))
TN = (((0,), (0,)), ((), ()))


def visit_order(reps):
    return [sorted((g for g in range(reps) if g != z), key=lambda g: (abs(g - z), g)) + [z] for z in range(reps)]


def moe_kernel(reps, side_lanes, experts_all, x_ref, cot_ref, eg_ref, eu_ref, ed_ref,
               row_ref, moe_ref, gout_ref, uout_ref, dout_ref,
               mid_ref, a_ref, b_ref, h_ref, xin_ref, yin_ref, zin_ref,
               wgu, wd, xbuf, cbuf, abuf, pbuf, sib_in, relay_in, sendbuf, ownbuf, rbuf, tmp, colbuf, gst, dst,
               own_sem, w_sem, x_sem, c_sem, ab_sem, t_sem, col_sem, g_sem, o_sem,
               zs, zr, ps, pr, cs, cr, ss, sr, hs, hr, qs, qr, fs, fr):
    f32, bf16 = jnp.float32, jnp.bfloat16
    z = lax.axis_index("rep")
    e = lax.axis_index("ep")
    core = e % 2
    chip = e // 2
    sib, chips = partners(e)
    rows = x_ref.shape[0]
    half = rows // 2
    width = cot_ref.shape[-1]
    W1 = x_ref.shape[1]
    WP = pbuf.shape[-1]
    exp_dev = eg_ref.shape[0]
    F = wgu.shape[2] // exp_dev
    EF = exp_dev * F
    steps = 4 * reps
    table = visit_order(reps)

    def group_of(s):
        g = 0
        for zi in range(reps):
            for si in range(reps):
                g = g + jnp.where((z == zi) & (s == si), table[zi][si], 0)
        return g

    def chip_of(k):
        return jnp.where(k == 0, chips[2] // 2, jnp.where(k == 1, chip, jnp.where(k == 2, chips[0] // 2, chips[1] // 2)))

    barrier = pltpu.get_barrier_semaphore()
    for other in (sib, *chips):
        pl.semaphore_signal(barrier, inc=1, device_id={"rep": z, "ep": other}, device_id_type=MESH)
    for d in range(1, reps):
        pl.semaphore_signal(barrier, inc=1, device_id={"rep": (z + d) % reps, "ep": e}, device_id_type=MESH)
    weights = []
    for j in range(exp_dev):
        cut = pl.ds(pl.multiple_of(z * F, F), F)
        weights.append(pltpu.make_async_copy(eg_ref.at[j, :, cut], wgu.at[0, :, pl.ds(j * F, F)], w_sem.at[j]))
        weights.append(pltpu.make_async_copy(eu_ref.at[j, :, cut], wgu.at[1, :, pl.ds(j * F, F)], w_sem.at[exp_dev + j]))
        weights.append(pltpu.make_async_copy(ed_ref.at[j, cut, :], wd.at[pl.ds(j * F, F), :], w_sem.at[2 * exp_dev + j]))
    for w in weights:
        w.start()
    local = pltpu.make_async_copy(x_ref, mid_ref.at[z, e], own_sem)
    local.start()
    pl.semaphore_wait(barrier, 4 + reps - 1)

    def zcopy(src, g, up):
        d = 0 if up else 1
        return pltpu.make_async_remote_copy(
            src_ref=src, dst_ref=mid_ref.at[g, e], send_sem=zs.at[d, g], recv_sem=zr.at[g],
            device_id={"rep": z + 1 if up else z - 1, "ep": e}, device_id_type=MESH)

    def pcopy(src, g, j):
        return pltpu.make_async_remote_copy(
            src_ref=src, dst_ref=mid_ref.at[g, e], send_sem=ps.at[g, j], recv_sem=pr.at[g, j],
            device_id={"rep": z, "ep": chips[j]}, device_id_type=MESH)

    def relay(g, j, source):
        part = mid_ref.at[g, source, pl.ds(half * j, half)]
        return pltpu.make_async_remote_copy(
            src_ref=part, dst_ref=part, send_sem=ps.at[g, 2 + j], recv_sem=pr.at[g, 2 + j],
            device_id={"rep": z, "ep": chips[1 - j]}, device_id_type=MESH)

    def ccopy(src, g, j):
        who = e if j == 0 else chips[j - 1]
        return pltpu.make_async_remote_copy(
            src_ref=src, dst_ref=mid_ref.at[g, who], send_sem=cs.at[g, j], recv_sem=cr.at[g, j],
            device_id={"rep": z, "ep": sib}, device_id_type=MESH)

    def spread(src, g):
        pcopy(src, g, 0).start()
        pcopy(src, g, 1).start()
        ccopy(src, g, 0).start()

    def pass_on(g):
        for j in range(2):
            pcopy(x_ref, g, j).wait_recv()
            relay(g, j, chips[j]).start()
            ccopy(mid_ref.at[g, chips[j]], g, j + 1).start()

    def finish_in(g):
        for j in range(2):
            relay(g, j, chips[2]).wait_recv()
        ccopy(mid_ref.at[g, chips[2]], g, 3).start()

    def at(k, fn):
        if k == 0:
            fn(z)
            return
        @pl.when(z - k >= 0)
        def _():
            fn(z - k)
        @pl.when(z + k < reps)
        def _():
            fn(z + k)

    def arrive(k):
        @pl.when(z - k >= 0)
        def _():
            g = z - k
            zcopy(x_ref, g, True).wait_recv()
            @pl.when(z < reps - 1)
            def _():
                zcopy(mid_ref.at[g, e], g, True).start()
            spread(mid_ref.at[g, e], g)
        @pl.when(z + k < reps)
        def _():
            g = z + k
            zcopy(x_ref, g, False).wait_recv()
            @pl.when(z > 0)
            def _():
                zcopy(mid_ref.at[g, e], g, False).start()
            spread(mid_ref.at[g, e], g)

    def ready(g):
        for j in range(4):
            ccopy(x_ref, g, j).wait_recv()

    def load_x(i):
        g, q = group_of(i // 4), chip_of(i % 4)
        return pltpu.make_async_copy(mid_ref.at[g, pl.ds(2 * q, 2)], xbuf.at[i % 2], x_sem.at[i % 2])

    def load_c(i):
        g, q = group_of(i // 4), chip_of(i % 4)
        return pltpu.make_async_copy(cot_ref.at[g, pl.ds(2 * q, 2)], cbuf.at[i % 2], c_sem.at[i % 2])

    def keep(i, m):
        g, q = group_of(i // 4), chip_of(i % 4)
        place = pl.ds(pl.multiple_of((g * 4 + q) * 2 * rows, 2 * rows), 2 * rows)
        return pltpu.make_async_copy(abuf.at[i % 2, m], (a_ref, b_ref, h_ref)[m].at[place], ab_sem.at[i % 2, m])

    def compute(i):
        slot = i % 2
        lane = lax.broadcasted_iota(jnp.int32, (2 * rows, side_lanes), 1)
        side = xbuf[slot, :, :, pl.ds(width, side_lanes)].reshape(2 * rows, side_lanes).astype(f32)

        def one(j, cots):
            cols = pl.ds(pl.multiple_of(j * F, F), F)
            x = xbuf[slot, :, :, pl.ds(0, width)].reshape(2 * rows, width)
            c = cbuf[slot].reshape(2 * rows, width)
            index = e * exp_dev + j
            w = jnp.sum(jnp.where((lane == index) | (lane == index + experts_all), side, 0.0), axis=1, keepdims=True)
            ga = jnp.dot(x, wgu[0, :, cols], preferred_element_type=f32)
            up = jnp.dot(x, wgu[1, :, cols], preferred_element_type=f32)
            hc = lax.dot_general(c, wd[cols, :], NT, preferred_element_type=f32)
            sigma = 1.0 / (1.0 + jnp.exp(-ga))
            silu = ga * sigma
            hid = (silu * up).astype(bf16).astype(f32)
            hcw = hc * w
            abuf[slot, 0, :, cols] = (hcw * up * (sigma * (1.0 + ga * (1.0 - sigma)))).astype(bf16)
            abuf[slot, 1, :, cols] = (hcw * silu).astype(bf16)
            abuf[slot, 2, :, cols] = (hid * w).astype(bf16)
            dots = jnp.sum(hid * hc, axis=1, keepdims=True)
            return cots + jnp.where(lane == index, dots, 0.0)

        cots = lax.fori_loop(0, exp_dev, one, jnp.zeros((2 * rows, side_lanes), f32))
        pbuf[slot, :, :, pl.ds(width, side_lanes)] = cots.astype(bf16).reshape(2, rows, side_lanes)
        block = min(512, width)

        @pl.loop(0, width // block)
        def _(n):
            cut = pl.ds(pl.multiple_of(n * block, block), block)
            t = lax.dot_general(abuf[slot, 0], wgu[0, cut, :], NT, preferred_element_type=f32)
            t = t + lax.dot_general(abuf[slot, 1], wgu[1, cut, :], NT, preferred_element_type=f32)
            pbuf[slot, :, :, cut] = t.astype(bf16).reshape(2, rows, block)
            t = jnp.dot(abuf[slot, 2], wd[:, cut], preferred_element_type=f32)
            cut = pl.ds(pl.multiple_of(W1 + n * block, 128), block)
            pbuf[slot, :, :, cut] = t.astype(bf16).reshape(2, rows, block)

    def sibcopy(i):
        return pltpu.make_async_remote_copy(
            src_ref=pbuf.at[i % 2, 1 - core], dst_ref=sib_in.at[i % 4], send_sem=ss.at[i], recv_sem=sr.at[i],
            device_id={"rep": z, "ep": sib}, device_id_type=MESH)

    def hcopy(s, j):
        part = pl.ds(half * j, half)
        return pltpu.make_async_remote_copy(
            src_ref=sendbuf.at[0, part], dst_ref=relay_in.at[s, j], send_sem=hs.at[s, j], recv_sem=hr.at[s, j],
            device_id={"rep": z, "ep": chips[j]}, device_id_type=MESH)

    def qcopy(s, j):
        return pltpu.make_async_remote_copy(
            src_ref=sendbuf.at[1 + j], dst_ref=(xin_ref, yin_ref)[j].at[s], send_sem=qs.at[s, j], recv_sem=qr.at[s, j],
            device_id={"rep": z, "ep": chips[j]}, device_id_type=MESH)

    def fcopy(s, g):
        return pltpu.make_async_remote_copy(
            src_ref=rbuf.at[s % 2], dst_ref=zin_ref.at[z], send_sem=fs.at[s], recv_sem=fr.at[z],
            device_id={"rep": g, "ep": e}, device_id_type=MESH)

    step = 16

    def add(out, terms, count=rows):
        @pl.loop(0, count // step)
        def _(i):
            r = pl.ds(pl.multiple_of(i * step, step), step)
            t = terms[0][r, :].astype(f32)
            for other in terms[1:]:
                t = t + other[r, :].astype(f32)
            out[r, :] = t.astype(out.dtype)

    def finish(i):
        s, k = i // 4, i % 4
        sibcopy(i).wait_recv()
        mine, other = pbuf.at[i % 2, core], sib_in.at[i % 4]
        lower, upper = pl.ds(0, half), pl.ds(half, half)
        @pl.when(k == 1)
        def _():
            add(ownbuf.at[s % 2], (mine, other))
        @pl.when(k == 0)
        def _():
            @pl.when(s > 0)
            def _():
                hcopy(s - 1, 0).wait_send()
                hcopy(s - 1, 1).wait_send()
            add(sendbuf.at[0], (mine, other))
            hcopy(s, 0).start()
            hcopy(s, 1).start()
        @pl.when(k == 2)
        def _():
            @pl.when(s > 0)
            def _():
                qcopy(s - 1, 0).wait_send()
            add(sendbuf.at[1, lower], (mine.at[lower], other.at[lower]), half)
            hcopy(s, 1).wait_recv()
            add(sendbuf.at[1, upper], (mine.at[upper], other.at[upper], relay_in.at[s, 1]), half)
            qcopy(s, 0).start()
        @pl.when(k == 3)
        def _():
            @pl.when(s > 0)
            def _():
                qcopy(s - 1, 1).wait_send()
            add(sendbuf.at[2, upper], (mine.at[upper], other.at[upper]), half)
            hcopy(s, 0).wait_recv()
            add(sendbuf.at[2, lower], (mine.at[lower], other.at[lower], relay_in.at[s, 0]), half)
            qcopy(s, 1).start()

    def load_t(src, m):
        return pltpu.make_async_copy(src, tmp.at[m], t_sem.at[m])

    def total(s):
        for j in range(2):
            qcopy(s, j).wait_recv()
            load_t((xin_ref, yin_ref)[j].at[s], j).start()
        for j in range(2):
            load_t((xin_ref, yin_ref)[j].at[s], j).wait()

    def plane_sum(s):
        total(s)
        @pl.when(s >= 2)
        def _():
            fcopy(s - 2, group_of(s - 2)).wait_send()
        add(rbuf.at[s % 2], (ownbuf.at[s % 2], tmp.at[0], tmp.at[1]))
        fcopy(s, group_of(s)).start()

    @pl.when(z < reps - 1)
    def _():
        zcopy(x_ref, z, True).start()
    @pl.when(z > 0)
    def _():
        zcopy(x_ref, z, False).start()
    spread(x_ref, z)
    arrive(1)
    pass_on(z)
    arrive(2)
    at(1, pass_on)
    finish_in(z)
    arrive(3)
    at(2, pass_on)
    at(1, finish_in)
    for w in weights:
        w.wait()
    ready(group_of(0))
    load_x(0).start()
    load_c(0).start()

    @pl.loop(0, steps)
    def _(i):
        load_x(i).wait()
        load_c(i).wait()
        @pl.when(i == 3)
        def _():
            at(3, pass_on)
            at(2, finish_in)
        @pl.when(i == 7)
        def _():
            at(3, finish_in)
        @pl.when(i == steps - 5)
        def _():
            local.wait()
        @pl.when(i < steps - 1)
        def _():
            @pl.when(i % 4 == 3)
            def _():
                ready(group_of(i // 4 + 1))
            load_x(i + 1).start()
            load_c(i + 1).start()
        @pl.when(i >= 2)
        def _():
            sibcopy(i - 2).wait_send()
            for m in range(3):
                keep(i - 2, m).wait()
        compute(i)
        sibcopy(i).start()
        for m in range(3):
            keep(i, m).start()
        @pl.when(i >= 1)
        def _():
            finish(i - 1)
        @pl.when((i % 4 == 3) & (i >= 7) & (i < steps - 1))
        def _():
            plane_sum(i // 4 - 1)

    for i in (steps - 2, steps - 1):
        sibcopy(i).wait_send()
        for m in range(3):
            keep(i, m).wait()
    finish(steps - 1)
    plane_sum(reps - 2)

    blocks = width // 256
    halves = wgu.shape[1]

    def resident(src, m):
        return pltpu.make_async_copy(src.at[pl.ds(m * halves, halves)], wgu.at[m], w_sem.at[m])

    def load_col(src, n):
        return pltpu.make_async_copy(src.at[:, :, :, pl.ds(pl.multiple_of(n * 256, 256), 256)], colbuf.at[n % 2], col_sem.at[n % 2])

    def product(n, m):
        left = colbuf[n % 2, pl.ds(m * (reps // 2), reps // 2)].reshape(halves, 256)
        return left, wgu[m]

    def grad_rows(src, out):
        def store(n, j):
            per = width // reps
            place = pl.ds(pl.multiple_of((n * 256) % per, 256), 256)
            return pltpu.make_async_copy(gst.at[n % 2, j], out.at[(n * 256) // per, j, place], g_sem.at[n % 2, j])
        for m in range(2):
            resident(src, m).start()
        load_col(mid_ref, 0).start()
        for m in range(2):
            resident(src, m).wait()
        @pl.loop(0, blocks)
        def _(n):
            load_col(mid_ref, n).wait()
            @pl.when(n < blocks - 1)
            def _():
                load_col(mid_ref, n + 1).start()
            @pl.when(n >= 2)
            def _():
                for j in range(exp_dev):
                    store(n - 2, j).wait()
            t = jnp.zeros((256, EF), f32)
            for m in range(2):
                left, right = product(n, m)
                t = t + lax.dot_general(left, right, TN, preferred_element_type=f32)
            for j in range(exp_dev):
                gst[n % 2, j] = t[:, j * F:(j + 1) * F].astype(bf16)
                store(n, j).start()
        for n in (blocks - 2, blocks - 1):
            for j in range(exp_dev):
                store(n, j).wait()

    def grad_down():
        def store(n):
            return pltpu.make_async_copy(dst.at[n % 2], dout_ref.at[:, :, pl.ds(pl.multiple_of(n * 256, 256), 256)], g_sem.at[n % 2, 0])
        for m in range(2):
            resident(h_ref, m).start()
        load_col(cot_ref, 0).start()
        for m in range(2):
            resident(h_ref, m).wait()
        @pl.loop(0, blocks)
        def _(n):
            load_col(cot_ref, n).wait()
            @pl.when(n < blocks - 1)
            def _():
                load_col(cot_ref, n + 1).start()
            @pl.when(n >= 2)
            def _():
                store(n - 2).wait()
            t = jnp.zeros((EF, 256), f32)
            for m in range(2):
                left, right = product(n, m)
                t = t + lax.dot_general(right, left, TN, preferred_element_type=f32)
            dst[n % 2] = t.reshape(exp_dev, F, 256)
            store(n).start()
        for n in (blocks - 2, blocks - 1):
            store(n).wait()

    grad_rows(a_ref, gout_ref)
    grad_rows(b_ref, uout_ref)
    grad_down()

    last = reps - 1
    total(last)
    for d in range(1, reps):
        src = (z + d) % reps
        pltpu.make_async_remote_copy(
            src_ref=rbuf.at[0], dst_ref=zin_ref.at[src], send_sem=fs.at[last], recv_sem=fr.at[src],
            device_id={"rep": src, "ep": e}, device_id_type=MESH).wait_recv()
        load_t(zin_ref.at[src], 1 + d).start()
    for d in range(1, reps):
        load_t(zin_ref.at[(z + d) % reps], 1 + d).wait()
    fcopy(reps - 3, group_of(reps - 3)).wait_send()
    add(rbuf.at[(reps - 3) % 2], (ownbuf.at[last % 2], *(tmp.at[m] for m in range(reps + 1))))
    outs = (
        pltpu.make_async_copy(rbuf.at[(reps - 3) % 2, :, pl.ds(0, W1)], row_ref, o_sem.at[0]),
        pltpu.make_async_copy(rbuf.at[(reps - 3) % 2, :, pl.ds(W1, width)], moe_ref, o_sem.at[1]),
    )
    for o in outs:
        o.start()
    for o in outs:
        o.wait()
    fcopy(reps - 2, group_of(reps - 2)).wait_send()
    for j in range(2):
        hcopy(last, j).wait_send()
        qcopy(last, j).wait_send()
    for g in range(reps):
        for j in range(4):
            ccopy(x_ref, g, j).wait_send()
        for j in range(2):
            pcopy(x_ref, g, j).wait_send()
            relay(g, j, chips[j]).wait_send()
        @pl.when((z < reps - 1) & (z >= g))
        def _():
            zcopy(x_ref, g, True).wait_send()
        @pl.when((z > 0) & (z <= g))
        def _():
            zcopy(x_ref, g, False).wait_send()


def moe(x, cot_all, eg, eu, ed, experts_all, cid):
    reps, eps, rows, width = cot_all.shape
    W1 = x.shape[1]
    side = W1 - width
    WP = W1 + width
    exp_dev, _, ff = eg.shape
    F = ff // reps
    EF = exp_dev * F
    f32, bf16 = jnp.float32, jnp.bfloat16
    D, V = pltpu.SemaphoreType.DMA, pltpu.VMEM
    S = jax.ShapeDtypeStruct
    tokens = reps * eps * rows
    steps = 4 * reps
    outs = (
        S((rows, W1), bf16), S((rows, width), bf16),
        S((reps, exp_dev, width // reps, F), bf16), S((reps, exp_dev, width // reps, F), bf16), S((exp_dev, F, width), f32),
        S((reps, eps, rows, W1), bf16), S((tokens, EF), bf16), S((tokens, EF), bf16), S((tokens, EF), bf16),
        S((reps, rows, WP), bf16), S((reps, rows, WP), bf16), S((reps, rows, WP), bf16),
    )
    return pl.pallas_call(
        partial(moe_kernel, reps, side, experts_all),
        out_shape=outs,
        in_specs=[pl.BlockSpec(memory_space=pl.ANY)] * 5,
        out_specs=[pl.BlockSpec(memory_space=pl.ANY)] * len(outs),
        scratch_shapes=[
            V((2, width, EF), bf16), V((EF, width), bf16),
            V((2, 2, rows, W1), bf16), V((2, 2, rows, width), bf16),
            V((2, 3, 2 * rows, EF), bf16), V((2, 2, rows, WP), bf16), V((4, rows, WP), bf16),
            V((reps, 2, rows // 2, WP), bf16), V((3, rows, WP), bf16), V((2, rows, WP), bf16), V((2, rows, WP), bf16),
            V((5, rows, WP), bf16), V((2, reps, eps, rows, 256), bf16),
            V((2, exp_dev, 256, F), bf16), V((2, exp_dev, F, 256), f32),
            D, D((3 * exp_dev,)), D((2,)), D((2,)), D((2, 3)), D((5,)), D((2,)), D((2, exp_dev)), D((2,)),
            D((2, reps)), D((reps,)), D((reps, 4)), D((reps, 4)), D((reps, 4)), D((reps, 4)),
            D((steps,)), D((steps,)), D((reps, 2)), D((reps, 2)), D((reps, 2)), D((reps, 2)), D((reps,)), D((reps,)),
        ],
        compiler_params=pltpu.CompilerParams(collective_id=cid, has_side_effects=True, vmem_limit_bytes=63 * 2**20),
    )(x, cot_all, eg, eu, ed)[:5]


def gather_block(block, axes):
    return lax.all_gather(block, axes, axis=0, tiled=True)


def scatter_sum(partial_sums, axes):
    return lax.psum_scatter(partial_sums, axes, scatter_dimension=0, tiled=True)


def on_device_split(
    tokens,
    cotangent,
    query_weight,
    key_weight,
    value_weight,
    output_weight,
    router_weight,
    gains,
    expert_gate,
    expert_up,
    expert_down,
    lengths,
    deal,
    routes,
    priority,
):
    bf16, f32 = jnp.bfloat16, jnp.float32
    tok_dev, width = tokens.shape
    ep_count, rep_count = lax.axis_size("ep"), lax.axis_size("rep")
    ep_index, rep_index = lax.axis_index("ep"), lax.axis_index("rep")
    exp_dev, _, ff_width = expert_gate.shape
    top_count = routes.shape[1]
    experts_all = exp_dev * ep_count
    group_rows = tok_dev * ep_count
    capacity = 5 * tok_dev * top_count // (4 * exp_dev)
    head_dim = HD
    heads_dev = width // head_dim // ep_count
    slice_width = heads_dev * head_dim
    rows_dev = query_weight.shape[0]
    score_scale = head_dim ** (-0.5)
    core = ep_index % 2
    every = ("rep", "ep")

    gains_dev = gains.shape[0]
    packed = jnp.concatenate(
        [gains, router_weight.reshape(-1), jnp.zeros((2048 - gains_dev - router_weight.size,), bf16)]
    ).reshape(16, 128)
    packed_all = gather_block(packed, every).reshape(rep_count * ep_count, 2048)
    gains_float = packed_all[:, :gains_dev].reshape(-1).astype(f32)
    router_full = packed_all[:, gains_dev : gains_dev + router_weight.size].reshape(width, experts_all)
    gain_in = gains_float[:width]
    gain_mid = gains_float[width : 2 * width]
    gain_query = gains_float[2 * width : 2 * width + head_dim]
    gain_key = gains_float[2 * width + head_dim :]
    numbers = jnp.concatenate([deal, priority, routes.T.reshape(-1)]).reshape(-1, 128)
    numbers_all = gather_block(numbers, "ep").reshape(ep_count, -1, tok_dev)
    deal_all = numbers_all[:, 0].reshape(-1)
    priority_all = numbers_all[:, 1].reshape(-1)
    routes_all = numbers_all[:, 2:].transpose(0, 2, 1).reshape(group_rows, top_count)
    segment_all, position_all = placement(deal_all, lengths[0])

    chips = ep_count // 2
    def columns_of(weight):
        parts = weight.reshape(rows_dev, 2, heads_dev, chips, head_dim).transpose(3, 1, 0, 2, 4)
        parts = parts.reshape(ep_count, rows_dev, slice_width)
        return lax.all_to_all(parts, "ep", split_axis=0, concat_axis=0, tiled=True)

    qkv_rows = jnp.concatenate(
        [columns_of(query_weight), columns_of(key_weight), columns_of(value_weight)], axis=2
    ).reshape(ep_count * rows_dev, 3 * slice_width)
    qkv_slice = gather_block(qkv_rows, "rep")
    out_rows = gather_block(output_weight, "rep").reshape(2, heads_dev, rows_dev, width)
    out_own = lax.dynamic_index_in_dim(out_rows, core, 0, keepdims=False)
    out_other = lax.ppermute(
        lax.dynamic_index_in_dim(out_rows, 1 - core, 0, keepdims=False),
        "ep",
        [(i, i + 1 - 2 * (i % 2)) for i in range(ep_count)],
    )
    out_slice = jnp.where(
        core == 0,
        jnp.concatenate([out_own, out_other], axis=1),
        jnp.concatenate([out_other, out_own], axis=1),
    ).reshape(slice_width, width)

    cot_all = all_gather(cotangent, rep_count, ep_count, True, 0)
    tokens_group = (
        all_gather(tokens, rep_count, ep_count, False, 1).reshape(group_rows, width).astype(f32)
    )
    normed_group = rms_scale(tokens_group, gain_in).astype(bf16)
    projected = jnp.dot(normed_group, qkv_slice, preferred_element_type=f32)
    query_pre = projected[:, :slice_width].reshape(group_rows, heads_dev, head_dim)
    key_pre = projected[:, slice_width : 2 * slice_width].reshape(group_rows, heads_dev, head_dim)
    value_low = projected[:, 2 * slice_width :].astype(bf16).reshape(group_rows, heads_dev, head_dim)
    query_low = rope_norm(query_pre, gain_query, position_all).astype(bf16)
    key_low = rope_norm(key_pre, gain_key, position_all).astype(bf16)
    same_seq = segment_all[:, None] == segment_all[None, :]
    mixed, top_score, total_sum = attend_forward(
        (query_low, key_low, value_low), same_seq, score_scale
    )
    mixed_low = mixed.reshape(group_rows, slice_width).astype(bf16)
    attn_part = jnp.dot(mixed_low, out_slice, preferred_element_type=f32).astype(bf16)
    residual = tokens.astype(f32)
    after_attn = residual + reduce_scatter(attn_part, rep_count, ep_count, False, 2).astype(f32)
    mid_low = rms_scale(after_attn, gain_mid).astype(bf16)

    logits = jnp.dot(mid_low, router_full, preferred_element_type=f32)
    expert_ids = jnp.arange(experts_all, dtype=jnp.int32)
    member = (routes[:, :, None] == expert_ids[None, None, :]).astype(f32)
    named = jnp.sum(member, axis=1)
    lifted = jnp.where(named > 0, logits, masked_score)
    lifted = jnp.exp(lifted - jnp.max(lifted, axis=-1, keepdims=True)) * named
    gate_dense = lifted / jnp.sum(lifted, axis=-1, keepdims=True)
    onehot_all = jnp.sum(
        (routes_all[:, :, None] == expert_ids[None, None, :]).astype(bf16), axis=1
    )
    earlier = (priority_all[None, :] < priority[:, None]).astype(bf16)
    slots = jnp.dot(earlier, onehot_all, preferred_element_type=f32)
    kept_dense = named * (slots < capacity).astype(f32)
    pair_weight = gate_dense * kept_dense

    weight_high = pair_weight.astype(bf16)
    weight_low = (pair_weight - weight_high.astype(f32)).astype(bf16)
    side = jnp.concatenate(
        [weight_high, weight_low, jnp.zeros((tok_dev, 128 - 2 * experts_all), bf16)], axis=1
    )
    row_sum, moe_sum, gate_term, up_term, down_w_grad = moe(
        jnp.concatenate([mid_low, side], axis=1),
        cot_all,
        expert_gate,
        expert_up,
        expert_down,
        experts_all,
        3,
    )
    moe_out = moe_sum.astype(f32)
    block_out = (after_attn + moe_out).astype(bf16)

    def rows_of(parts):
        got = lax.all_to_all(parts, "rep", split_axis=0, concat_axis=0, tiled=True)
        return got.transpose(1, 2, 0, 3).reshape(exp_dev, width // rep_count, ff_width).astype(f32)

    gate_w_grad = rows_of(gate_term)
    up_w_grad = rows_of(up_term)

    out_grad = cotangent.astype(f32)
    gate_cot = row_sum[:, width : width + experts_all].astype(f32) * kept_dense
    chosen_cot = gate_dense * (gate_cot - jnp.sum(gate_dense * gate_cot, axis=-1, keepdims=True))
    logit_cot = chosen_cot.astype(bf16)
    mid_cot = row_sum[:, :width].astype(f32) + jnp.dot(
        logit_cot, router_full.T, preferred_element_type=f32
    )
    router_term = jnp.dot(mid_low.T, logit_cot, preferred_element_type=f32)
    _, mid_pull = jax.vjp(rms_scale, after_attn, gain_mid)
    after_extra, gain_mid_cot = mid_pull(mid_cot)
    after_cot = out_grad + after_extra
    attn_cot_group = all_gather(
        after_cot.astype(bf16), rep_count, ep_count, False, 6
    ).reshape(group_rows, width)

    mixed_cot = jnp.dot(attn_cot_group, out_slice.T, preferred_element_type=f32).astype(bf16)
    output_term = jnp.dot(mixed_low.T, attn_cot_group, preferred_element_type=f32)
    query_cot, key_cot, value_cot = attend_backward(
        (
            query_low,
            key_low,
            value_low,
            mixed_cot.reshape(group_rows, heads_dev, head_dim),
            top_score,
            total_sum,
        ),
        same_seq,
        score_scale,
    )
    _, query_pull = jax.vjp(
        lambda pre, gain_vec: rope_norm(pre, gain_vec, position_all), query_pre, gain_query
    )
    query_pre_cot, gain_query_cot = query_pull(query_cot)
    _, key_pull = jax.vjp(
        lambda pre, gain_vec: rope_norm(pre, gain_vec, position_all), key_pre, gain_key
    )
    key_pre_cot, gain_key_cot = key_pull(key_cot)
    pre_cot = jnp.concatenate(
        [
            part.reshape(group_rows, slice_width).astype(bf16)
            for part in (query_pre_cot, key_pre_cot, value_cot)
        ],
        axis=1,
    )
    normed_part = jnp.dot(pre_cot, qkv_slice.T, preferred_element_type=f32).astype(bf16)
    normed_cot = reduce_scatter(normed_part, rep_count, ep_count, False, 7).astype(f32)
    _, input_pull = jax.vjp(rms_scale, residual, gain_in)
    input_extra, gain_in_cot = input_pull(normed_cot)
    input_grad = after_cot + input_extra
    qkv_term = jnp.dot(normed_group.T, pre_cot, preferred_element_type=f32)

    qkv_sum = scatter_sum(qkv_term.astype(bf16), "rep").reshape(ep_count, rows_dev, 3, slice_width)

    def whole_rows(part):
        got = lax.all_to_all(part, "ep", split_axis=0, concat_axis=0, tiled=True)
        got = got.reshape(chips, 2, rows_dev, heads_dev, head_dim).transpose(2, 1, 3, 0, 4)
        return got.reshape(rows_dev, width).astype(f32)

    query_sum, key_sum, value_sum = (whole_rows(qkv_sum[:, :, i]) for i in range(3))
    out_halves = output_term.astype(bf16).reshape(heads_dev, 2, rows_dev, width)
    out_keep = lax.dynamic_index_in_dim(out_halves, core, 1, keepdims=False)
    out_pass = lax.ppermute(
        lax.dynamic_index_in_dim(out_halves, 1 - core, 1, keepdims=False),
        "ep",
        [(i, i + 1 - 2 * (i % 2)) for i in range(ep_count)],
    )
    out_parts = jnp.where(
        core == 0, jnp.stack([out_keep, out_pass]), jnp.stack([out_pass, out_keep])
    ).reshape(2 * heads_dev * rows_dev, width)
    output_sum = scatter_sum(out_parts, "rep").astype(f32)
    gains_term = jnp.concatenate([gain_in_cot, gain_mid_cot, gain_query_cot, gain_key_cot])
    small_term = jnp.concatenate(
        [
            gains_term.reshape(rep_count * ep_count, gains_dev),
            router_term.reshape(rep_count * ep_count, router_weight.size),
            jnp.zeros((rep_count * ep_count, 2048 - gains_dev - router_weight.size), f32),
        ],
        axis=1,
    ).reshape(rep_count * ep_count * 16, 128)
    small_sum = scatter_sum(small_term, every).reshape(-1)
    gains_sum = small_sum[:gains_dev]
    router_sum = small_sum[gains_dev : gains_dev + router_weight.size].reshape(
        rows_dev, experts_all
    )
    return (
        block_out,
        input_grad,
        query_sum,
        key_sum,
        value_sum,
        output_sum,
        router_sum,
        gains_sum,
        gate_w_grad,
        up_w_grad,
        down_w_grad,
    )


def solution(mesh):
    placed = (
        P(("rep", "ep"), None),
        P(("rep", "ep"), None),
        P(("rep", "ep"), None),
        P(("rep", "ep"), None),
        P(("rep", "ep"), None),
        P(("rep", "ep"), None),
        P(("rep", "ep"), None),
        P(("rep", "ep")),
        P("ep", None, None),
        P("ep", None, None),
        P("ep", None, None),
        P("rep", None),
        P(("rep", "ep")),
        P(("rep", "ep"), None),
        P(("rep", "ep")),
    )
    return jax.shard_map(
        on_device_split if mesh.shape["rep"] == 4 else on_device_general,
        mesh=mesh,
        in_specs=placed,
        out_specs=(
            P(("rep", "ep"), None),
            P(("rep", "ep"), None),
            P(("rep", "ep"), None),
            P(("rep", "ep"), None),
            P(("rep", "ep"), None),
            P(("rep", "ep"), None),
            P(("rep", "ep"), None),
            P(("rep", "ep")),
            P("ep", "rep", None),
            P("ep", "rep", None),
            P("ep", "rep", None),
        ),
        check_vma=False,
    )
```

```python
from functools import partial

import jax
import jax.numpy as jnp
from jax import lax
from jax.experimental import pallas as pl
from jax.experimental.pallas import tpu as pltpu
from jax.sharding import PartitionSpec as P

HD = 128


norm_eps = 1e-06
rope_base = 10000.0
masked_score = -1e30
highest = lax.Precision.HIGHEST


def rms_scale(values, gain_vec):
    return (
        values * lax.rsqrt(jnp.mean(values * values, axis=-1, keepdims=True) + norm_eps) * gain_vec
    )


def rotate(values, positions):
    half_width = values.shape[-1] // 2
    frequency = rope_base ** (-2.0 * jnp.arange(half_width, dtype=jnp.float32) / values.shape[-1])
    angles = positions.astype(jnp.float32)[:, None] * frequency[None, :]
    cosine = jnp.cos(angles)[:, None, :]
    sine_part = jnp.sin(angles)[:, None, :]
    low_half = values[..., :half_width]
    high_half = values[..., half_width:]
    return jnp.concatenate(
        [low_half * cosine - high_half * sine_part, high_half * cosine + low_half * sine_part],
        axis=-1,
    )


def placement(deal_rows, lengths_row):
    seq_ends = jnp.cumsum(lengths_row)
    is_after = (seq_ends[None, :] <= deal_rows[:, None]).astype(jnp.int32)
    segment = jnp.sum(is_after, axis=1)
    seq_start = jnp.sum(is_after * lengths_row[None, :], axis=1)
    return (segment, deal_rows - seq_start)


def rope_norm(projected, gain_vec, positions):
    return rotate(rms_scale(projected, gain_vec), positions)


def attend_forward(parts, same_seq, score_scale):
    head_query, head_key, head_value = parts
    scores = (
        jnp.einsum("thd,shd->hts", head_query, head_key, preferred_element_type=jnp.float32)
        * score_scale
    )
    scores = jnp.where(same_seq[None], scores, masked_score)
    top_score = jnp.max(scores, axis=-1, keepdims=True)
    lifted = jnp.exp(scores - top_score)
    total_sum = jnp.sum(lifted, axis=-1, keepdims=True)
    prob_low = (lifted / total_sum).astype(jnp.bfloat16)
    mixed_out = jnp.einsum("hts,shd->thd", prob_low, head_value, preferred_element_type=jnp.float32)
    return (mixed_out, top_score, total_sum)


def attend_backward(parts, same_seq, score_scale):
    head_query, head_key, head_value, head_grad, top_score, total_sum = parts
    scores = (
        jnp.einsum("thd,shd->hts", head_query, head_key, preferred_element_type=jnp.float32)
        * score_scale
    )
    scores = jnp.where(same_seq[None], scores, masked_score)
    prob_full = jnp.exp(scores - top_score) / total_sum
    prob_low = prob_full.astype(jnp.bfloat16)
    prob_grad = jnp.einsum(
        "thd,shd->hts", head_grad, head_value, preferred_element_type=jnp.float32
    )
    row_dot = jnp.sum(prob_full * prob_grad, axis=-1, keepdims=True)
    score_grad = (prob_full * (prob_grad - row_dot)).astype(jnp.bfloat16)
    query_grad = (
        jnp.einsum("hts,shd->thd", score_grad, head_key, preferred_element_type=jnp.float32)
        * score_scale
    )
    key_grad = (
        jnp.einsum("hts,thd->shd", score_grad, head_query, preferred_element_type=jnp.float32)
        * score_scale
    )
    value_grad = jnp.einsum("hts,thd->shd", prob_low, head_grad, preferred_element_type=jnp.float32)
    return (query_grad, key_grad, value_grad)


def on_device_general(
    tokens,
    cotangent,
    query_weight,
    key_weight,
    value_weight,
    output_weight,
    router_weight,
    gains,
    expert_gate,
    expert_up,
    expert_down,
    lengths,
    deal,
    routes,
    priority,
):
    tok_dev, width = tokens.shape
    ep_count = lax.axis_size("ep")
    ep_index = lax.axis_index("ep")
    exp_dev = expert_gate.shape[0]
    top_count = routes.shape[1]
    experts_all = exp_dev * ep_count
    group_rows = tok_dev * ep_count
    send_most = min(tok_dev, 3 * tok_dev * top_count // (2 * experts_all))
    capacity = 5 * tok_dev * top_count // (4 * exp_dev)
    head_dim = HD
    head_count = width // head_dim
    per_group = min(head_count, 4)
    group_count = head_count // per_group
    score_scale = head_dim ** (-0.5)
    query_full, key_full, value_full, output_full, router_full, gains_full = (
        lax.all_gather(query_weight, ("rep", "ep"), axis=0, tiled=True),
        lax.all_gather(key_weight, ("rep", "ep"), axis=0, tiled=True),
        lax.all_gather(value_weight, ("rep", "ep"), axis=0, tiled=True),
        lax.all_gather(output_weight, ("rep", "ep"), axis=0, tiled=True),
        lax.all_gather(router_weight, ("rep", "ep"), axis=0, tiled=True),
        lax.all_gather(gains, ("rep", "ep"), axis=0, tiled=True),
    )
    gains_float = gains_full.astype(jnp.float32)
    gain_in = gains_float[:width]
    gain_mid = gains_float[width : 2 * width]
    gain_query = gains_float[2 * width : 2 * width + head_dim]
    gain_key = gains_float[2 * width + head_dim :]
    deal_all, priority_all, routes_all = (
        lax.all_gather(deal, "ep", axis=0, tiled=True),
        lax.all_gather(priority, "ep", axis=0, tiled=True),
        lax.all_gather(routes, "ep", axis=0, tiled=True),
    )
    segment_all, position_all = placement(deal_all, lengths[0])
    segment_own = lax.dynamic_slice_in_dim(segment_all, ep_index * tok_dev, tok_dev)
    position_own = lax.dynamic_slice_in_dim(position_all, ep_index * tok_dev, tok_dev)
    residual = tokens.astype(jnp.float32)
    normed_low = rms_scale(residual, gain_in).astype(jnp.bfloat16)
    query_pre = jnp.dot(normed_low, query_full, preferred_element_type=jnp.float32).reshape(
        tok_dev, head_count, head_dim
    )
    key_pre = jnp.dot(normed_low, key_full, preferred_element_type=jnp.float32).reshape(
        tok_dev, head_count, head_dim
    )
    value_low = jnp.dot(normed_low, value_full, preferred_element_type=jnp.float32).astype(
        jnp.bfloat16
    )
    query_low = rope_norm(query_pre, gain_query, position_own).astype(jnp.bfloat16)
    key_low = (
        rope_norm(key_pre, gain_key, position_own).astype(jnp.bfloat16).reshape(tok_dev, width)
    )
    key_group, value_group = (
        lax.all_gather(key_low, "ep", axis=0, tiled=True),
        lax.all_gather(value_low, "ep", axis=0, tiled=True),
    )
    same_seq = segment_own[:, None] == segment_all[None, :]
    query_heads = query_low.reshape(tok_dev, group_count, per_group, head_dim).transpose(1, 0, 2, 3)
    key_heads = key_group.reshape(group_rows, group_count, per_group, head_dim).transpose(
        1, 0, 2, 3
    )
    value_heads = value_group.reshape(group_rows, group_count, per_group, head_dim).transpose(
        1, 0, 2, 3
    )
    mixed_heads, top_heads, total_heads = lax.map(
        partial(attend_forward, same_seq=same_seq, score_scale=score_scale),
        (query_heads, key_heads, value_heads),
    )
    mixed_low = mixed_heads.transpose(1, 0, 2, 3).reshape(tok_dev, width).astype(jnp.bfloat16)
    after_attn = residual + jnp.dot(mixed_low, output_full, preferred_element_type=jnp.float32)
    mid_low = rms_scale(after_attn, gain_mid).astype(jnp.bfloat16)
    logits = jnp.dot(mid_low, router_full, preferred_element_type=jnp.float32)
    chosen = jnp.take_along_axis(logits, routes, axis=1)
    gate_prob = jax.nn.softmax(chosen, axis=-1)
    expert_ids = jnp.arange(experts_all, dtype=jnp.int32)
    onehot_all = jnp.sum(
        (routes_all[:, :, None] == expert_ids[None, None, :]).astype(jnp.float32), axis=1
    )
    earlier = (priority_all[None, :] < priority_all[:, None]).astype(jnp.float32)
    slot_all = jnp.take_along_axis(
        jnp.dot(earlier, onehot_all, precision=highest), routes_all, axis=1
    ).astype(jnp.int32)
    row_ids = jnp.arange(tok_dev, dtype=jnp.int32)
    lower_tri = (row_ids[:, None] > row_ids[None, :]).astype(jnp.float32)
    before = jnp.einsum(
        "ij,dje->die",
        lower_tri,
        onehot_all.reshape(ep_count, tok_dev, experts_all),
        precision=highest,
    ).reshape(group_rows, experts_all)
    place_all = jnp.take_along_axis(before, routes_all, axis=1).astype(jnp.int32)
    kept_all = slot_all < capacity
    kept_own = lax.dynamic_slice_in_dim(kept_all, ep_index * tok_dev, tok_dev)
    place_own = lax.dynamic_slice_in_dim(place_all, ep_index * tok_dev, tok_dev)
    buffer_index = (routes * send_most + place_own).reshape(-1)
    rows_out = jnp.where(
        kept_own[:, :, None], mid_low[:, None, :], jnp.zeros((), jnp.bfloat16)
    ).reshape(tok_dev * top_count, width)
    send_rows = (
        jnp.zeros((experts_all * send_most, width), jnp.bfloat16)
        .at[buffer_index]
        .set(rows_out)
        .reshape(experts_all, send_most, width)
    )
    received = lax.all_to_all(send_rows, "ep", split_axis=0, concat_axis=1, tiled=True)
    gate_part = jnp.einsum(
        "erd,edf->erf", received, expert_gate, preferred_element_type=jnp.float32
    )
    up_part = jnp.einsum("erd,edf->erf", received, expert_up, preferred_element_type=jnp.float32)
    hidden = (jax.nn.silu(gate_part) * up_part).astype(jnp.bfloat16)
    result = jnp.einsum(
        "erf,efd->erd", hidden, expert_down, preferred_element_type=jnp.float32
    ).astype(jnp.bfloat16)
    returned = lax.all_to_all(result, "ep", split_axis=1, concat_axis=0, tiled=True)
    pair_out = returned.reshape(experts_all * send_most, width)[buffer_index].reshape(
        tok_dev, top_count, width
    )
    pair_weight = gate_prob * kept_own.astype(jnp.float32)
    moe_out = jnp.einsum("tk,tkd->td", pair_weight, pair_out, preferred_element_type=jnp.float32)
    block_out = (after_attn + moe_out).astype(jnp.bfloat16)
    out_grad = cotangent.astype(jnp.float32)
    pair_gate_grad = kept_own.astype(jnp.float32) * jnp.einsum(
        "tkd,td->tk", pair_out, out_grad, preferred_element_type=jnp.float32
    )
    pair_grad = (
        (pair_weight[:, :, None] * out_grad[:, None, :])
        .astype(jnp.bfloat16)
        .reshape(tok_dev * top_count, width)
    )
    grad_send = (
        jnp.zeros((experts_all * send_most, width), jnp.bfloat16)
        .at[buffer_index]
        .set(pair_grad)
        .reshape(experts_all, send_most, width)
    )
    grad_received = lax.all_to_all(grad_send, "ep", split_axis=0, concat_axis=1, tiled=True)
    hidden_grad = jnp.einsum(
        "erd,efd->erf", grad_received, expert_down, preferred_element_type=jnp.float32
    )
    _, silu_pull = jax.vjp(lambda gate_in, up_in: jax.nn.silu(gate_in) * up_in, gate_part, up_part)
    gate_part_grad, up_part_grad = silu_pull(hidden_grad)
    gate_low_grad = gate_part_grad.astype(jnp.bfloat16)
    up_low_grad = up_part_grad.astype(jnp.bfloat16)
    down_term = jnp.einsum(
        "erf,erd->efd", hidden, grad_received, preferred_element_type=jnp.float32
    )
    gate_term = jnp.einsum(
        "erd,erf->edf", received, gate_low_grad, preferred_element_type=jnp.float32
    )
    up_term = jnp.einsum("erd,erf->edf", received, up_low_grad, preferred_element_type=jnp.float32)
    rows_grad = (
        jnp.einsum("erf,edf->erd", gate_low_grad, expert_gate, preferred_element_type=jnp.float32)
        + jnp.einsum("erf,edf->erd", up_low_grad, expert_up, preferred_element_type=jnp.float32)
    ).astype(jnp.bfloat16)
    back_rows = lax.all_to_all(rows_grad, "ep", split_axis=1, concat_axis=0, tiled=True)
    mid_grad = jnp.sum(
        back_rows.reshape(experts_all * send_most, width)[buffer_index]
        .reshape(tok_dev, top_count, width)
        .astype(jnp.float32),
        axis=1,
    )
    gate_w_grad, up_w_grad, down_w_grad = (
        lax.psum_scatter(
            gate_term.astype(jnp.bfloat16), "rep", scatter_dimension=1, tiled=True
        ).astype(jnp.float32),
        lax.psum_scatter(
            up_term.astype(jnp.bfloat16), "rep", scatter_dimension=1, tiled=True
        ).astype(jnp.float32),
        lax.psum_scatter(
            down_term.astype(jnp.bfloat16), "rep", scatter_dimension=1, tiled=True
        ).astype(jnp.float32),
    )
    _, soft_pull = jax.vjp(lambda values: jax.nn.softmax(values, axis=-1), chosen)
    (chosen_grad,) = soft_pull(pair_gate_grad)
    onehot_own = (routes[:, :, None] == expert_ids[None, None, :]).astype(jnp.float32)
    logit_grad = jnp.einsum("tk,tke->te", chosen_grad, onehot_own).astype(jnp.bfloat16)
    mid_grad = mid_grad + jnp.dot(logit_grad, router_full.T, preferred_element_type=jnp.float32)
    router_term = jnp.dot(mid_low.T, logit_grad, preferred_element_type=jnp.float32)
    _, mid_pull = jax.vjp(rms_scale, after_attn, gain_mid)
    after_extra, gain_mid_grad = mid_pull(mid_grad)
    after_grad = out_grad + after_extra
    attn_low_grad = after_grad.astype(jnp.bfloat16)
    output_term = jnp.dot(mixed_low.T, attn_low_grad, preferred_element_type=jnp.float32)
    mixed_grad = jnp.dot(attn_low_grad, output_full.T, preferred_element_type=jnp.float32).astype(
        jnp.bfloat16
    )
    mixed_grad_heads = mixed_grad.reshape(tok_dev, group_count, per_group, head_dim).transpose(
        1, 0, 2, 3
    )
    query_grad_h, key_grad_h, value_grad_h = lax.map(
        partial(attend_backward, same_seq=same_seq, score_scale=score_scale),
        (query_heads, key_heads, value_heads, mixed_grad_heads, top_heads, total_heads),
    )
    query_grad_own = query_grad_h.transpose(1, 0, 2, 3).reshape(tok_dev, head_count, head_dim)
    key_grad_group = key_grad_h.transpose(1, 0, 2, 3).reshape(group_rows, width)
    value_grad_group = value_grad_h.transpose(1, 0, 2, 3).reshape(group_rows, width)
    key_sum, value_sum = (
        lax.psum_scatter(
            key_grad_group.astype(jnp.bfloat16), "ep", scatter_dimension=0, tiled=True
        ).astype(jnp.float32),
        lax.psum_scatter(
            value_grad_group.astype(jnp.bfloat16), "ep", scatter_dimension=0, tiled=True
        ).astype(jnp.float32),
    )
    value_low_grad = value_sum.astype(jnp.bfloat16)
    _, query_pull = jax.vjp(
        lambda projected, gain_vec: rope_norm(projected, gain_vec, position_own),
        query_pre,
        gain_query,
    )
    query_pre_grad, gain_query_grad = query_pull(query_grad_own)
    _, key_pull = jax.vjp(
        lambda projected, gain_vec: rope_norm(projected, gain_vec, position_own), key_pre, gain_key
    )
    key_pre_grad, gain_key_grad = key_pull(key_sum.reshape(tok_dev, head_count, head_dim))
    query_low_grad = query_pre_grad.reshape(tok_dev, width).astype(jnp.bfloat16)
    key_low_grad = key_pre_grad.reshape(tok_dev, width).astype(jnp.bfloat16)
    normed_grad = jnp.dot(query_low_grad, query_full.T, preferred_element_type=jnp.float32)
    normed_grad = normed_grad + jnp.dot(
        key_low_grad, key_full.T, preferred_element_type=jnp.float32
    )
    normed_grad = normed_grad + jnp.dot(
        value_low_grad, value_full.T, preferred_element_type=jnp.float32
    )
    query_term = jnp.dot(normed_low.T, query_low_grad, preferred_element_type=jnp.float32)
    key_term = jnp.dot(normed_low.T, key_low_grad, preferred_element_type=jnp.float32)
    value_term = jnp.dot(normed_low.T, value_low_grad, preferred_element_type=jnp.float32)
    _, input_pull = jax.vjp(rms_scale, residual, gain_in)
    input_extra, gain_in_grad = input_pull(normed_grad)
    input_grad = after_grad + input_extra
    gains_term = jnp.concatenate([gain_in_grad, gain_mid_grad, gain_query_grad, gain_key_grad])
    query_sum, key_total, value_total, output_sum, router_sum, gains_sum = (
        lax.psum_scatter(query_term, ("rep", "ep"), scatter_dimension=0, tiled=True),
        lax.psum_scatter(key_term, ("rep", "ep"), scatter_dimension=0, tiled=True),
        lax.psum_scatter(value_term, ("rep", "ep"), scatter_dimension=0, tiled=True),
        lax.psum_scatter(output_term, ("rep", "ep"), scatter_dimension=0, tiled=True),
        lax.psum_scatter(router_term, ("rep", "ep"), scatter_dimension=0, tiled=True),
        lax.psum_scatter(gains_term, ("rep", "ep"), scatter_dimension=0, tiled=True),
    )
    return (
        block_out,
        input_grad,
        query_sum,
        key_total,
        value_total,
        output_sum,
        router_sum,
        gains_sum,
        gate_w_grad,
        up_w_grad,
        down_w_grad,
    )


MESH = pl.DeviceIdType.MESH


def partners(e):
    sib = e + 1 - 2 * (e % 2)
    xn = e + 2 - 4 * ((e // 2) % 2)
    yn = e + 4 - 8 * ((e // 4) % 2)
    dg = xn + 4 - 8 * ((e // 4) % 2)
    return sib, (xn, yn, dg)


def greet(z, e, reps, across):
    barrier = pltpu.get_barrier_semaphore()
    sib, chips = partners(e)
    for other in (sib, *chips):
        pl.semaphore_signal(barrier, inc=1, device_id={"rep": z, "ep": other}, device_id_type=MESH)
    if across:
        @pl.when(z > 0)
        def _():
            pl.semaphore_signal(barrier, inc=1, device_id={"rep": z - 1, "ep": e}, device_id_type=MESH)
        @pl.when(z < reps - 1)
        def _():
            pl.semaphore_signal(barrier, inc=1, device_id={"rep": z + 1, "ep": e}, device_id_type=MESH)
    peers = 4
    if across:
        peers = peers + jnp.where(z > 0, 1, 0) + jnp.where(z < reps - 1, 1, 0)
    pl.semaphore_wait(barrier, peers)


def ag_kernel(reps, across, x_ref, out_ref, own_sem, zs, zr, ps, pr, cs, cr):
    z = lax.axis_index("rep")
    e = lax.axis_index("ep")
    sib, chips = partners(e)
    greet(z, e, reps, across)
    own = z if across else 0
    groups = reps if across else 1
    half = x_ref.shape[0] // 2
    local = pltpu.make_async_copy(x_ref, out_ref.at[own, e], own_sem)
    local.start()

    def zcopy(src, g, up):
        d = 0 if up else 1
        return pltpu.make_async_remote_copy(
            src_ref=src, dst_ref=out_ref.at[g, e], send_sem=zs.at[d, g], recv_sem=zr.at[g],
            device_id={"rep": z + 1 if up else z - 1, "ep": e}, device_id_type=MESH)

    def pcopy(src, g, j):
        return pltpu.make_async_remote_copy(
            src_ref=src, dst_ref=out_ref.at[g, e], send_sem=ps.at[g, j], recv_sem=pr.at[g, j],
            device_id={"rep": z, "ep": chips[j]}, device_id_type=MESH)

    def relay(g, j):
        rows = pl.ds(half * j, half)
        part = out_ref.at[g, chips[j], rows]
        return pltpu.make_async_remote_copy(
            src_ref=part, dst_ref=part, send_sem=ps.at[g, 2 + j], recv_sem=pr.at[g, 2 + j],
            device_id={"rep": z, "ep": chips[1 - j]}, device_id_type=MESH)

    def relayed(g, j):
        part = out_ref.at[g, chips[2], pl.ds(half * j, half)]
        return pltpu.make_async_remote_copy(
            src_ref=part, dst_ref=part, send_sem=ps.at[g, 2 + j], recv_sem=pr.at[g, 2 + j],
            device_id={"rep": z, "ep": chips[1 - j]}, device_id_type=MESH)

    def ccopy(src, g, j):
        who = e if j == 0 else chips[j - 1]
        return pltpu.make_async_remote_copy(
            src_ref=src, dst_ref=out_ref.at[g, who], send_sem=cs.at[g, j], recv_sem=cr.at[g, j],
            device_id={"rep": z, "ep": sib}, device_id_type=MESH)

    def spread(src, g):
        pcopy(src, g, 0).start()
        pcopy(src, g, 1).start()
        ccopy(src, g, 0).start()

    def pass_on(g):
        for j in range(2):
            pcopy(x_ref, g, j).wait_recv()
            relay(g, j).start()
            ccopy(out_ref.at[g, chips[j]], g, j + 1).start()

    def finish(g):
        for j in range(2):
            relayed(g, j).wait_recv()
        ccopy(out_ref.at[g, chips[2]], g, 3).start()

    def at(k, fn):
        if k == 0:
            fn(own)
            return
        @pl.when(z - k >= 0)
        def _():
            fn(z - k)
        @pl.when(z + k < reps)
        def _():
            fn(z + k)

    if across:
        @pl.when(z < reps - 1)
        def _():
            zcopy(x_ref, z, True).start()
        @pl.when(z > 0)
        def _():
            zcopy(x_ref, z, False).start()
    spread(x_ref, own)
    for k in range(1, groups):
        @pl.when(z - k >= 0)
        def _():
            g = z - k
            zcopy(x_ref, g, True).wait_recv()
            @pl.when(z < reps - 1)
            def _():
                zcopy(out_ref.at[g, e], g, True).start()
            spread(out_ref.at[g, e], g)
        @pl.when(z + k < reps)
        def _():
            g = z + k
            zcopy(x_ref, g, False).wait_recv()
            @pl.when(z > 0)
            def _():
                zcopy(out_ref.at[g, e], g, False).start()
            spread(out_ref.at[g, e], g)
        at(k - 1, pass_on)
        if k >= 2:
            at(k - 2, finish)
    at(groups - 1, pass_on)
    if groups >= 2:
        at(groups - 2, finish)
    at(groups - 1, finish)
    local.wait()
    for g in range(groups):
        for j in range(4):
            ccopy(x_ref, g, j).wait()
        for j in range(2):
            pcopy(x_ref, g, j).wait_send()
            relay(g, j).wait_send()
        if across:
            @pl.when((z < reps - 1) & (z >= g))
            def _():
                zcopy(x_ref, g, True).wait_send()
            @pl.when((z > 0) & (z <= g))
            def _():
                zcopy(x_ref, g, False).wait_send()


def all_gather(x, reps, eps, across, cid):
    groups = reps if across else 1
    D = pltpu.SemaphoreType.DMA
    out = pl.pallas_call(
        partial(ag_kernel, reps, across),
        out_shape=jax.ShapeDtypeStruct((groups, eps, *x.shape), x.dtype),
        in_specs=[pl.BlockSpec(memory_space=pl.ANY)],
        out_specs=pl.BlockSpec(memory_space=pl.ANY),
        scratch_shapes=[D, D((2, reps)), D((reps,)), D((groups, 4)), D((groups, 4)), D((groups, 4)), D((groups, 4))],
        compiler_params=pltpu.CompilerParams(collective_id=cid, has_side_effects=True),
    )(x)
    return out


def rs_kernel(reps, across, p_ref, out_ref, own, sib_in, chip_in, up_in, down_in, res,
              own_sem, ss, sr, ps, pr, us, ur, ds, dr):
    z = lax.axis_index("rep")
    e = lax.axis_index("ep")
    core = e % 2
    chip = e // 2
    sib, chips = partners(e)
    groups = reps if across else 1
    greet(z, e, reps, across)
    rows, W = res.shape[1], res.shape[2]
    half = reps // 2

    def order(s):
        if not across:
            return 0
        t = reps - 1 - s
        down = jnp.where(t > z, t, t - 1)
        upw = jnp.where(s < z, s, s + 1)
        g = jnp.where(z < half, down, upw)
        return z if s == reps - 1 else g

    def sibcopy(g):
        return pltpu.make_async_remote_copy(
            src_ref=p_ref.at[g, :, 1 - core], dst_ref=sib_in.at[g], send_sem=ss.at[g], recv_sem=sr.at[g],
            device_id={"rep": z, "ep": sib}, device_id_type=MESH)

    def load(g):
        return pltpu.make_async_copy(p_ref.at[g, :, core], own.at[g], own_sem.at[g])

    def pcopy(g, j):
        return pltpu.make_async_remote_copy(
            src_ref=own.at[g, chips[j] // 2], dst_ref=chip_in.at[g, j], send_sem=ps.at[g, j], recv_sem=pr.at[g, j],
            device_id={"rep": z, "ep": chips[j]}, device_id_type=MESH)

    def zcopy(g, up):
        if up:
            return pltpu.make_async_remote_copy(
                src_ref=res.at[g], dst_ref=up_in.at[g], send_sem=us.at[g], recv_sem=ur.at[g],
                device_id={"rep": z + 1, "ep": e}, device_id_type=MESH)
        return pltpu.make_async_remote_copy(
            src_ref=res.at[g], dst_ref=down_in.at[g], send_sem=ds.at[g], recv_sem=dr.at[g],
            device_id={"rep": z - 1, "ep": e}, device_id_type=MESH)

    for s in range(groups):
        g = order(s)
        sibcopy(g).start()
        load(g).start()
    step = 16

    def add_in(g, q):
        @pl.loop(0, rows // step)
        def _(i):
            r = pl.ds(pl.multiple_of(i * step, step), step)
            own[g, q, r, :] = (own[g, q, r, :].astype(jnp.float32) + sib_in[g, q, r, :].astype(jnp.float32)).astype(own.dtype)

    def stage1(g):
        load(g).wait()
        sibcopy(g).wait_recv()
        for j in (2, 0, 1):
            add_in(g, chips[j] // 2)
            pcopy(g, j).start()

    def stage2(g):
        for j in range(3):
            pcopy(g, j).wait_recv()
        @pl.loop(0, rows // step)
        def _(i):
            r = pl.ds(pl.multiple_of(i * step, step), step)
            t = own[g, chip, r, :].astype(jnp.float32) + sib_in[g, chip, r, :].astype(jnp.float32)
            for j in range(3):
                t = t + chip_in[g, j, r, :].astype(jnp.float32)
            res[g, r, :] = t.astype(res.dtype)

    def plus(g, ref):
        @pl.loop(0, rows // step)
        def _(i):
            r = pl.ds(pl.multiple_of(i * step, step), step)
            res[g, r, :] = (res[g, r, :].astype(jnp.float32) + ref[g, r, :].astype(jnp.float32)).astype(res.dtype)

    def stage3(g):
        @pl.when(g > z)
        def _():
            @pl.when(z > 0)
            def _():
                zcopy(g, True).wait_recv()
                plus(g, up_in)
            zcopy(g, True).start()
        @pl.when(g < z)
        def _():
            @pl.when(z < reps - 1)
            def _():
                zcopy(g, False).wait_recv()
                plus(g, down_in)
            zcopy(g, False).start()

    stage1(order(0))
    for s in range(1, groups):
        stage1(order(s))
        stage2(order(s - 1))
        if s >= 2:
            stage3(order(s - 2))
    stage2(order(groups - 1))
    if across:
        stage3(order(groups - 2))
        @pl.when(z > 0)
        def _():
            zcopy(z, True).wait_recv()
            plus(z, up_in)
        @pl.when(z < reps - 1)
        def _():
            zcopy(z, False).wait_recv()
            plus(z, down_in)
    fin = res.at[z if across else 0]
    out = pltpu.make_async_copy(fin, out_ref, own_sem.at[0])
    out.start()
    out.wait()
    for g in range(groups):
        sibcopy(g).wait_send()
        for j in range(3):
            pcopy(g, j).wait_send()
        if across:
            @pl.when(g > z)
            def _():
                zcopy(g, True).wait_send()
            @pl.when(g < z)
            def _():
                zcopy(g, False).wait_send()


def reduce_scatter(p, reps, eps, across, cid):
    groups = reps if across else 1
    W = p.shape[1]
    rows = p.shape[0] // groups // eps
    p = p.reshape(groups, eps // 2, 2, rows, W)
    D = pltpu.SemaphoreType.DMA
    V = pltpu.VMEM
    q = eps // 2
    return pl.pallas_call(
        partial(rs_kernel, reps, across),
        out_shape=jax.ShapeDtypeStruct((rows, W), p.dtype),
        in_specs=[pl.BlockSpec(memory_space=pl.ANY)],
        out_specs=pl.BlockSpec(memory_space=pl.ANY),
        scratch_shapes=[V((groups, q, rows, W), p.dtype), V((groups, q, rows, W), p.dtype), V((groups, 3, rows, W), p.dtype),
                        V((groups, rows, W), p.dtype), V((groups, rows, W), p.dtype), V((groups, rows, W), p.dtype),
                        D((groups,)), D((groups,)), D((groups,)), D((groups, 3)), D((groups, 3)),
                        D((groups,)), D((groups,)), D((groups,)), D((groups,))],
        compiler_params=pltpu.CompilerParams(collective_id=cid, has_side_effects=True, vmem_limit_bytes=56 * 2**20),
    )(p)

NT = (((1,), (1,)), ((), ()))
TN = (((0,), (0,)), ((), ()))


def visit_order(reps):
    return [sorted((g for g in range(reps) if g != z), key=lambda g: (abs(g - z), g)) + [z] for z in range(reps)]


def moe_kernel(reps, side_lanes, experts_all, x_ref, cot_ref, eg_ref, eu_ref, ed_ref,
               row_ref, moe_ref, gout_ref, uout_ref, dout_ref,
               mid_ref, a_ref, b_ref, h_ref, xin_ref, yin_ref, zin_ref,
               wgu, wd, xbuf, cbuf, abuf, pbuf, sib_in, relay_in, sendbuf, ownbuf, rbuf, tmp, colbuf, gst, dst,
               own_sem, w_sem, x_sem, c_sem, ab_sem, t_sem, col_sem, g_sem, o_sem,
               zs, zr, ps, pr, cs, cr, ss, sr, hs, hr, qs, qr, fs, fr):
    f32, bf16 = jnp.float32, jnp.bfloat16
    z = lax.axis_index("rep")
    e = lax.axis_index("ep")
    core = e % 2
    chip = e // 2
    sib, chips = partners(e)
    rows = x_ref.shape[0]
    half = rows // 2
    width = cot_ref.shape[-1]
    W1 = x_ref.shape[1]
    WP = pbuf.shape[-1]
    exp_dev = eg_ref.shape[0]
    F = wgu.shape[2] // exp_dev
    EF = exp_dev * F
    steps = 4 * reps
    table = visit_order(reps)

    def group_of(s):
        g = 0
        for zi in range(reps):
            for si in range(reps):
                g = g + jnp.where((z == zi) & (s == si), table[zi][si], 0)
        return g

    def chip_of(k):
        return jnp.where(k == 0, chips[2] // 2, jnp.where(k == 1, chip, jnp.where(k == 2, chips[0] // 2, chips[1] // 2)))

    barrier = pltpu.get_barrier_semaphore()
    for other in (sib, *chips):
        pl.semaphore_signal(barrier, inc=1, device_id={"rep": z, "ep": other}, device_id_type=MESH)
    for d in range(1, reps):
        pl.semaphore_signal(barrier, inc=1, device_id={"rep": (z + d) % reps, "ep": e}, device_id_type=MESH)
    weights = []
    for j in range(exp_dev):
        cut = pl.ds(pl.multiple_of(z * F, F), F)
        weights.append(pltpu.make_async_copy(eg_ref.at[j, :, cut], wgu.at[0, :, pl.ds(j * F, F)], w_sem.at[j]))
        weights.append(pltpu.make_async_copy(eu_ref.at[j, :, cut], wgu.at[1, :, pl.ds(j * F, F)], w_sem.at[exp_dev + j]))
        weights.append(pltpu.make_async_copy(ed_ref.at[j, cut, :], wd.at[pl.ds(j * F, F), :], w_sem.at[2 * exp_dev + j]))
    for w in weights:
        w.start()
    local = pltpu.make_async_copy(x_ref, mid_ref.at[z, e], own_sem)
    local.start()
    pl.semaphore_wait(barrier, 4 + reps - 1)

    def zcopy(src, g, up):
        d = 0 if up else 1
        return pltpu.make_async_remote_copy(
            src_ref=src, dst_ref=mid_ref.at[g, e], send_sem=zs.at[d, g], recv_sem=zr.at[g],
            device_id={"rep": z + 1 if up else z - 1, "ep": e}, device_id_type=MESH)

    def pcopy(src, g, j):
        return pltpu.make_async_remote_copy(
            src_ref=src, dst_ref=mid_ref.at[g, e], send_sem=ps.at[g, j], recv_sem=pr.at[g, j],
            device_id={"rep": z, "ep": chips[j]}, device_id_type=MESH)

    def relay(g, j, source):
        part = mid_ref.at[g, source, pl.ds(half * j, half)]
        return pltpu.make_async_remote_copy(
            src_ref=part, dst_ref=part, send_sem=ps.at[g, 2 + j], recv_sem=pr.at[g, 2 + j],
            device_id={"rep": z, "ep": chips[1 - j]}, device_id_type=MESH)

    def ccopy(src, g, j):
        who = e if j == 0 else chips[j - 1]
        return pltpu.make_async_remote_copy(
            src_ref=src, dst_ref=mid_ref.at[g, who], send_sem=cs.at[g, j], recv_sem=cr.at[g, j],
            device_id={"rep": z, "ep": sib}, device_id_type=MESH)

    def spread(src, g):
        pcopy(src, g, 0).start()
        pcopy(src, g, 1).start()
        ccopy(src, g, 0).start()

    def pass_on(g):
        for j in range(2):
            pcopy(x_ref, g, j).wait_recv()
            relay(g, j, chips[j]).start()
            ccopy(mid_ref.at[g, chips[j]], g, j + 1).start()

    def finish_in(g):
        for j in range(2):
            relay(g, j, chips[2]).wait_recv()
        ccopy(mid_ref.at[g, chips[2]], g, 3).start()

    def at(k, fn):
        if k == 0:
            fn(z)
            return
        @pl.when(z - k >= 0)
        def _():
            fn(z - k)
        @pl.when(z + k < reps)
        def _():
            fn(z + k)

    def arrive(k):
        @pl.when(z - k >= 0)
        def _():
            g = z - k
            zcopy(x_ref, g, True).wait_recv()
            @pl.when(z < reps - 1)
            def _():
                zcopy(mid_ref.at[g, e], g, True).start()
            spread(mid_ref.at[g, e], g)
        @pl.when(z + k < reps)
        def _():
            g = z + k
            zcopy(x_ref, g, False).wait_recv()
            @pl.when(z > 0)
            def _():
                zcopy(mid_ref.at[g, e], g, False).start()
            spread(mid_ref.at[g, e], g)

    def ready(g):
        for j in range(4):
            ccopy(x_ref, g, j).wait_recv()

    def load_x(i):
        g, q = group_of(i // 4), chip_of(i % 4)
        return pltpu.make_async_copy(mid_ref.at[g, pl.ds(2 * q, 2)], xbuf.at[i % 2], x_sem.at[i % 2])

    def load_c(i):
        g, q = group_of(i // 4), chip_of(i % 4)
        return pltpu.make_async_copy(cot_ref.at[g, pl.ds(2 * q, 2)], cbuf.at[i % 2], c_sem.at[i % 2])

    def keep(i, m):
        g, q = group_of(i // 4), chip_of(i % 4)
        place = pl.ds(pl.multiple_of((g * 4 + q) * 2 * rows, 2 * rows), 2 * rows)
        return pltpu.make_async_copy(abuf.at[i % 2, m], (a_ref, b_ref, h_ref)[m].at[place], ab_sem.at[i % 2, m])

    def compute(i):
        slot = i % 2
        lane = lax.broadcasted_iota(jnp.int32, (2 * rows, side_lanes), 1)
        side = xbuf[slot, :, :, pl.ds(width, side_lanes)].reshape(2 * rows, side_lanes).astype(f32)

        def one(j, cots):
            cols = pl.ds(pl.multiple_of(j * F, F), F)
            x = xbuf[slot, :, :, pl.ds(0, width)].reshape(2 * rows, width)
            c = cbuf[slot].reshape(2 * rows, width)
            index = e * exp_dev + j
            w = jnp.sum(jnp.where((lane == index) | (lane == index + experts_all), side, 0.0), axis=1, keepdims=True)
            ga = jnp.dot(x, wgu[0, :, cols], preferred_element_type=f32)
            up = jnp.dot(x, wgu[1, :, cols], preferred_element_type=f32)
            hc = lax.dot_general(c, wd[cols, :], NT, preferred_element_type=f32)
            sigma = 1.0 / (1.0 + jnp.exp(-ga))
            silu = ga * sigma
            hid = (silu * up).astype(bf16).astype(f32)
            hcw = hc * w
            abuf[slot, 0, :, cols] = (hcw * up * (sigma * (1.0 + ga * (1.0 - sigma)))).astype(bf16)
            abuf[slot, 1, :, cols] = (hcw * silu).astype(bf16)
            abuf[slot, 2, :, cols] = (hid * w).astype(bf16)
            dots = jnp.sum(hid * hc, axis=1, keepdims=True)
            return cots + jnp.where(lane == index, dots, 0.0)

        cots = lax.fori_loop(0, exp_dev, one, jnp.zeros((2 * rows, side_lanes), f32))
        pbuf[slot, :, :, pl.ds(width, side_lanes)] = cots.astype(bf16).reshape(2, rows, side_lanes)
        block = min(512, width)

        @pl.loop(0, width // block)
        def _(n):
            cut = pl.ds(pl.multiple_of(n * block, block), block)
            t = lax.dot_general(abuf[slot, 0], wgu[0, cut, :], NT, preferred_element_type=f32)
            t = t + lax.dot_general(abuf[slot, 1], wgu[1, cut, :], NT, preferred_element_type=f32)
            pbuf[slot, :, :, cut] = t.astype(bf16).reshape(2, rows, block)
            t = jnp.dot(abuf[slot, 2], wd[:, cut], preferred_element_type=f32)
            cut = pl.ds(pl.multiple_of(W1 + n * block, 128), block)
            pbuf[slot, :, :, cut] = t.astype(bf16).reshape(2, rows, block)

    def sibcopy(i):
        return pltpu.make_async_remote_copy(
            src_ref=pbuf.at[i % 2, 1 - core], dst_ref=sib_in.at[i % 4], send_sem=ss.at[i], recv_sem=sr.at[i],
            device_id={"rep": z, "ep": sib}, device_id_type=MESH)

    def hcopy(s, j):
        part = pl.ds(half * j, half)
        return pltpu.make_async_remote_copy(
            src_ref=sendbuf.at[0, part], dst_ref=relay_in.at[s, j], send_sem=hs.at[s, j], recv_sem=hr.at[s, j],
            device_id={"rep": z, "ep": chips[j]}, device_id_type=MESH)

    def qcopy(s, j):
        return pltpu.make_async_remote_copy(
            src_ref=sendbuf.at[1 + j], dst_ref=(xin_ref, yin_ref)[j].at[s], send_sem=qs.at[s, j], recv_sem=qr.at[s, j],
            device_id={"rep": z, "ep": chips[j]}, device_id_type=MESH)

    def fcopy(s, g):
        return pltpu.make_async_remote_copy(
            src_ref=rbuf.at[s % 2], dst_ref=zin_ref.at[z], send_sem=fs.at[s], recv_sem=fr.at[z],
            device_id={"rep": g, "ep": e}, device_id_type=MESH)

    step = 16

    def add(out, terms, count=rows):
        @pl.loop(0, count // step)
        def _(i):
            r = pl.ds(pl.multiple_of(i * step, step), step)
            t = terms[0][r, :].astype(f32)
            for other in terms[1:]:
                t = t + other[r, :].astype(f32)
            out[r, :] = t.astype(out.dtype)

    def finish(i):
        s, k = i // 4, i % 4
        sibcopy(i).wait_recv()
        mine, other = pbuf.at[i % 2, core], sib_in.at[i % 4]
        lower, upper = pl.ds(0, half), pl.ds(half, half)
        @pl.when(k == 1)
        def _():
            add(ownbuf.at[s % 2], (mine, other))
        @pl.when(k == 0)
        def _():
            @pl.when(s > 0)
            def _():
                hcopy(s - 1, 0).wait_send()
                hcopy(s - 1, 1).wait_send()
            add(sendbuf.at[0], (mine, other))
            hcopy(s, 0).start()
            hcopy(s, 1).start()
        @pl.when(k == 2)
        def _():
            @pl.when(s > 0)
            def _():
                qcopy(s - 1, 0).wait_send()
            add(sendbuf.at[1, lower], (mine.at[lower], other.at[lower]), half)
            hcopy(s, 1).wait_recv()
            add(sendbuf.at[1, upper], (mine.at[upper], other.at[upper], relay_in.at[s, 1]), half)
            qcopy(s, 0).start()
        @pl.when(k == 3)
        def _():
            @pl.when(s > 0)
            def _():
                qcopy(s - 1, 1).wait_send()
            add(sendbuf.at[2, upper], (mine.at[upper], other.at[upper]), half)
            hcopy(s, 0).wait_recv()
            add(sendbuf.at[2, lower], (mine.at[lower], other.at[lower], relay_in.at[s, 0]), half)
            qcopy(s, 1).start()

    def load_t(src, m):
        return pltpu.make_async_copy(src, tmp.at[m], t_sem.at[m])

    def total(s):
        for j in range(2):
            qcopy(s, j).wait_recv()
            load_t((xin_ref, yin_ref)[j].at[s], j).start()
        for j in range(2):
            load_t((xin_ref, yin_ref)[j].at[s], j).wait()

    def plane_sum(s):
        total(s)
        @pl.when(s >= 2)
        def _():
            fcopy(s - 2, group_of(s - 2)).wait_send()
        add(rbuf.at[s % 2], (ownbuf.at[s % 2], tmp.at[0], tmp.at[1]))
        fcopy(s, group_of(s)).start()

    @pl.when(z < reps - 1)
    def _():
        zcopy(x_ref, z, True).start()
    @pl.when(z > 0)
    def _():
        zcopy(x_ref, z, False).start()
    spread(x_ref, z)
    arrive(1)
    pass_on(z)
    arrive(2)
    at(1, pass_on)
    finish_in(z)
    arrive(3)
    at(2, pass_on)
    at(1, finish_in)
    for w in weights:
        w.wait()
    ready(group_of(0))
    load_x(0).start()
    load_c(0).start()

    @pl.loop(0, steps)
    def _(i):
        load_x(i).wait()
        load_c(i).wait()
        @pl.when(i == 3)
        def _():
            at(3, pass_on)
            at(2, finish_in)
        @pl.when(i == 7)
        def _():
            at(3, finish_in)
        @pl.when(i == steps - 5)
        def _():
            local.wait()
        @pl.when(i < steps - 1)
        def _():
            @pl.when(i % 4 == 3)
            def _():
                ready(group_of(i // 4 + 1))
            load_x(i + 1).start()
            load_c(i + 1).start()
        @pl.when(i >= 2)
        def _():
            sibcopy(i - 2).wait_send()
            for m in range(3):
                keep(i - 2, m).wait()
        compute(i)
        sibcopy(i).start()
        for m in range(3):
            keep(i, m).start()
        @pl.when(i >= 1)
        def _():
            finish(i - 1)
        @pl.when((i % 4 == 3) & (i >= 7) & (i < steps - 1))
        def _():
            plane_sum(i // 4 - 1)

    for i in (steps - 2, steps - 1):
        sibcopy(i).wait_send()
        for m in range(3):
            keep(i, m).wait()
    finish(steps - 1)
    plane_sum(reps - 2)

    blocks = width // 256
    halves = wgu.shape[1]

    def resident(src, m):
        return pltpu.make_async_copy(src.at[pl.ds(m * halves, halves)], wgu.at[m], w_sem.at[m])

    def load_col(src, n):
        return pltpu.make_async_copy(src.at[:, :, :, pl.ds(pl.multiple_of(n * 256, 256), 256)], colbuf.at[n % 2], col_sem.at[n % 2])

    def product(n, m):
        left = colbuf[n % 2, pl.ds(m * (reps // 2), reps // 2)].reshape(halves, 256)
        return left, wgu[m]

    def grad_rows(src, out):
        def store(n, j):
            per = width // reps
            place = pl.ds(pl.multiple_of((n * 256) % per, 256), 256)
            return pltpu.make_async_copy(gst.at[n % 2, j], out.at[((n * 256) // per + reps - z) % reps, j, place], g_sem.at[n % 2, j])
        for m in range(2):
            resident(src, m).start()
        load_col(mid_ref, 0).start()
        for m in range(2):
            resident(src, m).wait()
        @pl.loop(0, blocks)
        def _(n):
            load_col(mid_ref, n).wait()
            @pl.when(n < blocks - 1)
            def _():
                load_col(mid_ref, n + 1).start()
            @pl.when(n >= 2)
            def _():
                for j in range(exp_dev):
                    store(n - 2, j).wait()
            t = jnp.zeros((256, EF), f32)
            for m in range(2):
                left, right = product(n, m)
                t = t + lax.dot_general(left, right, TN, preferred_element_type=f32)
            for j in range(exp_dev):
                gst[n % 2, j] = t[:, j * F:(j + 1) * F].astype(bf16)
                store(n, j).start()
        for n in (blocks - 2, blocks - 1):
            for j in range(exp_dev):
                store(n, j).wait()

    def grad_down():
        def store(n):
            return pltpu.make_async_copy(dst.at[n % 2], dout_ref.at[:, :, pl.ds(pl.multiple_of(n * 256, 256), 256)], g_sem.at[n % 2, 0])
        for m in range(2):
            resident(h_ref, m).start()
        load_col(cot_ref, 0).start()
        for m in range(2):
            resident(h_ref, m).wait()
        @pl.loop(0, blocks)
        def _(n):
            load_col(cot_ref, n).wait()
            @pl.when(n < blocks - 1)
            def _():
                load_col(cot_ref, n + 1).start()
            @pl.when(n >= 2)
            def _():
                store(n - 2).wait()
            t = jnp.zeros((EF, 256), f32)
            for m in range(2):
                left, right = product(n, m)
                t = t + lax.dot_general(right, left, TN, preferred_element_type=f32)
            dst[n % 2] = t.reshape(exp_dev, F, 256)
            store(n).start()
        for n in (blocks - 2, blocks - 1):
            store(n).wait()

    grad_rows(a_ref, gout_ref)
    grad_rows(b_ref, uout_ref)
    grad_down()

    last = reps - 1
    total(last)
    for d in range(1, reps):
        src = (z + d) % reps
        pltpu.make_async_remote_copy(
            src_ref=rbuf.at[0], dst_ref=zin_ref.at[src], send_sem=fs.at[last], recv_sem=fr.at[src],
            device_id={"rep": src, "ep": e}, device_id_type=MESH).wait_recv()
        load_t(zin_ref.at[src], 1 + d).start()
    for d in range(1, reps):
        load_t(zin_ref.at[(z + d) % reps], 1 + d).wait()
    fcopy(reps - 3, group_of(reps - 3)).wait_send()
    add(rbuf.at[(reps - 3) % 2], (ownbuf.at[last % 2], *(tmp.at[m] for m in range(reps + 1))))
    outs = (
        pltpu.make_async_copy(rbuf.at[(reps - 3) % 2, :, pl.ds(0, W1)], row_ref, o_sem.at[0]),
        pltpu.make_async_copy(rbuf.at[(reps - 3) % 2, :, pl.ds(W1, width)], moe_ref, o_sem.at[1]),
    )
    for o in outs:
        o.start()
    for o in outs:
        o.wait()
    fcopy(reps - 2, group_of(reps - 2)).wait_send()
    for j in range(2):
        hcopy(last, j).wait_send()
        qcopy(last, j).wait_send()
    for g in range(reps):
        for j in range(4):
            ccopy(x_ref, g, j).wait_send()
        for j in range(2):
            pcopy(x_ref, g, j).wait_send()
            relay(g, j, chips[j]).wait_send()
        @pl.when((z < reps - 1) & (z >= g))
        def _():
            zcopy(x_ref, g, True).wait_send()
        @pl.when((z > 0) & (z <= g))
        def _():
            zcopy(x_ref, g, False).wait_send()


def moe(x, cot_all, eg, eu, ed, experts_all, cid):
    reps, eps, rows, width = cot_all.shape
    W1 = x.shape[1]
    side = W1 - width
    WP = W1 + width
    exp_dev, _, ff = eg.shape
    F = ff // reps
    EF = exp_dev * F
    f32, bf16 = jnp.float32, jnp.bfloat16
    D, V = pltpu.SemaphoreType.DMA, pltpu.VMEM
    S = jax.ShapeDtypeStruct
    tokens = reps * eps * rows
    steps = 4 * reps
    outs = (
        S((rows, W1), bf16), S((rows, width), bf16),
        S((reps, exp_dev, width // reps, F), bf16), S((reps, exp_dev, width // reps, F), bf16), S((exp_dev, F, width), f32),
        S((reps, eps, rows, W1), bf16), S((tokens, EF), bf16), S((tokens, EF), bf16), S((tokens, EF), bf16),
        S((reps, rows, WP), bf16), S((reps, rows, WP), bf16), S((reps, rows, WP), bf16),
    )
    return pl.pallas_call(
        partial(moe_kernel, reps, side, experts_all),
        out_shape=outs,
        in_specs=[pl.BlockSpec(memory_space=pl.ANY)] * 5,
        out_specs=[pl.BlockSpec(memory_space=pl.ANY)] * len(outs),
        scratch_shapes=[
            V((2, width, EF), bf16), V((EF, width), bf16),
            V((2, 2, rows, W1), bf16), V((2, 2, rows, width), bf16),
            V((2, 3, 2 * rows, EF), bf16), V((2, 2, rows, WP), bf16), V((4, rows, WP), bf16),
            V((reps, 2, rows // 2, WP), bf16), V((3, rows, WP), bf16), V((2, rows, WP), bf16), V((2, rows, WP), bf16),
            V((5, rows, WP), bf16), V((2, reps, eps, rows, 256), bf16),
            V((2, exp_dev, 256, F), bf16), V((2, exp_dev, F, 256), f32),
            D, D((3 * exp_dev,)), D((2,)), D((2,)), D((2, 3)), D((5,)), D((2,)), D((2, exp_dev)), D((2,)),
            D((2, reps)), D((reps,)), D((reps, 4)), D((reps, 4)), D((reps, 4)), D((reps, 4)),
            D((steps,)), D((steps,)), D((reps, 2)), D((reps, 2)), D((reps, 2)), D((reps, 2)), D((reps,)), D((reps,)),
        ],
        compiler_params=pltpu.CompilerParams(collective_id=cid, has_side_effects=True, vmem_limit_bytes=63 * 2**20),
    )(x, cot_all, eg, eu, ed)[:5]


def last_kernel(reps, eps, part_ref, qkv_ref, out_ref, tok_ref, cot_ref, gain_ref, gains_ref, router_ref,
                input_ref, q_ref, k_ref, v_ref, o_ref, gsum_ref, rsum_ref,
                own, sib_in, relay_in, xin, yin, wo, qown, zq, zo, fin, gath, mats, omat, tok, cot, gain,
                gown, gin, gz, gmid, rown, rin, rz, rmid,
                l_sem, ss, sr, hs, hr, qs, qr, ws, wr, zs, zr, zos, zor, ps, pr, gs, gr, gzs, gzr, rs, rr, rzs, rzr):
    f32, bf16 = jnp.float32, jnp.bfloat16
    z = lax.axis_index("rep")
    e = lax.axis_index("ep")
    core = e % 2
    chip = e // 2
    sib, chips = partners(e)
    rows, width = tok_ref.shape
    half = rows // 2
    rows_dev = o_ref.shape[0]
    heads_dev = out_ref.shape[0]
    head_dim = width // (heads_dev * eps)
    slice_width = heads_dev * head_dim

    barrier = pltpu.get_barrier_semaphore()
    for d in range(1, eps):
        pl.semaphore_signal(barrier, inc=1, device_id={"rep": z, "ep": (e + d) % eps}, device_id_type=MESH)
    for d in range(1, reps):
        pl.semaphore_signal(barrier, inc=1, device_id={"rep": (z + d) % reps, "ep": e}, device_id_type=MESH)
    loads = [
        pltpu.make_async_copy(part_ref.at[:, core], own, l_sem.at[0]),
        pltpu.make_async_copy(qkv_ref.at[z], qown, l_sem.at[1]),
        pltpu.make_async_copy(out_ref.at[:, core], wo.at[core], l_sem.at[2]),
        pltpu.make_async_copy(tok_ref, tok, l_sem.at[3]),
        pltpu.make_async_copy(cot_ref, cot, l_sem.at[4]),
        pltpu.make_async_copy(gain_ref, gain, l_sem.at[5]),
        pltpu.make_async_copy(gains_ref, gown, l_sem.at[6]),
        pltpu.make_async_copy(router_ref, rown, l_sem.at[7]),
    ]
    for c in loads:
        c.start()
    pl.semaphore_wait(barrier, eps - 1 + reps - 1)

    def to_sib(src, dst, send, recv):
        return pltpu.make_async_remote_copy(src_ref=src, dst_ref=dst, send_sem=send, recv_sem=recv,
                                            device_id={"rep": z, "ep": sib}, device_id_type=MESH)

    def to_chip(src, dst, send, recv, j):
        return pltpu.make_async_remote_copy(src_ref=src, dst_ref=dst, send_sem=send, recv_sem=recv,
                                            device_id={"rep": z, "ep": chips[j]}, device_id_type=MESH)

    def to_plane(src, dst, send, recv, d):
        return pltpu.make_async_remote_copy(src_ref=src, dst_ref=dst, send_sem=send, recv_sem=recv,
                                            device_id={"rep": z, "ep": (e + d) % eps}, device_id_type=MESH)

    def to_rep(src, dst, send, recv, d):
        return pltpu.make_async_remote_copy(src_ref=src, dst_ref=dst, send_sem=send, recv_sem=recv,
                                            device_id={"rep": (z + d) % reps, "ep": e}, device_id_type=MESH)

    zcopies = [to_rep(qkv_ref.at[(z + d) % reps], zq.at[d - 1], zs.at[d - 1], zr.at[d - 1], d) for d in range(1, reps)]
    ocopies = [to_rep(wo.at[((z + d) % reps) // heads_dev, (z + d) % heads_dev], zo.at[d - 1], zos.at[d - 1], zor.at[d - 1], d)
               for d in range(1, reps)]
    wcopy = to_sib(out_ref.at[:, 1 - core], wo.at[core], ws, wr)
    order = (chips[2] // 2, chips[0] // 2, chips[1] // 2, chip)
    scopies = [to_sib(part_ref.at[q, 1 - core], sib_in.at[q], ss.at[n], sr.at[n]) for n, q in enumerate(order)]
    for c in scopies:
        c.start()
    wcopy.start()
    for c in zcopies:
        c.start()
    step = 16

    def add(out, terms, count):
        @pl.loop(0, count // step)
        def _(i):
            r = pl.ds(pl.multiple_of(i * step, step), step)
            t = terms[0][r, :].astype(f32)
            for other in terms[1:]:
                t = t + other[r, :].astype(f32)
            out[r, :] = t.astype(out.dtype)

    lower, upper = pl.ds(0, half), pl.ds(half, half)
    hcopies = [to_chip(own.at[order[0], (lower, upper)[j]], relay_in.at[j], hs.at[j], hr.at[j], j) for j in range(2)]
    qcopies = [to_chip(own.at[order[1 + j]], (xin, yin)[j], qs.at[j], qr.at[j], j) for j in range(2)]
    loads[0].wait()
    scopies[0].wait_recv()
    d = own.at[order[0]]
    add(d, (d, sib_in.at[order[0]]), rows)
    for c in hcopies:
        c.start()
    for j in range(2):
        mine, other = own.at[order[1 + j]], sib_in.at[order[1 + j]]
        scopies[1 + j].wait_recv()
        direct, through = ((lower, upper), (upper, lower))[j]
        add(mine.at[direct], (mine.at[direct], other.at[direct]), half)
        hcopies[1 - j].wait_recv()
        add(mine.at[through], (mine.at[through], other.at[through], relay_in.at[1 - j]), half)
        qcopies[j].start()
    loads[2].wait()
    wcopy.wait_recv()
    for c in ocopies:
        c.start()
    scopies[3].wait_recv()
    for c in loads[3:]:
        c.wait()
    for c in qcopies:
        c.wait_recv()

    gown[0:1, :] = jnp.zeros((1, width), f32)

    @pl.loop(0, rows // step)
    def _(i):
        r = pl.ds(pl.multiple_of(i * step, step), step)
        nc = (own[chip, r, :].astype(f32) + sib_in[chip, r, :].astype(f32) + xin[r, :].astype(f32) + yin[r, :].astype(f32))
        t = tok[r, :].astype(f32)
        scale = lax.rsqrt(jnp.mean(t * t, axis=-1, keepdims=True) + 1e-6)
        unit = t * scale
        scaled = nc * gain[0:1, :]
        cot[r, :] = cot[r, :] + scale * (scaled - unit * jnp.mean(scaled * unit, axis=-1, keepdims=True))
        gown[0:1, :] += jnp.sum(nc * unit, axis=0, keepdims=True)

    done = [pltpu.make_async_copy(cot, input_ref, l_sem.at[8])]
    done[0].start()

    gcopies = [to_plane(gown, gin.at[d - 1], gs.at[d - 1], gr.at[d - 1], d) for d in range(1, eps)]
    rcopies = [to_plane(rown.at[:, (e + d) % eps], rin.at[d - 1], rs.at[d - 1], rr.at[d - 1], d) for d in range(1, eps)]
    for c in (*gcopies, *rcopies):
        c.start()
    for c in (*gcopies, *rcopies):
        c.wait_recv()
    t = gown[...]
    for d in range(1, eps):
        t = t + gin[d - 1]
    gmid[...] = t
    t = rown[:, e]
    for d in range(1, eps):
        t = t + rin[d - 1]
    rmid[...] = t
    gzcopies = [to_rep(gmid, gz.at[d - 1], gzs.at[d - 1], gzr.at[d - 1], d) for d in range(1, reps)]
    rzcopies = [to_rep(rmid.at[(z + d) % reps], rz.at[d - 1], rzs.at[d - 1], rzr.at[d - 1], d) for d in range(1, reps)]
    for c in (*gzcopies, *rzcopies):
        c.start()

    loads[1].wait()
    for c in zcopies:
        c.wait_recv()
    for n in range(eps):
        @pl.loop(0, rows_dev // step)
        def _(i):
            r = pl.ds(pl.multiple_of(i * step, step), step)
            a = pl.ds(pl.multiple_of(n * rows_dev + i * step, step), step)
            t = qown[a, :].astype(f32)
            for d in range(reps - 1):
                t = t + zq[d, a, :].astype(f32)
            fin[n, r, :] = t.astype(bf16)
    pcopies = [to_plane(fin.at[(e + d) % eps], gath.at[e], ps.at[d - 1], pr.at[d - 1], d) for d in range(1, eps)]
    for c in pcopies:
        c.start()
    mine = pltpu.make_async_copy(fin.at[e], gath.at[e], l_sem.at[9])
    mine.start()
    for c in (*gzcopies, *rzcopies, *ocopies):
        c.wait_recv()
    for c in gcopies:
        c.wait_send()
    t = gmid[...]
    for d in range(reps - 1):
        t = t + gz[d]
    gown[...] = t
    t = rmid[z]
    for d in range(reps - 1):
        t = t + rz[d]
    rmid[z] = t
    done.append(pltpu.make_async_copy(gown, gsum_ref, l_sem.at[10]))
    done.append(pltpu.make_async_copy(rmid.at[z], rsum_ref, l_sem.at[11]))
    wmine = wo.at[z // heads_dev, z % heads_dev]

    @pl.loop(0, rows_dev // step)
    def _(i):
        r = pl.ds(pl.multiple_of(i * step, step), step)
        t = wmine[r, :].astype(f32)
        for d in range(reps - 1):
            t = t + zo[d, r, :].astype(f32)
        omat[r, :] = t
    done.append(pltpu.make_async_copy(omat, o_ref, l_sem.at[12]))
    for c in rzcopies:
        c.wait_send()
    for c in done[1:]:
        c.start()
    mine.wait()
    for c in pcopies:
        c.wait_recv()
    for src in range(eps):
        for m in range(3):
            for i in range(heads_dev):
                head = ((src % 2) * heads_dev + i) * (eps // 2) + src // 2
                mats[m, :, head * head_dim:(head + 1) * head_dim] = gath[src, :, m * slice_width + i * head_dim:m * slice_width + (i + 1) * head_dim].astype(f32)
    for m, ref in enumerate((q_ref, k_ref, v_ref)):
        done.append(pltpu.make_async_copy(mats.at[m], ref, l_sem.at[13 + m]))
        done[-1].start()
    for c in done:
        c.wait()
    for c in (*scopies, wcopy, *zcopies, *ocopies, *hcopies, *qcopies, *pcopies, *rcopies, *gzcopies):
        c.wait_send()


def last_sums(part, qkv_term, out_term, tokens, after_cot, gain_in, gains, router, rows_dev, reps, eps, cid):
    rows, width = tokens.shape
    f32, bf16 = jnp.float32, jnp.bfloat16
    heads_dev = out_term.shape[0]
    slices = qkv_term.shape[2]
    q = eps // 2
    half = rows // 2
    D, V = pltpu.SemaphoreType.DMA, pltpu.VMEM
    S = jax.ShapeDtypeStruct
    g8, rt = gains.shape, router.shape[2:]
    outs = (S((rows, width), f32), *[S((rows_dev, width), f32)] * 4, S(g8, f32), S(rt, f32))
    return pl.pallas_call(
        partial(last_kernel, reps, eps),
        out_shape=outs,
        in_specs=[pl.BlockSpec(memory_space=pl.ANY)] * 8,
        out_specs=[pl.BlockSpec(memory_space=pl.ANY)] * len(outs),
        scratch_shapes=[
            V((q, rows, width), bf16), V((q, rows, width), bf16), V((2, half, width), bf16), V((rows, width), bf16), V((rows, width), bf16),
            V((2, heads_dev, rows_dev, width), bf16), V((rows_dev * eps, slices), bf16), V((reps - 1, rows_dev * eps, slices), bf16),
            V((reps - 1, rows_dev, width), bf16), V((eps, rows_dev, slices), bf16), V((eps, rows_dev, slices), bf16),
            V((3, rows_dev, width), f32), V((rows_dev, width), f32), V((rows, width), bf16), V((rows, width), f32), V((1, width), f32),
            V(g8, f32), V((eps - 1, *g8), f32), V((reps - 1, *g8), f32), V(g8, f32),
            V(router.shape, f32), V((eps - 1, reps, *rt), f32), V((reps - 1, *rt), f32), V((reps, *rt), f32),
            D((16,)), D((4,)), D((4,)), D((2,)), D((2,)), D((2,)), D((2,)), D, D,
            D((reps - 1,)), D((reps - 1,)), D((reps - 1,)), D((reps - 1,)), D((eps - 1,)), D((eps - 1,)),
            D((eps - 1,)), D((eps - 1,)), D((reps - 1,)), D((reps - 1,)), D((eps - 1,)), D((eps - 1,)), D((reps - 1,)), D((reps - 1,)),
        ],
        compiler_params=pltpu.CompilerParams(collective_id=cid, has_side_effects=True, vmem_limit_bytes=56 * 2**20),
    )(part, qkv_term, out_term, tokens, after_cot, gain_in, gains, router)


def join_kernel(count, *refs):
    ins, out = refs[:count], refs[count]
    shift = (lax.axis_index("rep") + count - pl.program_id(1)) % count
    for k in range(count):
        @pl.when(shift == k)
        def _():
            out[...] = ins[k][...].astype(out.dtype)


def join_columns(pieces):
    count = len(pieces)
    exp_dev, rows, cols = pieces[0].shape
    return pl.pallas_call(
        partial(join_kernel, count),
        grid=(exp_dev, count),
        out_shape=jax.ShapeDtypeStruct((exp_dev, rows, cols * count), jnp.float32),
        in_specs=[pl.BlockSpec((1, rows, cols), lambda j, s: (j, 0, 0))] * count,
        out_specs=pl.BlockSpec((1, rows, cols), lambda j, s: (j, 0, s)),
    )(*pieces)


def gather_block(block, axes):
    return lax.all_gather(block, axes, axis=0, tiled=True)


def scatter_sum(partial_sums, axes):
    return lax.psum_scatter(partial_sums, axes, scatter_dimension=0, tiled=True)


def on_device_split(
    tokens,
    cotangent,
    query_weight,
    key_weight,
    value_weight,
    output_weight,
    router_weight,
    gains,
    expert_gate,
    expert_up,
    expert_down,
    lengths,
    deal,
    routes,
    priority,
):
    bf16, f32 = jnp.bfloat16, jnp.float32
    tok_dev, width = tokens.shape
    ep_count, rep_count = lax.axis_size("ep"), lax.axis_size("rep")
    ep_index, rep_index = lax.axis_index("ep"), lax.axis_index("rep")
    exp_dev, _, ff_width = expert_gate.shape
    top_count = routes.shape[1]
    experts_all = exp_dev * ep_count
    group_rows = tok_dev * ep_count
    capacity = 5 * tok_dev * top_count // (4 * exp_dev)
    head_dim = HD
    heads_dev = width // head_dim // ep_count
    slice_width = heads_dev * head_dim
    rows_dev = query_weight.shape[0]
    score_scale = head_dim ** (-0.5)
    core = ep_index % 2
    every = ("rep", "ep")

    gains_dev = gains.shape[0]
    packed = jnp.concatenate(
        [gains, router_weight.reshape(-1), jnp.zeros((2048 - gains_dev - router_weight.size,), bf16)]
    ).reshape(16, 128)
    packed_all = gather_block(packed, every).reshape(rep_count * ep_count, 2048)
    gains_float = packed_all[:, :gains_dev].reshape(-1).astype(f32)
    router_full = packed_all[:, gains_dev : gains_dev + router_weight.size].reshape(width, experts_all)
    gain_in = gains_float[:width]
    gain_mid = gains_float[width : 2 * width]
    gain_query = gains_float[2 * width : 2 * width + head_dim]
    gain_key = gains_float[2 * width + head_dim :]
    numbers = jnp.concatenate([deal, priority, routes.T.reshape(-1)]).reshape(-1, 128)
    numbers_all = gather_block(numbers, "ep").reshape(ep_count, -1, tok_dev)
    deal_all = numbers_all[:, 0].reshape(-1)
    priority_all = numbers_all[:, 1].reshape(-1)
    routes_all = numbers_all[:, 2:].transpose(0, 2, 1).reshape(group_rows, top_count)
    segment_all, position_all = placement(deal_all, lengths[0])

    chips = ep_count // 2
    def columns_of(weight):
        parts = weight.reshape(rows_dev, 2, heads_dev, chips, head_dim).transpose(3, 1, 0, 2, 4)
        parts = parts.reshape(ep_count, rows_dev, slice_width)
        return lax.all_to_all(parts, "ep", split_axis=0, concat_axis=0, tiled=True)

    qkv_rows = jnp.concatenate(
        [columns_of(query_weight), columns_of(key_weight), columns_of(value_weight)], axis=2
    ).reshape(ep_count * rows_dev, 3 * slice_width)
    qkv_slice = gather_block(qkv_rows, "rep")
    out_rows = gather_block(output_weight, "rep").reshape(2, heads_dev, rows_dev, width)
    out_own = lax.dynamic_index_in_dim(out_rows, core, 0, keepdims=False)
    out_other = lax.ppermute(
        lax.dynamic_index_in_dim(out_rows, 1 - core, 0, keepdims=False),
        "ep",
        [(i, i + 1 - 2 * (i % 2)) for i in range(ep_count)],
    )
    out_slice = jnp.where(
        core == 0,
        jnp.concatenate([out_own, out_other], axis=1),
        jnp.concatenate([out_other, out_own], axis=1),
    ).reshape(slice_width, width)

    cot_all = all_gather(cotangent, rep_count, ep_count, True, 0)
    tokens_group = (
        all_gather(tokens, rep_count, ep_count, False, 1).reshape(group_rows, width).astype(f32)
    )
    normed_group = rms_scale(tokens_group, gain_in).astype(bf16)
    projected = jnp.dot(normed_group, qkv_slice, preferred_element_type=f32)
    query_pre = projected[:, :slice_width].reshape(group_rows, heads_dev, head_dim)
    key_pre = projected[:, slice_width : 2 * slice_width].reshape(group_rows, heads_dev, head_dim)
    value_low = projected[:, 2 * slice_width :].astype(bf16).reshape(group_rows, heads_dev, head_dim)
    query_low = rope_norm(query_pre, gain_query, position_all).astype(bf16)
    key_low = rope_norm(key_pre, gain_key, position_all).astype(bf16)
    same_seq = segment_all[:, None] == segment_all[None, :]
    mixed, top_score, total_sum = attend_forward(
        (query_low, key_low, value_low), same_seq, score_scale
    )
    mixed_low = mixed.reshape(group_rows, slice_width).astype(bf16)
    attn_part = jnp.dot(mixed_low, out_slice, preferred_element_type=f32).astype(bf16)
    residual = tokens.astype(f32)
    after_attn = residual + reduce_scatter(attn_part, rep_count, ep_count, False, 2).astype(f32)
    mid_low = rms_scale(after_attn, gain_mid).astype(bf16)

    logits = jnp.dot(mid_low, router_full, preferred_element_type=f32)
    expert_ids = jnp.arange(experts_all, dtype=jnp.int32)
    member = (routes[:, :, None] == expert_ids[None, None, :]).astype(f32)
    named = jnp.sum(member, axis=1)
    lifted = jnp.where(named > 0, logits, masked_score)
    lifted = jnp.exp(lifted - jnp.max(lifted, axis=-1, keepdims=True)) * named
    gate_dense = lifted / jnp.sum(lifted, axis=-1, keepdims=True)
    onehot_all = jnp.sum(
        (routes_all[:, :, None] == expert_ids[None, None, :]).astype(bf16), axis=1
    )
    earlier = (priority_all[None, :] < priority[:, None]).astype(bf16)
    slots = jnp.dot(earlier, onehot_all, preferred_element_type=f32)
    kept_dense = named * (slots < capacity).astype(f32)
    pair_weight = gate_dense * kept_dense

    weight_high = pair_weight.astype(bf16)
    weight_low = (pair_weight - weight_high.astype(f32)).astype(bf16)
    side = jnp.concatenate(
        [weight_high, weight_low, jnp.zeros((tok_dev, 128 - 2 * experts_all), bf16)], axis=1
    )
    row_sum, moe_sum, gate_term, up_term, down_w_grad = moe(
        jnp.concatenate([mid_low, side], axis=1),
        cot_all,
        expert_gate,
        expert_up,
        expert_down,
        experts_all,
        3,
    )
    moe_out = moe_sum.astype(f32)
    block_out = (after_attn + moe_out).astype(bf16)

    def rows_of(parts):
        pieces = [parts[0]]
        for k in range(1, rep_count):
            pieces.append(
                lax.ppermute(parts[k], "rep", [(i, (i + k) % rep_count) for i in range(rep_count)])
            )
        return pieces

    gate_pieces, up_pieces = rows_of(gate_term), rows_of(up_term)

    out_grad = cotangent.astype(f32)
    gate_cot = row_sum[:, width : width + experts_all].astype(f32) * kept_dense
    chosen_cot = gate_dense * (gate_cot - jnp.sum(gate_dense * gate_cot, axis=-1, keepdims=True))
    logit_cot = chosen_cot.astype(bf16)
    mid_cot = row_sum[:, :width].astype(f32) + jnp.dot(
        logit_cot, router_full.T, preferred_element_type=f32
    )
    router_term = jnp.dot(mid_low.T, logit_cot, preferred_element_type=f32)
    _, mid_pull = jax.vjp(rms_scale, after_attn, gain_mid)
    after_extra, gain_mid_cot = mid_pull(mid_cot)
    after_cot = out_grad + after_extra
    attn_cot_group = all_gather(
        after_cot.astype(bf16), rep_count, ep_count, False, 6
    ).reshape(group_rows, width)

    mixed_cot = jnp.dot(attn_cot_group, out_slice.T, preferred_element_type=f32).astype(bf16)
    output_term = jnp.dot(mixed_low.T, attn_cot_group, preferred_element_type=f32)
    query_cot, key_cot, value_cot = attend_backward(
        (
            query_low,
            key_low,
            value_low,
            mixed_cot.reshape(group_rows, heads_dev, head_dim),
            top_score,
            total_sum,
        ),
        same_seq,
        score_scale,
    )
    _, query_pull = jax.vjp(
        lambda pre, gain_vec: rope_norm(pre, gain_vec, position_all), query_pre, gain_query
    )
    query_pre_cot, gain_query_cot = query_pull(query_cot)
    _, key_pull = jax.vjp(
        lambda pre, gain_vec: rope_norm(pre, gain_vec, position_all), key_pre, gain_key
    )
    key_pre_cot, gain_key_cot = key_pull(key_cot)
    pre_cot = jnp.concatenate(
        [
            part.reshape(group_rows, slice_width).astype(bf16)
            for part in (query_pre_cot, key_pre_cot, value_cot)
        ],
        axis=1,
    )
    normed_part = jnp.dot(pre_cot, qkv_slice.T, preferred_element_type=f32).astype(bf16)
    qkv_term = jnp.dot(normed_group.T, pre_cot, preferred_element_type=f32).astype(bf16)
    gains_term = jnp.concatenate(
        [
            jnp.zeros((width,), f32),
            gain_mid_cot,
            gain_query_cot,
            gain_key_cot,
            jnp.zeros((6 * width - 2 * head_dim,), f32),
        ]
    ).reshape(8, width)
    router_rows = router_weight.size // 128
    router_parts = jnp.pad(
        router_term.reshape(rep_count, ep_count, router_rows, 128),
        ((0, 0), (0, 0), (0, -router_rows % 8), (0, 0)),
    )
    input_grad, query_sum, key_sum, value_sum, output_sum, gains_all, router_own = last_sums(
        normed_part.reshape(ep_count // 2, 2, tok_dev, width),
        qkv_term.reshape(rep_count, ep_count * rows_dev, 3 * slice_width),
        output_term.astype(bf16).reshape(heads_dev, 2, rows_dev, width),
        tokens,
        after_cot,
        gain_in.reshape(1, width),
        gains_term,
        router_parts,
        rows_dev,
        rep_count,
        ep_count,
        4,
    )
    gains_sum = lax.dynamic_slice_in_dim(
        gains_all.reshape(-1), (rep_index * ep_count + ep_index) * gains_dev, gains_dev
    )
    router_sum = router_own[:router_rows].reshape(rows_dev, experts_all)
    gate_w_grad, up_w_grad = join_columns(gate_pieces), join_columns(up_pieces)
    return (
        block_out,
        input_grad,
        query_sum,
        key_sum,
        value_sum,
        output_sum,
        router_sum,
        gains_sum,
        gate_w_grad,
        up_w_grad,
        down_w_grad,
    )


def solution(mesh):
    placed = (
        P(("rep", "ep"), None),
        P(("rep", "ep"), None),
        P(("rep", "ep"), None),
        P(("rep", "ep"), None),
        P(("rep", "ep"), None),
        P(("rep", "ep"), None),
        P(("rep", "ep"), None),
        P(("rep", "ep")),
        P("ep", None, None),
        P("ep", None, None),
        P("ep", None, None),
        P("rep", None),
        P(("rep", "ep")),
        P(("rep", "ep"), None),
        P(("rep", "ep")),
    )
    return jax.shard_map(
        on_device_split if mesh.shape["rep"] == 4 else on_device_general,
        mesh=mesh,
        in_specs=placed,
        out_specs=(
            P(("rep", "ep"), None),
            P(("rep", "ep"), None),
            P(("rep", "ep"), None),
            P(("rep", "ep"), None),
            P(("rep", "ep"), None),
            P(("rep", "ep"), None),
            P(("rep", "ep"), None),
            P(("rep", "ep")),
            P("ep", "rep", None),
            P("ep", "rep", None),
            P("ep", "rep", None),
        ),
        check_vma=False,
    )
```

```python
from functools import partial

import jax
import jax.numpy as jnp
from jax import lax
from jax.experimental import pallas as pl
from jax.experimental.pallas import tpu as pltpu
from jax.sharding import PartitionSpec as P

HD = 128


norm_eps = 1e-06
rope_base = 10000.0
masked_score = -1e30
highest = lax.Precision.HIGHEST


def rms_scale(values, gain_vec):
    return (
        values * lax.rsqrt(jnp.mean(values * values, axis=-1, keepdims=True) + norm_eps) * gain_vec
    )


def rotate(values, positions):
    half_width = values.shape[-1] // 2
    frequency = rope_base ** (-2.0 * jnp.arange(half_width, dtype=jnp.float32) / values.shape[-1])
    angles = positions.astype(jnp.float32)[:, None] * frequency[None, :]
    cosine = jnp.cos(angles)[:, None, :]
    sine_part = jnp.sin(angles)[:, None, :]
    low_half = values[..., :half_width]
    high_half = values[..., half_width:]
    return jnp.concatenate(
        [low_half * cosine - high_half * sine_part, high_half * cosine + low_half * sine_part],
        axis=-1,
    )


def placement(deal_rows, lengths_row):
    seq_ends = jnp.cumsum(lengths_row)
    is_after = (seq_ends[None, :] <= deal_rows[:, None]).astype(jnp.int32)
    segment = jnp.sum(is_after, axis=1)
    seq_start = jnp.sum(is_after * lengths_row[None, :], axis=1)
    return (segment, deal_rows - seq_start)


def rope_norm(projected, gain_vec, positions):
    return rotate(rms_scale(projected, gain_vec), positions)


def attend_forward(parts, same_seq, score_scale):
    head_query, head_key, head_value = parts
    scores = (
        jnp.einsum("thd,shd->hts", head_query, head_key, preferred_element_type=jnp.float32)
        * score_scale
    )
    scores = jnp.where(same_seq[None], scores, masked_score)
    top_score = jnp.max(scores, axis=-1, keepdims=True)
    lifted = jnp.exp(scores - top_score)
    total_sum = jnp.sum(lifted, axis=-1, keepdims=True)
    prob_low = (lifted / total_sum).astype(jnp.bfloat16)
    mixed_out = jnp.einsum("hts,shd->thd", prob_low, head_value, preferred_element_type=jnp.float32)
    return (mixed_out, top_score, total_sum)


def attend_backward(parts, same_seq, score_scale):
    head_query, head_key, head_value, head_grad, top_score, total_sum = parts
    scores = (
        jnp.einsum("thd,shd->hts", head_query, head_key, preferred_element_type=jnp.float32)
        * score_scale
    )
    scores = jnp.where(same_seq[None], scores, masked_score)
    prob_full = jnp.exp(scores - top_score) / total_sum
    prob_low = prob_full.astype(jnp.bfloat16)
    prob_grad = jnp.einsum(
        "thd,shd->hts", head_grad, head_value, preferred_element_type=jnp.float32
    )
    row_dot = jnp.sum(prob_full * prob_grad, axis=-1, keepdims=True)
    score_grad = (prob_full * (prob_grad - row_dot)).astype(jnp.bfloat16)
    query_grad = (
        jnp.einsum("hts,shd->thd", score_grad, head_key, preferred_element_type=jnp.float32)
        * score_scale
    )
    key_grad = (
        jnp.einsum("hts,thd->shd", score_grad, head_query, preferred_element_type=jnp.float32)
        * score_scale
    )
    value_grad = jnp.einsum("hts,thd->shd", prob_low, head_grad, preferred_element_type=jnp.float32)
    return (query_grad, key_grad, value_grad)


def attend_again(parts, same_seq, score_scale):
    head_query, head_key, head_value, head_grad = parts
    _, top_score, total_sum = attend_forward(
        (head_query, head_key, head_value), same_seq, score_scale
    )
    return attend_backward((*parts, top_score, total_sum), same_seq, score_scale)


def on_device_general(
    tokens,
    cotangent,
    query_weight,
    key_weight,
    value_weight,
    output_weight,
    router_weight,
    gains,
    expert_gate,
    expert_up,
    expert_down,
    lengths,
    deal,
    routes,
    priority,
):
    tok_dev, width = tokens.shape
    ep_count = lax.axis_size("ep")
    ep_index = lax.axis_index("ep")
    exp_dev = expert_gate.shape[0]
    top_count = routes.shape[1]
    experts_all = exp_dev * ep_count
    group_rows = tok_dev * ep_count
    send_most = min(tok_dev, 3 * tok_dev * top_count // (2 * experts_all))
    capacity = 5 * tok_dev * top_count // (4 * exp_dev)
    head_dim = HD
    head_count = width // head_dim
    per_group = min(head_count, 4)
    group_count = head_count // per_group
    score_scale = head_dim ** (-0.5)
    query_full, key_full, value_full, output_full, router_full, gains_full = (
        lax.all_gather(query_weight, ("rep", "ep"), axis=0, tiled=True),
        lax.all_gather(key_weight, ("rep", "ep"), axis=0, tiled=True),
        lax.all_gather(value_weight, ("rep", "ep"), axis=0, tiled=True),
        lax.all_gather(output_weight, ("rep", "ep"), axis=0, tiled=True),
        lax.all_gather(router_weight, ("rep", "ep"), axis=0, tiled=True),
        lax.all_gather(gains, ("rep", "ep"), axis=0, tiled=True),
    )
    gains_float = gains_full.astype(jnp.float32)
    gain_in = gains_float[:width]
    gain_mid = gains_float[width : 2 * width]
    gain_query = gains_float[2 * width : 2 * width + head_dim]
    gain_key = gains_float[2 * width + head_dim :]
    deal_all, priority_all, routes_all = (
        lax.all_gather(deal, "ep", axis=0, tiled=True),
        lax.all_gather(priority, "ep", axis=0, tiled=True),
        lax.all_gather(routes, "ep", axis=0, tiled=True),
    )
    segment_all, position_all = placement(deal_all, lengths[0])
    segment_own = lax.dynamic_slice_in_dim(segment_all, ep_index * tok_dev, tok_dev)
    position_own = lax.dynamic_slice_in_dim(position_all, ep_index * tok_dev, tok_dev)
    residual = tokens.astype(jnp.float32)
    normed_low = rms_scale(residual, gain_in).astype(jnp.bfloat16)
    query_pre = jnp.dot(normed_low, query_full, preferred_element_type=jnp.float32).reshape(
        tok_dev, head_count, head_dim
    )
    key_pre = jnp.dot(normed_low, key_full, preferred_element_type=jnp.float32).reshape(
        tok_dev, head_count, head_dim
    )
    value_low = jnp.dot(normed_low, value_full, preferred_element_type=jnp.float32).astype(
        jnp.bfloat16
    )
    query_low = rope_norm(query_pre, gain_query, position_own).astype(jnp.bfloat16)
    key_low = (
        rope_norm(key_pre, gain_key, position_own).astype(jnp.bfloat16).reshape(tok_dev, width)
    )
    key_group, value_group = (
        lax.all_gather(key_low, "ep", axis=0, tiled=True),
        lax.all_gather(value_low, "ep", axis=0, tiled=True),
    )
    same_seq = segment_own[:, None] == segment_all[None, :]
    query_heads = query_low.reshape(tok_dev, group_count, per_group, head_dim).transpose(1, 0, 2, 3)
    key_heads = key_group.reshape(group_rows, group_count, per_group, head_dim).transpose(
        1, 0, 2, 3
    )
    value_heads = value_group.reshape(group_rows, group_count, per_group, head_dim).transpose(
        1, 0, 2, 3
    )
    mixed_heads, top_heads, total_heads = lax.map(
        partial(attend_forward, same_seq=same_seq, score_scale=score_scale),
        (query_heads, key_heads, value_heads),
    )
    mixed_low = mixed_heads.transpose(1, 0, 2, 3).reshape(tok_dev, width).astype(jnp.bfloat16)
    after_attn = residual + jnp.dot(mixed_low, output_full, preferred_element_type=jnp.float32)
    mid_low = rms_scale(after_attn, gain_mid).astype(jnp.bfloat16)
    logits = jnp.dot(mid_low, router_full, preferred_element_type=jnp.float32)
    chosen = jnp.take_along_axis(logits, routes, axis=1)
    gate_prob = jax.nn.softmax(chosen, axis=-1)
    expert_ids = jnp.arange(experts_all, dtype=jnp.int32)
    onehot_all = jnp.sum(
        (routes_all[:, :, None] == expert_ids[None, None, :]).astype(jnp.float32), axis=1
    )
    earlier = (priority_all[None, :] < priority_all[:, None]).astype(jnp.float32)
    slot_all = jnp.take_along_axis(
        jnp.dot(earlier, onehot_all, precision=highest), routes_all, axis=1
    ).astype(jnp.int32)
    row_ids = jnp.arange(tok_dev, dtype=jnp.int32)
    lower_tri = (row_ids[:, None] > row_ids[None, :]).astype(jnp.float32)
    before = jnp.einsum(
        "ij,dje->die",
        lower_tri,
        onehot_all.reshape(ep_count, tok_dev, experts_all),
        precision=highest,
    ).reshape(group_rows, experts_all)
    place_all = jnp.take_along_axis(before, routes_all, axis=1).astype(jnp.int32)
    kept_all = slot_all < capacity
    kept_own = lax.dynamic_slice_in_dim(kept_all, ep_index * tok_dev, tok_dev)
    place_own = lax.dynamic_slice_in_dim(place_all, ep_index * tok_dev, tok_dev)
    buffer_index = (routes * send_most + place_own).reshape(-1)
    rows_out = jnp.where(
        kept_own[:, :, None], mid_low[:, None, :], jnp.zeros((), jnp.bfloat16)
    ).reshape(tok_dev * top_count, width)
    send_rows = (
        jnp.zeros((experts_all * send_most, width), jnp.bfloat16)
        .at[buffer_index]
        .set(rows_out)
        .reshape(experts_all, send_most, width)
    )
    received = lax.all_to_all(send_rows, "ep", split_axis=0, concat_axis=1, tiled=True)
    gate_part = jnp.einsum(
        "erd,edf->erf", received, expert_gate, preferred_element_type=jnp.float32
    )
    up_part = jnp.einsum("erd,edf->erf", received, expert_up, preferred_element_type=jnp.float32)
    hidden = (jax.nn.silu(gate_part) * up_part).astype(jnp.bfloat16)
    result = jnp.einsum(
        "erf,efd->erd", hidden, expert_down, preferred_element_type=jnp.float32
    ).astype(jnp.bfloat16)
    returned = lax.all_to_all(result, "ep", split_axis=1, concat_axis=0, tiled=True)
    pair_out = returned.reshape(experts_all * send_most, width)[buffer_index].reshape(
        tok_dev, top_count, width
    )
    pair_weight = gate_prob * kept_own.astype(jnp.float32)
    moe_out = jnp.einsum("tk,tkd->td", pair_weight, pair_out, preferred_element_type=jnp.float32)
    block_out = (after_attn + moe_out).astype(jnp.bfloat16)
    out_grad = cotangent.astype(jnp.float32)
    pair_gate_grad = kept_own.astype(jnp.float32) * jnp.einsum(
        "tkd,td->tk", pair_out, out_grad, preferred_element_type=jnp.float32
    )
    pair_grad = (
        (pair_weight[:, :, None] * out_grad[:, None, :])
        .astype(jnp.bfloat16)
        .reshape(tok_dev * top_count, width)
    )
    grad_send = (
        jnp.zeros((experts_all * send_most, width), jnp.bfloat16)
        .at[buffer_index]
        .set(pair_grad)
        .reshape(experts_all, send_most, width)
    )
    grad_received = lax.all_to_all(grad_send, "ep", split_axis=0, concat_axis=1, tiled=True)
    hidden_grad = jnp.einsum(
        "erd,efd->erf", grad_received, expert_down, preferred_element_type=jnp.float32
    )
    _, silu_pull = jax.vjp(lambda gate_in, up_in: jax.nn.silu(gate_in) * up_in, gate_part, up_part)
    gate_part_grad, up_part_grad = silu_pull(hidden_grad)
    gate_low_grad = gate_part_grad.astype(jnp.bfloat16)
    up_low_grad = up_part_grad.astype(jnp.bfloat16)
    down_term = jnp.einsum(
        "erf,erd->efd", hidden, grad_received, preferred_element_type=jnp.float32
    )
    gate_term = jnp.einsum(
        "erd,erf->edf", received, gate_low_grad, preferred_element_type=jnp.float32
    )
    up_term = jnp.einsum("erd,erf->edf", received, up_low_grad, preferred_element_type=jnp.float32)
    rows_grad = (
        jnp.einsum("erf,edf->erd", gate_low_grad, expert_gate, preferred_element_type=jnp.float32)
        + jnp.einsum("erf,edf->erd", up_low_grad, expert_up, preferred_element_type=jnp.float32)
    ).astype(jnp.bfloat16)
    back_rows = lax.all_to_all(rows_grad, "ep", split_axis=1, concat_axis=0, tiled=True)
    mid_grad = jnp.sum(
        back_rows.reshape(experts_all * send_most, width)[buffer_index]
        .reshape(tok_dev, top_count, width)
        .astype(jnp.float32),
        axis=1,
    )
    gate_w_grad, up_w_grad, down_w_grad = (
        lax.psum_scatter(
            gate_term.astype(jnp.bfloat16), "rep", scatter_dimension=1, tiled=True
        ).astype(jnp.float32),
        lax.psum_scatter(
            up_term.astype(jnp.bfloat16), "rep", scatter_dimension=1, tiled=True
        ).astype(jnp.float32),
        lax.psum_scatter(
            down_term.astype(jnp.bfloat16), "rep", scatter_dimension=1, tiled=True
        ).astype(jnp.float32),
    )
    _, soft_pull = jax.vjp(lambda values: jax.nn.softmax(values, axis=-1), chosen)
    (chosen_grad,) = soft_pull(pair_gate_grad)
    onehot_own = (routes[:, :, None] == expert_ids[None, None, :]).astype(jnp.float32)
    logit_grad = jnp.einsum("tk,tke->te", chosen_grad, onehot_own).astype(jnp.bfloat16)
    mid_grad = mid_grad + jnp.dot(logit_grad, router_full.T, preferred_element_type=jnp.float32)
    router_term = jnp.dot(mid_low.T, logit_grad, preferred_element_type=jnp.float32)
    _, mid_pull = jax.vjp(rms_scale, after_attn, gain_mid)
    after_extra, gain_mid_grad = mid_pull(mid_grad)
    after_grad = out_grad + after_extra
    attn_low_grad = after_grad.astype(jnp.bfloat16)
    output_term = jnp.dot(mixed_low.T, attn_low_grad, preferred_element_type=jnp.float32)
    mixed_grad = jnp.dot(attn_low_grad, output_full.T, preferred_element_type=jnp.float32).astype(
        jnp.bfloat16
    )
    mixed_grad_heads = mixed_grad.reshape(tok_dev, group_count, per_group, head_dim).transpose(
        1, 0, 2, 3
    )
    query_grad_h, key_grad_h, value_grad_h = lax.map(
        partial(attend_backward, same_seq=same_seq, score_scale=score_scale),
        (query_heads, key_heads, value_heads, mixed_grad_heads, top_heads, total_heads),
    )
    query_grad_own = query_grad_h.transpose(1, 0, 2, 3).reshape(tok_dev, head_count, head_dim)
    key_grad_group = key_grad_h.transpose(1, 0, 2, 3).reshape(group_rows, width)
    value_grad_group = value_grad_h.transpose(1, 0, 2, 3).reshape(group_rows, width)
    key_sum, value_sum = (
        lax.psum_scatter(
            key_grad_group.astype(jnp.bfloat16), "ep", scatter_dimension=0, tiled=True
        ).astype(jnp.float32),
        lax.psum_scatter(
            value_grad_group.astype(jnp.bfloat16), "ep", scatter_dimension=0, tiled=True
        ).astype(jnp.float32),
    )
    value_low_grad = value_sum.astype(jnp.bfloat16)
    _, query_pull = jax.vjp(
        lambda projected, gain_vec: rope_norm(projected, gain_vec, position_own),
        query_pre,
        gain_query,
    )
    query_pre_grad, gain_query_grad = query_pull(query_grad_own)
    _, key_pull = jax.vjp(
        lambda projected, gain_vec: rope_norm(projected, gain_vec, position_own), key_pre, gain_key
    )
    key_pre_grad, gain_key_grad = key_pull(key_sum.reshape(tok_dev, head_count, head_dim))
    query_low_grad = query_pre_grad.reshape(tok_dev, width).astype(jnp.bfloat16)
    key_low_grad = key_pre_grad.reshape(tok_dev, width).astype(jnp.bfloat16)
    normed_grad = jnp.dot(query_low_grad, query_full.T, preferred_element_type=jnp.float32)
    normed_grad = normed_grad + jnp.dot(
        key_low_grad, key_full.T, preferred_element_type=jnp.float32
    )
    normed_grad = normed_grad + jnp.dot(
        value_low_grad, value_full.T, preferred_element_type=jnp.float32
    )
    query_term = jnp.dot(normed_low.T, query_low_grad, preferred_element_type=jnp.float32)
    key_term = jnp.dot(normed_low.T, key_low_grad, preferred_element_type=jnp.float32)
    value_term = jnp.dot(normed_low.T, value_low_grad, preferred_element_type=jnp.float32)
    _, input_pull = jax.vjp(rms_scale, residual, gain_in)
    input_extra, gain_in_grad = input_pull(normed_grad)
    input_grad = after_grad + input_extra
    gains_term = jnp.concatenate([gain_in_grad, gain_mid_grad, gain_query_grad, gain_key_grad])
    query_sum, key_total, value_total, output_sum, router_sum, gains_sum = (
        lax.psum_scatter(query_term, ("rep", "ep"), scatter_dimension=0, tiled=True),
        lax.psum_scatter(key_term, ("rep", "ep"), scatter_dimension=0, tiled=True),
        lax.psum_scatter(value_term, ("rep", "ep"), scatter_dimension=0, tiled=True),
        lax.psum_scatter(output_term, ("rep", "ep"), scatter_dimension=0, tiled=True),
        lax.psum_scatter(router_term, ("rep", "ep"), scatter_dimension=0, tiled=True),
        lax.psum_scatter(gains_term, ("rep", "ep"), scatter_dimension=0, tiled=True),
    )
    return (
        block_out,
        input_grad,
        query_sum,
        key_total,
        value_total,
        output_sum,
        router_sum,
        gains_sum,
        gate_w_grad,
        up_w_grad,
        down_w_grad,
    )


MESH = pl.DeviceIdType.MESH


def partners(e):
    sib = e + 1 - 2 * (e % 2)
    xn = e + 2 - 4 * ((e // 2) % 2)
    yn = e + 4 - 8 * ((e // 4) % 2)
    dg = xn + 4 - 8 * ((e // 4) % 2)
    return sib, (xn, yn, dg)


def greet(z, e, reps, across):
    barrier = pltpu.get_barrier_semaphore()
    sib, chips = partners(e)
    for other in (sib, *chips):
        pl.semaphore_signal(barrier, inc=1, device_id={"rep": z, "ep": other}, device_id_type=MESH)
    if across:
        @pl.when(z > 0)
        def _():
            pl.semaphore_signal(barrier, inc=1, device_id={"rep": z - 1, "ep": e}, device_id_type=MESH)
        @pl.when(z < reps - 1)
        def _():
            pl.semaphore_signal(barrier, inc=1, device_id={"rep": z + 1, "ep": e}, device_id_type=MESH)
    peers = 4
    if across:
        peers = peers + jnp.where(z > 0, 1, 0) + jnp.where(z < reps - 1, 1, 0)
    pl.semaphore_wait(barrier, peers)


def ag_kernel(reps, across, x_ref, out_ref, own_sem, zs, zr, ps, pr, cs, cr):
    z = lax.axis_index("rep")
    e = lax.axis_index("ep")
    sib, chips = partners(e)
    greet(z, e, reps, across)
    own = z if across else 0
    groups = reps if across else 1
    half = x_ref.shape[0] // 2
    local = pltpu.make_async_copy(x_ref, out_ref.at[own, e], own_sem)
    local.start()

    def zcopy(src, g, up):
        d = 0 if up else 1
        return pltpu.make_async_remote_copy(
            src_ref=src, dst_ref=out_ref.at[g, e], send_sem=zs.at[d, g], recv_sem=zr.at[g],
            device_id={"rep": z + 1 if up else z - 1, "ep": e}, device_id_type=MESH)

    def pcopy(src, g, j):
        return pltpu.make_async_remote_copy(
            src_ref=src, dst_ref=out_ref.at[g, e], send_sem=ps.at[g, j], recv_sem=pr.at[g, j],
            device_id={"rep": z, "ep": chips[j]}, device_id_type=MESH)

    def relay(g, j):
        rows = pl.ds(half * j, half)
        part = out_ref.at[g, chips[j], rows]
        return pltpu.make_async_remote_copy(
            src_ref=part, dst_ref=part, send_sem=ps.at[g, 2 + j], recv_sem=pr.at[g, 2 + j],
            device_id={"rep": z, "ep": chips[1 - j]}, device_id_type=MESH)

    def relayed(g, j):
        part = out_ref.at[g, chips[2], pl.ds(half * j, half)]
        return pltpu.make_async_remote_copy(
            src_ref=part, dst_ref=part, send_sem=ps.at[g, 2 + j], recv_sem=pr.at[g, 2 + j],
            device_id={"rep": z, "ep": chips[1 - j]}, device_id_type=MESH)

    def ccopy(src, g, j):
        who = e if j == 0 else chips[j - 1]
        return pltpu.make_async_remote_copy(
            src_ref=src, dst_ref=out_ref.at[g, who], send_sem=cs.at[g, j], recv_sem=cr.at[g, j],
            device_id={"rep": z, "ep": sib}, device_id_type=MESH)

    def spread(src, g):
        pcopy(src, g, 0).start()
        pcopy(src, g, 1).start()
        ccopy(src, g, 0).start()

    def pass_on(g):
        for j in range(2):
            pcopy(x_ref, g, j).wait_recv()
            relay(g, j).start()
            ccopy(out_ref.at[g, chips[j]], g, j + 1).start()

    def finish(g):
        for j in range(2):
            relayed(g, j).wait_recv()
        ccopy(out_ref.at[g, chips[2]], g, 3).start()

    def at(k, fn):
        if k == 0:
            fn(own)
            return
        @pl.when(z - k >= 0)
        def _():
            fn(z - k)
        @pl.when(z + k < reps)
        def _():
            fn(z + k)

    if across:
        @pl.when(z < reps - 1)
        def _():
            zcopy(x_ref, z, True).start()
        @pl.when(z > 0)
        def _():
            zcopy(x_ref, z, False).start()
    spread(x_ref, own)
    for k in range(1, groups):
        @pl.when(z - k >= 0)
        def _():
            g = z - k
            zcopy(x_ref, g, True).wait_recv()
            @pl.when(z < reps - 1)
            def _():
                zcopy(out_ref.at[g, e], g, True).start()
            spread(out_ref.at[g, e], g)
        @pl.when(z + k < reps)
        def _():
            g = z + k
            zcopy(x_ref, g, False).wait_recv()
            @pl.when(z > 0)
            def _():
                zcopy(out_ref.at[g, e], g, False).start()
            spread(out_ref.at[g, e], g)
        at(k - 1, pass_on)
        if k >= 2:
            at(k - 2, finish)
    at(groups - 1, pass_on)
    if groups >= 2:
        at(groups - 2, finish)
    at(groups - 1, finish)
    local.wait()
    for g in range(groups):
        for j in range(4):
            ccopy(x_ref, g, j).wait()
        for j in range(2):
            pcopy(x_ref, g, j).wait_send()
            relay(g, j).wait_send()
        if across:
            @pl.when((z < reps - 1) & (z >= g))
            def _():
                zcopy(x_ref, g, True).wait_send()
            @pl.when((z > 0) & (z <= g))
            def _():
                zcopy(x_ref, g, False).wait_send()


def all_gather(x, reps, eps, across, cid):
    groups = reps if across else 1
    D = pltpu.SemaphoreType.DMA
    out = pl.pallas_call(
        partial(ag_kernel, reps, across),
        out_shape=jax.ShapeDtypeStruct((groups, eps, *x.shape), x.dtype),
        in_specs=[pl.BlockSpec(memory_space=pl.ANY)],
        out_specs=pl.BlockSpec(memory_space=pl.ANY),
        scratch_shapes=[D, D((2, reps)), D((reps,)), D((groups, 4)), D((groups, 4)), D((groups, 4)), D((groups, 4))],
        compiler_params=pltpu.CompilerParams(collective_id=cid, has_side_effects=True),
    )(x)
    return out


def rs_kernel(reps, across, p_ref, out_ref, own, sib_in, chip_in, up_in, down_in, res,
              own_sem, ss, sr, ps, pr, us, ur, ds, dr):
    z = lax.axis_index("rep")
    e = lax.axis_index("ep")
    core = e % 2
    chip = e // 2
    sib, chips = partners(e)
    groups = reps if across else 1
    greet(z, e, reps, across)
    rows, W = res.shape[1], res.shape[2]
    half = reps // 2

    def order(s):
        if not across:
            return 0
        t = reps - 1 - s
        down = jnp.where(t > z, t, t - 1)
        upw = jnp.where(s < z, s, s + 1)
        g = jnp.where(z < half, down, upw)
        return z if s == reps - 1 else g

    def sibcopy(g):
        return pltpu.make_async_remote_copy(
            src_ref=p_ref.at[g, :, 1 - core], dst_ref=sib_in.at[g], send_sem=ss.at[g], recv_sem=sr.at[g],
            device_id={"rep": z, "ep": sib}, device_id_type=MESH)

    def load(g):
        return pltpu.make_async_copy(p_ref.at[g, :, core], own.at[g], own_sem.at[g])

    def pcopy(g, j):
        return pltpu.make_async_remote_copy(
            src_ref=own.at[g, chips[j] // 2], dst_ref=chip_in.at[g, j], send_sem=ps.at[g, j], recv_sem=pr.at[g, j],
            device_id={"rep": z, "ep": chips[j]}, device_id_type=MESH)

    def zcopy(g, up):
        if up:
            return pltpu.make_async_remote_copy(
                src_ref=res.at[g], dst_ref=up_in.at[g], send_sem=us.at[g], recv_sem=ur.at[g],
                device_id={"rep": z + 1, "ep": e}, device_id_type=MESH)
        return pltpu.make_async_remote_copy(
            src_ref=res.at[g], dst_ref=down_in.at[g], send_sem=ds.at[g], recv_sem=dr.at[g],
            device_id={"rep": z - 1, "ep": e}, device_id_type=MESH)

    for s in range(groups):
        g = order(s)
        sibcopy(g).start()
        load(g).start()
    step = 16

    def add_in(g, q):
        @pl.loop(0, rows // step)
        def _(i):
            r = pl.ds(pl.multiple_of(i * step, step), step)
            own[g, q, r, :] = (own[g, q, r, :].astype(jnp.float32) + sib_in[g, q, r, :].astype(jnp.float32)).astype(own.dtype)

    def stage1(g):
        load(g).wait()
        sibcopy(g).wait_recv()
        for j in (2, 0, 1):
            add_in(g, chips[j] // 2)
            pcopy(g, j).start()

    def stage2(g):
        for j in range(3):
            pcopy(g, j).wait_recv()
        @pl.loop(0, rows // step)
        def _(i):
            r = pl.ds(pl.multiple_of(i * step, step), step)
            t = own[g, chip, r, :].astype(jnp.float32) + sib_in[g, chip, r, :].astype(jnp.float32)
            for j in range(3):
                t = t + chip_in[g, j, r, :].astype(jnp.float32)
            res[g, r, :] = t.astype(res.dtype)

    def plus(g, ref):
        @pl.loop(0, rows // step)
        def _(i):
            r = pl.ds(pl.multiple_of(i * step, step), step)
            res[g, r, :] = (res[g, r, :].astype(jnp.float32) + ref[g, r, :].astype(jnp.float32)).astype(res.dtype)

    def stage3(g):
        @pl.when(g > z)
        def _():
            @pl.when(z > 0)
            def _():
                zcopy(g, True).wait_recv()
                plus(g, up_in)
            zcopy(g, True).start()
        @pl.when(g < z)
        def _():
            @pl.when(z < reps - 1)
            def _():
                zcopy(g, False).wait_recv()
                plus(g, down_in)
            zcopy(g, False).start()

    stage1(order(0))
    for s in range(1, groups):
        stage1(order(s))
        stage2(order(s - 1))
        if s >= 2:
            stage3(order(s - 2))
    stage2(order(groups - 1))
    if across:
        stage3(order(groups - 2))
        @pl.when(z > 0)
        def _():
            zcopy(z, True).wait_recv()
            plus(z, up_in)
        @pl.when(z < reps - 1)
        def _():
            zcopy(z, False).wait_recv()
            plus(z, down_in)
    fin = res.at[z if across else 0]
    out = pltpu.make_async_copy(fin, out_ref, own_sem.at[0])
    out.start()
    out.wait()
    for g in range(groups):
        sibcopy(g).wait_send()
        for j in range(3):
            pcopy(g, j).wait_send()
        if across:
            @pl.when(g > z)
            def _():
                zcopy(g, True).wait_send()
            @pl.when(g < z)
            def _():
                zcopy(g, False).wait_send()


def reduce_scatter(p, reps, eps, across, cid):
    groups = reps if across else 1
    W = p.shape[1]
    rows = p.shape[0] // groups // eps
    p = p.reshape(groups, eps // 2, 2, rows, W)
    D = pltpu.SemaphoreType.DMA
    V = pltpu.VMEM
    q = eps // 2
    return pl.pallas_call(
        partial(rs_kernel, reps, across),
        out_shape=jax.ShapeDtypeStruct((rows, W), p.dtype),
        in_specs=[pl.BlockSpec(memory_space=pl.ANY)],
        out_specs=pl.BlockSpec(memory_space=pl.ANY),
        scratch_shapes=[V((groups, q, rows, W), p.dtype), V((groups, q, rows, W), p.dtype), V((groups, 3, rows, W), p.dtype),
                        V((groups, rows, W), p.dtype), V((groups, rows, W), p.dtype), V((groups, rows, W), p.dtype),
                        D((groups,)), D((groups,)), D((groups,)), D((groups, 3)), D((groups, 3)),
                        D((groups,)), D((groups,)), D((groups,)), D((groups,))],
        compiler_params=pltpu.CompilerParams(collective_id=cid, has_side_effects=True, vmem_limit_bytes=56 * 2**20),
    )(p)

NT = (((1,), (1,)), ((), ()))
TN = (((0,), (0,)), ((), ()))


def visit_order(reps):
    return [sorted((g for g in range(reps) if g != z), key=lambda g: (abs(g - z), g)) + [z] for z in range(reps)]


def moe_kernel(reps, side_lanes, experts_all, x_ref, cot_ref, eg_ref, eu_ref, ed_ref,
               row_ref, moe_ref, gout_ref, uout_ref, dout_ref,
               mid_ref, a_ref, b_ref, h_ref, xin_ref, yin_ref, zin_ref,
               wgu, wd, xbuf, cbuf, abuf, pbuf, sib_in, relay_in, sendbuf, ownbuf, rbuf, tmp, colbuf, gst, dst,
               own_sem, w_sem, x_sem, c_sem, ab_sem, t_sem, col_sem, g_sem, o_sem,
               zs, zr, ps, pr, cs, cr, ss, sr, hs, hr, qs, qr, fs, fr):
    f32, bf16 = jnp.float32, jnp.bfloat16
    z = lax.axis_index("rep")
    e = lax.axis_index("ep")
    core = e % 2
    chip = e // 2
    sib, chips = partners(e)
    rows = x_ref.shape[0]
    half = rows // 2
    width = cot_ref.shape[-1]
    W1 = x_ref.shape[1]
    WP = pbuf.shape[-1]
    exp_dev = eg_ref.shape[0]
    F = wgu.shape[2] // exp_dev
    EF = exp_dev * F
    steps = 4 * reps
    table = visit_order(reps)

    def group_of(s):
        g = 0
        for zi in range(reps):
            for si in range(reps):
                g = g + jnp.where((z == zi) & (s == si), table[zi][si], 0)
        return g

    def chip_of(k):
        return jnp.where(k == 0, chips[2] // 2, jnp.where(k == 1, chip, jnp.where(k == 2, chips[0] // 2, chips[1] // 2)))

    barrier = pltpu.get_barrier_semaphore()
    for other in (sib, *chips):
        pl.semaphore_signal(barrier, inc=1, device_id={"rep": z, "ep": other}, device_id_type=MESH)
    for d in range(1, reps):
        pl.semaphore_signal(barrier, inc=1, device_id={"rep": (z + d) % reps, "ep": e}, device_id_type=MESH)
    weights = []
    for j in range(exp_dev):
        cut = pl.ds(pl.multiple_of(z * F, F), F)
        weights.append(pltpu.make_async_copy(eg_ref.at[j, :, cut], wgu.at[0, :, pl.ds(j * F, F)], w_sem.at[j]))
        weights.append(pltpu.make_async_copy(eu_ref.at[j, :, cut], wgu.at[1, :, pl.ds(j * F, F)], w_sem.at[exp_dev + j]))
        weights.append(pltpu.make_async_copy(ed_ref.at[j, cut, :], wd.at[pl.ds(j * F, F), :], w_sem.at[2 * exp_dev + j]))
    for w in weights:
        w.start()
    local = pltpu.make_async_copy(x_ref, mid_ref.at[z, e], own_sem)
    local.start()
    pl.semaphore_wait(barrier, 4 + reps - 1)

    def zcopy(src, g, up):
        d = 0 if up else 1
        return pltpu.make_async_remote_copy(
            src_ref=src, dst_ref=mid_ref.at[g, e], send_sem=zs.at[d, g], recv_sem=zr.at[g],
            device_id={"rep": z + 1 if up else z - 1, "ep": e}, device_id_type=MESH)

    def pcopy(src, g, j):
        return pltpu.make_async_remote_copy(
            src_ref=src, dst_ref=mid_ref.at[g, e], send_sem=ps.at[g, j], recv_sem=pr.at[g, j],
            device_id={"rep": z, "ep": chips[j]}, device_id_type=MESH)

    def relay(g, j, source):
        part = mid_ref.at[g, source, pl.ds(half * j, half)]
        return pltpu.make_async_remote_copy(
            src_ref=part, dst_ref=part, send_sem=ps.at[g, 2 + j], recv_sem=pr.at[g, 2 + j],
            device_id={"rep": z, "ep": chips[1 - j]}, device_id_type=MESH)

    def ccopy(src, g, j):
        who = e if j == 0 else chips[j - 1]
        return pltpu.make_async_remote_copy(
            src_ref=src, dst_ref=mid_ref.at[g, who], send_sem=cs.at[g, j], recv_sem=cr.at[g, j],
            device_id={"rep": z, "ep": sib}, device_id_type=MESH)

    def spread(src, g):
        pcopy(src, g, 0).start()
        pcopy(src, g, 1).start()
        ccopy(src, g, 0).start()

    def pass_on(g):
        for j in range(2):
            pcopy(x_ref, g, j).wait_recv()
            relay(g, j, chips[j]).start()
            ccopy(mid_ref.at[g, chips[j]], g, j + 1).start()

    def finish_in(g):
        for j in range(2):
            relay(g, j, chips[2]).wait_recv()
        ccopy(mid_ref.at[g, chips[2]], g, 3).start()

    def at(k, fn):
        if k == 0:
            fn(z)
            return
        @pl.when(z - k >= 0)
        def _():
            fn(z - k)
        @pl.when(z + k < reps)
        def _():
            fn(z + k)

    def arrive(k):
        @pl.when(z - k >= 0)
        def _():
            g = z - k
            zcopy(x_ref, g, True).wait_recv()
            @pl.when(z < reps - 1)
            def _():
                zcopy(mid_ref.at[g, e], g, True).start()
            spread(mid_ref.at[g, e], g)
        @pl.when(z + k < reps)
        def _():
            g = z + k
            zcopy(x_ref, g, False).wait_recv()
            @pl.when(z > 0)
            def _():
                zcopy(mid_ref.at[g, e], g, False).start()
            spread(mid_ref.at[g, e], g)

    def ready(g):
        for j in range(4):
            ccopy(x_ref, g, j).wait_recv()

    def load_x(i):
        g, q = group_of(i // 4), chip_of(i % 4)
        return pltpu.make_async_copy(mid_ref.at[g, pl.ds(2 * q, 2)], xbuf.at[i % 2], x_sem.at[i % 2])

    def load_c(i):
        g, q = group_of(i // 4), chip_of(i % 4)
        return pltpu.make_async_copy(cot_ref.at[g, pl.ds(2 * q, 2)], cbuf.at[i % 2], c_sem.at[i % 2])

    def keep(i, m):
        g, q = group_of(i // 4), chip_of(i % 4)
        place = pl.ds(pl.multiple_of((g * 4 + q) * 2 * rows, 2 * rows), 2 * rows)
        return pltpu.make_async_copy(abuf.at[i % 2, m], (a_ref, b_ref, h_ref)[m].at[place], ab_sem.at[i % 2, m])

    def compute(i):
        slot = i % 2
        lane = lax.broadcasted_iota(jnp.int32, (2 * rows, side_lanes), 1)
        side = xbuf[slot, :, :, pl.ds(width, side_lanes)].reshape(2 * rows, side_lanes).astype(f32)

        def one(j, cots):
            cols = pl.ds(pl.multiple_of(j * F, F), F)
            x = xbuf[slot, :, :, pl.ds(0, width)].reshape(2 * rows, width)
            c = cbuf[slot].reshape(2 * rows, width)
            index = e * exp_dev + j
            w = jnp.sum(jnp.where((lane == index) | (lane == index + experts_all), side, 0.0), axis=1, keepdims=True)
            ga = jnp.dot(x, wgu[0, :, cols], preferred_element_type=f32)
            up = jnp.dot(x, wgu[1, :, cols], preferred_element_type=f32)
            hc = lax.dot_general(c, wd[cols, :], NT, preferred_element_type=f32)
            sigma = 1.0 / (1.0 + jnp.exp(-ga))
            silu = ga * sigma
            hid = (silu * up).astype(bf16).astype(f32)
            hcw = hc * w
            abuf[slot, 0, :, cols] = (hcw * up * (sigma * (1.0 + ga * (1.0 - sigma)))).astype(bf16)
            abuf[slot, 1, :, cols] = (hcw * silu).astype(bf16)
            abuf[slot, 2, :, cols] = (hid * w).astype(bf16)
            dots = jnp.sum(hid * hc, axis=1, keepdims=True)
            return cots + jnp.where(lane == index, dots, 0.0)

        cots = lax.fori_loop(0, exp_dev, one, jnp.zeros((2 * rows, side_lanes), f32))
        pbuf[slot, :, :, pl.ds(width, side_lanes)] = cots.astype(bf16).reshape(2, rows, side_lanes)
        block = min(512, width)

        @pl.loop(0, width // block)
        def _(n):
            cut = pl.ds(pl.multiple_of(n * block, block), block)
            t = lax.dot_general(abuf[slot, 0], wgu[0, cut, :], NT, preferred_element_type=f32)
            t = t + lax.dot_general(abuf[slot, 1], wgu[1, cut, :], NT, preferred_element_type=f32)
            pbuf[slot, :, :, cut] = t.astype(bf16).reshape(2, rows, block)
            t = jnp.dot(abuf[slot, 2], wd[:, cut], preferred_element_type=f32)
            cut = pl.ds(pl.multiple_of(W1 + n * block, 128), block)
            pbuf[slot, :, :, cut] = t.astype(bf16).reshape(2, rows, block)

    def sibcopy(i):
        return pltpu.make_async_remote_copy(
            src_ref=pbuf.at[i % 2, 1 - core], dst_ref=sib_in.at[i % 4], send_sem=ss.at[i], recv_sem=sr.at[i],
            device_id={"rep": z, "ep": sib}, device_id_type=MESH)

    def hcopy(s, j):
        part = pl.ds(half * j, half)
        return pltpu.make_async_remote_copy(
            src_ref=sendbuf.at[0, part], dst_ref=relay_in.at[s, j], send_sem=hs.at[s, j], recv_sem=hr.at[s, j],
            device_id={"rep": z, "ep": chips[j]}, device_id_type=MESH)

    def qcopy(s, j):
        return pltpu.make_async_remote_copy(
            src_ref=sendbuf.at[1 + j], dst_ref=(xin_ref, yin_ref)[j].at[s], send_sem=qs.at[s, j], recv_sem=qr.at[s, j],
            device_id={"rep": z, "ep": chips[j]}, device_id_type=MESH)

    def fcopy(s, g):
        return pltpu.make_async_remote_copy(
            src_ref=rbuf.at[s % 2], dst_ref=zin_ref.at[z], send_sem=fs.at[s], recv_sem=fr.at[z],
            device_id={"rep": g, "ep": e}, device_id_type=MESH)

    step = 16

    def add(out, terms, count=rows):
        @pl.loop(0, count // step)
        def _(i):
            r = pl.ds(pl.multiple_of(i * step, step), step)
            t = terms[0][r, :].astype(f32)
            for other in terms[1:]:
                t = t + other[r, :].astype(f32)
            out[r, :] = t.astype(out.dtype)

    def finish(i):
        s, k = i // 4, i % 4
        sibcopy(i).wait_recv()
        mine, other = pbuf.at[i % 2, core], sib_in.at[i % 4]
        lower, upper = pl.ds(0, half), pl.ds(half, half)
        @pl.when(k == 1)
        def _():
            add(ownbuf.at[s % 2], (mine, other))
        @pl.when(k == 0)
        def _():
            @pl.when(s > 0)
            def _():
                hcopy(s - 1, 0).wait_send()
                hcopy(s - 1, 1).wait_send()
            add(sendbuf.at[0], (mine, other))
            hcopy(s, 0).start()
            hcopy(s, 1).start()
        @pl.when(k == 2)
        def _():
            @pl.when(s > 0)
            def _():
                qcopy(s - 1, 0).wait_send()
            add(sendbuf.at[1, lower], (mine.at[lower], other.at[lower]), half)
            hcopy(s, 1).wait_recv()
            add(sendbuf.at[1, upper], (mine.at[upper], other.at[upper], relay_in.at[s, 1]), half)
            qcopy(s, 0).start()
        @pl.when(k == 3)
        def _():
            @pl.when(s > 0)
            def _():
                qcopy(s - 1, 1).wait_send()
            add(sendbuf.at[2, upper], (mine.at[upper], other.at[upper]), half)
            hcopy(s, 0).wait_recv()
            add(sendbuf.at[2, lower], (mine.at[lower], other.at[lower], relay_in.at[s, 0]), half)
            qcopy(s, 1).start()

    def load_t(src, m):
        return pltpu.make_async_copy(src, tmp.at[m], t_sem.at[m])

    def total(s):
        for j in range(2):
            qcopy(s, j).wait_recv()
            load_t((xin_ref, yin_ref)[j].at[s], j).start()
        for j in range(2):
            load_t((xin_ref, yin_ref)[j].at[s], j).wait()

    def plane_sum(s):
        total(s)
        @pl.when(s >= 2)
        def _():
            fcopy(s - 2, group_of(s - 2)).wait_send()
        add(rbuf.at[s % 2], (ownbuf.at[s % 2], tmp.at[0], tmp.at[1]))
        fcopy(s, group_of(s)).start()

    @pl.when(z < reps - 1)
    def _():
        zcopy(x_ref, z, True).start()
    @pl.when(z > 0)
    def _():
        zcopy(x_ref, z, False).start()
    spread(x_ref, z)
    arrive(1)
    pass_on(z)
    arrive(2)
    at(1, pass_on)
    finish_in(z)
    arrive(3)
    at(2, pass_on)
    at(1, finish_in)
    for w in weights:
        w.wait()
    ready(group_of(0))
    load_x(0).start()
    load_c(0).start()

    @pl.loop(0, steps)
    def _(i):
        load_x(i).wait()
        load_c(i).wait()
        @pl.when(i == 3)
        def _():
            at(3, pass_on)
            at(2, finish_in)
        @pl.when(i == 7)
        def _():
            at(3, finish_in)
        @pl.when(i == steps - 5)
        def _():
            local.wait()
        @pl.when(i < steps - 1)
        def _():
            @pl.when(i % 4 == 3)
            def _():
                ready(group_of(i // 4 + 1))
            load_x(i + 1).start()
            load_c(i + 1).start()
        @pl.when(i >= 2)
        def _():
            sibcopy(i - 2).wait_send()
            for m in range(3):
                keep(i - 2, m).wait()
        compute(i)
        sibcopy(i).start()
        for m in range(3):
            keep(i, m).start()
        @pl.when(i >= 1)
        def _():
            finish(i - 1)
        @pl.when((i % 4 == 3) & (i >= 7) & (i < steps - 1))
        def _():
            plane_sum(i // 4 - 1)

    for i in (steps - 2, steps - 1):
        sibcopy(i).wait_send()
        for m in range(3):
            keep(i, m).wait()
    finish(steps - 1)
    plane_sum(reps - 2)

    blocks = width // 256
    halves = wgu.shape[1]

    def resident(src, m):
        return pltpu.make_async_copy(src.at[pl.ds(m * halves, halves)], wgu.at[m], w_sem.at[m])

    def load_col(src, n):
        return pltpu.make_async_copy(src.at[:, :, :, pl.ds(pl.multiple_of(n * 256, 256), 256)], colbuf.at[n % 2], col_sem.at[n % 2])

    def product(n, m):
        left = colbuf[n % 2, pl.ds(m * (reps // 2), reps // 2)].reshape(halves, 256)
        return left, wgu[m]

    def grad_rows(src, out):
        def store(n, j):
            per = width // reps
            place = pl.ds(pl.multiple_of((n * 256) % per, 256), 256)
            return pltpu.make_async_copy(gst.at[n % 2, j], out.at[((n * 256) // per + reps - z) % reps, j, place], g_sem.at[n % 2, j])
        for m in range(2):
            resident(src, m).start()
        load_col(mid_ref, 0).start()
        for m in range(2):
            resident(src, m).wait()
        @pl.loop(0, blocks)
        def _(n):
            load_col(mid_ref, n).wait()
            @pl.when(n < blocks - 1)
            def _():
                load_col(mid_ref, n + 1).start()
            @pl.when(n >= 2)
            def _():
                for j in range(exp_dev):
                    store(n - 2, j).wait()
            t = jnp.zeros((256, EF), f32)
            for m in range(2):
                left, right = product(n, m)
                t = t + lax.dot_general(left, right, TN, preferred_element_type=f32)
            for j in range(exp_dev):
                gst[n % 2, j] = t[:, j * F:(j + 1) * F].astype(bf16)
                store(n, j).start()
        for n in (blocks - 2, blocks - 1):
            for j in range(exp_dev):
                store(n, j).wait()

    def grad_down():
        def store(n):
            return pltpu.make_async_copy(dst.at[n % 2], dout_ref.at[:, :, pl.ds(pl.multiple_of(n * 256, 256), 256)], g_sem.at[n % 2, 0])
        for m in range(2):
            resident(h_ref, m).start()
        load_col(cot_ref, 0).start()
        for m in range(2):
            resident(h_ref, m).wait()
        @pl.loop(0, blocks)
        def _(n):
            load_col(cot_ref, n).wait()
            @pl.when(n < blocks - 1)
            def _():
                load_col(cot_ref, n + 1).start()
            @pl.when(n >= 2)
            def _():
                store(n - 2).wait()
            t = jnp.zeros((EF, 256), f32)
            for m in range(2):
                left, right = product(n, m)
                t = t + lax.dot_general(right, left, TN, preferred_element_type=f32)
            dst[n % 2] = t.reshape(exp_dev, F, 256)
            store(n).start()
        for n in (blocks - 2, blocks - 1):
            store(n).wait()

    grad_rows(a_ref, gout_ref)
    grad_rows(b_ref, uout_ref)
    grad_down()

    last = reps - 1
    total(last)
    for d in range(1, reps):
        src = (z + d) % reps
        pltpu.make_async_remote_copy(
            src_ref=rbuf.at[0], dst_ref=zin_ref.at[src], send_sem=fs.at[last], recv_sem=fr.at[src],
            device_id={"rep": src, "ep": e}, device_id_type=MESH).wait_recv()
        load_t(zin_ref.at[src], 1 + d).start()
    for d in range(1, reps):
        load_t(zin_ref.at[(z + d) % reps], 1 + d).wait()
    fcopy(reps - 3, group_of(reps - 3)).wait_send()
    add(rbuf.at[(reps - 3) % 2], (ownbuf.at[last % 2], *(tmp.at[m] for m in range(reps + 1))))
    outs = (
        pltpu.make_async_copy(rbuf.at[(reps - 3) % 2, :, pl.ds(0, W1)], row_ref, o_sem.at[0]),
        pltpu.make_async_copy(rbuf.at[(reps - 3) % 2, :, pl.ds(W1, width)], moe_ref, o_sem.at[1]),
    )
    for o in outs:
        o.start()
    for o in outs:
        o.wait()
    fcopy(reps - 2, group_of(reps - 2)).wait_send()
    for j in range(2):
        hcopy(last, j).wait_send()
        qcopy(last, j).wait_send()
    for g in range(reps):
        for j in range(4):
            ccopy(x_ref, g, j).wait_send()
        for j in range(2):
            pcopy(x_ref, g, j).wait_send()
            relay(g, j, chips[j]).wait_send()
        @pl.when((z < reps - 1) & (z >= g))
        def _():
            zcopy(x_ref, g, True).wait_send()
        @pl.when((z > 0) & (z <= g))
        def _():
            zcopy(x_ref, g, False).wait_send()


def moe(x, cot_all, eg, eu, ed, experts_all, cid):
    reps, eps, rows, width = cot_all.shape
    W1 = x.shape[1]
    side = W1 - width
    WP = W1 + width
    exp_dev, _, ff = eg.shape
    F = ff // reps
    EF = exp_dev * F
    f32, bf16 = jnp.float32, jnp.bfloat16
    D, V = pltpu.SemaphoreType.DMA, pltpu.VMEM
    S = jax.ShapeDtypeStruct
    tokens = reps * eps * rows
    steps = 4 * reps
    outs = (
        S((rows, W1), bf16), S((rows, width), bf16),
        S((reps, exp_dev, width // reps, F), bf16), S((reps, exp_dev, width // reps, F), bf16), S((exp_dev, F, width), f32),
        S((reps, eps, rows, W1), bf16), S((tokens, EF), bf16), S((tokens, EF), bf16), S((tokens, EF), bf16),
        S((reps, rows, WP), bf16), S((reps, rows, WP), bf16), S((reps, rows, WP), bf16),
    )
    return pl.pallas_call(
        partial(moe_kernel, reps, side, experts_all),
        out_shape=outs,
        in_specs=[pl.BlockSpec(memory_space=pl.ANY)] * 5,
        out_specs=[pl.BlockSpec(memory_space=pl.ANY)] * len(outs),
        scratch_shapes=[
            V((2, width, EF), bf16), V((EF, width), bf16),
            V((2, 2, rows, W1), bf16), V((2, 2, rows, width), bf16),
            V((2, 3, 2 * rows, EF), bf16), V((2, 2, rows, WP), bf16), V((4, rows, WP), bf16),
            V((reps, 2, rows // 2, WP), bf16), V((3, rows, WP), bf16), V((2, rows, WP), bf16), V((2, rows, WP), bf16),
            V((5, rows, WP), bf16), V((2, reps, eps, rows, 256), bf16),
            V((2, exp_dev, 256, F), bf16), V((2, exp_dev, F, 256), f32),
            D, D((3 * exp_dev,)), D((2,)), D((2,)), D((2, 3)), D((5,)), D((2,)), D((2, exp_dev)), D((2,)),
            D((2, reps)), D((reps,)), D((reps, 4)), D((reps, 4)), D((reps, 4)), D((reps, 4)),
            D((steps,)), D((steps,)), D((reps, 2)), D((reps, 2)), D((reps, 2)), D((reps, 2)), D((reps,)), D((reps,)),
        ],
        compiler_params=pltpu.CompilerParams(collective_id=cid, has_side_effects=True, vmem_limit_bytes=63 * 2**20),
    )(x, cot_all, eg, eu, ed)[:5]


def last_kernel(reps, eps, part_ref, qkv_ref, out_ref, tok_ref, cot_ref, gain_ref, gains_ref, router_ref,
                input_ref, q_ref, k_ref, v_ref, o_ref, gsum_ref, rsum_ref,
                own, sib_in, relay_in, xin, yin, wo, qown, zq, zo, fin, gath, mats, omat, tok, cot, gain,
                gown, gin, gz, gmid, rown, rin, rz, rmid,
                l_sem, ss, sr, hs, hr, qs, qr, ws, wr, zs, zr, zos, zor, ps, pr, gs, gr, gzs, gzr, rs, rr, rzs, rzr):
    f32, bf16 = jnp.float32, jnp.bfloat16
    z = lax.axis_index("rep")
    e = lax.axis_index("ep")
    core = e % 2
    chip = e // 2
    sib, chips = partners(e)
    rows, width = tok_ref.shape
    half = rows // 2
    rows_dev = o_ref.shape[0]
    heads_dev = out_ref.shape[0]
    head_dim = width // (heads_dev * eps)
    slice_width = heads_dev * head_dim

    barrier = pltpu.get_barrier_semaphore()
    for d in range(1, eps):
        pl.semaphore_signal(barrier, inc=1, device_id={"rep": z, "ep": (e + d) % eps}, device_id_type=MESH)
    for d in range(1, reps):
        pl.semaphore_signal(barrier, inc=1, device_id={"rep": (z + d) % reps, "ep": e}, device_id_type=MESH)
    loads = [
        pltpu.make_async_copy(part_ref.at[:, core], own, l_sem.at[0]),
        pltpu.make_async_copy(qkv_ref.at[z], qown, l_sem.at[1]),
        pltpu.make_async_copy(out_ref.at[:, core], wo.at[core], l_sem.at[2]),
        pltpu.make_async_copy(tok_ref, tok, l_sem.at[3]),
        pltpu.make_async_copy(cot_ref, cot, l_sem.at[4]),
        pltpu.make_async_copy(gain_ref, gain, l_sem.at[5]),
        pltpu.make_async_copy(gains_ref, gown, l_sem.at[6]),
        pltpu.make_async_copy(router_ref, rown, l_sem.at[7]),
    ]
    for c in loads:
        c.start()
    pl.semaphore_wait(barrier, eps - 1 + reps - 1)

    def to_sib(src, dst, send, recv):
        return pltpu.make_async_remote_copy(src_ref=src, dst_ref=dst, send_sem=send, recv_sem=recv,
                                            device_id={"rep": z, "ep": sib}, device_id_type=MESH)

    def to_chip(src, dst, send, recv, j):
        return pltpu.make_async_remote_copy(src_ref=src, dst_ref=dst, send_sem=send, recv_sem=recv,
                                            device_id={"rep": z, "ep": chips[j]}, device_id_type=MESH)

    def to_plane(src, dst, send, recv, d):
        return pltpu.make_async_remote_copy(src_ref=src, dst_ref=dst, send_sem=send, recv_sem=recv,
                                            device_id={"rep": z, "ep": (e + d) % eps}, device_id_type=MESH)

    def to_rep(src, dst, send, recv, d):
        return pltpu.make_async_remote_copy(src_ref=src, dst_ref=dst, send_sem=send, recv_sem=recv,
                                            device_id={"rep": (z + d) % reps, "ep": e}, device_id_type=MESH)

    zcopies = [to_rep(qkv_ref.at[(z + d) % reps], zq.at[d - 1], zs.at[d - 1], zr.at[d - 1], d) for d in range(1, reps)]
    ocopies = [to_rep(wo.at[((z + d) % reps) // heads_dev, (z + d) % heads_dev], zo.at[d - 1], zos.at[d - 1], zor.at[d - 1], d)
               for d in range(1, reps)]
    wcopy = to_sib(out_ref.at[:, 1 - core], wo.at[core], ws, wr)
    order = (chips[2] // 2, chips[0] // 2, chips[1] // 2, chip)
    scopies = [to_sib(part_ref.at[q, 1 - core], sib_in.at[q], ss.at[n], sr.at[n]) for n, q in enumerate(order)]
    for c in scopies:
        c.start()
    wcopy.start()
    for c in zcopies:
        c.start()
    step = 16

    def add(out, terms, count):
        @pl.loop(0, count // step)
        def _(i):
            r = pl.ds(pl.multiple_of(i * step, step), step)
            t = terms[0][r, :].astype(f32)
            for other in terms[1:]:
                t = t + other[r, :].astype(f32)
            out[r, :] = t.astype(out.dtype)

    lower, upper = pl.ds(0, half), pl.ds(half, half)
    hcopies = [to_chip(own.at[order[0], (lower, upper)[j]], relay_in.at[j], hs.at[j], hr.at[j], j) for j in range(2)]
    qcopies = [to_chip(own.at[order[1 + j]], (xin, yin)[j], qs.at[j], qr.at[j], j) for j in range(2)]
    loads[0].wait()
    scopies[0].wait_recv()
    d = own.at[order[0]]
    add(d, (d, sib_in.at[order[0]]), rows)
    for c in hcopies:
        c.start()
    for j in range(2):
        mine, other = own.at[order[1 + j]], sib_in.at[order[1 + j]]
        scopies[1 + j].wait_recv()
        direct, through = ((lower, upper), (upper, lower))[j]
        add(mine.at[direct], (mine.at[direct], other.at[direct]), half)
        hcopies[1 - j].wait_recv()
        add(mine.at[through], (mine.at[through], other.at[through], relay_in.at[1 - j]), half)
        qcopies[j].start()
    loads[2].wait()
    wcopy.wait_recv()
    for c in ocopies:
        c.start()
    scopies[3].wait_recv()
    for c in loads[3:]:
        c.wait()
    for c in qcopies:
        c.wait_recv()

    gown[0:1, :] = jnp.zeros((1, width), f32)

    @pl.loop(0, rows // step)
    def _(i):
        r = pl.ds(pl.multiple_of(i * step, step), step)
        nc = (own[chip, r, :].astype(f32) + sib_in[chip, r, :].astype(f32) + xin[r, :].astype(f32) + yin[r, :].astype(f32))
        t = tok[r, :].astype(f32)
        scale = lax.rsqrt(jnp.mean(t * t, axis=-1, keepdims=True) + 1e-6)
        unit = t * scale
        scaled = nc * gain[0:1, :]
        cot[r, :] = cot[r, :] + scale * (scaled - unit * jnp.mean(scaled * unit, axis=-1, keepdims=True))
        gown[0:1, :] += jnp.sum(nc * unit, axis=0, keepdims=True)

    done = [pltpu.make_async_copy(cot, input_ref, l_sem.at[8])]
    done[0].start()

    gcopies = [to_plane(gown, gin.at[d - 1], gs.at[d - 1], gr.at[d - 1], d) for d in range(1, eps)]
    rcopies = [to_plane(rown.at[:, (e + d) % eps], rin.at[d - 1], rs.at[d - 1], rr.at[d - 1], d) for d in range(1, eps)]
    for c in (*gcopies, *rcopies):
        c.start()
    for c in (*gcopies, *rcopies):
        c.wait_recv()
    t = gown[...]
    for d in range(1, eps):
        t = t + gin[d - 1]
    gmid[...] = t
    t = rown[:, e]
    for d in range(1, eps):
        t = t + rin[d - 1]
    rmid[...] = t
    gzcopies = [to_rep(gmid, gz.at[d - 1], gzs.at[d - 1], gzr.at[d - 1], d) for d in range(1, reps)]
    rzcopies = [to_rep(rmid.at[(z + d) % reps], rz.at[d - 1], rzs.at[d - 1], rzr.at[d - 1], d) for d in range(1, reps)]
    for c in (*gzcopies, *rzcopies):
        c.start()

    loads[1].wait()
    for c in zcopies:
        c.wait_recv()
    for n in range(eps):
        @pl.loop(0, rows_dev // step)
        def _(i):
            r = pl.ds(pl.multiple_of(i * step, step), step)
            a = pl.ds(pl.multiple_of(n * rows_dev + i * step, step), step)
            t = qown[a, :].astype(f32)
            for d in range(reps - 1):
                t = t + zq[d, a, :].astype(f32)
            fin[n, r, :] = t.astype(bf16)
    pcopies = [to_plane(fin.at[(e + d) % eps], gath.at[e], ps.at[d - 1], pr.at[d - 1], d) for d in range(1, eps)]
    for c in pcopies:
        c.start()
    mine = pltpu.make_async_copy(fin.at[e], gath.at[e], l_sem.at[9])
    mine.start()
    for c in (*gzcopies, *rzcopies, *ocopies):
        c.wait_recv()
    for c in gcopies:
        c.wait_send()
    t = gmid[...]
    for d in range(reps - 1):
        t = t + gz[d]
    gown[...] = t
    t = rmid[z]
    for d in range(reps - 1):
        t = t + rz[d]
    rmid[z] = t
    done.append(pltpu.make_async_copy(gown, gsum_ref, l_sem.at[10]))
    done.append(pltpu.make_async_copy(rmid.at[z], rsum_ref, l_sem.at[11]))
    wmine = wo.at[z // heads_dev, z % heads_dev]

    @pl.loop(0, rows_dev // step)
    def _(i):
        r = pl.ds(pl.multiple_of(i * step, step), step)
        t = wmine[r, :].astype(f32)
        for d in range(reps - 1):
            t = t + zo[d, r, :].astype(f32)
        omat[r, :] = t
    done.append(pltpu.make_async_copy(omat, o_ref, l_sem.at[12]))
    for c in rzcopies:
        c.wait_send()
    for c in done[1:]:
        c.start()
    mine.wait()
    for c in pcopies:
        c.wait_recv()
    for src in range(eps):
        for m in range(3):
            for i in range(heads_dev):
                head = ((src % 2) * heads_dev + i) * (eps // 2) + src // 2
                mats[m, :, head * head_dim:(head + 1) * head_dim] = gath[src, :, m * slice_width + i * head_dim:m * slice_width + (i + 1) * head_dim].astype(f32)
    for m, ref in enumerate((q_ref, k_ref, v_ref)):
        done.append(pltpu.make_async_copy(mats.at[m], ref, l_sem.at[13 + m]))
        done[-1].start()
    for c in done:
        c.wait()
    for c in (*scopies, wcopy, *zcopies, *ocopies, *hcopies, *qcopies, *pcopies, *rcopies, *gzcopies):
        c.wait_send()


def last_sums(part, qkv_term, out_term, tokens, after_cot, gain_in, gains, router, rows_dev, reps, eps, cid):
    rows, width = tokens.shape
    f32, bf16 = jnp.float32, jnp.bfloat16
    heads_dev = out_term.shape[0]
    slices = qkv_term.shape[2]
    q = eps // 2
    half = rows // 2
    D, V = pltpu.SemaphoreType.DMA, pltpu.VMEM
    S = jax.ShapeDtypeStruct
    g8, rt = gains.shape, router.shape[2:]
    outs = (S((rows, width), f32), *[S((rows_dev, width), f32)] * 4, S(g8, f32), S(rt, f32))
    return pl.pallas_call(
        partial(last_kernel, reps, eps),
        out_shape=outs,
        in_specs=[pl.BlockSpec(memory_space=pl.ANY)] * 8,
        out_specs=[pl.BlockSpec(memory_space=pl.ANY)] * len(outs),
        scratch_shapes=[
            V((q, rows, width), bf16), V((q, rows, width), bf16), V((2, half, width), bf16), V((rows, width), bf16), V((rows, width), bf16),
            V((2, heads_dev, rows_dev, width), bf16), V((rows_dev * eps, slices), bf16), V((reps - 1, rows_dev * eps, slices), bf16),
            V((reps - 1, rows_dev, width), bf16), V((eps, rows_dev, slices), bf16), V((eps, rows_dev, slices), bf16),
            V((3, rows_dev, width), f32), V((rows_dev, width), f32), V((rows, width), bf16), V((rows, width), f32), V((1, width), f32),
            V(g8, f32), V((eps - 1, *g8), f32), V((reps - 1, *g8), f32), V(g8, f32),
            V(router.shape, f32), V((eps - 1, reps, *rt), f32), V((reps - 1, *rt), f32), V((reps, *rt), f32),
            D((16,)), D((4,)), D((4,)), D((2,)), D((2,)), D((2,)), D((2,)), D, D,
            D((reps - 1,)), D((reps - 1,)), D((reps - 1,)), D((reps - 1,)), D((eps - 1,)), D((eps - 1,)),
            D((eps - 1,)), D((eps - 1,)), D((reps - 1,)), D((reps - 1,)), D((eps - 1,)), D((eps - 1,)), D((reps - 1,)), D((reps - 1,)),
        ],
        compiler_params=pltpu.CompilerParams(collective_id=cid, has_side_effects=True, vmem_limit_bytes=56 * 2**20),
    )(part, qkv_term, out_term, tokens, after_cot, gain_in, gains, router)


def join_kernel(count, *refs):
    ins, out = refs[:count], refs[count]
    shift = (lax.axis_index("rep") + count - pl.program_id(1)) % count
    for k in range(count):
        @pl.when(shift == k)
        def _():
            out[...] = ins[k][...].astype(out.dtype)


def join_columns(pieces):
    count = len(pieces)
    exp_dev, rows, cols = pieces[0].shape
    return pl.pallas_call(
        partial(join_kernel, count),
        grid=(exp_dev, count),
        out_shape=jax.ShapeDtypeStruct((exp_dev, rows, cols * count), jnp.float32),
        in_specs=[pl.BlockSpec((1, rows, cols), lambda j, s: (j, 0, 0))] * count,
        out_specs=pl.BlockSpec((1, rows, cols), lambda j, s: (j, 0, s)),
    )(*pieces)


def front_kernel(reps, eps, lengths_ref, tok_ref, cot_ref, wq_ref, wk_ref, wv_ref, wo_ref, gains_ref, router_ref, nums_ref, freq_ref,
                 cots_ref, router_all_ref, nums_all_ref, gsum_ref, normed_ref, pre_ref, qkv_ref, mixed_ref, wqkv_ref, wout_ref, turn_ref, attn_ref,
                 toks, normed, wraw, stage, wqkv, wz, wout, proj, qkv, mixed, turn, segs, part, sib_in, relay_in, xin, yin, acc,
                 gown, gz, gmid, gin, gall, nums, freq,
                 l_sem, o_sem, ws, wr, vs, vr, zs, zr, fs, fr, ts, tr, tcs, tcr, cps, cpr, ccs, ccr,
                 gzs, gzr, gps, gpr, rzs, rzr, rps, rpr, ns, nr, ss, sr, hs, hr, qs, qr, os, orr):
    f32, bf16 = jnp.float32, jnp.bfloat16
    z = lax.axis_index("rep")
    e = lax.axis_index("ep")
    core = e % 2
    chip = e // 2
    sib, chips = partners(e)
    rows, width = tok_ref.shape
    half = rows // 2
    rows_dev = wq_ref.shape[0]
    slice_width = mixed.shape[1]
    head_dim = turn.shape[2]
    heads_dev = slice_width // head_dim
    group_rows = eps * rows

    barrier = pltpu.get_barrier_semaphore()
    for d in range(1, eps):
        pl.semaphore_signal(barrier, inc=1, device_id={"rep": z, "ep": (e + d) % eps}, device_id_type=MESH)
    for d in range(1, reps):
        pl.semaphore_signal(barrier, inc=1, device_id={"rep": (z + d) % reps, "ep": e}, device_id_type=MESH)

    def local(src, dst, sem):
        c = pltpu.make_async_copy(src, dst, sem)
        c.start()
        return c

    raw = [local(r, wraw.at[m], l_sem.at[m]) for m, r in enumerate((wq_ref, wk_ref, wv_ref))]
    tok_own = local(tok_ref, toks.at[e], l_sem.at[3])
    wo_own = local(wo_ref, wz.at[z], l_sem.at[4])
    cot_own = local(cot_ref, cots_ref.at[z, e], l_sem.at[5])
    small = [
        local(gains_ref, gown, l_sem.at[6]),
        local(nums_ref, nums.at[e], l_sem.at[7]),
        local(freq_ref, freq, l_sem.at[8]),
        local(router_ref, router_all_ref.at[e, z], l_sem.at[9]),
    ]
    pl.semaphore_wait(barrier, eps - 1 + reps - 1)

    def remote(src, dst, send, recv, rep, ep):
        return pltpu.make_async_remote_copy(src_ref=src, dst_ref=dst, send_sem=send, recv_sem=recv,
                                            device_id={"rep": rep, "ep": ep}, device_id_type=MESH)

    def below(k, fn):
        @pl.when(z - k >= 0)
        def _():
            fn(z - k)

    def above(k, fn):
        @pl.when(z + k < reps)
        def _():
            fn(z + k)

    class Chain:
        def __init__(self, slot, send, recv):
            self.slot, self.send, self.recv = slot, send, recv

        def copy(self, src, g, up):
            d = 0 if up else 1
            return remote(src, self.slot(g), self.send.at[d, g], self.recv.at[g], z + 1 if up else z - 1, e)

        def begin(self, src):
            @pl.when(z < reps - 1)
            def _():
                self.copy(src, z, True).start()
            @pl.when(z > 0)
            def _():
                self.copy(src, z, False).start()

        def take(self, k, then=None):
            def from_below(g):
                self.copy(self.slot(g), g, True).wait_recv()
                if then is not None:
                    then(g)
            def from_above(g):
                self.copy(self.slot(g), g, False).wait_recv()
                if then is not None:
                    then(g)
            below(k, from_below)
            above(k, from_above)

        def forward(self, k):
            @pl.when((z - k >= 0) & (z < reps - 1))
            def _():
                self.copy(self.slot(z - k), z - k, True).start()
            @pl.when((z + k < reps) & (z > 0))
            def _():
                self.copy(self.slot(z + k), z + k, False).start()

        def arrive(self, k):
            self.take(k)
            self.forward(k)

        def sent(self):
            for g in range(reps):
                @pl.when((z < reps - 1) & (z >= g))
                def _():
                    self.copy(self.slot(g), g, True).wait_send()
                @pl.when((z > 0) & (z <= g))
                def _():
                    self.copy(self.slot(g), g, False).wait_send()

    class Spread:
        def __init__(self, slot, send, recv, csend, crecv):
            self.slot, self.send, self.recv, self.csend, self.crecv = slot, send, recv, csend, crecv

        def near(self, src, j):
            return remote(src, self.slot(e), self.send.at[j], self.recv.at[j], z, chips[j])

        def relay(self, j, source):
            p = self.slot(source).at[pl.ds(half * j, half)]
            return remote(p, p, self.send.at[2 + j], self.recv.at[2 + j], z, chips[1 - j])

        def core(self, src, j):
            return remote(src, self.slot(e if j == 0 else chips[j - 1]), self.csend.at[j], self.crecv.at[j], z, sib)

        def begin(self, src):
            self.near(src, 0).start()
            self.near(src, 1).start()
            self.core(src, 0).start()

        def pass_on(self):
            for j in range(2):
                self.near(self.slot(e), j).wait_recv()
                self.relay(j, chips[j]).start()
                self.core(self.slot(chips[j]), j + 1).start()

        def finish(self):
            for j in range(2):
                self.relay(j, chips[2]).wait_recv()
            self.core(self.slot(chips[2]), 3).start()

        def arrived(self):
            for j in range(4):
                self.core(self.slot(e), j).wait_recv()

        def sent(self):
            for j in range(2):
                self.near(self.slot(e), j).wait_send()
                self.relay(j, chips[j]).wait_send()
            for j in range(4):
                self.core(self.slot(e), j).wait_send()

    tok_spread = Spread(lambda who: toks.at[who], ts, tr, tcs, tcr)

    def cot_spread(g):
        return Spread(lambda who: cots_ref.at[g, who], cps.at[g], cpr.at[g], ccs.at[g], ccr.at[g])

    wo_chain = Chain(lambda g: wz.at[g], ws, wr)
    w_chain = Chain(lambda g: wqkv.at[g], vs, vr)
    cot_chain = Chain(lambda g: cots_ref.at[g, e], zs, zr)

    def cot_take(k):
        cot_chain.take(k, lambda g: cot_spread(g).begin(cots_ref.at[g, e]))

    def each(k, fn):
        below(k, lambda g: fn(cot_spread(g)))
        above(k, lambda g: fn(cot_spread(g)))

    gzc = [remote(gains_ref, gz.at[d - 1], gzs.at[d - 1], gzr.at[d - 1], (z + d) % reps, e) for d in range(1, reps)]
    rzc = [remote(router_ref, router_all_ref.at[e, z], rzs.at[d - 1], rzr.at[d - 1], (z + d) % reps, e) for d in range(1, reps)]
    nc = [remote(nums_ref, nums.at[e], ns.at[d - 1], nr.at[d - 1], z, (e + d) % eps) for d in range(1, eps)]
    for c in (*gzc, *rzc, *nc):
        c.start()
    wo_chain.begin(wo_ref)
    for m in range(3):
        raw[m].wait()
        for who in range(eps):
            for i in range(heads_dev):
                head = ((who % 2) * heads_dev + i) * (eps // 2) + who // 2
                at = m * slice_width + i * head_dim
                stage[who, :, at:at + head_dim] = wraw[m, :, head * head_dim:(head + 1) * head_dim]
    vc = [remote(stage.at[(e + d) % eps], wqkv.at[z, e], fs.at[d - 1], fr.at[d - 1], z, (e + d) % eps) for d in range(1, eps)]
    for c in vc:
        c.start()
    v_own = local(stage.at[e], wqkv.at[z, e], l_sem.at[10])
    tok_spread.begin(tok_ref)
    cot_chain.begin(cot_ref)
    cot_spread(z).begin(cot_ref)
    v_own.wait()
    for c in vc:
        c.wait_recv()
    w_chain.begin(wqkv.at[z])
    wo_chain.arrive(1)

    for c in gzc:
        c.wait_recv()
    small[0].wait()
    t = gown[...].astype(f32)
    for d in range(reps - 1):
        t = t + gz[d].astype(f32)
    gmid[...] = t.astype(bf16)
    gpc = [remote(gmid, gin.at[d - 1], gps.at[d - 1], gpr.at[d - 1], z, (e + d) % eps) for d in range(1, eps)]
    for c in gpc:
        c.start()
    small[3].wait()
    for c in rzc:
        c.wait_recv()
    rpc = [remote(router_all_ref.at[e], router_all_ref.at[e], rps.at[d - 1], rpr.at[d - 1], z, (e + d) % eps) for d in range(1, eps)]
    for c in rpc:
        c.start()
    tok_spread.pass_on()
    tok_spread.finish()
    wo_chain.arrive(2)
    cot_take(1)
    for c in gpc:
        c.wait_recv()
    t = gmid[...].astype(f32)
    for d in range(eps - 1):
        t = t + gin[d].astype(f32)
    gall[...] = t
    outs = [local(gall, gsum_ref, o_sem.at[0])]
    w_chain.arrive(1)
    wo_chain.arrive(3)
    cot_chain.forward(1)

    for c in small[1:3]:
        c.wait()
    for c in nc:
        c.wait_recv()
    outs.append(local(nums, nums_all_ref, o_sem.at[1]))
    deal = nums[:, 0, :]
    segment = jnp.zeros(deal.shape, jnp.int32)
    start = jnp.zeros(deal.shape, jnp.int32)
    end = 0
    for n in range(lengths_ref.shape[1]):
        end = end + lengths_ref[0, n]
        after = (deal >= end).astype(jnp.int32)
        segment = segment + after
        start = start + after * lengths_ref[0, n]
    position = (deal - start).astype(f32)
    segs[...] = segment.astype(f32)
    lane = lax.broadcasted_iota(jnp.int32, (rows, head_dim), 1)
    sign = jnp.where(lane < head_dim // 2, -1.0, 1.0)
    for n in range(eps):
        spot = jnp.broadcast_to(position[n:n + 1, :], (rows, rows)).T
        angle = spot * freq[0:1, :]
        here = pl.ds(n * rows, rows)
        turn[0, here, :] = jnp.cos(angle)
        turn[1, here, :] = jnp.sin(angle) * sign
    outs.append(local(turn, turn_ref, o_sem.at[2]))
    cot_spread(z).pass_on()

    tok_own.wait()
    tok_spread.arrived()
    gain_in = jnp.concatenate([gall[n:n + 1, :] for n in range(width // 128)], axis=1)
    step = 16
    for n in range(eps):
        @pl.loop(0, rows // step)
        def _(i):
            r = pl.ds(pl.multiple_of(i * step, step), step)
            t = toks[n, r, :].astype(f32)
            scale = lax.rsqrt(jnp.mean(t * t, axis=-1, keepdims=True) + norm_eps)
            normed[n, r, :] = (t * scale * gain_in).astype(bf16)
    outs.append(local(normed, normed_ref, o_sem.at[3]))
    w_chain.arrive(2)
    cot_take(2)
    cot_chain.forward(2)
    cot_spread(z).finish()

    wo_own.wait()
    wc = [remote(wz.at[(1 - core) * heads_dev + i], wout.at[i, core], os.at[i], orr.at[i], z, sib) for i in range(heads_dev)]
    wl = [local(wz.at[core * heads_dev + i], wout.at[i, core], l_sem.at[11 + i]) for i in range(heads_dev)]
    for c in wc:
        c.start()
    w_chain.arrive(3)
    each(1, lambda s: s.pass_on())


    @pl.loop(0, eps)
    def _(n):
        here = pl.ds(pl.multiple_of(n * rows, rows), rows)
        proj[here, :] = jnp.dot(normed[n], wqkv[...].reshape(width, 3 * slice_width), preferred_element_type=f32)
        for h in range(2 * heads_dev):
            cut = slice(h * head_dim, (h + 1) * head_dim)
            t = proj[here, cut]
            row = 2 * width // 128 + (0 if h < heads_dev else 1)
            t = t * lax.rsqrt(jnp.mean(t * t, axis=-1, keepdims=True) + norm_eps) * gall[row:row + 1, :]
            t = t * turn[0, here, :] + pltpu.roll(t, head_dim // 2, 1) * turn[1, here, :]
            qkv[here, cut] = t.astype(bf16)
        tail = slice(2 * slice_width, 3 * slice_width)
        qkv[here, tail] = proj[here, tail].astype(bf16)

    outs.append(local(proj.at[:, pl.ds(0, 2 * slice_width)], pre_ref, o_sem.at[4]))
    outs.append(local(qkv, qkv_ref, o_sem.at[5]))
    outs.append(local(wqkv, wqkv_ref, o_sem.at[6]))

    seg_row = jnp.concatenate([segs[n:n + 1, :] for n in range(eps)], axis=1)
    block = 2 * rows

    def attend(h):
        cut = slice(h * head_dim, (h + 1) * head_dim)
        kcut = slice(slice_width + h * head_dim, slice_width + (h + 1) * head_dim)
        vcut = slice(2 * slice_width + h * head_dim, 2 * slice_width + (h + 1) * head_dim)
        for n in range(eps // 2):
            here = pl.ds(n * block, block)
            s = lax.dot_general(qkv[here, cut], qkv[:, kcut], NT, preferred_element_type=f32) * (head_dim ** -0.5)
            seg_col = jnp.concatenate(
                [jnp.broadcast_to(segs[2 * n + j:2 * n + j + 1, :], (rows, rows)).T[:, 0:1] for j in range(2)], axis=0)
            s = jnp.where(seg_col == seg_row, s, masked_score)
            p = jnp.exp(s - jnp.max(s, axis=-1, keepdims=True))
            p = (p / jnp.sum(p, axis=-1, keepdims=True)).astype(bf16)
            mixed[here, cut] = jnp.dot(p, qkv[:, vcut], preferred_element_type=f32).astype(bf16)

    each(1, lambda s: s.finish())
    attend(0)
    each(2, lambda s: s.pass_on())
    for h in range(1, heads_dev):
        attend(h)
    outs.append(local(mixed, mixed_ref, o_sem.at[7]))
    for c in wl:
        c.wait()
    for c in wc:
        c.wait_recv()
    outs.append(local(wout, wout_ref, o_sem.at[8]))

    order = (chips[2] // 2, chips[0] // 2, chips[1] // 2, chip)
    scopies = [remote(part.at[q, 1 - core], sib_in.at[q], ss.at[n], sr.at[n], z, sib) for n, q in enumerate(order)]
    for n in range(eps // 2):
        q = order[n]
        here = pl.ds(pl.multiple_of(q * block, block), block)
        t = jnp.dot(mixed[here, :], wout[...].reshape(slice_width, width), preferred_element_type=f32)
        part[q] = t.astype(bf16).reshape(2, rows, width)
        scopies[n].start()

    cot_take(3)

    def add(out, terms, count):
        @pl.loop(0, count // step)
        def _(i):
            r = pl.ds(pl.multiple_of(i * step, step), step)
            t = terms[0][r, :].astype(f32)
            for other in terms[1:]:
                t = t + other[r, :].astype(f32)
            out[r, :] = t.astype(out.dtype)

    lower, upper = pl.ds(0, half), pl.ds(half, half)
    first = part.at[order[0], core]
    hcopies = [remote(first.at[(lower, upper)[j]], relay_in.at[j], hs.at[j], hr.at[j], z, chips[j]) for j in range(2)]
    qcopies = [remote(part.at[order[1 + j], core], (xin, yin)[j], qs.at[j], qr.at[j], z, chips[j]) for j in range(2)]
    scopies[0].wait_recv()
    add(first, (first, sib_in.at[order[0]]), rows)
    for c in hcopies:
        c.start()
    for j in range(2):
        mine, other = part.at[order[1 + j], core], sib_in.at[order[1 + j]]
        scopies[1 + j].wait_recv()
        direct, through = ((lower, upper), (upper, lower))[j]
        add(mine.at[direct], (mine.at[direct], other.at[direct]), half)
        hcopies[1 - j].wait_recv()
        add(mine.at[through], (mine.at[through], other.at[through], relay_in.at[1 - j]), half)
        qcopies[j].start()
    scopies[3].wait_recv()
    each(3, lambda s: s.pass_on())
    each(2, lambda s: s.finish())
    for c in qcopies:
        c.wait_recv()
    add(acc, (part.at[chip, core], sib_in.at[chip], xin, yin, toks.at[e]), rows)
    outs.append(local(acc, attn_ref, o_sem.at[9]))
    each(3, lambda s: s.finish())
    cot_own.wait()
    for g in range(reps):
        cot_spread(g).arrived()
        cot_spread(g).sent()
    for chain in (wo_chain, w_chain, cot_chain):
        chain.sent()
    tok_spread.sent()
    for c in rpc:
        c.wait_recv()
    for c in (*gzc, *rzc, *nc, *vc, *gpc, *rpc, *wc, *scopies, *hcopies, *qcopies):
        c.wait_send()
    for c in outs:
        c.wait()


def front(lengths, tokens, cot, wq, wk, wv, wo, gains, router, nums, freq, heads_dev, reps, eps, cid):
    rows, width = tokens.shape
    rows_dev = wq.shape[0]
    f32, bf16, i32 = jnp.float32, jnp.bfloat16, jnp.int32
    head_dim = freq.shape[1]
    sw = heads_dev * head_dim
    gr = eps * rows
    half = rows // 2
    q = eps // 2
    S, V, D = jax.ShapeDtypeStruct, pltpu.VMEM, pltpu.SemaphoreType.DMA
    outs = (
        S((reps, eps, rows, width), bf16), S((eps, reps, *router.shape), bf16), S((eps, *nums.shape), i32), S(gains.shape, f32),
        S((eps, rows, width), bf16), S((gr, 2 * sw), f32), S((gr, 3 * sw), bf16), S((gr, sw), bf16),
        S((reps, eps, rows_dev, 3 * sw), bf16), S((heads_dev, 2, rows_dev, width), bf16), S((2, gr, head_dim), f32), S((rows, width), f32),
    )
    return pl.pallas_call(
        partial(front_kernel, reps, eps),
        out_shape=outs,
        in_specs=[pl.BlockSpec(memory_space=pltpu.SMEM)] + [pl.BlockSpec(memory_space=pl.ANY)] * 10,
        out_specs=[pl.BlockSpec(memory_space=pl.ANY)] * len(outs),
        scratch_shapes=[
            V((eps, rows, width), bf16), V((eps, rows, width), bf16), V((3, rows_dev, width), bf16), V((eps, rows_dev, 3 * sw), bf16),
            V((reps, eps, rows_dev, 3 * sw), bf16), V((reps, rows_dev, width), bf16), V((heads_dev, 2, rows_dev, width), bf16),
            V((gr, 3 * sw), f32), V((gr, 3 * sw), bf16), V((gr, sw), bf16), V((2, gr, head_dim), f32), V((eps, rows), f32),
            V((q, 2, rows, width), bf16), V((q, rows, width), bf16), V((2, half, width), bf16), V((rows, width), bf16), V((rows, width), bf16),
            V((rows, width), f32),
            V(gains.shape, bf16), V((reps - 1, *gains.shape), bf16), V(gains.shape, bf16), V((eps - 1, *gains.shape), bf16), V(gains.shape, f32),
            V((eps, *nums.shape), i32), V(freq.shape, f32),
            D((16,)), D((16,)), D((2, reps)), D((reps,)), D((2, reps)), D((reps,)), D((2, reps)), D((reps,)), D((eps - 1,)), D((eps - 1,)),
            D((4,)), D((4,)), D((4,)), D((4,)), D((reps, 4)), D((reps, 4)), D((reps, 4)), D((reps, 4)),
            D((reps - 1,)), D((reps - 1,)), D((eps - 1,)), D((eps - 1,)), D((reps - 1,)), D((reps - 1,)), D((eps - 1,)), D((eps - 1,)),
            D((eps - 1,)), D((eps - 1,)), D((4,)), D((4,)), D((2,)), D((2,)), D((2,)), D((2,)), D((2,)), D((2,)),
        ],
        compiler_params=pltpu.CompilerParams(collective_id=cid, has_side_effects=True, vmem_limit_bytes=56 * 2**20),
    )(lengths, tokens, cot, wq, wk, wv, wo, gains, router, nums, freq)


def on_device_split(
    tokens,
    cotangent,
    query_weight,
    key_weight,
    value_weight,
    output_weight,
    router_weight,
    gains,
    expert_gate,
    expert_up,
    expert_down,
    lengths,
    deal,
    routes,
    priority,
):
    bf16, f32 = jnp.bfloat16, jnp.float32
    tok_dev, width = tokens.shape
    ep_count, rep_count = lax.axis_size("ep"), lax.axis_size("rep")
    ep_index, rep_index = lax.axis_index("ep"), lax.axis_index("rep")
    exp_dev, _, ff_width = expert_gate.shape
    top_count = routes.shape[1]
    experts_all = exp_dev * ep_count
    group_rows = tok_dev * ep_count
    capacity = 5 * tok_dev * top_count // (4 * exp_dev)
    head_dim = HD
    heads_dev = width // head_dim // ep_count
    slice_width = heads_dev * head_dim
    rows_dev = query_weight.shape[0]
    score_scale = head_dim ** (-0.5)
    core = ep_index % 2
    every = ("rep", "ep")

    chips = ep_count // 2
    gains_dev = gains.shape[0]
    gain_rows = -(-gains_dev * rep_count * ep_count // 2048) * 16
    gains_placed = lax.dynamic_update_slice_in_dim(
        jnp.zeros((gain_rows * 128,), bf16),
        gains,
        (rep_index * ep_count + ep_index) * gains_dev,
        axis=0,
    ).reshape(gain_rows, 128)
    router_rows = router_weight.size // 128
    router_placed = jnp.pad(router_weight.reshape(router_rows, 128), ((0, -router_rows % 16), (0, 0)))
    numbers = jnp.concatenate([deal[None], priority[None], routes.T])
    numbers = jnp.pad(numbers, ((0, -numbers.shape[0] % 8), (0, 0)))
    frequency = rope_base ** (
        -2.0 * jnp.arange(head_dim // 2, dtype=jnp.float32) / head_dim
    )
    (
        cot_all,
        router_all,
        numbers_all,
        gains_all,
        normed_group,
        pre,
        qkv_low,
        mixed_low,
        qkv_slice,
        out_slice,
        turn,
        after_attn,
    ) = front(
        lengths,
        tokens,
        cotangent,
        query_weight,
        key_weight,
        value_weight,
        output_weight,
        gains_placed,
        router_placed,
        numbers,
        jnp.concatenate([frequency, frequency]).reshape(1, head_dim),
        heads_dev,
        rep_count,
        ep_count,
        0,
    )
    gains_float = gains_all.reshape(-1)
    gain_in = gains_float[:width]
    gain_mid = gains_float[width : 2 * width]
    gain_query = gains_float[2 * width : 2 * width + head_dim]
    gain_key = gains_float[2 * width + head_dim : 2 * width + 2 * head_dim]
    router_full = (
        router_all[:, :, :router_rows].transpose(1, 0, 2, 3).reshape(width, experts_all)
    )
    deal_all = numbers_all[:, 0].reshape(-1)
    priority_all = numbers_all[:, 1].reshape(-1)
    routes_all = numbers_all[:, 2 : 2 + top_count].transpose(0, 2, 1).reshape(group_rows, top_count)
    segment_all, position_all = placement(deal_all, lengths[0])
    same_seq = segment_all[:, None] == segment_all[None, :]
    normed_group = normed_group.reshape(group_rows, width)
    qkv_slice = qkv_slice.reshape(width, 3 * slice_width)
    out_slice = out_slice.reshape(slice_width, width)
    query_pre = pre[:, :slice_width].reshape(group_rows, heads_dev, head_dim)
    key_pre = pre[:, slice_width:].reshape(group_rows, heads_dev, head_dim)
    query_low, key_low, value_low = (
        qkv_low[:, i * slice_width : (i + 1) * slice_width].reshape(
            group_rows, heads_dev, head_dim
        )
        for i in range(3)
    )
    residual = tokens.astype(f32)
    mid_low = rms_scale(after_attn, gain_mid).astype(bf16)

    logits = jnp.dot(mid_low, router_full, preferred_element_type=f32)
    expert_ids = jnp.arange(experts_all, dtype=jnp.int32)
    member = (routes[:, :, None] == expert_ids[None, None, :]).astype(f32)
    named = jnp.sum(member, axis=1)
    lifted = jnp.where(named > 0, logits, masked_score)
    lifted = jnp.exp(lifted - jnp.max(lifted, axis=-1, keepdims=True)) * named
    gate_dense = lifted / jnp.sum(lifted, axis=-1, keepdims=True)
    onehot_all = jnp.sum(
        (routes_all[:, :, None] == expert_ids[None, None, :]).astype(bf16), axis=1
    )
    earlier = (priority_all[None, :] < priority[:, None]).astype(bf16)
    slots = jnp.dot(earlier, onehot_all, preferred_element_type=f32)
    kept_dense = named * (slots < capacity).astype(f32)
    pair_weight = gate_dense * kept_dense

    weight_high = pair_weight.astype(bf16)
    weight_low = (pair_weight - weight_high.astype(f32)).astype(bf16)
    side = jnp.concatenate(
        [weight_high, weight_low, jnp.zeros((tok_dev, 128 - 2 * experts_all), bf16)], axis=1
    )
    row_sum, moe_sum, gate_term, up_term, down_w_grad = moe(
        jnp.concatenate([mid_low, side], axis=1),
        cot_all,
        expert_gate,
        expert_up,
        expert_down,
        experts_all,
        3,
    )
    moe_out = moe_sum.astype(f32)
    block_out = (after_attn + moe_out).astype(bf16)

    def rows_of(parts):
        pieces = [parts[0]]
        for k in range(1, rep_count):
            pieces.append(
                lax.ppermute(parts[k], "rep", [(i, (i + k) % rep_count) for i in range(rep_count)])
            )
        return pieces

    gate_pieces, up_pieces = rows_of(gate_term), rows_of(up_term)

    out_grad = cotangent.astype(f32)
    gate_cot = row_sum[:, width : width + experts_all].astype(f32) * kept_dense
    chosen_cot = gate_dense * (gate_cot - jnp.sum(gate_dense * gate_cot, axis=-1, keepdims=True))
    logit_cot = chosen_cot.astype(bf16)
    mid_cot = row_sum[:, :width].astype(f32) + jnp.dot(
        logit_cot, router_full.T, preferred_element_type=f32
    )
    router_term = jnp.dot(mid_low.T, logit_cot, preferred_element_type=f32)
    _, mid_pull = jax.vjp(rms_scale, after_attn, gain_mid)
    after_extra, gain_mid_cot = mid_pull(mid_cot)
    after_cot = out_grad + after_extra
    attn_cot_group = all_gather(
        after_cot.astype(bf16), rep_count, ep_count, False, 6
    ).reshape(group_rows, width)

    mixed_cot = jnp.dot(attn_cot_group, out_slice.T, preferred_element_type=f32).astype(bf16)
    output_term = jnp.dot(mixed_low.T, attn_cot_group, preferred_element_type=f32)
    query_cot, key_cot, value_cot = attend_again(
        (
            query_low,
            key_low,
            value_low,
            mixed_cot.reshape(group_rows, heads_dev, head_dim),
        ),
        same_seq,
        score_scale,
    )
    _, query_pull = jax.vjp(
        lambda pre, gain_vec: rope_norm(pre, gain_vec, position_all), query_pre, gain_query
    )
    query_pre_cot, gain_query_cot = query_pull(query_cot)
    _, key_pull = jax.vjp(
        lambda pre, gain_vec: rope_norm(pre, gain_vec, position_all), key_pre, gain_key
    )
    key_pre_cot, gain_key_cot = key_pull(key_cot)
    pre_cot = jnp.concatenate(
        [
            part.reshape(group_rows, slice_width).astype(bf16)
            for part in (query_pre_cot, key_pre_cot, value_cot)
        ],
        axis=1,
    )
    normed_part = jnp.dot(pre_cot, qkv_slice.T, preferred_element_type=f32).astype(bf16)
    qkv_term = jnp.dot(normed_group.T, pre_cot, preferred_element_type=f32).astype(bf16)
    gains_term = jnp.concatenate(
        [
            jnp.zeros((width,), f32),
            gain_mid_cot,
            gain_query_cot,
            gain_key_cot,
            jnp.zeros((6 * width - 2 * head_dim,), f32),
        ]
    ).reshape(8, width)
    router_parts = jnp.pad(
        router_term.reshape(rep_count, ep_count, router_rows, 128),
        ((0, 0), (0, 0), (0, -router_rows % 8), (0, 0)),
    )
    input_grad, query_sum, key_sum, value_sum, output_sum, gains_all, router_own = last_sums(
        normed_part.reshape(ep_count // 2, 2, tok_dev, width),
        qkv_term.reshape(rep_count, ep_count * rows_dev, 3 * slice_width),
        output_term.astype(bf16).reshape(heads_dev, 2, rows_dev, width),
        tokens,
        after_cot,
        gain_in.reshape(1, width),
        gains_term,
        router_parts,
        rows_dev,
        rep_count,
        ep_count,
        4,
    )
    gains_sum = lax.dynamic_slice_in_dim(
        gains_all.reshape(-1), (rep_index * ep_count + ep_index) * gains_dev, gains_dev
    )
    router_sum = router_own[:router_rows].reshape(rows_dev, experts_all)
    gate_w_grad, up_w_grad = join_columns(gate_pieces), join_columns(up_pieces)
    return (
        block_out,
        input_grad,
        query_sum,
        key_sum,
        value_sum,
        output_sum,
        router_sum,
        gains_sum,
        gate_w_grad,
        up_w_grad,
        down_w_grad,
    )


def solution(mesh):
    placed = (
        P(("rep", "ep"), None),
        P(("rep", "ep"), None),
        P(("rep", "ep"), None),
        P(("rep", "ep"), None),
        P(("rep", "ep"), None),
        P(("rep", "ep"), None),
        P(("rep", "ep"), None),
        P(("rep", "ep")),
        P("ep", None, None),
        P("ep", None, None),
        P("ep", None, None),
        P("rep", None),
        P(("rep", "ep")),
        P(("rep", "ep"), None),
        P(("rep", "ep")),
    )
    return jax.shard_map(
        on_device_split if mesh.shape["rep"] == 4 else on_device_general,
        mesh=mesh,
        in_specs=placed,
        out_specs=(
            P(("rep", "ep"), None),
            P(("rep", "ep"), None),
            P(("rep", "ep"), None),
            P(("rep", "ep"), None),
            P(("rep", "ep"), None),
            P(("rep", "ep"), None),
            P(("rep", "ep"), None),
            P(("rep", "ep")),
            P("ep", "rep", None),
            P("ep", "rep", None),
            P("ep", "rep", None),
        ),
        check_vma=False,
    )
```

```python
from functools import partial

import jax
import jax.numpy as jnp
from jax import lax
from jax.experimental import pallas as pl
from jax.experimental.pallas import tpu as pltpu
from jax.sharding import PartitionSpec as P

HD = 128


norm_eps = 1e-06
rope_base = 10000.0
masked_score = -1e30
highest = lax.Precision.HIGHEST


def rms_scale(values, gain_vec):
    return (
        values * lax.rsqrt(jnp.mean(values * values, axis=-1, keepdims=True) + norm_eps) * gain_vec
    )


def rotate(values, positions):
    half_width = values.shape[-1] // 2
    frequency = rope_base ** (-2.0 * jnp.arange(half_width, dtype=jnp.float32) / values.shape[-1])
    angles = positions.astype(jnp.float32)[:, None] * frequency[None, :]
    cosine = jnp.cos(angles)[:, None, :]
    sine_part = jnp.sin(angles)[:, None, :]
    low_half = values[..., :half_width]
    high_half = values[..., half_width:]
    return jnp.concatenate(
        [low_half * cosine - high_half * sine_part, high_half * cosine + low_half * sine_part],
        axis=-1,
    )


def placement(deal_rows, lengths_row):
    seq_ends = jnp.cumsum(lengths_row)
    is_after = (seq_ends[None, :] <= deal_rows[:, None]).astype(jnp.int32)
    segment = jnp.sum(is_after, axis=1)
    seq_start = jnp.sum(is_after * lengths_row[None, :], axis=1)
    return (segment, deal_rows - seq_start)


def rope_norm(projected, gain_vec, positions):
    return rotate(rms_scale(projected, gain_vec), positions)


def attend_forward(parts, same_seq, score_scale):
    head_query, head_key, head_value = parts
    scores = (
        jnp.einsum("thd,shd->hts", head_query, head_key, preferred_element_type=jnp.float32)
        * score_scale
    )
    scores = jnp.where(same_seq[None], scores, masked_score)
    top_score = jnp.max(scores, axis=-1, keepdims=True)
    lifted = jnp.exp(scores - top_score)
    total_sum = jnp.sum(lifted, axis=-1, keepdims=True)
    prob_low = (lifted / total_sum).astype(jnp.bfloat16)
    mixed_out = jnp.einsum("hts,shd->thd", prob_low, head_value, preferred_element_type=jnp.float32)
    return (mixed_out, top_score, total_sum)


def attend_backward(parts, same_seq, score_scale):
    head_query, head_key, head_value, head_grad, top_score, total_sum = parts
    scores = (
        jnp.einsum("thd,shd->hts", head_query, head_key, preferred_element_type=jnp.float32)
        * score_scale
    )
    scores = jnp.where(same_seq[None], scores, masked_score)
    prob_full = jnp.exp(scores - top_score) / total_sum
    prob_low = prob_full.astype(jnp.bfloat16)
    prob_grad = jnp.einsum(
        "thd,shd->hts", head_grad, head_value, preferred_element_type=jnp.float32
    )
    row_dot = jnp.sum(prob_full * prob_grad, axis=-1, keepdims=True)
    score_grad = (prob_full * (prob_grad - row_dot)).astype(jnp.bfloat16)
    query_grad = (
        jnp.einsum("hts,shd->thd", score_grad, head_key, preferred_element_type=jnp.float32)
        * score_scale
    )
    key_grad = (
        jnp.einsum("hts,thd->shd", score_grad, head_query, preferred_element_type=jnp.float32)
        * score_scale
    )
    value_grad = jnp.einsum("hts,thd->shd", prob_low, head_grad, preferred_element_type=jnp.float32)
    return (query_grad, key_grad, value_grad)


def on_device_general(
    tokens,
    cotangent,
    query_weight,
    key_weight,
    value_weight,
    output_weight,
    router_weight,
    gains,
    expert_gate,
    expert_up,
    expert_down,
    lengths,
    deal,
    routes,
    priority,
):
    tok_dev, width = tokens.shape
    ep_count = lax.axis_size("ep")
    ep_index = lax.axis_index("ep")
    exp_dev = expert_gate.shape[0]
    top_count = routes.shape[1]
    experts_all = exp_dev * ep_count
    group_rows = tok_dev * ep_count
    send_most = min(tok_dev, 3 * tok_dev * top_count // (2 * experts_all))
    capacity = 5 * tok_dev * top_count // (4 * exp_dev)
    head_dim = HD
    head_count = width // head_dim
    per_group = min(head_count, 4)
    group_count = head_count // per_group
    score_scale = head_dim ** (-0.5)
    query_full, key_full, value_full, output_full, router_full, gains_full = (
        lax.all_gather(query_weight, ("rep", "ep"), axis=0, tiled=True),
        lax.all_gather(key_weight, ("rep", "ep"), axis=0, tiled=True),
        lax.all_gather(value_weight, ("rep", "ep"), axis=0, tiled=True),
        lax.all_gather(output_weight, ("rep", "ep"), axis=0, tiled=True),
        lax.all_gather(router_weight, ("rep", "ep"), axis=0, tiled=True),
        lax.all_gather(gains, ("rep", "ep"), axis=0, tiled=True),
    )
    gains_float = gains_full.astype(jnp.float32)
    gain_in = gains_float[:width]
    gain_mid = gains_float[width : 2 * width]
    gain_query = gains_float[2 * width : 2 * width + head_dim]
    gain_key = gains_float[2 * width + head_dim :]
    deal_all, priority_all, routes_all = (
        lax.all_gather(deal, "ep", axis=0, tiled=True),
        lax.all_gather(priority, "ep", axis=0, tiled=True),
        lax.all_gather(routes, "ep", axis=0, tiled=True),
    )
    segment_all, position_all = placement(deal_all, lengths[0])
    segment_own = lax.dynamic_slice_in_dim(segment_all, ep_index * tok_dev, tok_dev)
    position_own = lax.dynamic_slice_in_dim(position_all, ep_index * tok_dev, tok_dev)
    residual = tokens.astype(jnp.float32)
    normed_low = rms_scale(residual, gain_in).astype(jnp.bfloat16)
    query_pre = jnp.dot(normed_low, query_full, preferred_element_type=jnp.float32).reshape(
        tok_dev, head_count, head_dim
    )
    key_pre = jnp.dot(normed_low, key_full, preferred_element_type=jnp.float32).reshape(
        tok_dev, head_count, head_dim
    )
    value_low = jnp.dot(normed_low, value_full, preferred_element_type=jnp.float32).astype(
        jnp.bfloat16
    )
    query_low = rope_norm(query_pre, gain_query, position_own).astype(jnp.bfloat16)
    key_low = (
        rope_norm(key_pre, gain_key, position_own).astype(jnp.bfloat16).reshape(tok_dev, width)
    )
    key_group, value_group = (
        lax.all_gather(key_low, "ep", axis=0, tiled=True),
        lax.all_gather(value_low, "ep", axis=0, tiled=True),
    )
    same_seq = segment_own[:, None] == segment_all[None, :]
    query_heads = query_low.reshape(tok_dev, group_count, per_group, head_dim).transpose(1, 0, 2, 3)
    key_heads = key_group.reshape(group_rows, group_count, per_group, head_dim).transpose(
        1, 0, 2, 3
    )
    value_heads = value_group.reshape(group_rows, group_count, per_group, head_dim).transpose(
        1, 0, 2, 3
    )
    mixed_heads, top_heads, total_heads = lax.map(
        partial(attend_forward, same_seq=same_seq, score_scale=score_scale),
        (query_heads, key_heads, value_heads),
    )
    mixed_low = mixed_heads.transpose(1, 0, 2, 3).reshape(tok_dev, width).astype(jnp.bfloat16)
    after_attn = residual + jnp.dot(mixed_low, output_full, preferred_element_type=jnp.float32)
    mid_low = rms_scale(after_attn, gain_mid).astype(jnp.bfloat16)
    logits = jnp.dot(mid_low, router_full, preferred_element_type=jnp.float32)
    chosen = jnp.take_along_axis(logits, routes, axis=1)
    gate_prob = jax.nn.softmax(chosen, axis=-1)
    expert_ids = jnp.arange(experts_all, dtype=jnp.int32)
    onehot_all = jnp.sum(
        (routes_all[:, :, None] == expert_ids[None, None, :]).astype(jnp.float32), axis=1
    )
    earlier = (priority_all[None, :] < priority_all[:, None]).astype(jnp.float32)
    slot_all = jnp.take_along_axis(
        jnp.dot(earlier, onehot_all, precision=highest), routes_all, axis=1
    ).astype(jnp.int32)
    row_ids = jnp.arange(tok_dev, dtype=jnp.int32)
    lower_tri = (row_ids[:, None] > row_ids[None, :]).astype(jnp.float32)
    before = jnp.einsum(
        "ij,dje->die",
        lower_tri,
        onehot_all.reshape(ep_count, tok_dev, experts_all),
        precision=highest,
    ).reshape(group_rows, experts_all)
    place_all = jnp.take_along_axis(before, routes_all, axis=1).astype(jnp.int32)
    kept_all = slot_all < capacity
    kept_own = lax.dynamic_slice_in_dim(kept_all, ep_index * tok_dev, tok_dev)
    place_own = lax.dynamic_slice_in_dim(place_all, ep_index * tok_dev, tok_dev)
    buffer_index = (routes * send_most + place_own).reshape(-1)
    rows_out = jnp.where(
        kept_own[:, :, None], mid_low[:, None, :], jnp.zeros((), jnp.bfloat16)
    ).reshape(tok_dev * top_count, width)
    send_rows = (
        jnp.zeros((experts_all * send_most, width), jnp.bfloat16)
        .at[buffer_index]
        .set(rows_out)
        .reshape(experts_all, send_most, width)
    )
    received = lax.all_to_all(send_rows, "ep", split_axis=0, concat_axis=1, tiled=True)
    gate_part = jnp.einsum(
        "erd,edf->erf", received, expert_gate, preferred_element_type=jnp.float32
    )
    up_part = jnp.einsum("erd,edf->erf", received, expert_up, preferred_element_type=jnp.float32)
    hidden = (jax.nn.silu(gate_part) * up_part).astype(jnp.bfloat16)
    result = jnp.einsum(
        "erf,efd->erd", hidden, expert_down, preferred_element_type=jnp.float32
    ).astype(jnp.bfloat16)
    returned = lax.all_to_all(result, "ep", split_axis=1, concat_axis=0, tiled=True)
    pair_out = returned.reshape(experts_all * send_most, width)[buffer_index].reshape(
        tok_dev, top_count, width
    )
    pair_weight = gate_prob * kept_own.astype(jnp.float32)
    moe_out = jnp.einsum("tk,tkd->td", pair_weight, pair_out, preferred_element_type=jnp.float32)
    block_out = (after_attn + moe_out).astype(jnp.bfloat16)
    out_grad = cotangent.astype(jnp.float32)
    pair_gate_grad = kept_own.astype(jnp.float32) * jnp.einsum(
        "tkd,td->tk", pair_out, out_grad, preferred_element_type=jnp.float32
    )
    pair_grad = (
        (pair_weight[:, :, None] * out_grad[:, None, :])
        .astype(jnp.bfloat16)
        .reshape(tok_dev * top_count, width)
    )
    grad_send = (
        jnp.zeros((experts_all * send_most, width), jnp.bfloat16)
        .at[buffer_index]
        .set(pair_grad)
        .reshape(experts_all, send_most, width)
    )
    grad_received = lax.all_to_all(grad_send, "ep", split_axis=0, concat_axis=1, tiled=True)
    hidden_grad = jnp.einsum(
        "erd,efd->erf", grad_received, expert_down, preferred_element_type=jnp.float32
    )
    _, silu_pull = jax.vjp(lambda gate_in, up_in: jax.nn.silu(gate_in) * up_in, gate_part, up_part)
    gate_part_grad, up_part_grad = silu_pull(hidden_grad)
    gate_low_grad = gate_part_grad.astype(jnp.bfloat16)
    up_low_grad = up_part_grad.astype(jnp.bfloat16)
    down_term = jnp.einsum(
        "erf,erd->efd", hidden, grad_received, preferred_element_type=jnp.float32
    )
    gate_term = jnp.einsum(
        "erd,erf->edf", received, gate_low_grad, preferred_element_type=jnp.float32
    )
    up_term = jnp.einsum("erd,erf->edf", received, up_low_grad, preferred_element_type=jnp.float32)
    rows_grad = (
        jnp.einsum("erf,edf->erd", gate_low_grad, expert_gate, preferred_element_type=jnp.float32)
        + jnp.einsum("erf,edf->erd", up_low_grad, expert_up, preferred_element_type=jnp.float32)
    ).astype(jnp.bfloat16)
    back_rows = lax.all_to_all(rows_grad, "ep", split_axis=1, concat_axis=0, tiled=True)
    mid_grad = jnp.sum(
        back_rows.reshape(experts_all * send_most, width)[buffer_index]
        .reshape(tok_dev, top_count, width)
        .astype(jnp.float32),
        axis=1,
    )
    gate_w_grad, up_w_grad, down_w_grad = (
        lax.psum_scatter(
            gate_term.astype(jnp.bfloat16), "rep", scatter_dimension=1, tiled=True
        ).astype(jnp.float32),
        lax.psum_scatter(
            up_term.astype(jnp.bfloat16), "rep", scatter_dimension=1, tiled=True
        ).astype(jnp.float32),
        lax.psum_scatter(
            down_term.astype(jnp.bfloat16), "rep", scatter_dimension=1, tiled=True
        ).astype(jnp.float32),
    )
    _, soft_pull = jax.vjp(lambda values: jax.nn.softmax(values, axis=-1), chosen)
    (chosen_grad,) = soft_pull(pair_gate_grad)
    onehot_own = (routes[:, :, None] == expert_ids[None, None, :]).astype(jnp.float32)
    logit_grad = jnp.einsum("tk,tke->te", chosen_grad, onehot_own).astype(jnp.bfloat16)
    mid_grad = mid_grad + jnp.dot(logit_grad, router_full.T, preferred_element_type=jnp.float32)
    router_term = jnp.dot(mid_low.T, logit_grad, preferred_element_type=jnp.float32)
    _, mid_pull = jax.vjp(rms_scale, after_attn, gain_mid)
    after_extra, gain_mid_grad = mid_pull(mid_grad)
    after_grad = out_grad + after_extra
    attn_low_grad = after_grad.astype(jnp.bfloat16)
    output_term = jnp.dot(mixed_low.T, attn_low_grad, preferred_element_type=jnp.float32)
    mixed_grad = jnp.dot(attn_low_grad, output_full.T, preferred_element_type=jnp.float32).astype(
        jnp.bfloat16
    )
    mixed_grad_heads = mixed_grad.reshape(tok_dev, group_count, per_group, head_dim).transpose(
        1, 0, 2, 3
    )
    query_grad_h, key_grad_h, value_grad_h = lax.map(
        partial(attend_backward, same_seq=same_seq, score_scale=score_scale),
        (query_heads, key_heads, value_heads, mixed_grad_heads, top_heads, total_heads),
    )
    query_grad_own = query_grad_h.transpose(1, 0, 2, 3).reshape(tok_dev, head_count, head_dim)
    key_grad_group = key_grad_h.transpose(1, 0, 2, 3).reshape(group_rows, width)
    value_grad_group = value_grad_h.transpose(1, 0, 2, 3).reshape(group_rows, width)
    key_sum, value_sum = (
        lax.psum_scatter(
            key_grad_group.astype(jnp.bfloat16), "ep", scatter_dimension=0, tiled=True
        ).astype(jnp.float32),
        lax.psum_scatter(
            value_grad_group.astype(jnp.bfloat16), "ep", scatter_dimension=0, tiled=True
        ).astype(jnp.float32),
    )
    value_low_grad = value_sum.astype(jnp.bfloat16)
    _, query_pull = jax.vjp(
        lambda projected, gain_vec: rope_norm(projected, gain_vec, position_own),
        query_pre,
        gain_query,
    )
    query_pre_grad, gain_query_grad = query_pull(query_grad_own)
    _, key_pull = jax.vjp(
        lambda projected, gain_vec: rope_norm(projected, gain_vec, position_own), key_pre, gain_key
    )
    key_pre_grad, gain_key_grad = key_pull(key_sum.reshape(tok_dev, head_count, head_dim))
    query_low_grad = query_pre_grad.reshape(tok_dev, width).astype(jnp.bfloat16)
    key_low_grad = key_pre_grad.reshape(tok_dev, width).astype(jnp.bfloat16)
    normed_grad = jnp.dot(query_low_grad, query_full.T, preferred_element_type=jnp.float32)
    normed_grad = normed_grad + jnp.dot(
        key_low_grad, key_full.T, preferred_element_type=jnp.float32
    )
    normed_grad = normed_grad + jnp.dot(
        value_low_grad, value_full.T, preferred_element_type=jnp.float32
    )
    query_term = jnp.dot(normed_low.T, query_low_grad, preferred_element_type=jnp.float32)
    key_term = jnp.dot(normed_low.T, key_low_grad, preferred_element_type=jnp.float32)
    value_term = jnp.dot(normed_low.T, value_low_grad, preferred_element_type=jnp.float32)
    _, input_pull = jax.vjp(rms_scale, residual, gain_in)
    input_extra, gain_in_grad = input_pull(normed_grad)
    input_grad = after_grad + input_extra
    gains_term = jnp.concatenate([gain_in_grad, gain_mid_grad, gain_query_grad, gain_key_grad])
    query_sum, key_total, value_total, output_sum, router_sum, gains_sum = (
        lax.psum_scatter(query_term, ("rep", "ep"), scatter_dimension=0, tiled=True),
        lax.psum_scatter(key_term, ("rep", "ep"), scatter_dimension=0, tiled=True),
        lax.psum_scatter(value_term, ("rep", "ep"), scatter_dimension=0, tiled=True),
        lax.psum_scatter(output_term, ("rep", "ep"), scatter_dimension=0, tiled=True),
        lax.psum_scatter(router_term, ("rep", "ep"), scatter_dimension=0, tiled=True),
        lax.psum_scatter(gains_term, ("rep", "ep"), scatter_dimension=0, tiled=True),
    )
    return (
        block_out,
        input_grad,
        query_sum,
        key_total,
        value_total,
        output_sum,
        router_sum,
        gains_sum,
        gate_w_grad,
        up_w_grad,
        down_w_grad,
    )


MESH = pl.DeviceIdType.MESH


def partners(e):
    sib = e + 1 - 2 * (e % 2)
    xn = e + 2 - 4 * ((e // 2) % 2)
    yn = e + 4 - 8 * ((e // 4) % 2)
    dg = xn + 4 - 8 * ((e // 4) % 2)
    return sib, (xn, yn, dg)


NT = (((1,), (1,)), ((), ()))
TN = (((0,), (0,)), ((), ()))


def visit_order(reps):
    return [sorted((g for g in range(reps) if g != z), key=lambda g: (abs(g - z), g)) + [z] for z in range(reps)]


def moe_kernel(reps, side_lanes, experts_all, x_ref, cot_ref, eg_ref, eu_ref, ed_ref,
               row_ref, moe_ref, gout_ref, uout_ref, dout_ref,
               mid_ref, a_ref, b_ref, h_ref, xin_ref, yin_ref, zin_ref,
               wgu, wd, xbuf, cbuf, abuf, pbuf, sib_in, relay_in, sendbuf, ownbuf, rbuf, tmp, colbuf, gst, dst,
               own_sem, w_sem, x_sem, c_sem, ab_sem, t_sem, col_sem, g_sem, o_sem,
               zs, zr, ps, pr, cs, cr, ss, sr, hs, hr, qs, qr, fs, fr):
    f32, bf16 = jnp.float32, jnp.bfloat16
    z = lax.axis_index("rep")
    e = lax.axis_index("ep")
    core = e % 2
    chip = e // 2
    sib, chips = partners(e)
    rows = x_ref.shape[0]
    half = rows // 2
    width = cot_ref.shape[-1]
    W1 = x_ref.shape[1]
    WP = pbuf.shape[-1]
    exp_dev = eg_ref.shape[0]
    F = wgu.shape[2] // exp_dev
    EF = exp_dev * F
    steps = 4 * reps
    table = visit_order(reps)

    def group_of(s):
        g = 0
        for zi in range(reps):
            for si in range(reps):
                g = g + jnp.where((z == zi) & (s == si), table[zi][si], 0)
        return g

    def chip_of(k):
        return jnp.where(k == 0, chips[2] // 2, jnp.where(k == 1, chip, jnp.where(k == 2, chips[0] // 2, chips[1] // 2)))

    barrier = pltpu.get_barrier_semaphore()
    for other in (sib, *chips):
        pl.semaphore_signal(barrier, inc=1, device_id={"rep": z, "ep": other}, device_id_type=MESH)
    for d in range(1, reps):
        pl.semaphore_signal(barrier, inc=1, device_id={"rep": (z + d) % reps, "ep": e}, device_id_type=MESH)
    weights = []
    for j in range(exp_dev):
        cut = pl.ds(pl.multiple_of(z * F, F), F)
        weights.append(pltpu.make_async_copy(eg_ref.at[j, :, cut], wgu.at[0, :, pl.ds(j * F, F)], w_sem.at[j]))
        weights.append(pltpu.make_async_copy(eu_ref.at[j, :, cut], wgu.at[1, :, pl.ds(j * F, F)], w_sem.at[exp_dev + j]))
        weights.append(pltpu.make_async_copy(ed_ref.at[j, cut, :], wd.at[pl.ds(j * F, F), :], w_sem.at[2 * exp_dev + j]))
    for w in weights:
        w.start()
    local = pltpu.make_async_copy(x_ref, mid_ref.at[z, e], own_sem)
    local.start()
    pl.semaphore_wait(barrier, 4 + reps - 1)

    def zcopy(src, g, up):
        d = 0 if up else 1
        return pltpu.make_async_remote_copy(
            src_ref=src, dst_ref=mid_ref.at[g, e], send_sem=zs.at[d, g], recv_sem=zr.at[g],
            device_id={"rep": z + 1 if up else z - 1, "ep": e}, device_id_type=MESH)

    def pcopy(src, g, j):
        return pltpu.make_async_remote_copy(
            src_ref=src, dst_ref=mid_ref.at[g, e], send_sem=ps.at[g, j], recv_sem=pr.at[g, j],
            device_id={"rep": z, "ep": chips[j]}, device_id_type=MESH)

    def relay(g, j, source):
        part = mid_ref.at[g, source, pl.ds(half * j, half)]
        return pltpu.make_async_remote_copy(
            src_ref=part, dst_ref=part, send_sem=ps.at[g, 2 + j], recv_sem=pr.at[g, 2 + j],
            device_id={"rep": z, "ep": chips[1 - j]}, device_id_type=MESH)

    def ccopy(src, g, j):
        who = e if j == 0 else chips[j - 1]
        return pltpu.make_async_remote_copy(
            src_ref=src, dst_ref=mid_ref.at[g, who], send_sem=cs.at[g, j], recv_sem=cr.at[g, j],
            device_id={"rep": z, "ep": sib}, device_id_type=MESH)

    def spread(src, g):
        pcopy(src, g, 0).start()
        pcopy(src, g, 1).start()
        ccopy(src, g, 0).start()

    def pass_on(g):
        for j in range(2):
            pcopy(x_ref, g, j).wait_recv()
            relay(g, j, chips[j]).start()
            ccopy(mid_ref.at[g, chips[j]], g, j + 1).start()

    def finish_in(g):
        for j in range(2):
            relay(g, j, chips[2]).wait_recv()
        ccopy(mid_ref.at[g, chips[2]], g, 3).start()

    def at(k, fn):
        if k == 0:
            fn(z)
            return
        @pl.when(z - k >= 0)
        def _():
            fn(z - k)
        @pl.when(z + k < reps)
        def _():
            fn(z + k)

    def arrive(k):
        @pl.when(z - k >= 0)
        def _():
            g = z - k
            zcopy(x_ref, g, True).wait_recv()
            @pl.when(z < reps - 1)
            def _():
                zcopy(mid_ref.at[g, e], g, True).start()
            spread(mid_ref.at[g, e], g)
        @pl.when(z + k < reps)
        def _():
            g = z + k
            zcopy(x_ref, g, False).wait_recv()
            @pl.when(z > 0)
            def _():
                zcopy(mid_ref.at[g, e], g, False).start()
            spread(mid_ref.at[g, e], g)

    def ready(g):
        for j in range(4):
            ccopy(x_ref, g, j).wait_recv()

    def load_x(i):
        g, q = group_of(i // 4), chip_of(i % 4)
        return pltpu.make_async_copy(mid_ref.at[g, pl.ds(2 * q, 2)], xbuf.at[i % 2], x_sem.at[i % 2])

    def load_c(i):
        g, q = group_of(i // 4), chip_of(i % 4)
        return pltpu.make_async_copy(cot_ref.at[g, pl.ds(2 * q, 2)], cbuf.at[i % 2], c_sem.at[i % 2])

    def keep(i, m):
        g, q = group_of(i // 4), chip_of(i % 4)
        place = pl.ds(pl.multiple_of((g * 4 + q) * 2 * rows, 2 * rows), 2 * rows)
        return pltpu.make_async_copy(abuf.at[i % 2, m], (a_ref, b_ref, h_ref)[m].at[place], ab_sem.at[i % 2, m])

    def compute(i):
        slot = i % 2
        lane = lax.broadcasted_iota(jnp.int32, (2 * rows, side_lanes), 1)
        side = xbuf[slot, :, :, pl.ds(width, side_lanes)].reshape(2 * rows, side_lanes).astype(f32)

        def one(j, cots):
            cols = pl.ds(pl.multiple_of(j * F, F), F)
            x = xbuf[slot, :, :, pl.ds(0, width)].reshape(2 * rows, width)
            c = cbuf[slot].reshape(2 * rows, width)
            index = e * exp_dev + j
            w = jnp.sum(jnp.where((lane == index) | (lane == index + experts_all), side, 0.0), axis=1, keepdims=True)
            ga = jnp.dot(x, wgu[0, :, cols], preferred_element_type=f32)
            up = jnp.dot(x, wgu[1, :, cols], preferred_element_type=f32)
            hc = lax.dot_general(c, wd[cols, :], NT, preferred_element_type=f32)
            sigma = 1.0 / (1.0 + jnp.exp(-ga))
            silu = ga * sigma
            hid = (silu * up).astype(bf16).astype(f32)
            hcw = hc * w
            abuf[slot, 0, :, cols] = (hcw * up * (sigma * (1.0 + ga * (1.0 - sigma)))).astype(bf16)
            abuf[slot, 1, :, cols] = (hcw * silu).astype(bf16)
            abuf[slot, 2, :, cols] = (hid * w).astype(bf16)
            dots = jnp.sum(hid * hc, axis=1, keepdims=True)
            return cots + jnp.where(lane == index, dots, 0.0)

        cots = lax.fori_loop(0, exp_dev, one, jnp.zeros((2 * rows, side_lanes), f32), unroll=True)
        pbuf[slot, :, :, pl.ds(width, side_lanes)] = cots.astype(bf16).reshape(2, rows, side_lanes)
        t = lax.dot_general(abuf[slot, 0], wgu[0], NT, preferred_element_type=f32)
        t = t + lax.dot_general(abuf[slot, 1], wgu[1], NT, preferred_element_type=f32)
        pbuf[slot, :, :, pl.ds(0, width)] = t.astype(bf16).reshape(2, rows, width)
        t = jnp.dot(abuf[slot, 2], wd[...], preferred_element_type=f32)
        pbuf[slot, :, :, pl.ds(W1, width)] = t.astype(bf16).reshape(2, rows, width)

    def sibcopy(i):
        return pltpu.make_async_remote_copy(
            src_ref=pbuf.at[i % 2, 1 - core], dst_ref=sib_in.at[i % 4], send_sem=ss.at[i], recv_sem=sr.at[i],
            device_id={"rep": z, "ep": sib}, device_id_type=MESH)

    def hcopy(s, j):
        part = pl.ds(half * j, half)
        return pltpu.make_async_remote_copy(
            src_ref=sendbuf.at[0, part], dst_ref=relay_in.at[s, j], send_sem=hs.at[s, j], recv_sem=hr.at[s, j],
            device_id={"rep": z, "ep": chips[j]}, device_id_type=MESH)

    def qcopy(s, j):
        return pltpu.make_async_remote_copy(
            src_ref=sendbuf.at[1 + j], dst_ref=(xin_ref, yin_ref)[j].at[s], send_sem=qs.at[s, j], recv_sem=qr.at[s, j],
            device_id={"rep": z, "ep": chips[j]}, device_id_type=MESH)

    def fcopy(s, g):
        return pltpu.make_async_remote_copy(
            src_ref=rbuf.at[s % 2], dst_ref=zin_ref.at[z], send_sem=fs.at[s], recv_sem=fr.at[z],
            device_id={"rep": g, "ep": e}, device_id_type=MESH)

    step = 16

    def add(out, terms, count=rows):
        @pl.loop(0, count // step)
        def _(i):
            r = pl.ds(pl.multiple_of(i * step, step), step)
            t = terms[0][r, :].astype(f32)
            for other in terms[1:]:
                t = t + other[r, :].astype(f32)
            out[r, :] = t.astype(out.dtype)

    def finish(i):
        s, k = i // 4, i % 4
        sibcopy(i).wait_recv()
        mine, other = pbuf.at[i % 2, core], sib_in.at[i % 4]
        lower, upper = pl.ds(0, half), pl.ds(half, half)
        @pl.when(k == 1)
        def _():
            add(ownbuf.at[s % 2], (mine, other))
        @pl.when(k == 0)
        def _():
            @pl.when(s > 0)
            def _():
                hcopy(s - 1, 0).wait_send()
                hcopy(s - 1, 1).wait_send()
            add(sendbuf.at[0], (mine, other))
            hcopy(s, 0).start()
            hcopy(s, 1).start()
        @pl.when(k == 2)
        def _():
            @pl.when(s > 0)
            def _():
                qcopy(s - 1, 0).wait_send()
            add(sendbuf.at[1, lower], (mine.at[lower], other.at[lower]), half)
            hcopy(s, 1).wait_recv()
            add(sendbuf.at[1, upper], (mine.at[upper], other.at[upper], relay_in.at[s, 1]), half)
            qcopy(s, 0).start()
        @pl.when(k == 3)
        def _():
            @pl.when(s > 0)
            def _():
                qcopy(s - 1, 1).wait_send()
            add(sendbuf.at[2, upper], (mine.at[upper], other.at[upper]), half)
            hcopy(s, 0).wait_recv()
            add(sendbuf.at[2, lower], (mine.at[lower], other.at[lower], relay_in.at[s, 0]), half)
            qcopy(s, 1).start()

    def load_t(src, m):
        return pltpu.make_async_copy(src, tmp.at[m], t_sem.at[m])

    def total(s):
        for j in range(2):
            qcopy(s, j).wait_recv()
            load_t((xin_ref, yin_ref)[j].at[s], j).start()
        for j in range(2):
            load_t((xin_ref, yin_ref)[j].at[s], j).wait()

    def plane_sum(s):
        total(s)
        @pl.when(s >= 2)
        def _():
            fcopy(s - 2, group_of(s - 2)).wait_send()
        add(rbuf.at[s % 2], (ownbuf.at[s % 2], tmp.at[0], tmp.at[1]))
        fcopy(s, group_of(s)).start()

    @pl.when(z < reps - 1)
    def _():
        zcopy(x_ref, z, True).start()
    @pl.when(z > 0)
    def _():
        zcopy(x_ref, z, False).start()
    spread(x_ref, z)
    arrive(1)
    pass_on(z)
    arrive(2)
    at(1, pass_on)
    finish_in(z)
    arrive(3)
    at(2, pass_on)
    at(1, finish_in)
    for w in weights:
        w.wait()
    ready(group_of(0))
    load_x(0).start()
    load_c(0).start()

    @pl.loop(0, steps)
    def _(i):
        load_x(i).wait()
        load_c(i).wait()
        @pl.when(i == 3)
        def _():
            at(3, pass_on)
            at(2, finish_in)
        @pl.when(i == 7)
        def _():
            at(3, finish_in)
        @pl.when(i == steps - 5)
        def _():
            local.wait()
        @pl.when(i < steps - 1)
        def _():
            @pl.when(i % 4 == 3)
            def _():
                ready(group_of(i // 4 + 1))
            load_x(i + 1).start()
            load_c(i + 1).start()
        @pl.when(i >= 2)
        def _():
            sibcopy(i - 2).wait_send()
            for m in range(3):
                keep(i - 2, m).wait()
        compute(i)
        sibcopy(i).start()
        for m in range(3):
            keep(i, m).start()
        @pl.when(i >= 1)
        def _():
            finish(i - 1)
        @pl.when((i % 4 == 3) & (i >= 7) & (i < steps - 1))
        def _():
            plane_sum(i // 4 - 1)

    for i in (steps - 2, steps - 1):
        sibcopy(i).wait_send()
        for m in range(3):
            keep(i, m).wait()
    finish(steps - 1)
    plane_sum(reps - 2)

    blocks = width // 256
    halves = wgu.shape[1]

    def resident(src, m):
        return pltpu.make_async_copy(src.at[pl.ds(m * halves, halves)], wgu.at[m], w_sem.at[m])

    def load_col(src, n):
        return pltpu.make_async_copy(src.at[:, :, :, pl.ds(pl.multiple_of(n * 256, 256), 256)], colbuf.at[n % 2], col_sem.at[n % 2])

    def product(n, m):
        left = colbuf[n % 2, pl.ds(m * (reps // 2), reps // 2)].reshape(halves, 256)
        return left, wgu[m]

    def grad_rows(src, out):
        def store(n, j):
            per = width // reps
            place = pl.ds(pl.multiple_of((n * 256) % per, 256), 256)
            return pltpu.make_async_copy(gst.at[n % 2, j], out.at[((n * 256) // per + reps - z) % reps, j, place], g_sem.at[n % 2, j])
        for m in range(2):
            resident(src, m).start()
        load_col(mid_ref, 0).start()
        for m in range(2):
            resident(src, m).wait()
        @pl.loop(0, blocks)
        def _(n):
            load_col(mid_ref, n).wait()
            @pl.when(n < blocks - 1)
            def _():
                load_col(mid_ref, n + 1).start()
            @pl.when(n >= 2)
            def _():
                for j in range(exp_dev):
                    store(n - 2, j).wait()
            t = jnp.zeros((256, EF), f32)
            for m in range(2):
                left, right = product(n, m)
                t = t + lax.dot_general(left, right, TN, preferred_element_type=f32)
            for j in range(exp_dev):
                gst[n % 2, j] = t[:, j * F:(j + 1) * F].astype(bf16)
                store(n, j).start()
        for n in (blocks - 2, blocks - 1):
            for j in range(exp_dev):
                store(n, j).wait()

    def grad_down():
        def store(n):
            return pltpu.make_async_copy(dst.at[n % 2], dout_ref.at[:, :, pl.ds(pl.multiple_of(n * 256, 256), 256)], g_sem.at[n % 2, 0])
        for m in range(2):
            resident(h_ref, m).start()
        load_col(cot_ref, 0).start()
        for m in range(2):
            resident(h_ref, m).wait()
        @pl.loop(0, blocks)
        def _(n):
            load_col(cot_ref, n).wait()
            @pl.when(n < blocks - 1)
            def _():
                load_col(cot_ref, n + 1).start()
            @pl.when(n >= 2)
            def _():
                store(n - 2).wait()
            t = jnp.zeros((EF, 256), f32)
            for m in range(2):
                left, right = product(n, m)
                t = t + lax.dot_general(right, left, TN, preferred_element_type=f32)
            dst[n % 2] = t.reshape(exp_dev, F, 256)
            store(n).start()
        for n in (blocks - 2, blocks - 1):
            store(n).wait()

    grad_rows(a_ref, gout_ref)
    grad_rows(b_ref, uout_ref)
    grad_down()

    last = reps - 1
    total(last)
    for d in range(1, reps):
        src = (z + d) % reps
        pltpu.make_async_remote_copy(
            src_ref=rbuf.at[0], dst_ref=zin_ref.at[src], send_sem=fs.at[last], recv_sem=fr.at[src],
            device_id={"rep": src, "ep": e}, device_id_type=MESH).wait_recv()
        load_t(zin_ref.at[src], 1 + d).start()
    for d in range(1, reps):
        load_t(zin_ref.at[(z + d) % reps], 1 + d).wait()
    fcopy(reps - 3, group_of(reps - 3)).wait_send()
    add(rbuf.at[(reps - 3) % 2], (ownbuf.at[last % 2], *(tmp.at[m] for m in range(reps + 1))))
    outs = (
        pltpu.make_async_copy(rbuf.at[(reps - 3) % 2, :, pl.ds(0, W1)], row_ref, o_sem.at[0]),
        pltpu.make_async_copy(rbuf.at[(reps - 3) % 2, :, pl.ds(W1, width)], moe_ref, o_sem.at[1]),
    )
    for o in outs:
        o.start()
    for o in outs:
        o.wait()
    fcopy(reps - 2, group_of(reps - 2)).wait_send()
    for j in range(2):
        hcopy(last, j).wait_send()
        qcopy(last, j).wait_send()
    for g in range(reps):
        for j in range(4):
            ccopy(x_ref, g, j).wait_send()
        for j in range(2):
            pcopy(x_ref, g, j).wait_send()
            relay(g, j, chips[j]).wait_send()
        @pl.when((z < reps - 1) & (z >= g))
        def _():
            zcopy(x_ref, g, True).wait_send()
        @pl.when((z > 0) & (z <= g))
        def _():
            zcopy(x_ref, g, False).wait_send()


def moe(x, cot_all, eg, eu, ed, experts_all, cid):
    reps, eps, rows, width = cot_all.shape
    W1 = x.shape[1]
    side = W1 - width
    WP = W1 + width
    exp_dev, _, ff = eg.shape
    F = ff // reps
    EF = exp_dev * F
    f32, bf16 = jnp.float32, jnp.bfloat16
    D, V = pltpu.SemaphoreType.DMA, pltpu.VMEM
    S = jax.ShapeDtypeStruct
    tokens = reps * eps * rows
    steps = 4 * reps
    outs = (
        S((rows, W1), bf16), S((rows, width), bf16),
        S((reps, exp_dev, width // reps, F), bf16), S((reps, exp_dev, width // reps, F), bf16), S((exp_dev, F, width), f32),
        S((reps, eps, rows, W1), bf16), S((tokens, EF), bf16), S((tokens, EF), bf16), S((tokens, EF), bf16),
        S((reps, rows, WP), bf16), S((reps, rows, WP), bf16), S((reps, rows, WP), bf16),
    )
    return pl.pallas_call(
        partial(moe_kernel, reps, side, experts_all),
        out_shape=outs,
        in_specs=[pl.BlockSpec(memory_space=pl.ANY)] * 5,
        out_specs=[pl.BlockSpec(memory_space=pl.ANY)] * len(outs),
        scratch_shapes=[
            V((2, width, EF), bf16), V((EF, width), bf16),
            V((2, 2, rows, W1), bf16), V((2, 2, rows, width), bf16),
            V((2, 3, 2 * rows, EF), bf16), V((2, 2, rows, WP), bf16), V((4, rows, WP), bf16),
            V((reps, 2, rows // 2, WP), bf16), V((3, rows, WP), bf16), V((2, rows, WP), bf16), V((2, rows, WP), bf16),
            V((5, rows, WP), bf16), V((2, reps, eps, rows, 256), bf16),
            V((2, exp_dev, 256, F), bf16), V((2, exp_dev, F, 256), f32),
            D, D((3 * exp_dev,)), D((2,)), D((2,)), D((2, 3)), D((5,)), D((2,)), D((2, exp_dev)), D((2,)),
            D((2, reps)), D((reps,)), D((reps, 4)), D((reps, 4)), D((reps, 4)), D((reps, 4)),
            D((steps,)), D((steps,)), D((reps, 2)), D((reps, 2)), D((reps, 2)), D((reps, 2)), D((reps,)), D((reps,)),
        ],
        compiler_params=pltpu.CompilerParams(collective_id=cid, has_side_effects=True, vmem_limit_bytes=63 * 2**20),
    )(x, cot_all, eg, eu, ed)[:5]


def back_kernel(heads_dev, cot_ref, wout_ref, mixed_ref, qkv_ref, pre_ref, turn_ref, segs_ref, gains_ref, normed_ref, wqkv_ref,
                part_ref, qkv_out, out_out, gain_out,
                cots, wout, mixed, qkv, pre, turn, segs, gains, normed, wqkv, probs, dsc, dmix, dkey, pcot, part, term, oterm, gsum,
                l_sem, o_sem, ts, tr, tcs, tcr):
    f32, bf16 = jnp.float32, jnp.bfloat16
    z = lax.axis_index("rep")
    e = lax.axis_index("ep")
    sib, chips = partners(e)
    eps, rows, width = cots.shape
    half = rows // 2
    group_rows = eps * rows
    slice_width = mixed.shape[1]
    head_dim = slice_width // heads_dev
    scale = head_dim ** -0.5

    barrier = pltpu.get_barrier_semaphore()
    for other in (sib, *chips):
        pl.semaphore_signal(barrier, inc=1, device_id={"rep": z, "ep": other}, device_id_type=MESH)
    pairs = ((qkv_ref, qkv), (segs_ref, segs), (wout_ref, wout), (mixed_ref, mixed), (pre_ref, pre), (turn_ref, turn),
             (gains_ref, gains), (normed_ref, normed), (wqkv_ref, wqkv), (cot_ref, cots.at[e]))
    loads = [pltpu.make_async_copy(a, b, l_sem.at[n]) for n, (a, b) in enumerate(pairs)]
    for c in loads:
        c.start()
    pl.semaphore_wait(barrier, 4)

    def remote(src, dst, send, recv, ep):
        return pltpu.make_async_remote_copy(src_ref=src, dst_ref=dst, send_sem=send, recv_sem=recv,
                                            device_id={"rep": z, "ep": ep}, device_id_type=MESH)

    def near(j):
        return remote(cot_ref, cots.at[e], ts.at[j], tr.at[j], chips[j])

    def relay(j, source):
        p = cots.at[source, pl.ds(half * j, half)]
        return remote(p, p, ts.at[2 + j], tr.at[2 + j], chips[1 - j])

    def other_core(j):
        if j == 0:
            return remote(cot_ref, cots.at[e], tcs.at[0], tcr.at[0], sib)
        p = cots.at[chips[j - 1]]
        return remote(p, p, tcs.at[j], tcr.at[j], sib)

    near(0).start()
    near(1).start()
    other_core(0).start()

    block = 2 * rows
    blocks = group_rows // block
    loads[0].wait()
    loads[1].wait()
    seg_row = jnp.concatenate([segs[n:n + 1, :] for n in range(eps)], axis=1)

    def softmax(h, n):
        here = pl.ds(n * block, block)
        cut = slice(h * head_dim, (h + 1) * head_dim)
        kcut = slice(slice_width + h * head_dim, slice_width + (h + 1) * head_dim)
        s = lax.dot_general(qkv[here, cut], qkv[:, kcut], NT, preferred_element_type=f32) * scale
        seg_col = jnp.concatenate(
            [jnp.broadcast_to(segs[2 * n + j:2 * n + j + 1, :], (rows, rows)).T[:, 0:1] for j in range(2)], axis=0)
        s = jnp.where(seg_col == seg_row, s, masked_score)
        p = jnp.exp(s - jnp.max(s, axis=-1, keepdims=True))
        probs[h, here, :] = p / jnp.sum(p, axis=-1, keepdims=True)

    for n in range(blocks):
        softmax(0, n)
    for j in range(2):
        near(j).wait_recv()
        relay(j, chips[j]).start()
        other_core(j + 1).start()
    for h in range(1, heads_dev):
        for n in range(blocks):
            softmax(h, n)
    for j in range(2):
        relay(j, chips[2]).wait_recv()
    other_core(3).start()
    for c in loads[2:]:
        c.wait()
    for j in range(4):
        other_core(j).wait_recv()

    flat = cots[...].reshape(group_rows, width)
    weight = wout[...].reshape(slice_width, width)
    for n in range(blocks):
        here = pl.ds(n * block, block)
        left = cots[pl.ds(2 * n, 2)].reshape(block, width)
        dmix[here, :] = lax.dot_general(left, weight, NT, preferred_element_type=f32).astype(bf16)
    oterm[...] = lax.dot_general(mixed[...], flat, TN, preferred_element_type=f32).astype(bf16).reshape(oterm.shape)
    outs = [pltpu.make_async_copy(oterm, out_out, o_sem.at[0])]
    outs[0].start()

    def through_norm(index, dy, here, gain_row):
        cut = slice(index * head_dim, (index + 1) * head_dim)
        x = pre[here, cut]
        dn = dy * turn[0, here, :] + pltpu.roll(dy * turn[1, here, :], head_dim // 2, 1)
        r = lax.rsqrt(jnp.mean(x * x, axis=-1, keepdims=True) + norm_eps)
        unit = x * r
        gsum[gain_row:gain_row + 1, :] += jnp.sum(dn * unit, axis=0, keepdims=True)
        base = 2 * width // 128 + gain_row
        w = dn * gains[base:base + 1, :]
        pcot[here, cut] = (r * (w - unit * jnp.mean(w * unit, axis=-1, keepdims=True))).astype(bf16)

    gsum[...] = jnp.zeros_like(gsum)
    for h in range(heads_dev):
        cut = slice(h * head_dim, (h + 1) * head_dim)
        kcut = slice(slice_width + h * head_dim, slice_width + (h + 1) * head_dim)
        vcut = slice(2 * slice_width + h * head_dim, 2 * slice_width + (h + 1) * head_dim)
        for n in range(blocks):
            here = pl.ds(n * block, block)
            p = probs[h, here, :]
            dp = lax.dot_general(dmix[here, cut], qkv[:, vcut], NT, preferred_element_type=f32)
            ds = (p * (dp - jnp.sum(p * dp, axis=-1, keepdims=True))).astype(bf16)
            dsc[0, here, :] = ds
            dsc[1, here, :] = p.astype(bf16)
            through_norm(h, jnp.dot(ds, qkv[:, kcut], preferred_element_type=f32) * scale, here, 0)
        dkey[...] = lax.dot_general(dsc[0], qkv[:, cut], TN, preferred_element_type=f32) * scale
        for n in range(blocks):
            here = pl.ds(n * block, block)
            through_norm(heads_dev + h, dkey[here, :], here, 1)
        pcot[:, vcut] = lax.dot_general(dsc[1], dmix[:, cut], TN, preferred_element_type=f32).astype(bf16)
    outs.append(pltpu.make_async_copy(gsum, gain_out, o_sem.at[1]))
    outs[-1].start()

    for n in range(blocks):
        here = pl.ds(n * block, block)
        t = lax.dot_general(pcot[here, :], wqkv[...], NT, preferred_element_type=f32)
        part[n] = t.astype(bf16).reshape(2, rows, width)
        outs.append(pltpu.make_async_copy(part.at[n], part_ref.at[n], o_sem.at[2 + n]))
        outs[-1].start()
    piece = width // term.shape[0]
    for n in range(term.shape[0]):
        left = normed[:, n * piece:(n + 1) * piece]
        term[n] = lax.dot_general(left, pcot[...], TN, preferred_element_type=f32).astype(bf16)
        outs.append(pltpu.make_async_copy(term.at[n], qkv_out.at[n], o_sem.at[2 + blocks + n]))
        outs[-1].start()
    for c in outs:
        c.wait()
    for j in range(2):
        near(j).wait_send()
        relay(j, chips[j]).wait_send()
    for j in range(4):
        other_core(j).wait_send()


def attention_back(cot, wout, mixed, qkv, pre, turn, segs, gains, normed, wqkv, reps, eps, cid):
    rows, width = cot.shape
    heads_dev = wout.shape[0]
    gr, sw = mixed.shape
    f32, bf16 = jnp.float32, jnp.bfloat16
    S, V, D = jax.ShapeDtypeStruct, pltpu.VMEM, pltpu.SemaphoreType.DMA
    hd = sw // heads_dev
    outs = (S((eps // 2, 2, rows, width), bf16), S((reps, width // reps, 3 * sw), bf16), S(wout.shape, bf16), S((8, hd), f32))
    return pl.pallas_call(
        partial(back_kernel, heads_dev),
        out_shape=outs,
        in_specs=[pl.BlockSpec(memory_space=pl.ANY)] * 10,
        out_specs=[pl.BlockSpec(memory_space=pl.ANY)] * len(outs),
        scratch_shapes=[
            V((eps, rows, width), bf16), *[V(a.shape, a.dtype) for a in (wout, mixed, qkv, pre, turn, segs, gains, normed, wqkv)],
            V((heads_dev, gr, gr), f32), V((2, gr, gr), bf16), V((gr, sw), bf16), V((gr, hd), f32), V((gr, 3 * sw), bf16),
            V(outs[0].shape, bf16), V(outs[1].shape, bf16), V(wout.shape, bf16), V((8, hd), f32),
            D((10,)), D((2 + eps // 2 + reps,)), D((4,)), D((4,)), D((4,)), D((4,)),
        ],
        compiler_params=pltpu.CompilerParams(collective_id=cid, has_side_effects=True, vmem_limit_bytes=58 * 2**20),
    )(cot, wout, mixed, qkv, pre, turn, segs, gains, normed, wqkv)


def last_kernel(reps, eps, part_ref, qkv_ref, out_ref, tok_ref, cot_ref, gain_ref, gains_ref, router_ref,
                input_ref, q_ref, k_ref, v_ref, o_ref, gsum_ref, rsum_ref,
                own, sib_in, relay_in, xin, yin, wo, qall, qup, qdown, wup, wdown, fin, gath, mats, omat, tok, cot, gain,
                gown, gin, gz, gmid, rown, rin, rz, rmid,
                l_sem, ss, sr, hs, hr, qs, qr, ws, wr, us, ur, ds, dr, wus, wur, wds, wdr, ps, pr, gs, gr, gzs, gzr, rs, rr, rzs, rzr):
    f32, bf16 = jnp.float32, jnp.bfloat16
    z = lax.axis_index("rep")
    e = lax.axis_index("ep")
    core = e % 2
    chip = e // 2
    sib, chips = partners(e)
    rows, width = tok_ref.shape
    half = rows // 2
    rows_dev = o_ref.shape[0]
    heads_dev = out_ref.shape[0]
    head_dim = width // (heads_dev * eps)
    slice_width = heads_dev * head_dim

    barrier = pltpu.get_barrier_semaphore()
    for d in range(1, eps):
        pl.semaphore_signal(barrier, inc=1, device_id={"rep": z, "ep": (e + d) % eps}, device_id_type=MESH)
    for d in range(1, reps):
        pl.semaphore_signal(barrier, inc=1, device_id={"rep": (z + d) % reps, "ep": e}, device_id_type=MESH)
    loads = [
        pltpu.make_async_copy(part_ref.at[:, core], own, l_sem.at[0]),
        pltpu.make_async_copy(qkv_ref, qall, l_sem.at[1]),
        pltpu.make_async_copy(out_ref.at[:, core], wo.at[core], l_sem.at[2]),
        pltpu.make_async_copy(tok_ref, tok, l_sem.at[3]),
        pltpu.make_async_copy(cot_ref, cot, l_sem.at[4]),
        pltpu.make_async_copy(gain_ref, gain, l_sem.at[5]),
        pltpu.make_async_copy(gains_ref, gown, l_sem.at[6]),
        pltpu.make_async_copy(router_ref, rown, l_sem.at[7]),
    ]
    for c in loads:
        c.start()
    pl.semaphore_wait(barrier, eps - 1 + reps - 1)

    def to_sib(src, dst, send, recv):
        return pltpu.make_async_remote_copy(src_ref=src, dst_ref=dst, send_sem=send, recv_sem=recv,
                                            device_id={"rep": z, "ep": sib}, device_id_type=MESH)

    def to_chip(src, dst, send, recv, j):
        return pltpu.make_async_remote_copy(src_ref=src, dst_ref=dst, send_sem=send, recv_sem=recv,
                                            device_id={"rep": z, "ep": chips[j]}, device_id_type=MESH)

    def to_plane(src, dst, send, recv, d):
        return pltpu.make_async_remote_copy(src_ref=src, dst_ref=dst, send_sem=send, recv_sem=recv,
                                            device_id={"rep": z, "ep": (e + d) % eps}, device_id_type=MESH)

    def to_rep(src, dst, send, recv, d):
        return pltpu.make_async_remote_copy(src_ref=src, dst_ref=dst, send_sem=send, recv_sem=recv,
                                            device_id={"rep": (z + d) % reps, "ep": e}, device_id_type=MESH)

    def along(src, slot, send, recv, up):
        return pltpu.make_async_remote_copy(src_ref=src, dst_ref=slot, send_sem=send, recv_sem=recv,
                                            device_id={"rep": z + 1 if up else z - 1, "ep": e}, device_id_type=MESH)

    class Sum:
        def __init__(self, mine, up, down, usend, urecv, dsend, drecv, count):
            self.mine, self.up, self.down, self.count = mine, up, down, count
            self.usend, self.urecv, self.dsend, self.drecv = usend, urecv, dsend, drecv

        def hop(self, src, g, up):
            if up:
                return along(src, self.up.at[g], self.usend.at[g], self.urecv.at[g], True)
            return along(src, self.down.at[g], self.dsend.at[g], self.drecv.at[g], False)

        def begin(self):
            @pl.when(z == 0)
            def _():
                for g in range(reps - 1, 0, -1):
                    self.hop(self.mine(g), g, True).start()
            @pl.when(z == reps - 1)
            def _():
                for g in range(reps - 1):
                    self.hop(self.mine(g), g, False).start()

        def forward(self, n):
            g = reps - 1 - n
            @pl.when((z > 0) & (z < g))
            def _():
                self.hop(self.mine(g), g, True).wait_recv()
                add(self.up.at[g], (self.up.at[g], self.mine(g)), self.count)
                self.hop(self.up.at[g], g, True).start()
            @pl.when((z < reps - 1) & (z > n))
            def _():
                self.hop(self.mine(n), n, False).wait_recv()
                add(self.down.at[n], (self.down.at[n], self.mine(n)), self.count)
                self.hop(self.down.at[n], n, False).start()

        def arrived(self):
            @pl.when(z > 0)
            def _():
                self.hop(self.mine(0), z, True).wait_recv()
            @pl.when(z == 0)
            def _():
                self.up[z] = jnp.zeros(self.up.shape[1:], bf16)
            @pl.when(z < reps - 1)
            def _():
                self.hop(self.mine(0), z, False).wait_recv()
            @pl.when(z == reps - 1)
            def _():
                self.down[z] = jnp.zeros(self.down.shape[1:], bf16)

        def sent(self):
            for g in range(reps):
                @pl.when(z < g)
                def _():
                    self.hop(self.mine(g), g, True).wait_send()
                @pl.when(z > g)
                def _():
                    self.hop(self.mine(g), g, False).wait_send()

    step = 16

    def add(out, terms, count):
        @pl.loop(0, count // step)
        def _(i):
            r = pl.ds(pl.multiple_of(i * step, step), step)
            t = terms[0][r, :].astype(f32)
            for other in terms[1:]:
                t = t + other[r, :].astype(f32)
            out[r, :] = t.astype(out.dtype)

    lower, upper = pl.ds(0, half), pl.ds(half, half)
    qkv_sum = Sum(lambda g: qall.at[g], qup, qdown, us, ur, ds, dr, rows_dev * eps)
    out_sum = Sum(lambda g: wo.at[g // heads_dev, g % heads_dev], wup, wdown, wus, wur, wds, wdr, rows_dev)
    wcopy = to_sib(out_ref.at[:, 1 - core], wo.at[core], ws, wr)
    order = (chips[2] // 2, chips[0] // 2, chips[1] // 2, chip)
    scopies = [to_sib(part_ref.at[q, 1 - core], sib_in.at[q], ss.at[n], sr.at[n]) for n, q in enumerate(order)]
    for c in scopies:
        c.start()
    wcopy.start()

    loads[1].wait()
    qkv_sum.begin()
    hcopies = [to_chip(own.at[order[0], (lower, upper)[j]], relay_in.at[j], hs.at[j], hr.at[j], j) for j in range(2)]
    qcopies = [to_chip(own.at[order[1 + j]], (xin, yin)[j], qs.at[j], qr.at[j], j) for j in range(2)]
    loads[0].wait()
    scopies[0].wait_recv()
    d = own.at[order[0]]
    add(d, (d, sib_in.at[order[0]]), rows)
    for c in hcopies:
        c.start()
    for j in range(2):
        mine, other = own.at[order[1 + j]], sib_in.at[order[1 + j]]
        scopies[1 + j].wait_recv()
        direct, through = ((lower, upper), (upper, lower))[j]
        add(mine.at[direct], (mine.at[direct], other.at[direct]), half)
        hcopies[1 - j].wait_recv()
        add(mine.at[through], (mine.at[through], other.at[through], relay_in.at[1 - j]), half)
        qcopies[j].start()
    loads[2].wait()
    wcopy.wait_recv()
    out_sum.begin()
    qkv_sum.forward(0)
    scopies[3].wait_recv()
    for c in loads[3:8]:
        c.wait()
    for c in qcopies:
        c.wait_recv()

    gown[0:1, :] = jnp.zeros((1, width), f32)

    @pl.loop(0, rows // step)
    def _(i):
        r = pl.ds(pl.multiple_of(i * step, step), step)
        nc = (own[chip, r, :].astype(f32) + sib_in[chip, r, :].astype(f32) + xin[r, :].astype(f32) + yin[r, :].astype(f32))
        t = tok[r, :].astype(f32)
        scale = lax.rsqrt(jnp.mean(t * t, axis=-1, keepdims=True) + 1e-6)
        unit = t * scale
        scaled = nc * gain[0:1, :]
        cot[r, :] = cot[r, :] + scale * (scaled - unit * jnp.mean(scaled * unit, axis=-1, keepdims=True))
        gown[0:1, :] += jnp.sum(nc * unit, axis=0, keepdims=True)

    done = [pltpu.make_async_copy(cot, input_ref, l_sem.at[8])]
    done[0].start()

    gcopies = [to_plane(gown, gin.at[d - 1], gs.at[d - 1], gr.at[d - 1], d) for d in range(1, eps)]
    rcopies = [to_plane(rown.at[:, (e + d) % eps], rin.at[d - 1], rs.at[d - 1], rr.at[d - 1], d) for d in range(1, eps)]
    for c in (*gcopies, *rcopies):
        c.start()
    qkv_sum.forward(1)
    out_sum.forward(0)
    for n in range(2, reps - 1):
        qkv_sum.forward(n)
    for n in range(1, reps - 1):
        out_sum.forward(n)
    for c in (*gcopies, *rcopies):
        c.wait_recv()
    t = gown[...]
    for d in range(1, eps):
        t = t + gin[d - 1]
    gmid[...] = t
    t = rown[:, e]
    for d in range(1, eps):
        t = t + rin[d - 1]
    rmid[...] = t
    gzcopies = [to_rep(gmid, gz.at[d - 1], gzs.at[d - 1], gzr.at[d - 1], d) for d in range(1, reps)]
    rzcopies = [to_rep(rmid.at[(z + d) % reps], rz.at[d - 1], rzs.at[d - 1], rzr.at[d - 1], d) for d in range(1, reps)]
    for c in (*gzcopies, *rzcopies):
        c.start()

    qkv_sum.arrived()
    for n in range(eps):
        @pl.loop(0, rows_dev // step)
        def _(i):
            r = pl.ds(pl.multiple_of(i * step, step), step)
            a = pl.ds(pl.multiple_of(n * rows_dev + i * step, step), step)
            t = qall[z, a, :].astype(f32) + qup[z, a, :].astype(f32) + qdown[z, a, :].astype(f32)
            fin[n, r, :] = t.astype(bf16)
    pcopies = [to_plane(fin.at[(e + d) % eps], gath.at[e], ps.at[d - 1], pr.at[d - 1], d) for d in range(1, eps)]
    for c in pcopies:
        c.start()
    mine = pltpu.make_async_copy(fin.at[e], gath.at[e], l_sem.at[9])
    mine.start()
    out_sum.arrived()
    for c in (*gzcopies, *rzcopies):
        c.wait_recv()
    for c in gcopies:
        c.wait_send()
    t = gmid[...]
    for d in range(reps - 1):
        t = t + gz[d]
    gown[...] = t
    t = rmid[z]
    for d in range(reps - 1):
        t = t + rz[d]
    rmid[z] = t
    done.append(pltpu.make_async_copy(gown, gsum_ref, l_sem.at[10]))
    done.append(pltpu.make_async_copy(rmid.at[z], rsum_ref, l_sem.at[11]))
    wmine = wo.at[z // heads_dev, z % heads_dev]

    @pl.loop(0, rows_dev // step)
    def _(i):
        r = pl.ds(pl.multiple_of(i * step, step), step)
        t = wmine[r, :].astype(f32) + wup[z, r, :].astype(f32) + wdown[z, r, :].astype(f32)
        omat[r, :] = t
    done.append(pltpu.make_async_copy(omat, o_ref, l_sem.at[12]))
    for c in rzcopies:
        c.wait_send()
    for c in done[1:]:
        c.start()
    mine.wait()
    for c in pcopies:
        c.wait_recv()
    for src in range(eps):
        for m in range(3):
            for i in range(heads_dev):
                head = ((src % 2) * heads_dev + i) * (eps // 2) + src // 2
                mats[m, :, head * head_dim:(head + 1) * head_dim] = gath[src, :, m * slice_width + i * head_dim:m * slice_width + (i + 1) * head_dim].astype(f32)
    for m, ref in enumerate((q_ref, k_ref, v_ref)):
        done.append(pltpu.make_async_copy(mats.at[m], ref, l_sem.at[13 + m]))
        done[-1].start()
    for c in done:
        c.wait()
    qkv_sum.sent()
    out_sum.sent()
    for c in (*scopies, wcopy, *hcopies, *qcopies, *pcopies, *rcopies, *gzcopies):
        c.wait_send()


def last_sums(part, qkv_term, out_term, tokens, after_cot, gain_in, gains, router, rows_dev, reps, eps, cid):
    rows, width = tokens.shape
    f32, bf16 = jnp.float32, jnp.bfloat16
    heads_dev = out_term.shape[0]
    slices = qkv_term.shape[2]
    q = eps // 2
    half = rows // 2
    D, V = pltpu.SemaphoreType.DMA, pltpu.VMEM
    S = jax.ShapeDtypeStruct
    g8, rt = gains.shape, router.shape[2:]
    outs = (S((rows, width), f32), *[S((rows_dev, width), f32)] * 4, S(g8, f32), S(rt, f32))
    return pl.pallas_call(
        partial(last_kernel, reps, eps),
        out_shape=outs,
        in_specs=[pl.BlockSpec(memory_space=pl.ANY)] * 8,
        out_specs=[pl.BlockSpec(memory_space=pl.ANY)] * len(outs),
        scratch_shapes=[
            V((q, rows, width), bf16), V((q, rows, width), bf16), V((2, half, width), bf16), V((rows, width), bf16), V((rows, width), bf16),
            V((2, heads_dev, rows_dev, width), bf16), *[V((reps, rows_dev * eps, slices), bf16)] * 3, *[V((reps, rows_dev, width), bf16)] * 2,
            V((eps, rows_dev, slices), bf16), V((eps, rows_dev, slices), bf16),
            V((3, rows_dev, width), f32), V((rows_dev, width), f32), V((rows, width), bf16), V((rows, width), f32), V((1, width), f32),
            V(g8, f32), V((eps - 1, *g8), f32), V((reps - 1, *g8), f32), V(g8, f32),
            V(router.shape, f32), V((eps - 1, reps, *rt), f32), V((reps - 1, *rt), f32), V((reps, *rt), f32),
            D((17,)), D((4,)), D((4,)), D((2,)), D((2,)), D((2,)), D((2,)), D, D,
            *[D((reps,))] * 8, D((eps - 1,)), D((eps - 1,)),
            D((eps - 1,)), D((eps - 1,)), D((reps - 1,)), D((reps - 1,)), D((eps - 1,)), D((eps - 1,)), D((reps - 1,)), D((reps - 1,)),
        ],
        compiler_params=pltpu.CompilerParams(collective_id=cid, has_side_effects=True, vmem_limit_bytes=60 * 2**20),
    )(part, qkv_term, out_term, tokens, after_cot, gain_in, gains, router)


def join_kernel(count, *refs):
    z = lax.axis_index("rep")
    cols = refs[0].shape[2]
    for n in range(2):
        ins, out = refs[n * count:(n + 1) * count], refs[2 * count + n]
        for k in range(count):
            place = pl.multiple_of((z + count - k) % count * cols, cols)
            out[:, :, pl.ds(place, cols)] = ins[k][...].astype(out.dtype)


def join_columns(first, second):
    count = len(first)
    exp_dev, rows, cols = first[0].shape
    whole = jax.ShapeDtypeStruct((exp_dev, rows, cols * count), jnp.float32)
    piece = pl.BlockSpec((1, rows // 2, cols), lambda j, i: (j, i, 0))
    return pl.pallas_call(
        partial(join_kernel, count),
        grid=(exp_dev, 2),
        out_shape=(whole, whole),
        in_specs=[piece] * (2 * count),
        out_specs=[pl.BlockSpec((1, rows // 2, cols * count), lambda j, i: (j, i, 0))] * 2,
    )(*first, *second)


def front_kernel(reps, eps, lengths_ref, tok_ref, cot_ref, wq_ref, wk_ref, wv_ref, wo_ref, gains_ref, router_ref, nums_ref, freq_ref,
                 cots_ref, router_all_ref, nums_all_ref, gsum_ref, normed_ref, pre_ref, qkv_ref, mixed_ref, wqkv_ref, wout_ref, turn_ref, attn_ref,
                 toks, normed, wraw, stage, wqkv, wz, wout, proj, qkv, mixed, turn, segs, part, sib_in, relay_in, xin, yin, acc,
                 gown, gz, gmid, gin, gall, nums, freq,
                 l_sem, o_sem, ws, wr, vs, vr, zs, zr, fs, fr, ts, tr, tcs, tcr, cps, cpr, ccs, ccr,
                 gzs, gzr, gps, gpr, rzs, rzr, rps, rpr, ns, nr, ss, sr, hs, hr, qs, qr, os, orr):
    f32, bf16 = jnp.float32, jnp.bfloat16
    z = lax.axis_index("rep")
    e = lax.axis_index("ep")
    core = e % 2
    chip = e // 2
    sib, chips = partners(e)
    rows, width = tok_ref.shape
    half = rows // 2
    rows_dev = wq_ref.shape[0]
    slice_width = mixed.shape[1]
    head_dim = turn.shape[2]
    heads_dev = slice_width // head_dim
    group_rows = eps * rows

    barrier = pltpu.get_barrier_semaphore()
    for d in range(1, eps):
        pl.semaphore_signal(barrier, inc=1, device_id={"rep": z, "ep": (e + d) % eps}, device_id_type=MESH)
    for d in range(1, reps):
        pl.semaphore_signal(barrier, inc=1, device_id={"rep": (z + d) % reps, "ep": e}, device_id_type=MESH)

    def local(src, dst, sem):
        c = pltpu.make_async_copy(src, dst, sem)
        c.start()
        return c

    raw = [local(r, wraw.at[m], l_sem.at[m]) for m, r in enumerate((wq_ref, wk_ref, wv_ref))]
    tok_own = local(tok_ref, toks.at[e], l_sem.at[3])
    wo_own = local(wo_ref, wz.at[z], l_sem.at[4])
    cot_own = local(cot_ref, cots_ref.at[z, e], l_sem.at[5])
    small = [
        local(gains_ref, gown, l_sem.at[6]),
        local(nums_ref, nums.at[e], l_sem.at[7]),
        local(freq_ref, freq, l_sem.at[8]),
        local(router_ref, router_all_ref.at[e, z], l_sem.at[9]),
    ]
    pl.semaphore_wait(barrier, eps - 1 + reps - 1)

    def remote(src, dst, send, recv, rep, ep):
        return pltpu.make_async_remote_copy(src_ref=src, dst_ref=dst, send_sem=send, recv_sem=recv,
                                            device_id={"rep": rep, "ep": ep}, device_id_type=MESH)

    def below(k, fn):
        @pl.when(z - k >= 0)
        def _():
            fn(z - k)

    def above(k, fn):
        @pl.when(z + k < reps)
        def _():
            fn(z + k)

    class Chain:
        def __init__(self, slot, send, recv):
            self.slot, self.send, self.recv = slot, send, recv

        def copy(self, src, g, up):
            d = 0 if up else 1
            return remote(src, self.slot(g), self.send.at[d, g], self.recv.at[g], z + 1 if up else z - 1, e)

        def begin(self, src):
            @pl.when(z < reps - 1)
            def _():
                self.copy(src, z, True).start()
            @pl.when(z > 0)
            def _():
                self.copy(src, z, False).start()

        def take(self, k, then=None):
            def from_below(g):
                self.copy(self.slot(g), g, True).wait_recv()
                if then is not None:
                    then(g)
            def from_above(g):
                self.copy(self.slot(g), g, False).wait_recv()
                if then is not None:
                    then(g)
            below(k, from_below)
            above(k, from_above)

        def forward(self, k):
            @pl.when((z - k >= 0) & (z < reps - 1))
            def _():
                self.copy(self.slot(z - k), z - k, True).start()
            @pl.when((z + k < reps) & (z > 0))
            def _():
                self.copy(self.slot(z + k), z + k, False).start()

        def arrive(self, k):
            self.take(k)
            self.forward(k)

        def sent(self):
            for g in range(reps):
                @pl.when((z < reps - 1) & (z >= g))
                def _():
                    self.copy(self.slot(g), g, True).wait_send()
                @pl.when((z > 0) & (z <= g))
                def _():
                    self.copy(self.slot(g), g, False).wait_send()

    class Spread:
        def __init__(self, slot, send, recv, csend, crecv):
            self.slot, self.send, self.recv, self.csend, self.crecv = slot, send, recv, csend, crecv

        def near(self, src, j):
            return remote(src, self.slot(e), self.send.at[j], self.recv.at[j], z, chips[j])

        def relay(self, j, source):
            p = self.slot(source).at[pl.ds(half * j, half)]
            return remote(p, p, self.send.at[2 + j], self.recv.at[2 + j], z, chips[1 - j])

        def core(self, src, j):
            return remote(src, self.slot(e if j == 0 else chips[j - 1]), self.csend.at[j], self.crecv.at[j], z, sib)

        def begin(self, src):
            self.near(src, 0).start()
            self.near(src, 1).start()
            self.core(src, 0).start()

        def pass_on(self):
            for j in range(2):
                self.near(self.slot(e), j).wait_recv()
                self.relay(j, chips[j]).start()
                self.core(self.slot(chips[j]), j + 1).start()

        def finish(self):
            for j in range(2):
                self.relay(j, chips[2]).wait_recv()
            self.core(self.slot(chips[2]), 3).start()

        def arrived(self):
            for j in range(4):
                self.core(self.slot(e), j).wait_recv()

        def sent(self):
            for j in range(2):
                self.near(self.slot(e), j).wait_send()
                self.relay(j, chips[j]).wait_send()
            for j in range(4):
                self.core(self.slot(e), j).wait_send()

    tok_spread = Spread(lambda who: toks.at[who], ts, tr, tcs, tcr)

    def cot_spread(g):
        return Spread(lambda who: cots_ref.at[g, who], cps.at[g], cpr.at[g], ccs.at[g], ccr.at[g])

    wo_chain = Chain(lambda g: wz.at[g], ws, wr)
    w_chain = Chain(lambda g: wqkv.at[g], vs, vr)
    cot_chain = Chain(lambda g: cots_ref.at[g, e], zs, zr)

    def cot_take(k):
        cot_chain.take(k, lambda g: cot_spread(g).begin(cots_ref.at[g, e]))

    def each(k, fn):
        below(k, lambda g: fn(cot_spread(g)))
        above(k, lambda g: fn(cot_spread(g)))

    gzc = [remote(gains_ref, gz.at[d - 1], gzs.at[d - 1], gzr.at[d - 1], (z + d) % reps, e) for d in range(1, reps)]
    rzc = [remote(router_ref, router_all_ref.at[e, z], rzs.at[d - 1], rzr.at[d - 1], (z + d) % reps, e) for d in range(1, reps)]
    nc = [remote(nums_ref, nums.at[e], ns.at[d - 1], nr.at[d - 1], z, (e + d) % eps) for d in range(1, eps)]
    for c in (*gzc, *rzc, *nc):
        c.start()
    wo_chain.begin(wo_ref)
    for m in range(3):
        raw[m].wait()
        for who in range(eps):
            for i in range(heads_dev):
                head = ((who % 2) * heads_dev + i) * (eps // 2) + who // 2
                at = m * slice_width + i * head_dim
                stage[who, :, at:at + head_dim] = wraw[m, :, head * head_dim:(head + 1) * head_dim]
    vc = [remote(stage.at[(e + d) % eps], wqkv.at[z, e], fs.at[d - 1], fr.at[d - 1], z, (e + d) % eps) for d in range(1, eps)]
    for c in vc:
        c.start()
    v_own = local(stage.at[e], wqkv.at[z, e], l_sem.at[10])
    tok_spread.begin(tok_ref)
    cot_chain.begin(cot_ref)
    cot_spread(z).begin(cot_ref)
    v_own.wait()
    for c in vc:
        c.wait_recv()
    w_chain.begin(wqkv.at[z])
    wo_chain.arrive(1)

    for c in gzc:
        c.wait_recv()
    small[0].wait()
    t = gown[...].astype(f32)
    for d in range(reps - 1):
        t = t + gz[d].astype(f32)
    gmid[...] = t.astype(bf16)
    gpc = [remote(gmid, gin.at[d - 1], gps.at[d - 1], gpr.at[d - 1], z, (e + d) % eps) for d in range(1, eps)]
    for c in gpc:
        c.start()
    small[3].wait()
    for c in rzc:
        c.wait_recv()
    rpc = [remote(router_all_ref.at[e], router_all_ref.at[e], rps.at[d - 1], rpr.at[d - 1], z, (e + d) % eps) for d in range(1, eps)]
    for c in rpc:
        c.start()
    tok_spread.pass_on()
    tok_spread.finish()
    wo_chain.arrive(2)
    cot_take(1)
    for c in gpc:
        c.wait_recv()
    t = gmid[...].astype(f32)
    for d in range(eps - 1):
        t = t + gin[d].astype(f32)
    gall[...] = t
    outs = [local(gall, gsum_ref, o_sem.at[0])]
    w_chain.arrive(1)
    wo_chain.arrive(3)
    cot_chain.forward(1)

    for c in small[1:3]:
        c.wait()
    for c in nc:
        c.wait_recv()
    outs.append(local(nums, nums_all_ref, o_sem.at[1]))
    deal = nums[:, 0, :]
    segment = jnp.zeros(deal.shape, jnp.int32)
    start = jnp.zeros(deal.shape, jnp.int32)
    end = 0
    for n in range(lengths_ref.shape[1]):
        end = end + lengths_ref[0, n]
        after = (deal >= end).astype(jnp.int32)
        segment = segment + after
        start = start + after * lengths_ref[0, n]
    position = (deal - start).astype(f32)
    segs[...] = segment.astype(f32)
    lane = lax.broadcasted_iota(jnp.int32, (rows, head_dim), 1)
    sign = jnp.where(lane < head_dim // 2, -1.0, 1.0)
    for n in range(eps):
        spot = jnp.broadcast_to(position[n:n + 1, :], (rows, rows)).T
        angle = spot * freq[0:1, :]
        here = pl.ds(n * rows, rows)
        turn[0, here, :] = jnp.cos(angle)
        turn[1, here, :] = jnp.sin(angle) * sign
    outs.append(local(turn, turn_ref, o_sem.at[2]))
    cot_spread(z).pass_on()

    tok_own.wait()
    tok_spread.arrived()
    gain_in = jnp.concatenate([gall[n:n + 1, :] for n in range(width // 128)], axis=1)
    step = 16
    for n in range(eps):
        @pl.loop(0, rows // step)
        def _(i):
            r = pl.ds(pl.multiple_of(i * step, step), step)
            t = toks[n, r, :].astype(f32)
            scale = lax.rsqrt(jnp.mean(t * t, axis=-1, keepdims=True) + norm_eps)
            normed[n, r, :] = (t * scale * gain_in).astype(bf16)
    outs.append(local(normed, normed_ref, o_sem.at[3]))
    w_chain.arrive(2)
    cot_take(2)
    cot_chain.forward(2)
    cot_spread(z).finish()

    wo_own.wait()
    wc = [remote(wz.at[(1 - core) * heads_dev + i], wout.at[i, core], os.at[i], orr.at[i], z, sib) for i in range(heads_dev)]
    wl = [local(wz.at[core * heads_dev + i], wout.at[i, core], l_sem.at[11 + i]) for i in range(heads_dev)]
    for c in wc:
        c.start()
    w_chain.arrive(3)
    each(1, lambda s: s.pass_on())


    @pl.loop(0, eps)
    def _(n):
        here = pl.ds(pl.multiple_of(n * rows, rows), rows)
        proj[here, :] = jnp.dot(normed[n], wqkv[...].reshape(width, 3 * slice_width), preferred_element_type=f32)
        for h in range(2 * heads_dev):
            cut = slice(h * head_dim, (h + 1) * head_dim)
            t = proj[here, cut]
            row = 2 * width // 128 + (0 if h < heads_dev else 1)
            t = t * lax.rsqrt(jnp.mean(t * t, axis=-1, keepdims=True) + norm_eps) * gall[row:row + 1, :]
            t = t * turn[0, here, :] + pltpu.roll(t, head_dim // 2, 1) * turn[1, here, :]
            qkv[here, cut] = t.astype(bf16)
        tail = slice(2 * slice_width, 3 * slice_width)
        qkv[here, tail] = proj[here, tail].astype(bf16)

    outs.append(local(proj.at[:, pl.ds(0, 2 * slice_width)], pre_ref, o_sem.at[4]))
    outs.append(local(qkv, qkv_ref, o_sem.at[5]))
    outs.append(local(wqkv, wqkv_ref, o_sem.at[6]))

    seg_row = jnp.concatenate([segs[n:n + 1, :] for n in range(eps)], axis=1)
    block = 2 * rows

    def attend(h):
        cut = slice(h * head_dim, (h + 1) * head_dim)
        kcut = slice(slice_width + h * head_dim, slice_width + (h + 1) * head_dim)
        vcut = slice(2 * slice_width + h * head_dim, 2 * slice_width + (h + 1) * head_dim)
        for n in range(eps // 2):
            here = pl.ds(n * block, block)
            s = lax.dot_general(qkv[here, cut], qkv[:, kcut], NT, preferred_element_type=f32) * (head_dim ** -0.5)
            seg_col = jnp.concatenate(
                [jnp.broadcast_to(segs[2 * n + j:2 * n + j + 1, :], (rows, rows)).T[:, 0:1] for j in range(2)], axis=0)
            s = jnp.where(seg_col == seg_row, s, masked_score)
            p = jnp.exp(s - jnp.max(s, axis=-1, keepdims=True))
            p = (p / jnp.sum(p, axis=-1, keepdims=True)).astype(bf16)
            mixed[here, cut] = jnp.dot(p, qkv[:, vcut], preferred_element_type=f32).astype(bf16)

    each(1, lambda s: s.finish())
    attend(0)
    each(2, lambda s: s.pass_on())
    for h in range(1, heads_dev):
        attend(h)
    outs.append(local(mixed, mixed_ref, o_sem.at[7]))
    for c in wl:
        c.wait()
    for c in wc:
        c.wait_recv()
    outs.append(local(wout, wout_ref, o_sem.at[8]))

    order = (chips[2] // 2, chips[0] // 2, chips[1] // 2, chip)
    scopies = [remote(part.at[q, 1 - core], sib_in.at[q], ss.at[n], sr.at[n], z, sib) for n, q in enumerate(order)]
    for n in range(eps // 2):
        q = order[n]
        here = pl.ds(pl.multiple_of(q * block, block), block)
        t = jnp.dot(mixed[here, :], wout[...].reshape(slice_width, width), preferred_element_type=f32)
        part[q] = t.astype(bf16).reshape(2, rows, width)
        scopies[n].start()

    cot_take(3)

    def add(out, terms, count):
        @pl.loop(0, count // step)
        def _(i):
            r = pl.ds(pl.multiple_of(i * step, step), step)
            t = terms[0][r, :].astype(f32)
            for other in terms[1:]:
                t = t + other[r, :].astype(f32)
            out[r, :] = t.astype(out.dtype)

    lower, upper = pl.ds(0, half), pl.ds(half, half)
    first = part.at[order[0], core]
    hcopies = [remote(first.at[(lower, upper)[j]], relay_in.at[j], hs.at[j], hr.at[j], z, chips[j]) for j in range(2)]
    qcopies = [remote(part.at[order[1 + j], core], (xin, yin)[j], qs.at[j], qr.at[j], z, chips[j]) for j in range(2)]
    scopies[0].wait_recv()
    add(first, (first, sib_in.at[order[0]]), rows)
    for c in hcopies:
        c.start()
    for j in range(2):
        mine, other = part.at[order[1 + j], core], sib_in.at[order[1 + j]]
        scopies[1 + j].wait_recv()
        direct, through = ((lower, upper), (upper, lower))[j]
        add(mine.at[direct], (mine.at[direct], other.at[direct]), half)
        hcopies[1 - j].wait_recv()
        add(mine.at[through], (mine.at[through], other.at[through], relay_in.at[1 - j]), half)
        qcopies[j].start()
    scopies[3].wait_recv()
    each(3, lambda s: s.pass_on())
    each(2, lambda s: s.finish())
    for c in qcopies:
        c.wait_recv()
    add(acc, (part.at[chip, core], sib_in.at[chip], xin, yin, toks.at[e]), rows)
    outs.append(local(acc, attn_ref, o_sem.at[9]))
    each(3, lambda s: s.finish())
    cot_own.wait()
    for g in range(reps):
        cot_spread(g).arrived()
        cot_spread(g).sent()
    for chain in (wo_chain, w_chain, cot_chain):
        chain.sent()
    tok_spread.sent()
    for c in rpc:
        c.wait_recv()
    for c in (*gzc, *rzc, *nc, *vc, *gpc, *rpc, *wc, *scopies, *hcopies, *qcopies):
        c.wait_send()
    for c in outs:
        c.wait()


def front(lengths, tokens, cot, wq, wk, wv, wo, gains, router, nums, freq, heads_dev, reps, eps, cid):
    rows, width = tokens.shape
    rows_dev = wq.shape[0]
    f32, bf16, i32 = jnp.float32, jnp.bfloat16, jnp.int32
    head_dim = freq.shape[1]
    sw = heads_dev * head_dim
    gr = eps * rows
    half = rows // 2
    q = eps // 2
    S, V, D = jax.ShapeDtypeStruct, pltpu.VMEM, pltpu.SemaphoreType.DMA
    outs = (
        S((reps, eps, rows, width), bf16), S((eps, reps, *router.shape), bf16), S((eps, *nums.shape), i32), S(gains.shape, f32),
        S((eps, rows, width), bf16), S((gr, 2 * sw), f32), S((gr, 3 * sw), bf16), S((gr, sw), bf16),
        S((reps, eps, rows_dev, 3 * sw), bf16), S((heads_dev, 2, rows_dev, width), bf16), S((2, gr, head_dim), f32), S((rows, width), f32),
    )
    return pl.pallas_call(
        partial(front_kernel, reps, eps),
        out_shape=outs,
        in_specs=[pl.BlockSpec(memory_space=pltpu.SMEM)] + [pl.BlockSpec(memory_space=pl.ANY)] * 10,
        out_specs=[pl.BlockSpec(memory_space=pl.ANY)] * len(outs),
        scratch_shapes=[
            V((eps, rows, width), bf16), V((eps, rows, width), bf16), V((3, rows_dev, width), bf16), V((eps, rows_dev, 3 * sw), bf16),
            V((reps, eps, rows_dev, 3 * sw), bf16), V((reps, rows_dev, width), bf16), V((heads_dev, 2, rows_dev, width), bf16),
            V((gr, 3 * sw), f32), V((gr, 3 * sw), bf16), V((gr, sw), bf16), V((2, gr, head_dim), f32), V((eps, rows), f32),
            V((q, 2, rows, width), bf16), V((q, rows, width), bf16), V((2, half, width), bf16), V((rows, width), bf16), V((rows, width), bf16),
            V((rows, width), f32),
            V(gains.shape, bf16), V((reps - 1, *gains.shape), bf16), V(gains.shape, bf16), V((eps - 1, *gains.shape), bf16), V(gains.shape, f32),
            V((eps, *nums.shape), i32), V(freq.shape, f32),
            D((16,)), D((16,)), D((2, reps)), D((reps,)), D((2, reps)), D((reps,)), D((2, reps)), D((reps,)), D((eps - 1,)), D((eps - 1,)),
            D((4,)), D((4,)), D((4,)), D((4,)), D((reps, 4)), D((reps, 4)), D((reps, 4)), D((reps, 4)),
            D((reps - 1,)), D((reps - 1,)), D((eps - 1,)), D((eps - 1,)), D((reps - 1,)), D((reps - 1,)), D((eps - 1,)), D((eps - 1,)),
            D((eps - 1,)), D((eps - 1,)), D((4,)), D((4,)), D((2,)), D((2,)), D((2,)), D((2,)), D((2,)), D((2,)),
        ],
        compiler_params=pltpu.CompilerParams(collective_id=cid, has_side_effects=True, vmem_limit_bytes=56 * 2**20),
    )(lengths, tokens, cot, wq, wk, wv, wo, gains, router, nums, freq)


def on_device_split(
    tokens,
    cotangent,
    query_weight,
    key_weight,
    value_weight,
    output_weight,
    router_weight,
    gains,
    expert_gate,
    expert_up,
    expert_down,
    lengths,
    deal,
    routes,
    priority,
):
    bf16, f32 = jnp.bfloat16, jnp.float32
    tok_dev, width = tokens.shape
    ep_count, rep_count = lax.axis_size("ep"), lax.axis_size("rep")
    ep_index, rep_index = lax.axis_index("ep"), lax.axis_index("rep")
    exp_dev, _, ff_width = expert_gate.shape
    top_count = routes.shape[1]
    experts_all = exp_dev * ep_count
    group_rows = tok_dev * ep_count
    capacity = 5 * tok_dev * top_count // (4 * exp_dev)
    head_dim = HD
    heads_dev = width // head_dim // ep_count
    slice_width = heads_dev * head_dim
    rows_dev = query_weight.shape[0]

    gains_dev = gains.shape[0]
    gain_rows = -(-gains_dev * rep_count * ep_count // 2048) * 16
    gains_placed = lax.dynamic_update_slice_in_dim(
        jnp.zeros((gain_rows * 128,), bf16),
        gains,
        (rep_index * ep_count + ep_index) * gains_dev,
        axis=0,
    ).reshape(gain_rows, 128)
    router_rows = router_weight.size // 128
    router_placed = jnp.pad(router_weight.reshape(router_rows, 128), ((0, -router_rows % 16), (0, 0)))
    numbers = jnp.concatenate([deal[None], priority[None], routes.T])
    numbers = jnp.pad(numbers, ((0, -numbers.shape[0] % 8), (0, 0)))
    frequency = rope_base ** (
        -2.0 * jnp.arange(head_dim // 2, dtype=jnp.float32) / head_dim
    )
    (
        cot_all,
        router_all,
        numbers_all,
        gains_all,
        normed_group,
        pre,
        qkv_low,
        mixed_low,
        qkv_slice,
        out_slice,
        turn,
        after_attn,
    ) = front(
        lengths,
        tokens,
        cotangent,
        query_weight,
        key_weight,
        value_weight,
        output_weight,
        gains_placed,
        router_placed,
        numbers,
        jnp.concatenate([frequency, frequency]).reshape(1, head_dim),
        heads_dev,
        rep_count,
        ep_count,
        0,
    )
    gains_float = gains_all.reshape(-1)
    gain_in = gains_float[:width]
    gain_mid = gains_float[width : 2 * width]
    router_full = (
        router_all[:, :, :router_rows].transpose(1, 0, 2, 3).reshape(width, experts_all)
    )
    deal_all = numbers_all[:, 0].reshape(-1)
    priority_all = numbers_all[:, 1].reshape(-1)
    routes_all = numbers_all[:, 2 : 2 + top_count].transpose(0, 2, 1).reshape(group_rows, top_count)
    segment_all, _ = placement(deal_all, lengths[0])
    normed_group = normed_group.reshape(group_rows, width)
    qkv_slice = qkv_slice.reshape(width, 3 * slice_width)
    mid_low = rms_scale(after_attn, gain_mid).astype(bf16)

    logits = jnp.dot(mid_low, router_full, preferred_element_type=f32)
    expert_ids = jnp.arange(experts_all, dtype=jnp.int32)
    member = (routes[:, :, None] == expert_ids[None, None, :]).astype(f32)
    named = jnp.sum(member, axis=1)
    lifted = jnp.where(named > 0, logits, masked_score)
    lifted = jnp.exp(lifted - jnp.max(lifted, axis=-1, keepdims=True)) * named
    gate_dense = lifted / jnp.sum(lifted, axis=-1, keepdims=True)
    onehot_all = jnp.sum(
        (routes_all[:, :, None] == expert_ids[None, None, :]).astype(bf16), axis=1
    )
    earlier = (priority_all[None, :] < priority[:, None]).astype(bf16)
    slots = jnp.dot(earlier, onehot_all, preferred_element_type=f32)
    kept_dense = named * (slots < capacity).astype(f32)
    pair_weight = gate_dense * kept_dense

    weight_high = pair_weight.astype(bf16)
    weight_low = (pair_weight - weight_high.astype(f32)).astype(bf16)
    side = jnp.concatenate(
        [weight_high, weight_low, jnp.zeros((tok_dev, 128 - 2 * experts_all), bf16)], axis=1
    )
    row_sum, moe_sum, gate_term, up_term, down_w_grad = moe(
        jnp.concatenate([mid_low, side], axis=1),
        cot_all,
        expert_gate,
        expert_up,
        expert_down,
        experts_all,
        3,
    )
    moe_out = moe_sum.astype(f32)
    block_out = (after_attn + moe_out).astype(bf16)

    def rows_of(parts):
        pieces = [parts[0]]
        for k in range(1, rep_count):
            pieces.append(
                lax.ppermute(parts[k], "rep", [(i, (i + k) % rep_count) for i in range(rep_count)])
            )
        return pieces

    gate_pieces, up_pieces = rows_of(gate_term), rows_of(up_term)

    out_grad = cotangent.astype(f32)
    gate_cot = row_sum[:, width : width + experts_all].astype(f32) * kept_dense
    chosen_cot = gate_dense * (gate_cot - jnp.sum(gate_dense * gate_cot, axis=-1, keepdims=True))
    logit_cot = chosen_cot.astype(bf16)
    mid_cot = row_sum[:, :width].astype(f32) + jnp.dot(
        logit_cot, router_full.T, preferred_element_type=f32
    )
    router_term = jnp.dot(mid_low.T, logit_cot, preferred_element_type=f32)
    _, mid_pull = jax.vjp(rms_scale, after_attn, gain_mid)
    after_extra, gain_mid_cot = mid_pull(mid_cot)
    after_cot = out_grad + after_extra
    normed_part, qkv_term, output_term, head_gains = attention_back(
        after_cot.astype(bf16),
        out_slice,
        mixed_low,
        qkv_low,
        pre,
        turn,
        segment_all.astype(f32).reshape(ep_count, tok_dev),
        gains_all,
        normed_group,
        qkv_slice,
        rep_count,
        ep_count,
        1,
    )
    gains_term = jnp.concatenate(
        [
            jnp.zeros((width,), f32),
            gain_mid_cot,
            head_gains[:2].reshape(-1),
            jnp.zeros((6 * width - 2 * head_dim,), f32),
        ]
    ).reshape(8, width)
    router_parts = jnp.pad(
        router_term.reshape(rep_count, ep_count, router_rows, 128),
        ((0, 0), (0, 0), (0, -router_rows % 8), (0, 0)),
    )
    input_grad, query_sum, key_sum, value_sum, output_sum, gains_all, router_own = last_sums(
        normed_part,
        qkv_term,
        output_term,
        tokens,
        after_cot,
        gain_in.reshape(1, width),
        gains_term,
        router_parts,
        rows_dev,
        rep_count,
        ep_count,
        4,
    )
    gains_sum = lax.dynamic_slice_in_dim(
        gains_all.reshape(-1), (rep_index * ep_count + ep_index) * gains_dev, gains_dev
    )
    router_sum = router_own[:router_rows].reshape(rows_dev, experts_all)
    gate_w_grad, up_w_grad = join_columns(gate_pieces, up_pieces)
    return (
        block_out,
        input_grad,
        query_sum,
        key_sum,
        value_sum,
        output_sum,
        router_sum,
        gains_sum,
        gate_w_grad,
        up_w_grad,
        down_w_grad,
    )


def solution(mesh):
    placed = (
        P(("rep", "ep"), None),
        P(("rep", "ep"), None),
        P(("rep", "ep"), None),
        P(("rep", "ep"), None),
        P(("rep", "ep"), None),
        P(("rep", "ep"), None),
        P(("rep", "ep"), None),
        P(("rep", "ep")),
        P("ep", None, None),
        P("ep", None, None),
        P("ep", None, None),
        P("rep", None),
        P(("rep", "ep")),
        P(("rep", "ep"), None),
        P(("rep", "ep")),
    )
    return jax.shard_map(
        on_device_split if mesh.shape["rep"] == 4 else on_device_general,
        mesh=mesh,
        in_specs=placed,
        out_specs=(
            P(("rep", "ep"), None),
            P(("rep", "ep"), None),
            P(("rep", "ep"), None),
            P(("rep", "ep"), None),
            P(("rep", "ep"), None),
            P(("rep", "ep"), None),
            P(("rep", "ep"), None),
            P(("rep", "ep")),
            P("ep", "rep", None),
            P("ep", "rep", None),
            P("ep", "rep", None),
        ),
        check_vma=False,
    )
```

```python
from functools import partial

import jax
import jax.numpy as jnp
from jax import lax
from jax.experimental import pallas as pl
from jax.experimental.pallas import tpu as pltpu
from jax.sharding import PartitionSpec as P

HD = 128


norm_eps = 1e-06
rope_base = 10000.0
masked_score = -1e30
highest = lax.Precision.HIGHEST


def rms_scale(values, gain_vec):
    return (
        values * lax.rsqrt(jnp.mean(values * values, axis=-1, keepdims=True) + norm_eps) * gain_vec
    )


def rotate(values, positions):
    half_width = values.shape[-1] // 2
    frequency = rope_base ** (-2.0 * jnp.arange(half_width, dtype=jnp.float32) / values.shape[-1])
    angles = positions.astype(jnp.float32)[:, None] * frequency[None, :]
    cosine = jnp.cos(angles)[:, None, :]
    sine_part = jnp.sin(angles)[:, None, :]
    low_half = values[..., :half_width]
    high_half = values[..., half_width:]
    return jnp.concatenate(
        [low_half * cosine - high_half * sine_part, high_half * cosine + low_half * sine_part],
        axis=-1,
    )


def placement(deal_rows, lengths_row):
    seq_ends = jnp.cumsum(lengths_row)
    is_after = (seq_ends[None, :] <= deal_rows[:, None]).astype(jnp.int32)
    segment = jnp.sum(is_after, axis=1)
    seq_start = jnp.sum(is_after * lengths_row[None, :], axis=1)
    return (segment, deal_rows - seq_start)


def rope_norm(projected, gain_vec, positions):
    return rotate(rms_scale(projected, gain_vec), positions)


def attend_forward(parts, same_seq, score_scale):
    head_query, head_key, head_value = parts
    scores = (
        jnp.einsum("thd,shd->hts", head_query, head_key, preferred_element_type=jnp.float32)
        * score_scale
    )
    scores = jnp.where(same_seq[None], scores, masked_score)
    top_score = jnp.max(scores, axis=-1, keepdims=True)
    lifted = jnp.exp(scores - top_score)
    total_sum = jnp.sum(lifted, axis=-1, keepdims=True)
    prob_low = (lifted / total_sum).astype(jnp.bfloat16)
    mixed_out = jnp.einsum("hts,shd->thd", prob_low, head_value, preferred_element_type=jnp.float32)
    return (mixed_out, top_score, total_sum)


def attend_backward(parts, same_seq, score_scale):
    head_query, head_key, head_value, head_grad, top_score, total_sum = parts
    scores = (
        jnp.einsum("thd,shd->hts", head_query, head_key, preferred_element_type=jnp.float32)
        * score_scale
    )
    scores = jnp.where(same_seq[None], scores, masked_score)
    prob_full = jnp.exp(scores - top_score) / total_sum
    prob_low = prob_full.astype(jnp.bfloat16)
    prob_grad = jnp.einsum(
        "thd,shd->hts", head_grad, head_value, preferred_element_type=jnp.float32
    )
    row_dot = jnp.sum(prob_full * prob_grad, axis=-1, keepdims=True)
    score_grad = (prob_full * (prob_grad - row_dot)).astype(jnp.bfloat16)
    query_grad = (
        jnp.einsum("hts,shd->thd", score_grad, head_key, preferred_element_type=jnp.float32)
        * score_scale
    )
    key_grad = (
        jnp.einsum("hts,thd->shd", score_grad, head_query, preferred_element_type=jnp.float32)
        * score_scale
    )
    value_grad = jnp.einsum("hts,thd->shd", prob_low, head_grad, preferred_element_type=jnp.float32)
    return (query_grad, key_grad, value_grad)


def on_device_general(
    tokens,
    cotangent,
    query_weight,
    key_weight,
    value_weight,
    output_weight,
    router_weight,
    gains,
    expert_gate,
    expert_up,
    expert_down,
    lengths,
    deal,
    routes,
    priority,
):
    tok_dev, width = tokens.shape
    ep_count = lax.axis_size("ep")
    ep_index = lax.axis_index("ep")
    exp_dev = expert_gate.shape[0]
    top_count = routes.shape[1]
    experts_all = exp_dev * ep_count
    group_rows = tok_dev * ep_count
    send_most = min(tok_dev, 3 * tok_dev * top_count // (2 * experts_all))
    capacity = 5 * tok_dev * top_count // (4 * exp_dev)
    head_dim = HD
    head_count = width // head_dim
    per_group = min(head_count, 4)
    group_count = head_count // per_group
    score_scale = head_dim ** (-0.5)
    query_full, key_full, value_full, output_full, router_full, gains_full = (
        lax.all_gather(query_weight, ("rep", "ep"), axis=0, tiled=True),
        lax.all_gather(key_weight, ("rep", "ep"), axis=0, tiled=True),
        lax.all_gather(value_weight, ("rep", "ep"), axis=0, tiled=True),
        lax.all_gather(output_weight, ("rep", "ep"), axis=0, tiled=True),
        lax.all_gather(router_weight, ("rep", "ep"), axis=0, tiled=True),
        lax.all_gather(gains, ("rep", "ep"), axis=0, tiled=True),
    )
    gains_float = gains_full.astype(jnp.float32)
    gain_in = gains_float[:width]
    gain_mid = gains_float[width : 2 * width]
    gain_query = gains_float[2 * width : 2 * width + head_dim]
    gain_key = gains_float[2 * width + head_dim :]
    deal_all, priority_all, routes_all = (
        lax.all_gather(deal, "ep", axis=0, tiled=True),
        lax.all_gather(priority, "ep", axis=0, tiled=True),
        lax.all_gather(routes, "ep", axis=0, tiled=True),
    )
    segment_all, position_all = placement(deal_all, lengths[0])
    segment_own = lax.dynamic_slice_in_dim(segment_all, ep_index * tok_dev, tok_dev)
    position_own = lax.dynamic_slice_in_dim(position_all, ep_index * tok_dev, tok_dev)
    residual = tokens.astype(jnp.float32)
    normed_low = rms_scale(residual, gain_in).astype(jnp.bfloat16)
    query_pre = jnp.dot(normed_low, query_full, preferred_element_type=jnp.float32).reshape(
        tok_dev, head_count, head_dim
    )
    key_pre = jnp.dot(normed_low, key_full, preferred_element_type=jnp.float32).reshape(
        tok_dev, head_count, head_dim
    )
    value_low = jnp.dot(normed_low, value_full, preferred_element_type=jnp.float32).astype(
        jnp.bfloat16
    )
    query_low = rope_norm(query_pre, gain_query, position_own).astype(jnp.bfloat16)
    key_low = (
        rope_norm(key_pre, gain_key, position_own).astype(jnp.bfloat16).reshape(tok_dev, width)
    )
    key_group, value_group = (
        lax.all_gather(key_low, "ep", axis=0, tiled=True),
        lax.all_gather(value_low, "ep", axis=0, tiled=True),
    )
    same_seq = segment_own[:, None] == segment_all[None, :]
    query_heads = query_low.reshape(tok_dev, group_count, per_group, head_dim).transpose(1, 0, 2, 3)
    key_heads = key_group.reshape(group_rows, group_count, per_group, head_dim).transpose(
        1, 0, 2, 3
    )
    value_heads = value_group.reshape(group_rows, group_count, per_group, head_dim).transpose(
        1, 0, 2, 3
    )
    mixed_heads, top_heads, total_heads = lax.map(
        partial(attend_forward, same_seq=same_seq, score_scale=score_scale),
        (query_heads, key_heads, value_heads),
    )
    mixed_low = mixed_heads.transpose(1, 0, 2, 3).reshape(tok_dev, width).astype(jnp.bfloat16)
    after_attn = residual + jnp.dot(mixed_low, output_full, preferred_element_type=jnp.float32)
    mid_low = rms_scale(after_attn, gain_mid).astype(jnp.bfloat16)
    logits = jnp.dot(mid_low, router_full, preferred_element_type=jnp.float32)
    chosen = jnp.take_along_axis(logits, routes, axis=1)
    gate_prob = jax.nn.softmax(chosen, axis=-1)
    expert_ids = jnp.arange(experts_all, dtype=jnp.int32)
    onehot_all = jnp.sum(
        (routes_all[:, :, None] == expert_ids[None, None, :]).astype(jnp.float32), axis=1
    )
    earlier = (priority_all[None, :] < priority_all[:, None]).astype(jnp.float32)
    slot_all = jnp.take_along_axis(
        jnp.dot(earlier, onehot_all, precision=highest), routes_all, axis=1
    ).astype(jnp.int32)
    row_ids = jnp.arange(tok_dev, dtype=jnp.int32)
    lower_tri = (row_ids[:, None] > row_ids[None, :]).astype(jnp.float32)
    before = jnp.einsum(
        "ij,dje->die",
        lower_tri,
        onehot_all.reshape(ep_count, tok_dev, experts_all),
        precision=highest,
    ).reshape(group_rows, experts_all)
    place_all = jnp.take_along_axis(before, routes_all, axis=1).astype(jnp.int32)
    kept_all = slot_all < capacity
    kept_own = lax.dynamic_slice_in_dim(kept_all, ep_index * tok_dev, tok_dev)
    place_own = lax.dynamic_slice_in_dim(place_all, ep_index * tok_dev, tok_dev)
    buffer_index = (routes * send_most + place_own).reshape(-1)
    rows_out = jnp.where(
        kept_own[:, :, None], mid_low[:, None, :], jnp.zeros((), jnp.bfloat16)
    ).reshape(tok_dev * top_count, width)
    send_rows = (
        jnp.zeros((experts_all * send_most, width), jnp.bfloat16)
        .at[buffer_index]
        .set(rows_out)
        .reshape(experts_all, send_most, width)
    )
    received = lax.all_to_all(send_rows, "ep", split_axis=0, concat_axis=1, tiled=True)
    gate_part = jnp.einsum(
        "erd,edf->erf", received, expert_gate, preferred_element_type=jnp.float32
    )
    up_part = jnp.einsum("erd,edf->erf", received, expert_up, preferred_element_type=jnp.float32)
    hidden = (jax.nn.silu(gate_part) * up_part).astype(jnp.bfloat16)
    result = jnp.einsum(
        "erf,efd->erd", hidden, expert_down, preferred_element_type=jnp.float32
    ).astype(jnp.bfloat16)
    returned = lax.all_to_all(result, "ep", split_axis=1, concat_axis=0, tiled=True)
    pair_out = returned.reshape(experts_all * send_most, width)[buffer_index].reshape(
        tok_dev, top_count, width
    )
    pair_weight = gate_prob * kept_own.astype(jnp.float32)
    moe_out = jnp.einsum("tk,tkd->td", pair_weight, pair_out, preferred_element_type=jnp.float32)
    block_out = (after_attn + moe_out).astype(jnp.bfloat16)
    out_grad = cotangent.astype(jnp.float32)
    pair_gate_grad = kept_own.astype(jnp.float32) * jnp.einsum(
        "tkd,td->tk", pair_out, out_grad, preferred_element_type=jnp.float32
    )
    pair_grad = (
        (pair_weight[:, :, None] * out_grad[:, None, :])
        .astype(jnp.bfloat16)
        .reshape(tok_dev * top_count, width)
    )
    grad_send = (
        jnp.zeros((experts_all * send_most, width), jnp.bfloat16)
        .at[buffer_index]
        .set(pair_grad)
        .reshape(experts_all, send_most, width)
    )
    grad_received = lax.all_to_all(grad_send, "ep", split_axis=0, concat_axis=1, tiled=True)
    hidden_grad = jnp.einsum(
        "erd,efd->erf", grad_received, expert_down, preferred_element_type=jnp.float32
    )
    _, silu_pull = jax.vjp(lambda gate_in, up_in: jax.nn.silu(gate_in) * up_in, gate_part, up_part)
    gate_part_grad, up_part_grad = silu_pull(hidden_grad)
    gate_low_grad = gate_part_grad.astype(jnp.bfloat16)
    up_low_grad = up_part_grad.astype(jnp.bfloat16)
    down_term = jnp.einsum(
        "erf,erd->efd", hidden, grad_received, preferred_element_type=jnp.float32
    )
    gate_term = jnp.einsum(
        "erd,erf->edf", received, gate_low_grad, preferred_element_type=jnp.float32
    )
    up_term = jnp.einsum("erd,erf->edf", received, up_low_grad, preferred_element_type=jnp.float32)
    rows_grad = (
        jnp.einsum("erf,edf->erd", gate_low_grad, expert_gate, preferred_element_type=jnp.float32)
        + jnp.einsum("erf,edf->erd", up_low_grad, expert_up, preferred_element_type=jnp.float32)
    ).astype(jnp.bfloat16)
    back_rows = lax.all_to_all(rows_grad, "ep", split_axis=1, concat_axis=0, tiled=True)
    mid_grad = jnp.sum(
        back_rows.reshape(experts_all * send_most, width)[buffer_index]
        .reshape(tok_dev, top_count, width)
        .astype(jnp.float32),
        axis=1,
    )
    gate_w_grad, up_w_grad, down_w_grad = (
        lax.psum_scatter(
            gate_term.astype(jnp.bfloat16), "rep", scatter_dimension=1, tiled=True
        ).astype(jnp.float32),
        lax.psum_scatter(
            up_term.astype(jnp.bfloat16), "rep", scatter_dimension=1, tiled=True
        ).astype(jnp.float32),
        lax.psum_scatter(
            down_term.astype(jnp.bfloat16), "rep", scatter_dimension=1, tiled=True
        ).astype(jnp.float32),
    )
    _, soft_pull = jax.vjp(lambda values: jax.nn.softmax(values, axis=-1), chosen)
    (chosen_grad,) = soft_pull(pair_gate_grad)
    onehot_own = (routes[:, :, None] == expert_ids[None, None, :]).astype(jnp.float32)
    logit_grad = jnp.einsum("tk,tke->te", chosen_grad, onehot_own).astype(jnp.bfloat16)
    mid_grad = mid_grad + jnp.dot(logit_grad, router_full.T, preferred_element_type=jnp.float32)
    router_term = jnp.dot(mid_low.T, logit_grad, preferred_element_type=jnp.float32)
    _, mid_pull = jax.vjp(rms_scale, after_attn, gain_mid)
    after_extra, gain_mid_grad = mid_pull(mid_grad)
    after_grad = out_grad + after_extra
    attn_low_grad = after_grad.astype(jnp.bfloat16)
    output_term = jnp.dot(mixed_low.T, attn_low_grad, preferred_element_type=jnp.float32)
    mixed_grad = jnp.dot(attn_low_grad, output_full.T, preferred_element_type=jnp.float32).astype(
        jnp.bfloat16
    )
    mixed_grad_heads = mixed_grad.reshape(tok_dev, group_count, per_group, head_dim).transpose(
        1, 0, 2, 3
    )
    query_grad_h, key_grad_h, value_grad_h = lax.map(
        partial(attend_backward, same_seq=same_seq, score_scale=score_scale),
        (query_heads, key_heads, value_heads, mixed_grad_heads, top_heads, total_heads),
    )
    query_grad_own = query_grad_h.transpose(1, 0, 2, 3).reshape(tok_dev, head_count, head_dim)
    key_grad_group = key_grad_h.transpose(1, 0, 2, 3).reshape(group_rows, width)
    value_grad_group = value_grad_h.transpose(1, 0, 2, 3).reshape(group_rows, width)
    key_sum, value_sum = (
        lax.psum_scatter(
            key_grad_group.astype(jnp.bfloat16), "ep", scatter_dimension=0, tiled=True
        ).astype(jnp.float32),
        lax.psum_scatter(
            value_grad_group.astype(jnp.bfloat16), "ep", scatter_dimension=0, tiled=True
        ).astype(jnp.float32),
    )
    value_low_grad = value_sum.astype(jnp.bfloat16)
    _, query_pull = jax.vjp(
        lambda projected, gain_vec: rope_norm(projected, gain_vec, position_own),
        query_pre,
        gain_query,
    )
    query_pre_grad, gain_query_grad = query_pull(query_grad_own)
    _, key_pull = jax.vjp(
        lambda projected, gain_vec: rope_norm(projected, gain_vec, position_own), key_pre, gain_key
    )
    key_pre_grad, gain_key_grad = key_pull(key_sum.reshape(tok_dev, head_count, head_dim))
    query_low_grad = query_pre_grad.reshape(tok_dev, width).astype(jnp.bfloat16)
    key_low_grad = key_pre_grad.reshape(tok_dev, width).astype(jnp.bfloat16)
    normed_grad = jnp.dot(query_low_grad, query_full.T, preferred_element_type=jnp.float32)
    normed_grad = normed_grad + jnp.dot(
        key_low_grad, key_full.T, preferred_element_type=jnp.float32
    )
    normed_grad = normed_grad + jnp.dot(
        value_low_grad, value_full.T, preferred_element_type=jnp.float32
    )
    query_term = jnp.dot(normed_low.T, query_low_grad, preferred_element_type=jnp.float32)
    key_term = jnp.dot(normed_low.T, key_low_grad, preferred_element_type=jnp.float32)
    value_term = jnp.dot(normed_low.T, value_low_grad, preferred_element_type=jnp.float32)
    _, input_pull = jax.vjp(rms_scale, residual, gain_in)
    input_extra, gain_in_grad = input_pull(normed_grad)
    input_grad = after_grad + input_extra
    gains_term = jnp.concatenate([gain_in_grad, gain_mid_grad, gain_query_grad, gain_key_grad])
    query_sum, key_total, value_total, output_sum, router_sum, gains_sum = (
        lax.psum_scatter(query_term, ("rep", "ep"), scatter_dimension=0, tiled=True),
        lax.psum_scatter(key_term, ("rep", "ep"), scatter_dimension=0, tiled=True),
        lax.psum_scatter(value_term, ("rep", "ep"), scatter_dimension=0, tiled=True),
        lax.psum_scatter(output_term, ("rep", "ep"), scatter_dimension=0, tiled=True),
        lax.psum_scatter(router_term, ("rep", "ep"), scatter_dimension=0, tiled=True),
        lax.psum_scatter(gains_term, ("rep", "ep"), scatter_dimension=0, tiled=True),
    )
    return (
        block_out,
        input_grad,
        query_sum,
        key_total,
        value_total,
        output_sum,
        router_sum,
        gains_sum,
        gate_w_grad,
        up_w_grad,
        down_w_grad,
    )


MESH = pl.DeviceIdType.MESH


def partners(e):
    sib = e + 1 - 2 * (e % 2)
    xn = e + 2 - 4 * ((e // 2) % 2)
    yn = e + 4 - 8 * ((e // 4) % 2)
    dg = xn + 4 - 8 * ((e // 4) % 2)
    return sib, (xn, yn, dg)


NT = (((1,), (1,)), ((), ()))
TN = (((0,), (0,)), ((), ()))


def visit_order(reps):
    if reps != 4:
        return [sorted((g for g in range(reps) if g != z), key=lambda g: (abs(g - z), g)) + [z] for z in range(reps)]
    return [[2, 3, 1, 0], [2, 3, 0, 1], [1, 0, 3, 2], [1, 0, 2, 3]]


def moe_kernel(reps, side_lanes, experts_all, x_ref, cot_ref, eg_ref, eu_ref, ed_ref,
               row_ref, moe_ref, gout_ref, uout_ref, dout_ref, gin_ref,
               mid_ref, a_ref, b_ref, h_ref, xin_ref, yin_ref, zin_ref,
               wgu, wd, xbuf, cbuf, abuf, pbuf, sib_in, relay_in, sendbuf, ownbuf, rbuf, tmp, colbuf, gst, dst,
               own_sem, w_sem, x_sem, c_sem, ab_sem, t_sem, col_sem, g_sem, o_sem,
               zs, zr, ps, pr, cs, cr, ss, sr, hs, hr, qs, qr, fs, fr, xs, xr):
    f32, bf16 = jnp.float32, jnp.bfloat16
    z = lax.axis_index("rep")
    e = lax.axis_index("ep")
    core = e % 2
    chip = e // 2
    sib, chips = partners(e)
    rows = x_ref.shape[0]
    half = rows // 2
    width = cot_ref.shape[-1]
    W1 = x_ref.shape[1]
    WP = pbuf.shape[-1]
    exp_dev = eg_ref.shape[0]
    F = wgu.shape[2] // exp_dev
    EF = exp_dev * F
    steps = 4 * reps
    table = visit_order(reps)

    def group_of(s):
        g = 0
        for zi in range(reps):
            for si in range(reps):
                g = g + jnp.where((z == zi) & (s == si), table[zi][si], 0)
        return g

    def chip_of(k):
        return jnp.where(k == 0, chips[2] // 2, jnp.where(k == 1, chip, jnp.where(k == 2, chips[0] // 2, chips[1] // 2)))

    barrier = pltpu.get_barrier_semaphore()
    for other in (sib, *chips):
        pl.semaphore_signal(barrier, inc=1, device_id={"rep": z, "ep": other}, device_id_type=MESH)
    for d in range(1, reps):
        pl.semaphore_signal(barrier, inc=1, device_id={"rep": (z + d) % reps, "ep": e}, device_id_type=MESH)
    weights = []
    for j in range(exp_dev):
        cut = pl.ds(pl.multiple_of(z * F, F), F)
        weights.append(pltpu.make_async_copy(eg_ref.at[j, :, cut], wgu.at[0, :, pl.ds(j * F, F)], w_sem.at[j]))
        weights.append(pltpu.make_async_copy(eu_ref.at[j, :, cut], wgu.at[1, :, pl.ds(j * F, F)], w_sem.at[exp_dev + j]))
        weights.append(pltpu.make_async_copy(ed_ref.at[j, cut, :], wd.at[pl.ds(j * F, F), :], w_sem.at[2 * exp_dev + j]))
    for w in weights:
        w.start()
    local = pltpu.make_async_copy(x_ref, mid_ref.at[z, e], own_sem)
    local.start()
    pl.semaphore_wait(barrier, 4 + reps - 1)

    def zcopy(src, g, up):
        d = 0 if up else 1
        return pltpu.make_async_remote_copy(
            src_ref=src, dst_ref=mid_ref.at[g, e], send_sem=zs.at[d, g], recv_sem=zr.at[g],
            device_id={"rep": z + 1 if up else z - 1, "ep": e}, device_id_type=MESH)

    def pcopy(src, g, j):
        return pltpu.make_async_remote_copy(
            src_ref=src, dst_ref=mid_ref.at[g, e], send_sem=ps.at[g, j], recv_sem=pr.at[g, j],
            device_id={"rep": z, "ep": chips[j]}, device_id_type=MESH)

    def relay(g, j, source):
        part = mid_ref.at[g, source, pl.ds(half * j, half)]
        return pltpu.make_async_remote_copy(
            src_ref=part, dst_ref=part, send_sem=ps.at[g, 2 + j], recv_sem=pr.at[g, 2 + j],
            device_id={"rep": z, "ep": chips[1 - j]}, device_id_type=MESH)

    def ccopy(src, g, j):
        who = e if j == 0 else chips[j - 1]
        return pltpu.make_async_remote_copy(
            src_ref=src, dst_ref=mid_ref.at[g, who], send_sem=cs.at[g, j], recv_sem=cr.at[g, j],
            device_id={"rep": z, "ep": sib}, device_id_type=MESH)

    def spread(src, g):
        pcopy(src, g, 0).start()
        pcopy(src, g, 1).start()
        ccopy(src, g, 0).start()

    def pass_on(g):
        for j in range(2):
            pcopy(x_ref, g, j).wait_recv()
            relay(g, j, chips[j]).start()
            ccopy(mid_ref.at[g, chips[j]], g, j + 1).start()

    def finish_in(g):
        for j in range(2):
            relay(g, j, chips[2]).wait_recv()
        ccopy(mid_ref.at[g, chips[2]], g, 3).start()

    def at(k, fn):
        if k == 0:
            fn(z)
            return
        @pl.when(z - k >= 0)
        def _():
            fn(z - k)
        @pl.when(z + k < reps)
        def _():
            fn(z + k)

    def arrive(k):
        @pl.when(z - k >= 0)
        def _():
            g = z - k
            zcopy(x_ref, g, True).wait_recv()
            @pl.when(z < reps - 1)
            def _():
                zcopy(mid_ref.at[g, e], g, True).start()
            spread(mid_ref.at[g, e], g)
        @pl.when(z + k < reps)
        def _():
            g = z + k
            zcopy(x_ref, g, False).wait_recv()
            @pl.when(z > 0)
            def _():
                zcopy(mid_ref.at[g, e], g, False).start()
            spread(mid_ref.at[g, e], g)

    def ready(g):
        for j in range(4):
            ccopy(x_ref, g, j).wait_recv()

    def load_x(i):
        g, q = group_of(i // 4), chip_of(i % 4)
        return pltpu.make_async_copy(mid_ref.at[g, pl.ds(2 * q, 2)], xbuf.at[i % 2], x_sem.at[i % 2])

    def load_c(i):
        g, q = group_of(i // 4), chip_of(i % 4)
        return pltpu.make_async_copy(cot_ref.at[g, pl.ds(2 * q, 2)], cbuf.at[i % 2], c_sem.at[i % 2])

    def keep(i, m):
        g, q = group_of(i // 4), chip_of(i % 4)
        place = pl.ds(pl.multiple_of((g * 4 + q) * 2 * rows, 2 * rows), 2 * rows)
        return pltpu.make_async_copy(abuf.at[i % 2, m], (a_ref, b_ref, h_ref)[m].at[place], ab_sem.at[i % 2, m])

    def compute(i):
        slot = i % 2
        lane = lax.broadcasted_iota(jnp.int32, (2 * rows, side_lanes), 1)
        side = xbuf[slot, :, :, pl.ds(width, side_lanes)].reshape(2 * rows, side_lanes).astype(f32)

        def one(j, cots):
            cols = pl.ds(pl.multiple_of(j * F, F), F)
            x = xbuf[slot, :, :, pl.ds(0, width)].reshape(2 * rows, width)
            c = cbuf[slot].reshape(2 * rows, width)
            index = e * exp_dev + j
            w = jnp.sum(jnp.where((lane == index) | (lane == index + experts_all), side, 0.0), axis=1, keepdims=True)
            ga = jnp.dot(x, wgu[0, :, cols], preferred_element_type=f32)
            up = jnp.dot(x, wgu[1, :, cols], preferred_element_type=f32)
            hc = lax.dot_general(c, wd[cols, :], NT, preferred_element_type=f32)
            sigma = 1.0 / (1.0 + jnp.exp(-ga))
            silu = ga * sigma
            hid = (silu * up).astype(bf16).astype(f32)
            hcw = hc * w
            abuf[slot, 0, :, cols] = (hcw * up * (sigma * (1.0 + ga * (1.0 - sigma)))).astype(bf16)
            abuf[slot, 1, :, cols] = (hcw * silu).astype(bf16)
            abuf[slot, 2, :, cols] = (hid * w).astype(bf16)
            dots = jnp.sum(hid * hc, axis=1, keepdims=True)
            return cots + jnp.where(lane == index, dots, 0.0)

        cots = lax.fori_loop(0, exp_dev, one, jnp.zeros((2 * rows, side_lanes), f32), unroll=True)
        pbuf[slot, :, :, pl.ds(width, side_lanes)] = cots.astype(bf16).reshape(2, rows, side_lanes)
        t = lax.dot_general(abuf[slot, 0], wgu[0], NT, preferred_element_type=f32)
        t = t + lax.dot_general(abuf[slot, 1], wgu[1], NT, preferred_element_type=f32)
        pbuf[slot, :, :, pl.ds(0, width)] = t.astype(bf16).reshape(2, rows, width)
        t = jnp.dot(abuf[slot, 2], wd[...], preferred_element_type=f32)
        pbuf[slot, :, :, pl.ds(W1, width)] = t.astype(bf16).reshape(2, rows, width)

    def sibcopy(i):
        return pltpu.make_async_remote_copy(
            src_ref=pbuf.at[i % 2, 1 - core], dst_ref=sib_in.at[i % 4], send_sem=ss.at[i], recv_sem=sr.at[i],
            device_id={"rep": z, "ep": sib}, device_id_type=MESH)

    def hcopy(s, j):
        part = pl.ds(half * j, half)
        return pltpu.make_async_remote_copy(
            src_ref=sendbuf.at[0, part], dst_ref=relay_in.at[s, j], send_sem=hs.at[s, j], recv_sem=hr.at[s, j],
            device_id={"rep": z, "ep": chips[j]}, device_id_type=MESH)

    def qcopy(s, j):
        return pltpu.make_async_remote_copy(
            src_ref=sendbuf.at[1 + j], dst_ref=(xin_ref, yin_ref)[j].at[s], send_sem=qs.at[s, j], recv_sem=qr.at[s, j],
            device_id={"rep": z, "ep": chips[j]}, device_id_type=MESH)

    def fcopy(s, g):
        return pltpu.make_async_remote_copy(
            src_ref=rbuf.at[s % 2], dst_ref=zin_ref.at[z], send_sem=fs.at[s], recv_sem=fr.at[z],
            device_id={"rep": g, "ep": e}, device_id_type=MESH)

    step = 16

    def add(out, terms, count=rows):
        @pl.loop(0, count // step)
        def _(i):
            r = pl.ds(pl.multiple_of(i * step, step), step)
            t = terms[0][r, :].astype(f32)
            for other in terms[1:]:
                t = t + other[r, :].astype(f32)
            out[r, :] = t.astype(out.dtype)

    def finish(i):
        s, k = i // 4, i % 4
        sibcopy(i).wait_recv()
        mine, other = pbuf.at[i % 2, core], sib_in.at[i % 4]
        lower, upper = pl.ds(0, half), pl.ds(half, half)
        @pl.when(k == 1)
        def _():
            add(ownbuf.at[s % 2], (mine, other))
        @pl.when(k == 0)
        def _():
            @pl.when(s > 0)
            def _():
                hcopy(s - 1, 0).wait_send()
                hcopy(s - 1, 1).wait_send()
            add(sendbuf.at[0], (mine, other))
            hcopy(s, 0).start()
            hcopy(s, 1).start()
        @pl.when(k == 2)
        def _():
            @pl.when(s > 0)
            def _():
                qcopy(s - 1, 0).wait_send()
            add(sendbuf.at[1, lower], (mine.at[lower], other.at[lower]), half)
            hcopy(s, 1).wait_recv()
            add(sendbuf.at[1, upper], (mine.at[upper], other.at[upper], relay_in.at[s, 1]), half)
            qcopy(s, 0).start()
        @pl.when(k == 3)
        def _():
            @pl.when(s > 0)
            def _():
                qcopy(s - 1, 1).wait_send()
            add(sendbuf.at[2, upper], (mine.at[upper], other.at[upper]), half)
            hcopy(s, 0).wait_recv()
            add(sendbuf.at[2, lower], (mine.at[lower], other.at[lower], relay_in.at[s, 0]), half)
            qcopy(s, 1).start()

    def load_t(src, m):
        return pltpu.make_async_copy(src, tmp.at[m], t_sem.at[m])

    def total(s):
        for j in range(2):
            qcopy(s, j).wait_recv()
            load_t((xin_ref, yin_ref)[j].at[s], j).start()
        for j in range(2):
            load_t((xin_ref, yin_ref)[j].at[s], j).wait()

    def plane_sum(s):
        total(s)
        @pl.when(s >= 2)
        def _():
            fcopy(s - 2, group_of(s - 2)).wait_send()
        add(rbuf.at[s % 2], (ownbuf.at[s % 2], tmp.at[0], tmp.at[1]))
        fcopy(s, group_of(s)).start()

    @pl.when(z < reps - 1)
    def _():
        zcopy(x_ref, z, True).start()
    @pl.when(z > 0)
    def _():
        zcopy(x_ref, z, False).start()
    spread(x_ref, z)
    arrive(1)
    pass_on(z)
    arrive(2)
    at(1, pass_on)
    finish_in(z)
    arrive(3)
    at(2, pass_on)
    at(1, finish_in)
    end = (z == 0) | (z == reps - 1)

    @pl.when(end)
    def _():
        at(2, finish_in)
    for w in weights:
        w.wait()
    ready(group_of(0))
    load_x(0).start()
    load_c(0).start()

    @pl.loop(0, steps)
    def _(i):
        load_x(i).wait()
        load_c(i).wait()
        @pl.when(i == 1)
        def _():
            at(3, pass_on)
        @pl.when(i == 3)
        def _():
            at(3, finish_in)

            @pl.when(jnp.logical_not(end))
            def _():
                at(2, finish_in)
        @pl.when(i == steps - 5)
        def _():
            local.wait()
        @pl.when(i < steps - 1)
        def _():
            @pl.when(i % 4 == 3)
            def _():
                ready(group_of(i // 4 + 1))
            load_x(i + 1).start()
            load_c(i + 1).start()
        @pl.when(i >= 2)
        def _():
            sibcopy(i - 2).wait_send()
            for m in range(3):
                keep(i - 2, m).wait()
        compute(i)
        sibcopy(i).start()
        for m in range(3):
            keep(i, m).start()
        @pl.when(i >= 1)
        def _():
            finish(i - 1)
        @pl.when((i % 4 == 3) & (i >= 7) & (i < steps - 1))
        def _():
            plane_sum(i // 4 - 1)

    for i in (steps - 2, steps - 1):
        sibcopy(i).wait_send()
        for m in range(3):
            keep(i, m).wait()
    finish(steps - 1)
    plane_sum(reps - 2)

    blocks = width // 256
    halves = wgu.shape[1]

    def resident(src, m):
        return pltpu.make_async_copy(src.at[pl.ds(m * halves, halves)], wgu.at[m], w_sem.at[m])

    def load_col(src, n):
        return pltpu.make_async_copy(src.at[:, :, :, pl.ds(pl.multiple_of(n * 256, 256), 256)], colbuf.at[n % 2], col_sem.at[n % 2])

    def product(n, m):
        left = colbuf[n % 2, pl.ds(m * (reps // 2), reps // 2)].reshape(halves, 256)
        return left, wgu[m]

    def hand_over(k):
        return pltpu.make_async_remote_copy(
            src_ref=gout_ref.at[k], dst_ref=gin_ref.at[k], send_sem=xs.at[k], recv_sem=xr.at[k],
            device_id={"rep": (z + k) % reps, "ep": e}, device_id_type=MESH)

    per_piece = width // reps // 256

    def piece_done(n):
        k = (n // per_piece + reps - z) % reps
        @pl.when((n % per_piece == per_piece - 1) & (k > 0))
        def _():
            hand_over(k).start()

    def grad_rows(src, out, send):
        def store(n, j):
            per = width // reps
            place = pl.ds(pl.multiple_of((n * 256) % per, 256), 256)
            return pltpu.make_async_copy(gst.at[n % 2, j], out.at[((n * 256) // per + reps - z) % reps, j, place], g_sem.at[n % 2, j])
        for m in range(2):
            resident(src, m).start()
        load_col(mid_ref, 0).start()
        for m in range(2):
            resident(src, m).wait()
        @pl.loop(0, blocks)
        def _(n):
            load_col(mid_ref, n).wait()
            @pl.when(n < blocks - 1)
            def _():
                load_col(mid_ref, n + 1).start()
            @pl.when(n >= 2)
            def _():
                for j in range(exp_dev):
                    store(n - 2, j).wait()
                if send:
                    piece_done(n - 2)
            t = jnp.zeros((256, EF), f32)
            for m in range(2):
                left, right = product(n, m)
                t = t + lax.dot_general(left, right, TN, preferred_element_type=f32)
            for j in range(exp_dev):
                gst[n % 2, j] = t[:, j * F:(j + 1) * F].astype(bf16)
                store(n, j).start()
        for n in (blocks - 2, blocks - 1):
            for j in range(exp_dev):
                store(n, j).wait()
            if send:
                piece_done(n)

    def grad_down():
        def store(n):
            return pltpu.make_async_copy(dst.at[n % 2], dout_ref.at[:, :, pl.ds(pl.multiple_of(n * 256, 256), 256)], g_sem.at[n % 2, 0])
        for m in range(2):
            resident(h_ref, m).start()
        load_col(cot_ref, 0).start()
        for m in range(2):
            resident(h_ref, m).wait()
        @pl.loop(0, blocks)
        def _(n):
            load_col(cot_ref, n).wait()
            @pl.when(n < blocks - 1)
            def _():
                load_col(cot_ref, n + 1).start()
            @pl.when(n >= 2)
            def _():
                store(n - 2).wait()
            t = jnp.zeros((EF, 256), f32)
            for m in range(2):
                left, right = product(n, m)
                t = t + lax.dot_general(right, left, TN, preferred_element_type=f32)
            dst[n % 2] = t.reshape(exp_dev, F, 256).astype(bf16)
            store(n).start()
        for n in (blocks - 2, blocks - 1):
            store(n).wait()

    grad_rows(a_ref, gout_ref, True)
    grad_rows(b_ref, uout_ref, False)
    grad_down()

    last = reps - 1
    total(last)
    for d in range(1, reps):
        src = (z + d) % reps
        pltpu.make_async_remote_copy(
            src_ref=rbuf.at[0], dst_ref=zin_ref.at[src], send_sem=fs.at[last], recv_sem=fr.at[src],
            device_id={"rep": src, "ep": e}, device_id_type=MESH).wait_recv()
        load_t(zin_ref.at[src], 1 + d).start()
    for d in range(1, reps):
        load_t(zin_ref.at[(z + d) % reps], 1 + d).wait()
    fcopy(reps - 3, group_of(reps - 3)).wait_send()
    add(rbuf.at[(reps - 3) % 2], (ownbuf.at[last % 2], *(tmp.at[m] for m in range(reps + 1))))
    outs = (
        pltpu.make_async_copy(rbuf.at[(reps - 3) % 2, :, pl.ds(0, W1)], row_ref, o_sem.at[0]),
        pltpu.make_async_copy(rbuf.at[(reps - 3) % 2, :, pl.ds(W1, width)], moe_ref, o_sem.at[1]),
    )
    for o in outs:
        o.start()
    for o in outs:
        o.wait()
    fcopy(reps - 2, group_of(reps - 2)).wait_send()
    for k in range(1, reps):
        hand_over(k).wait()
    for j in range(2):
        hcopy(last, j).wait_send()
        qcopy(last, j).wait_send()
    for g in range(reps):
        for j in range(4):
            ccopy(x_ref, g, j).wait_send()
        for j in range(2):
            pcopy(x_ref, g, j).wait_send()
            relay(g, j, chips[j]).wait_send()
        @pl.when((z < reps - 1) & (z >= g))
        def _():
            zcopy(x_ref, g, True).wait_send()
        @pl.when((z > 0) & (z <= g))
        def _():
            zcopy(x_ref, g, False).wait_send()


def moe(x, cot_all, eg, eu, ed, experts_all, cid):
    reps, eps, rows, width = cot_all.shape
    W1 = x.shape[1]
    side = W1 - width
    WP = W1 + width
    exp_dev, _, ff = eg.shape
    F = ff // reps
    EF = exp_dev * F
    f32, bf16 = jnp.float32, jnp.bfloat16
    D, V = pltpu.SemaphoreType.DMA, pltpu.VMEM
    S = jax.ShapeDtypeStruct
    tokens = reps * eps * rows
    steps = 4 * reps
    outs = (
        S((rows, W1), bf16), S((rows, width), bf16),
        S((reps, exp_dev, width // reps, F), bf16), S((reps, exp_dev, width // reps, F), bf16), S((exp_dev, F, width), bf16),
        S((reps, exp_dev, width // reps, F), bf16),
        S((reps, eps, rows, W1), bf16), S((tokens, EF), bf16), S((tokens, EF), bf16), S((tokens, EF), bf16),
        S((reps, rows, WP), bf16), S((reps, rows, WP), bf16), S((reps, rows, WP), bf16),
    )
    return pl.pallas_call(
        partial(moe_kernel, reps, side, experts_all),
        out_shape=outs,
        in_specs=[pl.BlockSpec(memory_space=pl.ANY)] * 5,
        out_specs=[pl.BlockSpec(memory_space=pl.ANY)] * len(outs),
        scratch_shapes=[
            V((2, width, EF), bf16), V((EF, width), bf16),
            V((2, 2, rows, W1), bf16), V((2, 2, rows, width), bf16),
            V((2, 3, 2 * rows, EF), bf16), V((2, 2, rows, WP), bf16), V((4, rows, WP), bf16),
            V((reps, 2, rows // 2, WP), bf16), V((3, rows, WP), bf16), V((2, rows, WP), bf16), V((2, rows, WP), bf16),
            V((5, rows, WP), bf16), V((2, reps, eps, rows, 256), bf16),
            V((2, exp_dev, 256, F), bf16), V((2, exp_dev, F, 256), bf16),
            D, D((3 * exp_dev,)), D((2,)), D((2,)), D((2, 3)), D((5,)), D((2,)), D((2, exp_dev)), D((2,)),
            D((2, reps)), D((reps,)), D((reps, 4)), D((reps, 4)), D((reps, 4)), D((reps, 4)),
            D((steps,)), D((steps,)), D((reps, 2)), D((reps, 2)), D((reps, 2)), D((reps, 2)), D((reps,)), D((reps,)), D((reps,)), D((reps,)),
        ],
        compiler_params=pltpu.CompilerParams(collective_id=cid, has_side_effects=True, vmem_limit_bytes=63 * 2**20),
    )(x, cot_all, eg, eu, ed)[:6]


def back_kernel(heads_dev, cot_ref, wout_ref, mixed_ref, qkv_ref, pre_ref, turn_ref, segs_ref, gains_ref, normed_ref, wqkv_ref,
                part_ref, qkv_out, out_out, gain_out,
                cots, wout, mixed, qkv, pre, turn, segs, gains, normed, wqkv, probs, dsc, dmix, dkey, pcot, part, term, oterm, gsum,
                l_sem, o_sem, ts, tr, tcs, tcr):
    f32, bf16 = jnp.float32, jnp.bfloat16
    z = lax.axis_index("rep")
    e = lax.axis_index("ep")
    sib, chips = partners(e)
    eps, rows, width = cots.shape
    half = rows // 2
    group_rows = eps * rows
    slice_width = mixed.shape[1]
    head_dim = slice_width // heads_dev
    scale = head_dim ** -0.5

    barrier = pltpu.get_barrier_semaphore()
    for other in (sib, *chips):
        pl.semaphore_signal(barrier, inc=1, device_id={"rep": z, "ep": other}, device_id_type=MESH)
    pairs = ((qkv_ref, qkv), (segs_ref, segs), (wout_ref, wout), (mixed_ref, mixed), (pre_ref, pre), (turn_ref, turn),
             (gains_ref, gains), (normed_ref, normed), (wqkv_ref, wqkv), (cot_ref, cots.at[e]))
    loads = [pltpu.make_async_copy(a, b, l_sem.at[n]) for n, (a, b) in enumerate(pairs)]
    for c in loads:
        c.start()
    pl.semaphore_wait(barrier, 4)

    def remote(src, dst, send, recv, ep):
        return pltpu.make_async_remote_copy(src_ref=src, dst_ref=dst, send_sem=send, recv_sem=recv,
                                            device_id={"rep": z, "ep": ep}, device_id_type=MESH)

    def near(j):
        return remote(cot_ref, cots.at[e], ts.at[j], tr.at[j], chips[j])

    def relay(j, source):
        p = cots.at[source, pl.ds(half * j, half)]
        return remote(p, p, ts.at[2 + j], tr.at[2 + j], chips[1 - j])

    def other_core(j):
        if j == 0:
            return remote(cot_ref, cots.at[e], tcs.at[0], tcr.at[0], sib)
        p = cots.at[chips[j - 1]]
        return remote(p, p, tcs.at[j], tcr.at[j], sib)

    near(0).start()
    near(1).start()
    other_core(0).start()

    block = 2 * rows
    blocks = group_rows // block
    loads[0].wait()
    loads[1].wait()
    seg_row = jnp.concatenate([segs[n:n + 1, :] for n in range(eps)], axis=1)

    def softmax(h, n):
        here = pl.ds(n * block, block)
        cut = slice(h * head_dim, (h + 1) * head_dim)
        kcut = slice(slice_width + h * head_dim, slice_width + (h + 1) * head_dim)
        s = lax.dot_general(qkv[here, cut], qkv[:, kcut], NT, preferred_element_type=f32) * scale
        seg_col = jnp.concatenate(
            [jnp.broadcast_to(segs[2 * n + j:2 * n + j + 1, :], (rows, rows)).T[:, 0:1] for j in range(2)], axis=0)
        s = jnp.where(seg_col == seg_row, s, masked_score)
        p = jnp.exp(s - jnp.max(s, axis=-1, keepdims=True))
        probs[h, here, :] = p / jnp.sum(p, axis=-1, keepdims=True)

    for n in range(blocks):
        softmax(0, n)
    for j in range(2):
        near(j).wait_recv()
        relay(j, chips[j]).start()
        other_core(j + 1).start()
    for h in range(1, heads_dev):
        for n in range(blocks):
            softmax(h, n)
    for j in range(2):
        relay(j, chips[2]).wait_recv()
    other_core(3).start()
    for c in loads[2:]:
        c.wait()
    for j in range(4):
        other_core(j).wait_recv()

    flat = cots[...].reshape(group_rows, width)
    weight = wout[...].reshape(slice_width, width)
    for n in range(blocks):
        here = pl.ds(n * block, block)
        left = cots[pl.ds(2 * n, 2)].reshape(block, width)
        dmix[here, :] = lax.dot_general(left, weight, NT, preferred_element_type=f32).astype(bf16)
    oterm[...] = lax.dot_general(mixed[...], flat, TN, preferred_element_type=f32).astype(bf16).reshape(oterm.shape)
    outs = [pltpu.make_async_copy(oterm, out_out, o_sem.at[0])]
    outs[0].start()

    def through_norm(index, dy, here, gain_row):
        cut = slice(index * head_dim, (index + 1) * head_dim)
        x = pre[here, cut]
        dn = dy * turn[0, here, :] + pltpu.roll(dy * turn[1, here, :], head_dim // 2, 1)
        r = lax.rsqrt(jnp.mean(x * x, axis=-1, keepdims=True) + norm_eps)
        unit = x * r
        gsum[gain_row:gain_row + 1, :] += jnp.sum(dn * unit, axis=0, keepdims=True)
        base = 2 * width // 128 + gain_row
        w = dn * gains[base:base + 1, :]
        pcot[here, cut] = (r * (w - unit * jnp.mean(w * unit, axis=-1, keepdims=True))).astype(bf16)

    gsum[...] = jnp.zeros_like(gsum)
    for h in range(heads_dev):
        cut = slice(h * head_dim, (h + 1) * head_dim)
        kcut = slice(slice_width + h * head_dim, slice_width + (h + 1) * head_dim)
        vcut = slice(2 * slice_width + h * head_dim, 2 * slice_width + (h + 1) * head_dim)
        for n in range(blocks):
            here = pl.ds(n * block, block)
            p = probs[h, here, :]
            dp = lax.dot_general(dmix[here, cut], qkv[:, vcut], NT, preferred_element_type=f32)
            ds = (p * (dp - jnp.sum(p * dp, axis=-1, keepdims=True))).astype(bf16)
            dsc[0, here, :] = ds
            dsc[1, here, :] = p.astype(bf16)
            through_norm(h, jnp.dot(ds, qkv[:, kcut], preferred_element_type=f32) * scale, here, 0)
        dkey[...] = lax.dot_general(dsc[0], qkv[:, cut], TN, preferred_element_type=f32) * scale
        for n in range(blocks):
            here = pl.ds(n * block, block)
            through_norm(heads_dev + h, dkey[here, :], here, 1)
        pcot[:, vcut] = lax.dot_general(dsc[1], dmix[:, cut], TN, preferred_element_type=f32).astype(bf16)
    outs.append(pltpu.make_async_copy(gsum, gain_out, o_sem.at[1]))
    outs[-1].start()

    for n in range(blocks):
        here = pl.ds(n * block, block)
        t = lax.dot_general(pcot[here, :], wqkv[...], NT, preferred_element_type=f32)
        part[n] = t.astype(bf16).reshape(2, rows, width)
        outs.append(pltpu.make_async_copy(part.at[n], part_ref.at[n], o_sem.at[2 + n]))
        outs[-1].start()
    piece = width // term.shape[0]
    for n in range(term.shape[0]):
        left = normed[:, n * piece:(n + 1) * piece]
        term[n] = lax.dot_general(left, pcot[...], TN, preferred_element_type=f32).astype(bf16)
        outs.append(pltpu.make_async_copy(term.at[n], qkv_out.at[n], o_sem.at[2 + blocks + n]))
        outs[-1].start()
    for c in outs:
        c.wait()
    for j in range(2):
        near(j).wait_send()
        relay(j, chips[j]).wait_send()
    for j in range(4):
        other_core(j).wait_send()


def attention_back(cot, wout, mixed, qkv, pre, turn, segs, gains, normed, wqkv, reps, eps, cid):
    rows, width = cot.shape
    heads_dev = wout.shape[0]
    gr, sw = mixed.shape
    f32, bf16 = jnp.float32, jnp.bfloat16
    S, V, D = jax.ShapeDtypeStruct, pltpu.VMEM, pltpu.SemaphoreType.DMA
    hd = sw // heads_dev
    outs = (S((eps // 2, 2, rows, width), bf16), S((reps, width // reps, 3 * sw), bf16), S(wout.shape, bf16), S((8, hd), f32))
    return pl.pallas_call(
        partial(back_kernel, heads_dev),
        out_shape=outs,
        in_specs=[pl.BlockSpec(memory_space=pl.ANY)] * 10,
        out_specs=[pl.BlockSpec(memory_space=pl.ANY)] * len(outs),
        scratch_shapes=[
            V((eps, rows, width), bf16), *[V(a.shape, a.dtype) for a in (wout, mixed, qkv, pre, turn, segs, gains, normed, wqkv)],
            V((heads_dev, gr, gr), f32), V((2, gr, gr), bf16), V((gr, sw), bf16), V((gr, hd), f32), V((gr, 3 * sw), bf16),
            V(outs[0].shape, bf16), V(outs[1].shape, bf16), V(wout.shape, bf16), V((8, hd), f32),
            D((10,)), D((2 + eps // 2 + reps,)), D((4,)), D((4,)), D((4,)), D((4,)),
        ],
        compiler_params=pltpu.CompilerParams(collective_id=cid, has_side_effects=True, vmem_limit_bytes=58 * 2**20),
    )(cot, wout, mixed, qkv, pre, turn, segs, gains, normed, wqkv)


def last_kernel(reps, eps, part_ref, qkv_ref, out_ref, tok_ref, cot_ref, gain_ref, gains_ref, router_ref,
                input_ref, q_ref, k_ref, v_ref, o_ref, gsum_ref, rsum_ref,
                own, sib_in, relay_in, xin, yin, wo, qall, qup, qdown, wup, wdown, fin, gath, mats, omat, tok, cot, gain,
                gown, gin, gz, gmid, rown, rin, rz, rmid,
                l_sem, ss, sr, hs, hr, qs, qr, ws, wr, us, ur, ds, dr, wus, wur, wds, wdr, ps, pr, gs, gr, gzs, gzr, rs, rr, rzs, rzr):
    f32, bf16 = jnp.float32, jnp.bfloat16
    z = lax.axis_index("rep")
    e = lax.axis_index("ep")
    core = e % 2
    chip = e // 2
    sib, chips = partners(e)
    rows, width = tok_ref.shape
    half = rows // 2
    rows_dev = o_ref.shape[0]
    heads_dev = out_ref.shape[0]
    head_dim = width // (heads_dev * eps)
    slice_width = heads_dev * head_dim

    barrier = pltpu.get_barrier_semaphore()
    for d in range(1, eps):
        pl.semaphore_signal(barrier, inc=1, device_id={"rep": z, "ep": (e + d) % eps}, device_id_type=MESH)
    for d in range(1, reps):
        pl.semaphore_signal(barrier, inc=1, device_id={"rep": (z + d) % reps, "ep": e}, device_id_type=MESH)
    loads = [
        pltpu.make_async_copy(part_ref.at[:, core], own, l_sem.at[0]),
        pltpu.make_async_copy(qkv_ref, qall, l_sem.at[1]),
        pltpu.make_async_copy(out_ref.at[:, core], wo.at[core], l_sem.at[2]),
        pltpu.make_async_copy(tok_ref, tok, l_sem.at[3]),
        pltpu.make_async_copy(cot_ref, cot, l_sem.at[4]),
        pltpu.make_async_copy(gain_ref, gain, l_sem.at[5]),
        pltpu.make_async_copy(gains_ref, gown, l_sem.at[6]),
        pltpu.make_async_copy(router_ref, rown, l_sem.at[7]),
    ]
    for c in loads:
        c.start()
    pl.semaphore_wait(barrier, eps - 1 + reps - 1)

    def to_sib(src, dst, send, recv):
        return pltpu.make_async_remote_copy(src_ref=src, dst_ref=dst, send_sem=send, recv_sem=recv,
                                            device_id={"rep": z, "ep": sib}, device_id_type=MESH)

    def to_chip(src, dst, send, recv, j):
        return pltpu.make_async_remote_copy(src_ref=src, dst_ref=dst, send_sem=send, recv_sem=recv,
                                            device_id={"rep": z, "ep": chips[j]}, device_id_type=MESH)

    def to_plane(src, dst, send, recv, d):
        return pltpu.make_async_remote_copy(src_ref=src, dst_ref=dst, send_sem=send, recv_sem=recv,
                                            device_id={"rep": z, "ep": (e + d) % eps}, device_id_type=MESH)

    def to_rep(src, dst, send, recv, d):
        return pltpu.make_async_remote_copy(src_ref=src, dst_ref=dst, send_sem=send, recv_sem=recv,
                                            device_id={"rep": (z + d) % reps, "ep": e}, device_id_type=MESH)

    def along(src, slot, send, recv, up):
        return pltpu.make_async_remote_copy(src_ref=src, dst_ref=slot, send_sem=send, recv_sem=recv,
                                            device_id={"rep": z + 1 if up else z - 1, "ep": e}, device_id_type=MESH)

    class Sum:
        def __init__(self, mine, up, down, usend, urecv, dsend, drecv, count):
            self.mine, self.up, self.down, self.count = mine, up, down, count
            self.usend, self.urecv, self.dsend, self.drecv = usend, urecv, dsend, drecv

        def hop(self, src, g, up):
            if up:
                return along(src, self.up.at[g], self.usend.at[g], self.urecv.at[g], True)
            return along(src, self.down.at[g], self.dsend.at[g], self.drecv.at[g], False)

        def begin(self):
            @pl.when(z == 0)
            def _():
                for g in range(reps - 1, 0, -1):
                    self.hop(self.mine(g), g, True).start()
            @pl.when(z == reps - 1)
            def _():
                for g in range(reps - 1):
                    self.hop(self.mine(g), g, False).start()

        def forward(self, n):
            g = reps - 1 - n
            @pl.when((z > 0) & (z < g))
            def _():
                self.hop(self.mine(g), g, True).wait_recv()
                add(self.up.at[g], (self.up.at[g], self.mine(g)), self.count)
                self.hop(self.up.at[g], g, True).start()
            @pl.when((z < reps - 1) & (z > n))
            def _():
                self.hop(self.mine(n), n, False).wait_recv()
                add(self.down.at[n], (self.down.at[n], self.mine(n)), self.count)
                self.hop(self.down.at[n], n, False).start()

        def arrived(self):
            @pl.when(z > 0)
            def _():
                self.hop(self.mine(0), z, True).wait_recv()
            @pl.when(z == 0)
            def _():
                self.up[z] = jnp.zeros(self.up.shape[1:], bf16)
            @pl.when(z < reps - 1)
            def _():
                self.hop(self.mine(0), z, False).wait_recv()
            @pl.when(z == reps - 1)
            def _():
                self.down[z] = jnp.zeros(self.down.shape[1:], bf16)

        def sent(self):
            for g in range(reps):
                @pl.when(z < g)
                def _():
                    self.hop(self.mine(g), g, True).wait_send()
                @pl.when(z > g)
                def _():
                    self.hop(self.mine(g), g, False).wait_send()

    step = 16

    def add(out, terms, count):
        @pl.loop(0, count // step)
        def _(i):
            r = pl.ds(pl.multiple_of(i * step, step), step)
            t = terms[0][r, :].astype(f32)
            for other in terms[1:]:
                t = t + other[r, :].astype(f32)
            out[r, :] = t.astype(out.dtype)

    lower, upper = pl.ds(0, half), pl.ds(half, half)
    qkv_sum = Sum(lambda g: qall.at[g], qup, qdown, us, ur, ds, dr, rows_dev * eps)
    out_sum = Sum(lambda g: wo.at[g // heads_dev, g % heads_dev], wup, wdown, wus, wur, wds, wdr, rows_dev)
    wcopy = to_sib(out_ref.at[:, 1 - core], wo.at[core], ws, wr)
    order = (chips[2] // 2, chips[0] // 2, chips[1] // 2, chip)
    scopies = [to_sib(part_ref.at[q, 1 - core], sib_in.at[q], ss.at[n], sr.at[n]) for n, q in enumerate(order)]
    for c in scopies:
        c.start()
    wcopy.start()

    loads[1].wait()
    qkv_sum.begin()
    hcopies = [to_chip(own.at[order[0], (lower, upper)[j]], relay_in.at[j], hs.at[j], hr.at[j], j) for j in range(2)]
    qcopies = [to_chip(own.at[order[1 + j]], (xin, yin)[j], qs.at[j], qr.at[j], j) for j in range(2)]
    loads[0].wait()
    scopies[0].wait_recv()
    d = own.at[order[0]]
    add(d, (d, sib_in.at[order[0]]), rows)
    for c in hcopies:
        c.start()
    for j in range(2):
        mine, other = own.at[order[1 + j]], sib_in.at[order[1 + j]]
        scopies[1 + j].wait_recv()
        direct, through = ((lower, upper), (upper, lower))[j]
        add(mine.at[direct], (mine.at[direct], other.at[direct]), half)
        hcopies[1 - j].wait_recv()
        add(mine.at[through], (mine.at[through], other.at[through], relay_in.at[1 - j]), half)
        qcopies[j].start()
    loads[2].wait()
    wcopy.wait_recv()
    out_sum.begin()
    qkv_sum.forward(0)
    scopies[3].wait_recv()
    for c in loads[3:8]:
        c.wait()
    for c in qcopies:
        c.wait_recv()

    gown[0:1, :] = jnp.zeros((1, width), f32)

    @pl.loop(0, rows // step)
    def _(i):
        r = pl.ds(pl.multiple_of(i * step, step), step)
        nc = (own[chip, r, :].astype(f32) + sib_in[chip, r, :].astype(f32) + xin[r, :].astype(f32) + yin[r, :].astype(f32))
        t = tok[r, :].astype(f32)
        scale = lax.rsqrt(jnp.mean(t * t, axis=-1, keepdims=True) + 1e-6)
        unit = t * scale
        scaled = nc * gain[0:1, :]
        cot[r, :] = cot[r, :] + scale * (scaled - unit * jnp.mean(scaled * unit, axis=-1, keepdims=True))
        gown[0:1, :] += jnp.sum(nc * unit, axis=0, keepdims=True)

    done = [pltpu.make_async_copy(cot, input_ref, l_sem.at[8])]
    done[0].start()

    gcopies = [to_plane(gown, gin.at[d - 1], gs.at[d - 1], gr.at[d - 1], d) for d in range(1, eps)]
    rcopies = [to_plane(rown.at[:, (e + d) % eps], rin.at[d - 1], rs.at[d - 1], rr.at[d - 1], d) for d in range(1, eps)]
    for c in (*gcopies, *rcopies):
        c.start()
    qkv_sum.forward(1)
    out_sum.forward(0)
    for n in range(2, reps - 1):
        qkv_sum.forward(n)
    for n in range(1, reps - 1):
        out_sum.forward(n)
    for c in (*gcopies, *rcopies):
        c.wait_recv()
    t = gown[...]
    for d in range(1, eps):
        t = t + gin[d - 1]
    gmid[...] = t
    t = rown[:, e]
    for d in range(1, eps):
        t = t + rin[d - 1]
    rmid[...] = t
    gzcopies = [to_rep(gmid, gz.at[d - 1], gzs.at[d - 1], gzr.at[d - 1], d) for d in range(1, reps)]
    rzcopies = [to_rep(rmid.at[(z + d) % reps], rz.at[d - 1], rzs.at[d - 1], rzr.at[d - 1], d) for d in range(1, reps)]
    for c in (*gzcopies, *rzcopies):
        c.start()

    qkv_sum.arrived()
    for n in range(eps):
        @pl.loop(0, rows_dev // step)
        def _(i):
            r = pl.ds(pl.multiple_of(i * step, step), step)
            a = pl.ds(pl.multiple_of(n * rows_dev + i * step, step), step)
            t = qall[z, a, :].astype(f32) + qup[z, a, :].astype(f32) + qdown[z, a, :].astype(f32)
            fin[n, r, :] = t.astype(bf16)
    pcopies = [to_plane(fin.at[(e + d) % eps], gath.at[e], ps.at[d - 1], pr.at[d - 1], d) for d in range(1, eps)]
    for c in pcopies:
        c.start()
    mine = pltpu.make_async_copy(fin.at[e], gath.at[e], l_sem.at[9])
    mine.start()
    out_sum.arrived()
    for c in (*gzcopies, *rzcopies):
        c.wait_recv()
    for c in gcopies:
        c.wait_send()
    t = gmid[...]
    for d in range(reps - 1):
        t = t + gz[d]
    gown[...] = t
    t = rmid[z]
    for d in range(reps - 1):
        t = t + rz[d]
    rmid[z] = t
    done.append(pltpu.make_async_copy(gown, gsum_ref, l_sem.at[10]))
    done.append(pltpu.make_async_copy(rmid.at[z], rsum_ref, l_sem.at[11]))
    wmine = wo.at[z // heads_dev, z % heads_dev]

    @pl.loop(0, rows_dev // step)
    def _(i):
        r = pl.ds(pl.multiple_of(i * step, step), step)
        t = wmine[r, :].astype(f32) + wup[z, r, :].astype(f32) + wdown[z, r, :].astype(f32)
        omat[r, :] = t
    done.append(pltpu.make_async_copy(omat, o_ref, l_sem.at[12]))
    for c in rzcopies:
        c.wait_send()
    for c in done[1:]:
        c.start()
    mine.wait()
    for c in pcopies:
        c.wait_recv()
    for src in range(eps):
        for m in range(3):
            for i in range(heads_dev):
                head = ((src % 2) * heads_dev + i) * (eps // 2) + src // 2
                mats[m, :, head * head_dim:(head + 1) * head_dim] = gath[src, :, m * slice_width + i * head_dim:m * slice_width + (i + 1) * head_dim].astype(f32)
    for m, ref in enumerate((q_ref, k_ref, v_ref)):
        done.append(pltpu.make_async_copy(mats.at[m], ref, l_sem.at[13 + m]))
        done[-1].start()
    for c in done:
        c.wait()
    qkv_sum.sent()
    out_sum.sent()
    for c in (*scopies, wcopy, *hcopies, *qcopies, *pcopies, *rcopies, *gzcopies):
        c.wait_send()


def last_sums(part, qkv_term, out_term, tokens, after_cot, gain_in, gains, router, rows_dev, reps, eps, cid):
    rows, width = tokens.shape
    f32, bf16 = jnp.float32, jnp.bfloat16
    heads_dev = out_term.shape[0]
    slices = qkv_term.shape[2]
    q = eps // 2
    half = rows // 2
    D, V = pltpu.SemaphoreType.DMA, pltpu.VMEM
    S = jax.ShapeDtypeStruct
    g8, rt = gains.shape, router.shape[2:]
    outs = (S((rows, width), f32), *[S((rows_dev, width), f32)] * 4, S(g8, f32), S(rt, f32))
    return pl.pallas_call(
        partial(last_kernel, reps, eps),
        out_shape=outs,
        in_specs=[pl.BlockSpec(memory_space=pl.ANY)] * 8,
        out_specs=[pl.BlockSpec(memory_space=pl.ANY)] * len(outs),
        scratch_shapes=[
            V((q, rows, width), bf16), V((q, rows, width), bf16), V((2, half, width), bf16), V((rows, width), bf16), V((rows, width), bf16),
            V((2, heads_dev, rows_dev, width), bf16), *[V((reps, rows_dev * eps, slices), bf16)] * 3, *[V((reps, rows_dev, width), bf16)] * 2,
            V((eps, rows_dev, slices), bf16), V((eps, rows_dev, slices), bf16),
            V((3, rows_dev, width), f32), V((rows_dev, width), f32), V((rows, width), bf16), V((rows, width), f32), V((1, width), f32),
            V(g8, f32), V((eps - 1, *g8), f32), V((reps - 1, *g8), f32), V(g8, f32),
            V(router.shape, f32), V((eps - 1, reps, *rt), f32), V((reps - 1, *rt), f32), V((reps, *rt), f32),
            D((17,)), D((4,)), D((4,)), D((2,)), D((2,)), D((2,)), D((2,)), D, D,
            *[D((reps,))] * 8, D((eps - 1,)), D((eps - 1,)),
            D((eps - 1,)), D((eps - 1,)), D((reps - 1,)), D((reps - 1,)), D((eps - 1,)), D((eps - 1,)), D((reps - 1,)), D((reps - 1,)),
        ],
        compiler_params=pltpu.CompilerParams(collective_id=cid, has_side_effects=True, vmem_limit_bytes=60 * 2**20),
    )(part, qkv_term, out_term, tokens, after_cot, gain_in, gains, router)


def join_kernel(count, *refs):
    z = lax.axis_index("rep")
    cols = refs[0].shape[2]
    down, outs = refs[2 * count], refs[2 * count + 1:]
    outs[2][...] = down[...].astype(outs[2].dtype)
    for n in range(2):
        ins, out = refs[n * count:(n + 1) * count], outs[n]
        for k in range(count):
            place = pl.multiple_of((z + count - k) % count * cols, cols)
            out[:, :, pl.ds(place, cols)] = ins[k][...].astype(out.dtype)


def join_columns(first, first_got, second, second_got, down):
    count, exp_dev, rows, cols = first.shape
    whole = jax.ShapeDtypeStruct((exp_dev, rows, cols * count), jnp.float32)

    def part(k):
        return pl.BlockSpec((None, 1, rows // 2, cols), lambda j, i: (k, j, i, 0))

    piece = pl.BlockSpec((1, rows // 2, cols), lambda j, i: (j, i, 0))
    tall = pl.BlockSpec((1, down.shape[1] // 2, down.shape[2]), lambda j, i: (j, i, 0))
    return pl.pallas_call(
        partial(join_kernel, count),
        grid=(exp_dev, 2),
        out_shape=(whole, whole, jax.ShapeDtypeStruct(down.shape, jnp.float32)),
        in_specs=[part(0)] + [part(k) for k in range(1, count)] + [part(0)] + [piece] * (count - 1) + [tall],
        out_specs=[pl.BlockSpec((1, rows // 2, cols * count), lambda j, i: (j, i, 0))] * 2 + [tall],
    )(first, *[first_got] * (count - 1), second, *second_got, down)


def front_kernel(reps, eps, lengths_ref, tok_ref, cot_ref, wq_ref, wk_ref, wv_ref, wo_ref, gains_ref, router_ref, nums_ref, freq_ref,
                 cots_ref, router_all_ref, nums_all_ref, gsum_ref, normed_ref, pre_ref, qkv_ref, mixed_ref, wqkv_ref, wout_ref, turn_ref, attn_ref,
                 toks, normed, wraw, stage, wqkv, wz, wout, proj, qkv, mixed, turn, segs, part, sib_in, relay_in, xin, yin, acc,
                 gown, gz, gmid, gin, gall, nums, freq,
                 l_sem, o_sem, ws, wr, vs, vr, zs, zr, fs, fr, ts, tr, tcs, tcr, cps, cpr, ccs, ccr,
                 gzs, gzr, gps, gpr, rzs, rzr, rps, rpr, ns, nr, ss, sr, hs, hr, qs, qr, os, orr):
    f32, bf16 = jnp.float32, jnp.bfloat16
    z = lax.axis_index("rep")
    e = lax.axis_index("ep")
    core = e % 2
    chip = e // 2
    sib, chips = partners(e)
    rows, width = tok_ref.shape
    half = rows // 2
    rows_dev = wq_ref.shape[0]
    slice_width = mixed.shape[1]
    head_dim = turn.shape[2]
    heads_dev = slice_width // head_dim
    group_rows = eps * rows

    barrier = pltpu.get_barrier_semaphore()
    for d in range(1, eps):
        pl.semaphore_signal(barrier, inc=1, device_id={"rep": z, "ep": (e + d) % eps}, device_id_type=MESH)
    for d in range(1, reps):
        pl.semaphore_signal(barrier, inc=1, device_id={"rep": (z + d) % reps, "ep": e}, device_id_type=MESH)

    def local(src, dst, sem):
        c = pltpu.make_async_copy(src, dst, sem)
        c.start()
        return c

    raw = [local(r, wraw.at[m], l_sem.at[m]) for m, r in enumerate((wq_ref, wk_ref, wv_ref))]
    tok_own = local(tok_ref, toks.at[e], l_sem.at[3])
    wo_own = local(wo_ref, wz.at[z], l_sem.at[4])
    cot_own = local(cot_ref, cots_ref.at[z, e], l_sem.at[5])
    small = [
        local(gains_ref, gown, l_sem.at[6]),
        local(nums_ref, nums.at[e], l_sem.at[7]),
        local(freq_ref, freq, l_sem.at[8]),
        local(router_ref, router_all_ref.at[e, z], l_sem.at[9]),
    ]
    pl.semaphore_wait(barrier, eps - 1 + reps - 1)

    def remote(src, dst, send, recv, rep, ep):
        return pltpu.make_async_remote_copy(src_ref=src, dst_ref=dst, send_sem=send, recv_sem=recv,
                                            device_id={"rep": rep, "ep": ep}, device_id_type=MESH)

    def below(k, fn):
        @pl.when(z - k >= 0)
        def _():
            fn(z - k)

    def above(k, fn):
        @pl.when(z + k < reps)
        def _():
            fn(z + k)

    class Chain:
        def __init__(self, slot, send, recv):
            self.slot, self.send, self.recv = slot, send, recv

        def copy(self, src, g, up):
            d = 0 if up else 1
            return remote(src, self.slot(g), self.send.at[d, g], self.recv.at[g], z + 1 if up else z - 1, e)

        def begin(self, src):
            @pl.when(z < reps - 1)
            def _():
                self.copy(src, z, True).start()
            @pl.when(z > 0)
            def _():
                self.copy(src, z, False).start()

        def take(self, k, then=None):
            def from_below(g):
                self.copy(self.slot(g), g, True).wait_recv()
                if then is not None:
                    then(g)
            def from_above(g):
                self.copy(self.slot(g), g, False).wait_recv()
                if then is not None:
                    then(g)
            below(k, from_below)
            above(k, from_above)

        def forward(self, k):
            @pl.when((z - k >= 0) & (z < reps - 1))
            def _():
                self.copy(self.slot(z - k), z - k, True).start()
            @pl.when((z + k < reps) & (z > 0))
            def _():
                self.copy(self.slot(z + k), z + k, False).start()

        def arrive(self, k):
            self.take(k)
            self.forward(k)

        def sent(self):
            for g in range(reps):
                @pl.when((z < reps - 1) & (z >= g))
                def _():
                    self.copy(self.slot(g), g, True).wait_send()
                @pl.when((z > 0) & (z <= g))
                def _():
                    self.copy(self.slot(g), g, False).wait_send()

    class Spread:
        def __init__(self, slot, send, recv, csend, crecv):
            self.slot, self.send, self.recv, self.csend, self.crecv = slot, send, recv, csend, crecv

        def near(self, src, j):
            return remote(src, self.slot(e), self.send.at[j], self.recv.at[j], z, chips[j])

        def relay(self, j, source):
            p = self.slot(source).at[pl.ds(half * j, half)]
            return remote(p, p, self.send.at[2 + j], self.recv.at[2 + j], z, chips[1 - j])

        def core(self, src, j):
            return remote(src, self.slot(e if j == 0 else chips[j - 1]), self.csend.at[j], self.crecv.at[j], z, sib)

        def begin(self, src):
            self.near(src, 0).start()
            self.near(src, 1).start()
            self.core(src, 0).start()

        def pass_on(self):
            for j in range(2):
                self.near(self.slot(e), j).wait_recv()
                self.relay(j, chips[j]).start()
                self.core(self.slot(chips[j]), j + 1).start()

        def finish(self):
            for j in range(2):
                self.relay(j, chips[2]).wait_recv()
            self.core(self.slot(chips[2]), 3).start()

        def arrived(self):
            for j in range(4):
                self.core(self.slot(e), j).wait_recv()

        def sent(self):
            for j in range(2):
                self.near(self.slot(e), j).wait_send()
                self.relay(j, chips[j]).wait_send()
            for j in range(4):
                self.core(self.slot(e), j).wait_send()

    tok_spread = Spread(lambda who: toks.at[who], ts, tr, tcs, tcr)

    def cot_spread(g):
        return Spread(lambda who: cots_ref.at[g, who], cps.at[g], cpr.at[g], ccs.at[g], ccr.at[g])

    wo_chain = Chain(lambda g: wz.at[g], ws, wr)
    w_chain = Chain(lambda g: wqkv.at[g], vs, vr)
    cot_chain = Chain(lambda g: cots_ref.at[g, e], zs, zr)

    def cot_take(k):
        cot_chain.take(k, lambda g: cot_spread(g).begin(cots_ref.at[g, e]))

    def each(k, fn):
        below(k, lambda g: fn(cot_spread(g)))
        above(k, lambda g: fn(cot_spread(g)))

    gzc = [remote(gains_ref, gz.at[d - 1], gzs.at[d - 1], gzr.at[d - 1], (z + d) % reps, e) for d in range(1, reps)]
    rzc = [remote(router_ref, router_all_ref.at[e, z], rzs.at[d - 1], rzr.at[d - 1], (z + d) % reps, e) for d in range(1, reps)]
    nc = [remote(nums_ref, nums.at[e], ns.at[d - 1], nr.at[d - 1], z, (e + d) % eps) for d in range(1, eps)]
    for c in (*gzc, *rzc, *nc):
        c.start()
    wo_chain.begin(wo_ref)
    for m in range(3):
        raw[m].wait()
        for who in range(eps):
            for i in range(heads_dev):
                head = ((who % 2) * heads_dev + i) * (eps // 2) + who // 2
                at = m * slice_width + i * head_dim
                stage[who, :, at:at + head_dim] = wraw[m, :, head * head_dim:(head + 1) * head_dim]
    vc = [remote(stage.at[(e + d) % eps], wqkv.at[z, e], fs.at[d - 1], fr.at[d - 1], z, (e + d) % eps) for d in range(1, eps)]
    for c in vc:
        c.start()
    v_own = local(stage.at[e], wqkv.at[z, e], l_sem.at[10])
    tok_spread.begin(tok_ref)
    cot_chain.begin(cot_ref)
    cot_spread(z).begin(cot_ref)
    v_own.wait()
    for c in vc:
        c.wait_recv()
    w_chain.begin(wqkv.at[z])
    wo_chain.arrive(1)

    for c in gzc:
        c.wait_recv()
    small[0].wait()
    t = gown[...].astype(f32)
    for d in range(reps - 1):
        t = t + gz[d].astype(f32)
    gmid[...] = t.astype(bf16)
    gpc = [remote(gmid, gin.at[d - 1], gps.at[d - 1], gpr.at[d - 1], z, (e + d) % eps) for d in range(1, eps)]
    for c in gpc:
        c.start()
    small[3].wait()
    for c in rzc:
        c.wait_recv()
    rpc = [remote(router_all_ref.at[e], router_all_ref.at[e], rps.at[d - 1], rpr.at[d - 1], z, (e + d) % eps) for d in range(1, eps)]
    for c in rpc:
        c.start()
    tok_spread.pass_on()
    tok_spread.finish()
    wo_chain.arrive(2)
    cot_take(1)
    for c in gpc:
        c.wait_recv()
    t = gmid[...].astype(f32)
    for d in range(eps - 1):
        t = t + gin[d].astype(f32)
    gall[...] = t
    outs = [local(gall, gsum_ref, o_sem.at[0])]
    w_chain.arrive(1)
    wo_chain.arrive(3)
    cot_chain.forward(1)

    for c in small[1:3]:
        c.wait()
    for c in nc:
        c.wait_recv()
    outs.append(local(nums, nums_all_ref, o_sem.at[1]))
    deal = nums[:, 0, :]
    segment = jnp.zeros(deal.shape, jnp.int32)
    start = jnp.zeros(deal.shape, jnp.int32)
    end = 0
    for n in range(lengths_ref.shape[1]):
        end = end + lengths_ref[0, n]
        after = (deal >= end).astype(jnp.int32)
        segment = segment + after
        start = start + after * lengths_ref[0, n]
    position = (deal - start).astype(f32)
    segs[...] = segment.astype(f32)
    lane = lax.broadcasted_iota(jnp.int32, (rows, head_dim), 1)
    sign = jnp.where(lane < head_dim // 2, -1.0, 1.0)
    for n in range(eps):
        spot = jnp.broadcast_to(position[n:n + 1, :], (rows, rows)).T
        angle = spot * freq[0:1, :]
        here = pl.ds(n * rows, rows)
        turn[0, here, :] = jnp.cos(angle)
        turn[1, here, :] = jnp.sin(angle) * sign
    outs.append(local(turn, turn_ref, o_sem.at[2]))
    cot_spread(z).pass_on()

    tok_own.wait()
    tok_spread.arrived()
    gain_in = jnp.concatenate([gall[n:n + 1, :] for n in range(width // 128)], axis=1)
    step = 16
    for n in range(eps):
        @pl.loop(0, rows // step)
        def _(i):
            r = pl.ds(pl.multiple_of(i * step, step), step)
            t = toks[n, r, :].astype(f32)
            scale = lax.rsqrt(jnp.mean(t * t, axis=-1, keepdims=True) + norm_eps)
            normed[n, r, :] = (t * scale * gain_in).astype(bf16)
    outs.append(local(normed, normed_ref, o_sem.at[3]))
    w_chain.arrive(2)
    cot_take(2)
    cot_chain.forward(2)
    cot_spread(z).finish()

    wo_own.wait()
    wc = [remote(wz.at[(1 - core) * heads_dev + i], wout.at[i, core], os.at[i], orr.at[i], z, sib) for i in range(heads_dev)]
    wl = [local(wz.at[core * heads_dev + i], wout.at[i, core], l_sem.at[11 + i]) for i in range(heads_dev)]
    for c in wc:
        c.start()
    w_chain.arrive(3)
    each(1, lambda s: s.pass_on())


    @pl.loop(0, eps)
    def _(n):
        here = pl.ds(pl.multiple_of(n * rows, rows), rows)
        proj[here, :] = jnp.dot(normed[n], wqkv[...].reshape(width, 3 * slice_width), preferred_element_type=f32)
        for h in range(2 * heads_dev):
            cut = slice(h * head_dim, (h + 1) * head_dim)
            t = proj[here, cut]
            row = 2 * width // 128 + (0 if h < heads_dev else 1)
            t = t * lax.rsqrt(jnp.mean(t * t, axis=-1, keepdims=True) + norm_eps) * gall[row:row + 1, :]
            t = t * turn[0, here, :] + pltpu.roll(t, head_dim // 2, 1) * turn[1, here, :]
            qkv[here, cut] = t.astype(bf16)
        tail = slice(2 * slice_width, 3 * slice_width)
        qkv[here, tail] = proj[here, tail].astype(bf16)

    outs.append(local(proj.at[:, pl.ds(0, 2 * slice_width)], pre_ref, o_sem.at[4]))
    outs.append(local(qkv, qkv_ref, o_sem.at[5]))
    outs.append(local(wqkv, wqkv_ref, o_sem.at[6]))

    seg_row = jnp.concatenate([segs[n:n + 1, :] for n in range(eps)], axis=1)
    block = 2 * rows

    def attend(h):
        cut = slice(h * head_dim, (h + 1) * head_dim)
        kcut = slice(slice_width + h * head_dim, slice_width + (h + 1) * head_dim)
        vcut = slice(2 * slice_width + h * head_dim, 2 * slice_width + (h + 1) * head_dim)
        for n in range(eps // 2):
            here = pl.ds(n * block, block)
            s = lax.dot_general(qkv[here, cut], qkv[:, kcut], NT, preferred_element_type=f32) * (head_dim ** -0.5)
            seg_col = jnp.concatenate(
                [jnp.broadcast_to(segs[2 * n + j:2 * n + j + 1, :], (rows, rows)).T[:, 0:1] for j in range(2)], axis=0)
            s = jnp.where(seg_col == seg_row, s, masked_score)
            p = jnp.exp(s - jnp.max(s, axis=-1, keepdims=True))
            p = (p / jnp.sum(p, axis=-1, keepdims=True)).astype(bf16)
            mixed[here, cut] = jnp.dot(p, qkv[:, vcut], preferred_element_type=f32).astype(bf16)

    each(1, lambda s: s.finish())
    attend(0)
    each(2, lambda s: s.pass_on())
    for h in range(1, heads_dev):
        attend(h)
    outs.append(local(mixed, mixed_ref, o_sem.at[7]))
    for c in wl:
        c.wait()
    for c in wc:
        c.wait_recv()
    outs.append(local(wout, wout_ref, o_sem.at[8]))

    order = (chips[2] // 2, chips[0] // 2, chips[1] // 2, chip)
    scopies = [remote(part.at[q, 1 - core], sib_in.at[q], ss.at[n], sr.at[n], z, sib) for n, q in enumerate(order)]
    for n in range(eps // 2):
        q = order[n]
        here = pl.ds(pl.multiple_of(q * block, block), block)
        t = jnp.dot(mixed[here, :], wout[...].reshape(slice_width, width), preferred_element_type=f32)
        part[q] = t.astype(bf16).reshape(2, rows, width)
        scopies[n].start()

    cot_take(3)

    def add(out, terms, count):
        @pl.loop(0, count // step)
        def _(i):
            r = pl.ds(pl.multiple_of(i * step, step), step)
            t = terms[0][r, :].astype(f32)
            for other in terms[1:]:
                t = t + other[r, :].astype(f32)
            out[r, :] = t.astype(out.dtype)

    lower, upper = pl.ds(0, half), pl.ds(half, half)
    first = part.at[order[0], core]
    hcopies = [remote(first.at[(lower, upper)[j]], relay_in.at[j], hs.at[j], hr.at[j], z, chips[j]) for j in range(2)]
    qcopies = [remote(part.at[order[1 + j], core], (xin, yin)[j], qs.at[j], qr.at[j], z, chips[j]) for j in range(2)]
    scopies[0].wait_recv()
    add(first, (first, sib_in.at[order[0]]), rows)
    for c in hcopies:
        c.start()
    for j in range(2):
        mine, other = part.at[order[1 + j], core], sib_in.at[order[1 + j]]
        scopies[1 + j].wait_recv()
        direct, through = ((lower, upper), (upper, lower))[j]
        add(mine.at[direct], (mine.at[direct], other.at[direct]), half)
        hcopies[1 - j].wait_recv()
        add(mine.at[through], (mine.at[through], other.at[through], relay_in.at[1 - j]), half)
        qcopies[j].start()
    scopies[3].wait_recv()
    each(3, lambda s: s.pass_on())
    each(2, lambda s: s.finish())
    for c in qcopies:
        c.wait_recv()
    add(acc, (part.at[chip, core], sib_in.at[chip], xin, yin, toks.at[e]), rows)
    outs.append(local(acc, attn_ref, o_sem.at[9]))
    each(3, lambda s: s.finish())
    cot_own.wait()
    for g in range(reps):
        cot_spread(g).arrived()
        cot_spread(g).sent()
    for chain in (wo_chain, w_chain, cot_chain):
        chain.sent()
    tok_spread.sent()
    for c in rpc:
        c.wait_recv()
    for c in (*gzc, *rzc, *nc, *vc, *gpc, *rpc, *wc, *scopies, *hcopies, *qcopies):
        c.wait_send()
    for c in outs:
        c.wait()


def front(lengths, tokens, cot, wq, wk, wv, wo, gains, router, nums, freq, heads_dev, reps, eps, cid):
    rows, width = tokens.shape
    rows_dev = wq.shape[0]
    f32, bf16, i32 = jnp.float32, jnp.bfloat16, jnp.int32
    head_dim = freq.shape[1]
    sw = heads_dev * head_dim
    gr = eps * rows
    half = rows // 2
    q = eps // 2
    S, V, D = jax.ShapeDtypeStruct, pltpu.VMEM, pltpu.SemaphoreType.DMA
    outs = (
        S((reps, eps, rows, width), bf16), S((eps, reps, *router.shape), bf16), S((eps, *nums.shape), i32), S(gains.shape, f32),
        S((eps, rows, width), bf16), S((gr, 2 * sw), f32), S((gr, 3 * sw), bf16), S((gr, sw), bf16),
        S((reps, eps, rows_dev, 3 * sw), bf16), S((heads_dev, 2, rows_dev, width), bf16), S((2, gr, head_dim), f32), S((rows, width), f32),
    )
    return pl.pallas_call(
        partial(front_kernel, reps, eps),
        out_shape=outs,
        in_specs=[pl.BlockSpec(memory_space=pltpu.SMEM)] + [pl.BlockSpec(memory_space=pl.ANY)] * 10,
        out_specs=[pl.BlockSpec(memory_space=pl.ANY)] * len(outs),
        scratch_shapes=[
            V((eps, rows, width), bf16), V((eps, rows, width), bf16), V((3, rows_dev, width), bf16), V((eps, rows_dev, 3 * sw), bf16),
            V((reps, eps, rows_dev, 3 * sw), bf16), V((reps, rows_dev, width), bf16), V((heads_dev, 2, rows_dev, width), bf16),
            V((gr, 3 * sw), f32), V((gr, 3 * sw), bf16), V((gr, sw), bf16), V((2, gr, head_dim), f32), V((eps, rows), f32),
            V((q, 2, rows, width), bf16), V((q, rows, width), bf16), V((2, half, width), bf16), V((rows, width), bf16), V((rows, width), bf16),
            V((rows, width), f32),
            V(gains.shape, bf16), V((reps - 1, *gains.shape), bf16), V(gains.shape, bf16), V((eps - 1, *gains.shape), bf16), V(gains.shape, f32),
            V((eps, *nums.shape), i32), V(freq.shape, f32),
            D((16,)), D((16,)), D((2, reps)), D((reps,)), D((2, reps)), D((reps,)), D((2, reps)), D((reps,)), D((eps - 1,)), D((eps - 1,)),
            D((4,)), D((4,)), D((4,)), D((4,)), D((reps, 4)), D((reps, 4)), D((reps, 4)), D((reps, 4)),
            D((reps - 1,)), D((reps - 1,)), D((eps - 1,)), D((eps - 1,)), D((reps - 1,)), D((reps - 1,)), D((eps - 1,)), D((eps - 1,)),
            D((eps - 1,)), D((eps - 1,)), D((4,)), D((4,)), D((2,)), D((2,)), D((2,)), D((2,)), D((2,)), D((2,)),
        ],
        compiler_params=pltpu.CompilerParams(collective_id=cid, has_side_effects=True, vmem_limit_bytes=56 * 2**20),
    )(lengths, tokens, cot, wq, wk, wv, wo, gains, router, nums, freq)


def on_device_split(
    tokens,
    cotangent,
    query_weight,
    key_weight,
    value_weight,
    output_weight,
    router_weight,
    gains,
    expert_gate,
    expert_up,
    expert_down,
    lengths,
    deal,
    routes,
    priority,
):
    bf16, f32 = jnp.bfloat16, jnp.float32
    tok_dev, width = tokens.shape
    ep_count, rep_count = lax.axis_size("ep"), lax.axis_size("rep")
    ep_index, rep_index = lax.axis_index("ep"), lax.axis_index("rep")
    exp_dev, _, ff_width = expert_gate.shape
    top_count = routes.shape[1]
    experts_all = exp_dev * ep_count
    group_rows = tok_dev * ep_count
    capacity = 5 * tok_dev * top_count // (4 * exp_dev)
    head_dim = HD
    heads_dev = width // head_dim // ep_count
    slice_width = heads_dev * head_dim
    rows_dev = query_weight.shape[0]

    gains_dev = gains.shape[0]
    gain_rows = -(-gains_dev * rep_count * ep_count // 2048) * 16
    gains_placed = lax.dynamic_update_slice_in_dim(
        jnp.zeros((gain_rows * 128,), bf16),
        gains,
        (rep_index * ep_count + ep_index) * gains_dev,
        axis=0,
    ).reshape(gain_rows, 128)
    router_rows = router_weight.size // 128
    router_placed = jnp.pad(router_weight.reshape(router_rows, 128), ((0, -router_rows % 16), (0, 0)))
    numbers = jnp.concatenate([deal[None], priority[None], routes.T])
    numbers = jnp.pad(numbers, ((0, -numbers.shape[0] % 8), (0, 0)))
    frequency = rope_base ** (
        -2.0 * jnp.arange(head_dim // 2, dtype=jnp.float32) / head_dim
    )
    (
        cot_all,
        router_all,
        numbers_all,
        gains_all,
        normed_group,
        pre,
        qkv_low,
        mixed_low,
        qkv_slice,
        out_slice,
        turn,
        after_attn,
    ) = front(
        lengths,
        tokens,
        cotangent,
        query_weight,
        key_weight,
        value_weight,
        output_weight,
        gains_placed,
        router_placed,
        numbers,
        jnp.concatenate([frequency, frequency]).reshape(1, head_dim),
        heads_dev,
        rep_count,
        ep_count,
        0,
    )
    gains_float = gains_all.reshape(-1)
    gain_in = gains_float[:width]
    gain_mid = gains_float[width : 2 * width]
    router_full = (
        router_all[:, :, :router_rows].transpose(1, 0, 2, 3).reshape(width, experts_all)
    )
    deal_all = numbers_all[:, 0].reshape(-1)
    priority_all = numbers_all[:, 1].reshape(-1)
    routes_all = numbers_all[:, 2 : 2 + top_count].transpose(0, 2, 1).reshape(group_rows, top_count)
    segment_all, _ = placement(deal_all, lengths[0])
    normed_group = normed_group.reshape(group_rows, width)
    qkv_slice = qkv_slice.reshape(width, 3 * slice_width)
    mid_low = rms_scale(after_attn, gain_mid).astype(bf16)

    logits = jnp.dot(mid_low, router_full, preferred_element_type=f32)
    expert_ids = jnp.arange(experts_all, dtype=jnp.int32)
    member = (routes[:, :, None] == expert_ids[None, None, :]).astype(f32)
    named = jnp.sum(member, axis=1)
    lifted = jnp.where(named > 0, logits, masked_score)
    lifted = jnp.exp(lifted - jnp.max(lifted, axis=-1, keepdims=True)) * named
    gate_dense = lifted / jnp.sum(lifted, axis=-1, keepdims=True)
    onehot_all = jnp.sum(
        (routes_all[:, :, None] == expert_ids[None, None, :]).astype(bf16), axis=1
    )
    earlier = (priority_all[None, :] < priority[:, None]).astype(bf16)
    slots = jnp.dot(earlier, onehot_all, preferred_element_type=f32)
    kept_dense = named * (slots < capacity).astype(f32)
    pair_weight = gate_dense * kept_dense

    weight_high = pair_weight.astype(bf16)
    weight_low = (pair_weight - weight_high.astype(f32)).astype(bf16)
    side = jnp.concatenate(
        [weight_high, weight_low, jnp.zeros((tok_dev, 128 - 2 * experts_all), bf16)], axis=1
    )
    row_sum, moe_sum, gate_term, up_term, down_term, gate_got = moe(
        jnp.concatenate([mid_low, side], axis=1),
        cot_all,
        expert_gate,
        expert_up,
        expert_down,
        experts_all,
        3,
    )
    moe_out = moe_sum.astype(f32)
    block_out = (after_attn + moe_out).astype(bf16)

    def rows_of(parts):
        pieces = []
        for k in range(1, rep_count):
            pieces.append(
                lax.ppermute(parts[k], "rep", [(i, (i + k) % rep_count) for i in range(rep_count)])
            )
        return pieces

    up_pieces = rows_of(up_term)

    out_grad = cotangent.astype(f32)
    gate_cot = row_sum[:, width : width + experts_all].astype(f32) * kept_dense
    chosen_cot = gate_dense * (gate_cot - jnp.sum(gate_dense * gate_cot, axis=-1, keepdims=True))
    logit_cot = chosen_cot.astype(bf16)
    mid_cot = row_sum[:, :width].astype(f32) + jnp.dot(
        logit_cot, router_full.T, preferred_element_type=f32
    )
    router_term = jnp.dot(mid_low.T, logit_cot, preferred_element_type=f32)
    _, mid_pull = jax.vjp(rms_scale, after_attn, gain_mid)
    after_extra, gain_mid_cot = mid_pull(mid_cot)
    after_cot = out_grad + after_extra
    normed_part, qkv_term, output_term, head_gains = attention_back(
        after_cot.astype(bf16),
        out_slice,
        mixed_low,
        qkv_low,
        pre,
        turn,
        segment_all.astype(f32).reshape(ep_count, tok_dev),
        gains_all,
        normed_group,
        qkv_slice,
        rep_count,
        ep_count,
        1,
    )
    gains_term = jnp.concatenate(
        [
            jnp.zeros((width,), f32),
            gain_mid_cot,
            head_gains[:2].reshape(-1),
            jnp.zeros((6 * width - 2 * head_dim,), f32),
        ]
    ).reshape(8, width)
    router_parts = jnp.pad(
        router_term.reshape(rep_count, ep_count, router_rows, 128),
        ((0, 0), (0, 0), (0, -router_rows % 8), (0, 0)),
    )
    input_grad, query_sum, key_sum, value_sum, output_sum, gains_all, router_own = last_sums(
        normed_part,
        qkv_term,
        output_term,
        tokens,
        after_cot,
        gain_in.reshape(1, width),
        gains_term,
        router_parts,
        rows_dev,
        rep_count,
        ep_count,
        4,
    )
    gains_sum = lax.dynamic_slice_in_dim(
        gains_all.reshape(-1), (rep_index * ep_count + ep_index) * gains_dev, gains_dev
    )
    router_sum = router_own[:router_rows].reshape(rows_dev, experts_all)
    gate_w_grad, up_w_grad, down_w_grad = join_columns(
        gate_term, gate_got, up_term, up_pieces, down_term
    )
    return (
        block_out,
        input_grad,
        query_sum,
        key_sum,
        value_sum,
        output_sum,
        router_sum,
        gains_sum,
        gate_w_grad,
        up_w_grad,
        down_w_grad,
    )


def solution(mesh):
    placed = (
        P(("rep", "ep"), None),
        P(("rep", "ep"), None),
        P(("rep", "ep"), None),
        P(("rep", "ep"), None),
        P(("rep", "ep"), None),
        P(("rep", "ep"), None),
        P(("rep", "ep"), None),
        P(("rep", "ep")),
        P("ep", None, None),
        P("ep", None, None),
        P("ep", None, None),
        P("rep", None),
        P(("rep", "ep")),
        P(("rep", "ep"), None),
        P(("rep", "ep")),
    )
    return jax.shard_map(
        on_device_split if mesh.shape["rep"] == 4 else on_device_general,
        mesh=mesh,
        in_specs=placed,
        out_specs=(
            P(("rep", "ep"), None),
            P(("rep", "ep"), None),
            P(("rep", "ep"), None),
            P(("rep", "ep"), None),
            P(("rep", "ep"), None),
            P(("rep", "ep"), None),
            P(("rep", "ep"), None),
            P(("rep", "ep")),
            P("ep", "rep", None),
            P("ep", "rep", None),
            P("ep", "rep", None),
        ),
        check_vma=False,
    )
```

```python
from functools import partial

import jax
import jax.numpy as jnp
from jax import lax
from jax.experimental import pallas as pl
from jax.experimental.pallas import tpu as pltpu
from jax.sharding import PartitionSpec as P

HD = 128


norm_eps = 1e-06
rope_base = 10000.0
masked_score = -1e30
highest = lax.Precision.HIGHEST


def rms_scale(values, gain_vec):
    return (
        values * lax.rsqrt(jnp.mean(values * values, axis=-1, keepdims=True) + norm_eps) * gain_vec
    )


def rotate(values, positions):
    half_width = values.shape[-1] // 2
    frequency = rope_base ** (-2.0 * jnp.arange(half_width, dtype=jnp.float32) / values.shape[-1])
    angles = positions.astype(jnp.float32)[:, None] * frequency[None, :]
    cosine = jnp.cos(angles)[:, None, :]
    sine_part = jnp.sin(angles)[:, None, :]
    low_half = values[..., :half_width]
    high_half = values[..., half_width:]
    return jnp.concatenate(
        [low_half * cosine - high_half * sine_part, high_half * cosine + low_half * sine_part],
        axis=-1,
    )


def placement(deal_rows, lengths_row):
    seq_ends = jnp.cumsum(lengths_row)
    is_after = (seq_ends[None, :] <= deal_rows[:, None]).astype(jnp.int32)
    segment = jnp.sum(is_after, axis=1)
    seq_start = jnp.sum(is_after * lengths_row[None, :], axis=1)
    return (segment, deal_rows - seq_start)


def rope_norm(projected, gain_vec, positions):
    return rotate(rms_scale(projected, gain_vec), positions)


def attend_forward(parts, same_seq, score_scale):
    head_query, head_key, head_value = parts
    scores = (
        jnp.einsum("thd,shd->hts", head_query, head_key, preferred_element_type=jnp.float32)
        * score_scale
    )
    scores = jnp.where(same_seq[None], scores, masked_score)
    top_score = jnp.max(scores, axis=-1, keepdims=True)
    lifted = jnp.exp(scores - top_score)
    total_sum = jnp.sum(lifted, axis=-1, keepdims=True)
    prob_low = (lifted / total_sum).astype(jnp.bfloat16)
    mixed_out = jnp.einsum("hts,shd->thd", prob_low, head_value, preferred_element_type=jnp.float32)
    return (mixed_out, top_score, total_sum)


def attend_backward(parts, same_seq, score_scale):
    head_query, head_key, head_value, head_grad, top_score, total_sum = parts
    scores = (
        jnp.einsum("thd,shd->hts", head_query, head_key, preferred_element_type=jnp.float32)
        * score_scale
    )
    scores = jnp.where(same_seq[None], scores, masked_score)
    prob_full = jnp.exp(scores - top_score) / total_sum
    prob_low = prob_full.astype(jnp.bfloat16)
    prob_grad = jnp.einsum(
        "thd,shd->hts", head_grad, head_value, preferred_element_type=jnp.float32
    )
    row_dot = jnp.sum(prob_full * prob_grad, axis=-1, keepdims=True)
    score_grad = (prob_full * (prob_grad - row_dot)).astype(jnp.bfloat16)
    query_grad = (
        jnp.einsum("hts,shd->thd", score_grad, head_key, preferred_element_type=jnp.float32)
        * score_scale
    )
    key_grad = (
        jnp.einsum("hts,thd->shd", score_grad, head_query, preferred_element_type=jnp.float32)
        * score_scale
    )
    value_grad = jnp.einsum("hts,thd->shd", prob_low, head_grad, preferred_element_type=jnp.float32)
    return (query_grad, key_grad, value_grad)


def on_device_general(
    tokens,
    cotangent,
    query_weight,
    key_weight,
    value_weight,
    output_weight,
    router_weight,
    gains,
    expert_gate,
    expert_up,
    expert_down,
    lengths,
    deal,
    routes,
    priority,
):
    tok_dev, width = tokens.shape
    ep_count = lax.axis_size("ep")
    ep_index = lax.axis_index("ep")
    exp_dev = expert_gate.shape[0]
    top_count = routes.shape[1]
    experts_all = exp_dev * ep_count
    group_rows = tok_dev * ep_count
    send_most = min(tok_dev, 3 * tok_dev * top_count // (2 * experts_all))
    capacity = 5 * tok_dev * top_count // (4 * exp_dev)
    head_dim = HD
    head_count = width // head_dim
    per_group = min(head_count, 4)
    group_count = head_count // per_group
    score_scale = head_dim ** (-0.5)
    query_full, key_full, value_full, output_full, router_full, gains_full = (
        lax.all_gather(query_weight, ("rep", "ep"), axis=0, tiled=True),
        lax.all_gather(key_weight, ("rep", "ep"), axis=0, tiled=True),
        lax.all_gather(value_weight, ("rep", "ep"), axis=0, tiled=True),
        lax.all_gather(output_weight, ("rep", "ep"), axis=0, tiled=True),
        lax.all_gather(router_weight, ("rep", "ep"), axis=0, tiled=True),
        lax.all_gather(gains, ("rep", "ep"), axis=0, tiled=True),
    )
    gains_float = gains_full.astype(jnp.float32)
    gain_in = gains_float[:width]
    gain_mid = gains_float[width : 2 * width]
    gain_query = gains_float[2 * width : 2 * width + head_dim]
    gain_key = gains_float[2 * width + head_dim :]
    deal_all, priority_all, routes_all = (
        lax.all_gather(deal, "ep", axis=0, tiled=True),
        lax.all_gather(priority, "ep", axis=0, tiled=True),
        lax.all_gather(routes, "ep", axis=0, tiled=True),
    )
    segment_all, position_all = placement(deal_all, lengths[0])
    segment_own = lax.dynamic_slice_in_dim(segment_all, ep_index * tok_dev, tok_dev)
    position_own = lax.dynamic_slice_in_dim(position_all, ep_index * tok_dev, tok_dev)
    residual = tokens.astype(jnp.float32)
    normed_low = rms_scale(residual, gain_in).astype(jnp.bfloat16)
    query_pre = jnp.dot(normed_low, query_full, preferred_element_type=jnp.float32).reshape(
        tok_dev, head_count, head_dim
    )
    key_pre = jnp.dot(normed_low, key_full, preferred_element_type=jnp.float32).reshape(
        tok_dev, head_count, head_dim
    )
    value_low = jnp.dot(normed_low, value_full, preferred_element_type=jnp.float32).astype(
        jnp.bfloat16
    )
    query_low = rope_norm(query_pre, gain_query, position_own).astype(jnp.bfloat16)
    key_low = (
        rope_norm(key_pre, gain_key, position_own).astype(jnp.bfloat16).reshape(tok_dev, width)
    )
    key_group, value_group = (
        lax.all_gather(key_low, "ep", axis=0, tiled=True),
        lax.all_gather(value_low, "ep", axis=0, tiled=True),
    )
    same_seq = segment_own[:, None] == segment_all[None, :]
    query_heads = query_low.reshape(tok_dev, group_count, per_group, head_dim).transpose(1, 0, 2, 3)
    key_heads = key_group.reshape(group_rows, group_count, per_group, head_dim).transpose(
        1, 0, 2, 3
    )
    value_heads = value_group.reshape(group_rows, group_count, per_group, head_dim).transpose(
        1, 0, 2, 3
    )
    mixed_heads, top_heads, total_heads = lax.map(
        partial(attend_forward, same_seq=same_seq, score_scale=score_scale),
        (query_heads, key_heads, value_heads),
    )
    mixed_low = mixed_heads.transpose(1, 0, 2, 3).reshape(tok_dev, width).astype(jnp.bfloat16)
    after_attn = residual + jnp.dot(mixed_low, output_full, preferred_element_type=jnp.float32)
    mid_low = rms_scale(after_attn, gain_mid).astype(jnp.bfloat16)
    logits = jnp.dot(mid_low, router_full, preferred_element_type=jnp.float32)
    chosen = jnp.take_along_axis(logits, routes, axis=1)
    gate_prob = jax.nn.softmax(chosen, axis=-1)
    expert_ids = jnp.arange(experts_all, dtype=jnp.int32)
    onehot_all = jnp.sum(
        (routes_all[:, :, None] == expert_ids[None, None, :]).astype(jnp.float32), axis=1
    )
    earlier = (priority_all[None, :] < priority_all[:, None]).astype(jnp.float32)
    slot_all = jnp.take_along_axis(
        jnp.dot(earlier, onehot_all, precision=highest), routes_all, axis=1
    ).astype(jnp.int32)
    row_ids = jnp.arange(tok_dev, dtype=jnp.int32)
    lower_tri = (row_ids[:, None] > row_ids[None, :]).astype(jnp.float32)
    before = jnp.einsum(
        "ij,dje->die",
        lower_tri,
        onehot_all.reshape(ep_count, tok_dev, experts_all),
        precision=highest,
    ).reshape(group_rows, experts_all)
    place_all = jnp.take_along_axis(before, routes_all, axis=1).astype(jnp.int32)
    kept_all = slot_all < capacity
    kept_own = lax.dynamic_slice_in_dim(kept_all, ep_index * tok_dev, tok_dev)
    place_own = lax.dynamic_slice_in_dim(place_all, ep_index * tok_dev, tok_dev)
    buffer_index = (routes * send_most + place_own).reshape(-1)
    rows_out = jnp.where(
        kept_own[:, :, None], mid_low[:, None, :], jnp.zeros((), jnp.bfloat16)
    ).reshape(tok_dev * top_count, width)
    send_rows = (
        jnp.zeros((experts_all * send_most, width), jnp.bfloat16)
        .at[buffer_index]
        .set(rows_out)
        .reshape(experts_all, send_most, width)
    )
    received = lax.all_to_all(send_rows, "ep", split_axis=0, concat_axis=1, tiled=True)
    gate_part = jnp.einsum(
        "erd,edf->erf", received, expert_gate, preferred_element_type=jnp.float32
    )
    up_part = jnp.einsum("erd,edf->erf", received, expert_up, preferred_element_type=jnp.float32)
    hidden = (jax.nn.silu(gate_part) * up_part).astype(jnp.bfloat16)
    result = jnp.einsum(
        "erf,efd->erd", hidden, expert_down, preferred_element_type=jnp.float32
    ).astype(jnp.bfloat16)
    returned = lax.all_to_all(result, "ep", split_axis=1, concat_axis=0, tiled=True)
    pair_out = returned.reshape(experts_all * send_most, width)[buffer_index].reshape(
        tok_dev, top_count, width
    )
    pair_weight = gate_prob * kept_own.astype(jnp.float32)
    moe_out = jnp.einsum("tk,tkd->td", pair_weight, pair_out, preferred_element_type=jnp.float32)
    block_out = (after_attn + moe_out).astype(jnp.bfloat16)
    out_grad = cotangent.astype(jnp.float32)
    pair_gate_grad = kept_own.astype(jnp.float32) * jnp.einsum(
        "tkd,td->tk", pair_out, out_grad, preferred_element_type=jnp.float32
    )
    pair_grad = (
        (pair_weight[:, :, None] * out_grad[:, None, :])
        .astype(jnp.bfloat16)
        .reshape(tok_dev * top_count, width)
    )
    grad_send = (
        jnp.zeros((experts_all * send_most, width), jnp.bfloat16)
        .at[buffer_index]
        .set(pair_grad)
        .reshape(experts_all, send_most, width)
    )
    grad_received = lax.all_to_all(grad_send, "ep", split_axis=0, concat_axis=1, tiled=True)
    hidden_grad = jnp.einsum(
        "erd,efd->erf", grad_received, expert_down, preferred_element_type=jnp.float32
    )
    _, silu_pull = jax.vjp(lambda gate_in, up_in: jax.nn.silu(gate_in) * up_in, gate_part, up_part)
    gate_part_grad, up_part_grad = silu_pull(hidden_grad)
    gate_low_grad = gate_part_grad.astype(jnp.bfloat16)
    up_low_grad = up_part_grad.astype(jnp.bfloat16)
    down_term = jnp.einsum(
        "erf,erd->efd", hidden, grad_received, preferred_element_type=jnp.float32
    )
    gate_term = jnp.einsum(
        "erd,erf->edf", received, gate_low_grad, preferred_element_type=jnp.float32
    )
    up_term = jnp.einsum("erd,erf->edf", received, up_low_grad, preferred_element_type=jnp.float32)
    rows_grad = (
        jnp.einsum("erf,edf->erd", gate_low_grad, expert_gate, preferred_element_type=jnp.float32)
        + jnp.einsum("erf,edf->erd", up_low_grad, expert_up, preferred_element_type=jnp.float32)
    ).astype(jnp.bfloat16)
    back_rows = lax.all_to_all(rows_grad, "ep", split_axis=1, concat_axis=0, tiled=True)
    mid_grad = jnp.sum(
        back_rows.reshape(experts_all * send_most, width)[buffer_index]
        .reshape(tok_dev, top_count, width)
        .astype(jnp.float32),
        axis=1,
    )
    gate_w_grad, up_w_grad, down_w_grad = (
        lax.psum_scatter(
            gate_term.astype(jnp.bfloat16), "rep", scatter_dimension=1, tiled=True
        ).astype(jnp.float32),
        lax.psum_scatter(
            up_term.astype(jnp.bfloat16), "rep", scatter_dimension=1, tiled=True
        ).astype(jnp.float32),
        lax.psum_scatter(
            down_term.astype(jnp.bfloat16), "rep", scatter_dimension=1, tiled=True
        ).astype(jnp.float32),
    )
    _, soft_pull = jax.vjp(lambda values: jax.nn.softmax(values, axis=-1), chosen)
    (chosen_grad,) = soft_pull(pair_gate_grad)
    onehot_own = (routes[:, :, None] == expert_ids[None, None, :]).astype(jnp.float32)
    logit_grad = jnp.einsum("tk,tke->te", chosen_grad, onehot_own).astype(jnp.bfloat16)
    mid_grad = mid_grad + jnp.dot(logit_grad, router_full.T, preferred_element_type=jnp.float32)
    router_term = jnp.dot(mid_low.T, logit_grad, preferred_element_type=jnp.float32)
    _, mid_pull = jax.vjp(rms_scale, after_attn, gain_mid)
    after_extra, gain_mid_grad = mid_pull(mid_grad)
    after_grad = out_grad + after_extra
    attn_low_grad = after_grad.astype(jnp.bfloat16)
    output_term = jnp.dot(mixed_low.T, attn_low_grad, preferred_element_type=jnp.float32)
    mixed_grad = jnp.dot(attn_low_grad, output_full.T, preferred_element_type=jnp.float32).astype(
        jnp.bfloat16
    )
    mixed_grad_heads = mixed_grad.reshape(tok_dev, group_count, per_group, head_dim).transpose(
        1, 0, 2, 3
    )
    query_grad_h, key_grad_h, value_grad_h = lax.map(
        partial(attend_backward, same_seq=same_seq, score_scale=score_scale),
        (query_heads, key_heads, value_heads, mixed_grad_heads, top_heads, total_heads),
    )
    query_grad_own = query_grad_h.transpose(1, 0, 2, 3).reshape(tok_dev, head_count, head_dim)
    key_grad_group = key_grad_h.transpose(1, 0, 2, 3).reshape(group_rows, width)
    value_grad_group = value_grad_h.transpose(1, 0, 2, 3).reshape(group_rows, width)
    key_sum, value_sum = (
        lax.psum_scatter(
            key_grad_group.astype(jnp.bfloat16), "ep", scatter_dimension=0, tiled=True
        ).astype(jnp.float32),
        lax.psum_scatter(
            value_grad_group.astype(jnp.bfloat16), "ep", scatter_dimension=0, tiled=True
        ).astype(jnp.float32),
    )
    value_low_grad = value_sum.astype(jnp.bfloat16)
    _, query_pull = jax.vjp(
        lambda projected, gain_vec: rope_norm(projected, gain_vec, position_own),
        query_pre,
        gain_query,
    )
    query_pre_grad, gain_query_grad = query_pull(query_grad_own)
    _, key_pull = jax.vjp(
        lambda projected, gain_vec: rope_norm(projected, gain_vec, position_own), key_pre, gain_key
    )
    key_pre_grad, gain_key_grad = key_pull(key_sum.reshape(tok_dev, head_count, head_dim))
    query_low_grad = query_pre_grad.reshape(tok_dev, width).astype(jnp.bfloat16)
    key_low_grad = key_pre_grad.reshape(tok_dev, width).astype(jnp.bfloat16)
    normed_grad = jnp.dot(query_low_grad, query_full.T, preferred_element_type=jnp.float32)
    normed_grad = normed_grad + jnp.dot(
        key_low_grad, key_full.T, preferred_element_type=jnp.float32
    )
    normed_grad = normed_grad + jnp.dot(
        value_low_grad, value_full.T, preferred_element_type=jnp.float32
    )
    query_term = jnp.dot(normed_low.T, query_low_grad, preferred_element_type=jnp.float32)
    key_term = jnp.dot(normed_low.T, key_low_grad, preferred_element_type=jnp.float32)
    value_term = jnp.dot(normed_low.T, value_low_grad, preferred_element_type=jnp.float32)
    _, input_pull = jax.vjp(rms_scale, residual, gain_in)
    input_extra, gain_in_grad = input_pull(normed_grad)
    input_grad = after_grad + input_extra
    gains_term = jnp.concatenate([gain_in_grad, gain_mid_grad, gain_query_grad, gain_key_grad])
    query_sum, key_total, value_total, output_sum, router_sum, gains_sum = (
        lax.psum_scatter(query_term, ("rep", "ep"), scatter_dimension=0, tiled=True),
        lax.psum_scatter(key_term, ("rep", "ep"), scatter_dimension=0, tiled=True),
        lax.psum_scatter(value_term, ("rep", "ep"), scatter_dimension=0, tiled=True),
        lax.psum_scatter(output_term, ("rep", "ep"), scatter_dimension=0, tiled=True),
        lax.psum_scatter(router_term, ("rep", "ep"), scatter_dimension=0, tiled=True),
        lax.psum_scatter(gains_term, ("rep", "ep"), scatter_dimension=0, tiled=True),
    )
    return (
        block_out,
        input_grad,
        query_sum,
        key_total,
        value_total,
        output_sum,
        router_sum,
        gains_sum,
        gate_w_grad,
        up_w_grad,
        down_w_grad,
    )


MESH = pl.DeviceIdType.MESH


def partners(e):
    sib = e + 1 - 2 * (e % 2)
    xn = e + 2 - 4 * ((e // 2) % 2)
    yn = e + 4 - 8 * ((e // 4) % 2)
    dg = xn + 4 - 8 * ((e // 4) % 2)
    return sib, (xn, yn, dg)


NT = (((1,), (1,)), ((), ()))
TN = (((0,), (0,)), ((), ()))


def visit_order(reps):
    if reps != 4:
        return [sorted((g for g in range(reps) if g != z), key=lambda g: (abs(g - z), g)) + [z] for z in range(reps)]
    return [[2, 3, 1, 0], [2, 3, 0, 1], [1, 0, 3, 2], [1, 0, 2, 3]]


def moe_kernel(reps, side_lanes, experts_all, x_ref, cot_ref, eg_ref, eu_ref, ed_ref,
               row_ref, moe_ref, gout_ref, uout_ref, dout_ref, gin_ref,
               mid_ref, a_ref, b_ref, h_ref, xin_ref, yin_ref, zin_ref,
               wgu, wd, xbuf, cbuf, abuf, pbuf, sib_in, relay_in, sendbuf, ownbuf, rbuf, tmp, colbuf, gst, dst,
               own_sem, w_sem, x_sem, c_sem, ab_sem, t_sem, col_sem, g_sem, o_sem,
               zs, zr, ps, pr, cs, cr, ss, sr, hs, hr, qs, qr, fs, fr, xs, xr):
    f32, bf16 = jnp.float32, jnp.bfloat16
    z = lax.axis_index("rep")
    e = lax.axis_index("ep")
    core = e % 2
    chip = e // 2
    sib, chips = partners(e)
    rows = x_ref.shape[0]
    half = rows // 2
    width = cot_ref.shape[-1]
    W1 = x_ref.shape[1]
    WP = pbuf.shape[-1]
    exp_dev = eg_ref.shape[0]
    F = wgu.shape[2] // exp_dev
    EF = exp_dev * F
    steps = 4 * reps
    table = visit_order(reps)

    def group_of(s):
        g = 0
        for zi in range(reps):
            for si in range(reps):
                g = g + jnp.where((z == zi) & (s == si), table[zi][si], 0)
        return g

    def chip_of(k):
        return jnp.where(k == 0, chips[2] // 2, jnp.where(k == 1, chip, jnp.where(k == 2, chips[0] // 2, chips[1] // 2)))

    barrier = pltpu.get_barrier_semaphore()
    for other in (sib, *chips):
        pl.semaphore_signal(barrier, inc=1, device_id={"rep": z, "ep": other}, device_id_type=MESH)
    for d in range(1, reps):
        pl.semaphore_signal(barrier, inc=1, device_id={"rep": (z + d) % reps, "ep": e}, device_id_type=MESH)
    weights = []
    for j in range(exp_dev):
        cut = pl.ds(pl.multiple_of(z * F, F), F)
        weights.append(pltpu.make_async_copy(eg_ref.at[j, :, cut], wgu.at[0, :, pl.ds(j * F, F)], w_sem.at[j]))
        weights.append(pltpu.make_async_copy(eu_ref.at[j, :, cut], wgu.at[1, :, pl.ds(j * F, F)], w_sem.at[exp_dev + j]))
        weights.append(pltpu.make_async_copy(ed_ref.at[j, cut, :], wd.at[pl.ds(j * F, F), :], w_sem.at[2 * exp_dev + j]))
    for w in weights:
        w.start()
    local = pltpu.make_async_copy(x_ref, mid_ref.at[z, e], own_sem)
    local.start()
    pl.semaphore_wait(barrier, 4 + reps - 1)

    def zcopy(src, g, up):
        d = 0 if up else 1
        return pltpu.make_async_remote_copy(
            src_ref=src, dst_ref=mid_ref.at[g, e], send_sem=zs.at[d, g], recv_sem=zr.at[g],
            device_id={"rep": z + 1 if up else z - 1, "ep": e}, device_id_type=MESH)

    def pcopy(src, g, j):
        return pltpu.make_async_remote_copy(
            src_ref=src, dst_ref=mid_ref.at[g, e], send_sem=ps.at[g, j], recv_sem=pr.at[g, j],
            device_id={"rep": z, "ep": chips[j]}, device_id_type=MESH)

    def relay(g, j, source):
        part = mid_ref.at[g, source, pl.ds(half * j, half)]
        return pltpu.make_async_remote_copy(
            src_ref=part, dst_ref=part, send_sem=ps.at[g, 2 + j], recv_sem=pr.at[g, 2 + j],
            device_id={"rep": z, "ep": chips[1 - j]}, device_id_type=MESH)

    def ccopy(src, g, j):
        who = e if j == 0 else chips[j - 1]
        return pltpu.make_async_remote_copy(
            src_ref=src, dst_ref=mid_ref.at[g, who], send_sem=cs.at[g, j], recv_sem=cr.at[g, j],
            device_id={"rep": z, "ep": sib}, device_id_type=MESH)

    def spread(src, g):
        pcopy(src, g, 0).start()
        pcopy(src, g, 1).start()
        ccopy(src, g, 0).start()

    def pass_on(g):
        for j in range(2):
            pcopy(x_ref, g, j).wait_recv()
            relay(g, j, chips[j]).start()
            ccopy(mid_ref.at[g, chips[j]], g, j + 1).start()

    def finish_in(g):
        for j in range(2):
            relay(g, j, chips[2]).wait_recv()
        ccopy(mid_ref.at[g, chips[2]], g, 3).start()

    def at(k, fn):
        if k == 0:
            fn(z)
            return
        @pl.when(z - k >= 0)
        def _():
            fn(z - k)
        @pl.when(z + k < reps)
        def _():
            fn(z + k)

    def arrive(k):
        @pl.when(z - k >= 0)
        def _():
            g = z - k
            zcopy(x_ref, g, True).wait_recv()
            @pl.when(z < reps - 1)
            def _():
                zcopy(mid_ref.at[g, e], g, True).start()
            spread(mid_ref.at[g, e], g)
        @pl.when(z + k < reps)
        def _():
            g = z + k
            zcopy(x_ref, g, False).wait_recv()
            @pl.when(z > 0)
            def _():
                zcopy(mid_ref.at[g, e], g, False).start()
            spread(mid_ref.at[g, e], g)

    def ready(g):
        for j in range(4):
            ccopy(x_ref, g, j).wait_recv()

    def load_x(i):
        g, q = group_of(i // 4), chip_of(i % 4)
        return pltpu.make_async_copy(mid_ref.at[g, pl.ds(2 * q, 2)], xbuf.at[i % 2], x_sem.at[i % 2])

    def load_c(i):
        g, q = group_of(i // 4), chip_of(i % 4)
        return pltpu.make_async_copy(cot_ref.at[g, pl.ds(2 * q, 2)], cbuf.at[i % 2], c_sem.at[i % 2])

    def keep(i, m):
        g, q = group_of(i // 4), chip_of(i % 4)
        place = pl.ds(pl.multiple_of((g * 4 + q) * 2 * rows, 2 * rows), 2 * rows)
        return pltpu.make_async_copy(abuf.at[i % 2, m], (a_ref, b_ref, h_ref)[m].at[place], ab_sem.at[i % 2, m])

    def compute(i):
        slot = i % 2
        lane = lax.broadcasted_iota(jnp.int32, (2 * rows, side_lanes), 1)
        side = xbuf[slot, :, :, pl.ds(width, side_lanes)].reshape(2 * rows, side_lanes).astype(f32)

        def one(j, cots):
            cols = pl.ds(pl.multiple_of(j * F, F), F)
            x = xbuf[slot, :, :, pl.ds(0, width)].reshape(2 * rows, width)
            c = cbuf[slot].reshape(2 * rows, width)
            index = e * exp_dev + j
            w = jnp.sum(jnp.where((lane == index) | (lane == index + experts_all), side, 0.0), axis=1, keepdims=True)
            ga = jnp.dot(x, wgu[0, :, cols], preferred_element_type=f32)
            up = jnp.dot(x, wgu[1, :, cols], preferred_element_type=f32)
            hc = lax.dot_general(c, wd[cols, :], NT, preferred_element_type=f32)
            sigma = 1.0 / (1.0 + jnp.exp(-ga))
            silu = ga * sigma
            hid = (silu * up).astype(bf16).astype(f32)
            hcw = hc * w
            abuf[slot, 0, :, cols] = (hcw * up * (sigma * (1.0 + ga * (1.0 - sigma)))).astype(bf16)
            abuf[slot, 1, :, cols] = (hcw * silu).astype(bf16)
            abuf[slot, 2, :, cols] = (hid * w).astype(bf16)
            dots = jnp.sum(hid * hc, axis=1, keepdims=True)
            return cots + jnp.where(lane == index, dots, 0.0)

        cots = lax.fori_loop(0, exp_dev, one, jnp.zeros((2 * rows, side_lanes), f32), unroll=True)
        pbuf[slot, :, :, pl.ds(width, side_lanes)] = cots.astype(bf16).reshape(2, rows, side_lanes)
        t = lax.dot_general(abuf[slot, 0], wgu[0], NT, preferred_element_type=f32)
        t = t + lax.dot_general(abuf[slot, 1], wgu[1], NT, preferred_element_type=f32)
        pbuf[slot, :, :, pl.ds(0, width)] = t.astype(bf16).reshape(2, rows, width)
        t = jnp.dot(abuf[slot, 2], wd[...], preferred_element_type=f32)
        pbuf[slot, :, :, pl.ds(W1, width)] = t.astype(bf16).reshape(2, rows, width)

    def sibcopy(i):
        return pltpu.make_async_remote_copy(
            src_ref=pbuf.at[i % 2, 1 - core], dst_ref=sib_in.at[i % 4], send_sem=ss.at[i], recv_sem=sr.at[i],
            device_id={"rep": z, "ep": sib}, device_id_type=MESH)

    def hcopy(s, j):
        part = pl.ds(half * j, half)
        return pltpu.make_async_remote_copy(
            src_ref=sendbuf.at[0, part], dst_ref=relay_in.at[s, j], send_sem=hs.at[s, j], recv_sem=hr.at[s, j],
            device_id={"rep": z, "ep": chips[j]}, device_id_type=MESH)

    def qcopy(s, j):
        return pltpu.make_async_remote_copy(
            src_ref=sendbuf.at[1 + j], dst_ref=(xin_ref, yin_ref)[j].at[s], send_sem=qs.at[s, j], recv_sem=qr.at[s, j],
            device_id={"rep": z, "ep": chips[j]}, device_id_type=MESH)

    def fcopy(s, g):
        return pltpu.make_async_remote_copy(
            src_ref=rbuf.at[s % 2], dst_ref=zin_ref.at[z], send_sem=fs.at[s], recv_sem=fr.at[z],
            device_id={"rep": g, "ep": e}, device_id_type=MESH)

    step = 16

    def add(out, terms, count=rows):
        @pl.loop(0, count // step)
        def _(i):
            r = pl.ds(pl.multiple_of(i * step, step), step)
            t = terms[0][r, :].astype(f32)
            for other in terms[1:]:
                t = t + other[r, :].astype(f32)
            out[r, :] = t.astype(out.dtype)

    def finish(i):
        s, k = i // 4, i % 4
        sibcopy(i).wait_recv()
        mine, other = pbuf.at[i % 2, core], sib_in.at[i % 4]
        lower, upper = pl.ds(0, half), pl.ds(half, half)
        @pl.when(k == 1)
        def _():
            add(ownbuf.at[s % 2], (mine, other))
        @pl.when(k == 0)
        def _():
            @pl.when(s > 0)
            def _():
                hcopy(s - 1, 0).wait_send()
                hcopy(s - 1, 1).wait_send()
            add(sendbuf.at[0], (mine, other))
            hcopy(s, 0).start()
            hcopy(s, 1).start()
        @pl.when(k == 2)
        def _():
            @pl.when(s > 0)
            def _():
                qcopy(s - 1, 0).wait_send()
            add(sendbuf.at[1, lower], (mine.at[lower], other.at[lower]), half)
            hcopy(s, 1).wait_recv()
            add(sendbuf.at[1, upper], (mine.at[upper], other.at[upper], relay_in.at[s, 1]), half)
            qcopy(s, 0).start()
        @pl.when(k == 3)
        def _():
            @pl.when(s > 0)
            def _():
                qcopy(s - 1, 1).wait_send()
            add(sendbuf.at[2, upper], (mine.at[upper], other.at[upper]), half)
            hcopy(s, 0).wait_recv()
            add(sendbuf.at[2, lower], (mine.at[lower], other.at[lower], relay_in.at[s, 0]), half)
            qcopy(s, 1).start()

    def load_t(src, m):
        return pltpu.make_async_copy(src, tmp.at[m], t_sem.at[m])

    def total(s):
        for j in range(2):
            qcopy(s, j).wait_recv()
            load_t((xin_ref, yin_ref)[j].at[s], j).start()
        for j in range(2):
            load_t((xin_ref, yin_ref)[j].at[s], j).wait()

    def plane_sum(s):
        total(s)
        @pl.when(s >= 2)
        def _():
            fcopy(s - 2, group_of(s - 2)).wait_send()
        add(rbuf.at[s % 2], (ownbuf.at[s % 2], tmp.at[0], tmp.at[1]))
        fcopy(s, group_of(s)).start()

    @pl.when(z < reps - 1)
    def _():
        zcopy(x_ref, z, True).start()
    @pl.when(z > 0)
    def _():
        zcopy(x_ref, z, False).start()
    spread(x_ref, z)
    arrive(1)
    pass_on(z)
    arrive(2)
    at(1, pass_on)
    finish_in(z)
    arrive(3)
    at(2, pass_on)
    at(1, finish_in)
    end = (z == 0) | (z == reps - 1)

    @pl.when(end)
    def _():
        at(2, finish_in)
    for w in weights:
        w.wait()
    ready(group_of(0))
    load_x(0).start()
    load_c(0).start()

    @pl.loop(0, steps)
    def _(i):
        load_x(i).wait()
        load_c(i).wait()
        @pl.when(i == 1)
        def _():
            at(3, pass_on)
        @pl.when(i == 3)
        def _():
            at(3, finish_in)

            @pl.when(jnp.logical_not(end))
            def _():
                at(2, finish_in)
        @pl.when(i == steps - 5)
        def _():
            local.wait()
        @pl.when(i < steps - 1)
        def _():
            @pl.when(i % 4 == 3)
            def _():
                ready(group_of(i // 4 + 1))
            load_x(i + 1).start()
            load_c(i + 1).start()
        @pl.when(i >= 2)
        def _():
            sibcopy(i - 2).wait_send()
            for m in range(3):
                keep(i - 2, m).wait()
        compute(i)
        sibcopy(i).start()
        for m in range(3):
            keep(i, m).start()
        @pl.when(i >= 1)
        def _():
            finish(i - 1)
        @pl.when((i % 4 == 3) & (i >= 7) & (i < steps - 1))
        def _():
            plane_sum(i // 4 - 1)

    for i in (steps - 2, steps - 1):
        sibcopy(i).wait_send()
        for m in range(3):
            keep(i, m).wait()
    finish(steps - 1)
    plane_sum(reps - 2)

    blocks = width // 256
    halves = wgu.shape[1]

    def resident(src, m):
        return pltpu.make_async_copy(src.at[pl.ds(m * halves, halves)], wgu.at[m], w_sem.at[m])

    def load_col(src, n):
        return pltpu.make_async_copy(src.at[:, :, :, pl.ds(pl.multiple_of(n * 256, 256), 256)], colbuf.at[n % 2], col_sem.at[n % 2])

    def product(n, m):
        left = colbuf[n % 2, pl.ds(m * (reps // 2), reps // 2)].reshape(halves, 256)
        return left, wgu[m]

    def hand_over(k):
        return pltpu.make_async_remote_copy(
            src_ref=gout_ref.at[k], dst_ref=gin_ref.at[k], send_sem=xs.at[k], recv_sem=xr.at[k],
            device_id={"rep": (z + k) % reps, "ep": e}, device_id_type=MESH)

    per_piece = width // reps // 256

    def piece_done(n):
        k = (n // per_piece + reps - z) % reps
        @pl.when((n % per_piece == per_piece - 1) & (k % 2 == 1))
        def _():
            hand_over(k).start()

    def grad_rows(src, out, send):
        def store(n, j):
            per = width // reps
            place = pl.ds(pl.multiple_of((n * 256) % per, 256), 256)
            return pltpu.make_async_copy(gst.at[n % 2, j], out.at[((n * 256) // per + reps - z) % reps, j, place], g_sem.at[n % 2, j])
        for m in range(2):
            resident(src, m).start()
        load_col(mid_ref, 0).start()
        for m in range(2):
            resident(src, m).wait()
        @pl.loop(0, blocks)
        def _(n):
            load_col(mid_ref, n).wait()
            @pl.when(n < blocks - 1)
            def _():
                load_col(mid_ref, n + 1).start()
            @pl.when(n >= 2)
            def _():
                for j in range(exp_dev):
                    store(n - 2, j).wait()
                if send:
                    piece_done(n - 2)
            t = jnp.zeros((256, EF), f32)
            for m in range(2):
                left, right = product(n, m)
                t = t + lax.dot_general(left, right, TN, preferred_element_type=f32)
            for j in range(exp_dev):
                gst[n % 2, j] = t[:, j * F:(j + 1) * F].astype(bf16)
                store(n, j).start()
        for n in (blocks - 2, blocks - 1):
            for j in range(exp_dev):
                store(n, j).wait()
            if send:
                piece_done(n)

    def grad_down():
        def store(n):
            return pltpu.make_async_copy(dst.at[n % 2], dout_ref.at[:, :, pl.ds(pl.multiple_of(n * 256, 256), 256)], g_sem.at[n % 2, 0])
        for m in range(2):
            resident(h_ref, m).start()
        load_col(cot_ref, 0).start()
        for m in range(2):
            resident(h_ref, m).wait()
        @pl.loop(0, blocks)
        def _(n):
            load_col(cot_ref, n).wait()
            @pl.when(n < blocks - 1)
            def _():
                load_col(cot_ref, n + 1).start()
            @pl.when(n >= 2)
            def _():
                store(n - 2).wait()
            t = jnp.zeros((EF, 256), f32)
            for m in range(2):
                left, right = product(n, m)
                t = t + lax.dot_general(right, left, TN, preferred_element_type=f32)
            dst[n % 2] = t.reshape(exp_dev, F, 256).astype(bf16)
            store(n).start()
        for n in (blocks - 2, blocks - 1):
            store(n).wait()

    grad_rows(a_ref, gout_ref, True)
    grad_rows(b_ref, uout_ref, False)
    grad_down()

    last = reps - 1
    total(last)
    for d in range(1, reps):
        src = (z + d) % reps
        pltpu.make_async_remote_copy(
            src_ref=rbuf.at[0], dst_ref=zin_ref.at[src], send_sem=fs.at[last], recv_sem=fr.at[src],
            device_id={"rep": src, "ep": e}, device_id_type=MESH).wait_recv()
        load_t(zin_ref.at[src], 1 + d).start()
    for d in range(1, reps):
        load_t(zin_ref.at[(z + d) % reps], 1 + d).wait()
    fcopy(reps - 3, group_of(reps - 3)).wait_send()
    add(rbuf.at[(reps - 3) % 2], (ownbuf.at[last % 2], *(tmp.at[m] for m in range(reps + 1))))
    outs = (
        pltpu.make_async_copy(rbuf.at[(reps - 3) % 2, :, pl.ds(0, W1)], row_ref, o_sem.at[0]),
        pltpu.make_async_copy(rbuf.at[(reps - 3) % 2, :, pl.ds(W1, width)], moe_ref, o_sem.at[1]),
    )
    for o in outs:
        o.start()
    for o in outs:
        o.wait()
    fcopy(reps - 2, group_of(reps - 2)).wait_send()
    for k in range(1, reps, 2):
        hand_over(k).wait()
    for j in range(2):
        hcopy(last, j).wait_send()
        qcopy(last, j).wait_send()
    for g in range(reps):
        for j in range(4):
            ccopy(x_ref, g, j).wait_send()
        for j in range(2):
            pcopy(x_ref, g, j).wait_send()
            relay(g, j, chips[j]).wait_send()
        @pl.when((z < reps - 1) & (z >= g))
        def _():
            zcopy(x_ref, g, True).wait_send()
        @pl.when((z > 0) & (z <= g))
        def _():
            zcopy(x_ref, g, False).wait_send()


def moe(x, cot_all, eg, eu, ed, experts_all, cid):
    reps, eps, rows, width = cot_all.shape
    W1 = x.shape[1]
    side = W1 - width
    WP = W1 + width
    exp_dev, _, ff = eg.shape
    F = ff // reps
    EF = exp_dev * F
    f32, bf16 = jnp.float32, jnp.bfloat16
    D, V = pltpu.SemaphoreType.DMA, pltpu.VMEM
    S = jax.ShapeDtypeStruct
    tokens = reps * eps * rows
    steps = 4 * reps
    outs = (
        S((rows, W1), bf16), S((rows, width), bf16),
        S((reps, exp_dev, width // reps, F), bf16), S((reps, exp_dev, width // reps, F), bf16), S((exp_dev, F, width), bf16),
        S((reps, exp_dev, width // reps, F), bf16),
        S((reps, eps, rows, W1), bf16), S((tokens, EF), bf16), S((tokens, EF), bf16), S((tokens, EF), bf16),
        S((reps, rows, WP), bf16), S((reps, rows, WP), bf16), S((reps, rows, WP), bf16),
    )
    return pl.pallas_call(
        partial(moe_kernel, reps, side, experts_all),
        out_shape=outs,
        in_specs=[pl.BlockSpec(memory_space=pl.ANY)] * 5,
        out_specs=[pl.BlockSpec(memory_space=pl.ANY)] * len(outs),
        scratch_shapes=[
            V((2, width, EF), bf16), V((EF, width), bf16),
            V((2, 2, rows, W1), bf16), V((2, 2, rows, width), bf16),
            V((2, 3, 2 * rows, EF), bf16), V((2, 2, rows, WP), bf16), V((4, rows, WP), bf16),
            V((reps, 2, rows // 2, WP), bf16), V((3, rows, WP), bf16), V((2, rows, WP), bf16), V((2, rows, WP), bf16),
            V((5, rows, WP), bf16), V((2, reps, eps, rows, 256), bf16),
            V((2, exp_dev, 256, F), bf16), V((2, exp_dev, F, 256), bf16),
            D, D((3 * exp_dev,)), D((2,)), D((2,)), D((2, 3)), D((5,)), D((2,)), D((2, exp_dev)), D((2,)),
            D((2, reps)), D((reps,)), D((reps, 4)), D((reps, 4)), D((reps, 4)), D((reps, 4)),
            D((steps,)), D((steps,)), D((reps, 2)), D((reps, 2)), D((reps, 2)), D((reps, 2)), D((reps,)), D((reps,)), D((reps,)), D((reps,)),
        ],
        compiler_params=pltpu.CompilerParams(collective_id=cid, has_side_effects=True, vmem_limit_bytes=63 * 2**20),
    )(x, cot_all, eg, eu, ed)[:6]


def back_kernel(heads_dev, cot_ref, wout_ref, mixed_ref, qkv_ref, pre_ref, turn_ref, segs_ref, gains_ref, normed_ref, wqkv_ref,
                part_ref, qkv_out, out_out, gain_out,
                cots, wout, mixed, qkv, pre, turn, segs, gains, normed, wqkv, probs, dsc, dmix, dkey, pcot, part, term, oterm, gsum,
                l_sem, o_sem, ts, tr, tcs, tcr):
    f32, bf16 = jnp.float32, jnp.bfloat16
    z = lax.axis_index("rep")
    e = lax.axis_index("ep")
    sib, chips = partners(e)
    eps, rows, width = cots.shape
    half = rows // 2
    group_rows = eps * rows
    slice_width = mixed.shape[1]
    head_dim = slice_width // heads_dev
    scale = head_dim ** -0.5

    barrier = pltpu.get_barrier_semaphore()
    for other in (sib, *chips):
        pl.semaphore_signal(barrier, inc=1, device_id={"rep": z, "ep": other}, device_id_type=MESH)
    pairs = ((qkv_ref, qkv), (segs_ref, segs), (wout_ref, wout), (mixed_ref, mixed), (pre_ref, pre), (turn_ref, turn),
             (gains_ref, gains), (normed_ref, normed), (wqkv_ref, wqkv), (cot_ref, cots.at[e]))
    loads = [pltpu.make_async_copy(a, b, l_sem.at[n]) for n, (a, b) in enumerate(pairs)]
    for c in loads:
        c.start()
    pl.semaphore_wait(barrier, 4)

    def remote(src, dst, send, recv, ep):
        return pltpu.make_async_remote_copy(src_ref=src, dst_ref=dst, send_sem=send, recv_sem=recv,
                                            device_id={"rep": z, "ep": ep}, device_id_type=MESH)

    def near(j):
        return remote(cot_ref, cots.at[e], ts.at[j], tr.at[j], chips[j])

    def relay(j, source):
        p = cots.at[source, pl.ds(half * j, half)]
        return remote(p, p, ts.at[2 + j], tr.at[2 + j], chips[1 - j])

    def other_core(j):
        if j == 0:
            return remote(cot_ref, cots.at[e], tcs.at[0], tcr.at[0], sib)
        p = cots.at[chips[j - 1]]
        return remote(p, p, tcs.at[j], tcr.at[j], sib)

    near(0).start()
    near(1).start()
    other_core(0).start()

    block = 2 * rows
    blocks = group_rows // block
    loads[0].wait()
    loads[1].wait()
    seg_row = jnp.concatenate([segs[n:n + 1, :] for n in range(eps)], axis=1)

    def softmax(h, n):
        here = pl.ds(n * block, block)
        cut = slice(h * head_dim, (h + 1) * head_dim)
        kcut = slice(slice_width + h * head_dim, slice_width + (h + 1) * head_dim)
        s = lax.dot_general(qkv[here, cut], qkv[:, kcut], NT, preferred_element_type=f32) * scale
        seg_col = jnp.concatenate(
            [jnp.broadcast_to(segs[2 * n + j:2 * n + j + 1, :], (rows, rows)).T[:, 0:1] for j in range(2)], axis=0)
        s = jnp.where(seg_col == seg_row, s, masked_score)
        p = jnp.exp(s - jnp.max(s, axis=-1, keepdims=True))
        probs[h, here, :] = p / jnp.sum(p, axis=-1, keepdims=True)

    for n in range(blocks):
        softmax(0, n)
    for j in range(2):
        near(j).wait_recv()
        relay(j, chips[j]).start()
        other_core(j + 1).start()
    for h in range(1, heads_dev):
        for n in range(blocks):
            softmax(h, n)
    for j in range(2):
        relay(j, chips[2]).wait_recv()
    other_core(3).start()
    for c in loads[2:]:
        c.wait()
    for j in range(4):
        other_core(j).wait_recv()

    flat = cots[...].reshape(group_rows, width)
    weight = wout[...].reshape(slice_width, width)
    for n in range(blocks):
        here = pl.ds(n * block, block)
        left = cots[pl.ds(2 * n, 2)].reshape(block, width)
        dmix[here, :] = lax.dot_general(left, weight, NT, preferred_element_type=f32).astype(bf16)
    oterm[...] = lax.dot_general(mixed[...], flat, TN, preferred_element_type=f32).astype(bf16).reshape(oterm.shape)
    outs = [pltpu.make_async_copy(oterm, out_out, o_sem.at[0])]
    outs[0].start()

    def through_norm(index, dy, here, gain_row):
        cut = slice(index * head_dim, (index + 1) * head_dim)
        x = pre[here, cut]
        dn = dy * turn[0, here, :] + pltpu.roll(dy * turn[1, here, :], head_dim // 2, 1)
        r = lax.rsqrt(jnp.mean(x * x, axis=-1, keepdims=True) + norm_eps)
        unit = x * r
        gsum[gain_row:gain_row + 1, :] += jnp.sum(dn * unit, axis=0, keepdims=True)
        base = 2 * width // 128 + gain_row
        w = dn * gains[base:base + 1, :]
        pcot[here, cut] = (r * (w - unit * jnp.mean(w * unit, axis=-1, keepdims=True))).astype(bf16)

    gsum[...] = jnp.zeros_like(gsum)
    for h in range(heads_dev):
        cut = slice(h * head_dim, (h + 1) * head_dim)
        kcut = slice(slice_width + h * head_dim, slice_width + (h + 1) * head_dim)
        vcut = slice(2 * slice_width + h * head_dim, 2 * slice_width + (h + 1) * head_dim)
        for n in range(blocks):
            here = pl.ds(n * block, block)
            p = probs[h, here, :]
            dp = lax.dot_general(dmix[here, cut], qkv[:, vcut], NT, preferred_element_type=f32)
            ds = (p * (dp - jnp.sum(p * dp, axis=-1, keepdims=True))).astype(bf16)
            dsc[0, here, :] = ds
            dsc[1, here, :] = p.astype(bf16)
            through_norm(h, jnp.dot(ds, qkv[:, kcut], preferred_element_type=f32) * scale, here, 0)
        dkey[...] = lax.dot_general(dsc[0], qkv[:, cut], TN, preferred_element_type=f32) * scale
        for n in range(blocks):
            here = pl.ds(n * block, block)
            through_norm(heads_dev + h, dkey[here, :], here, 1)
        pcot[:, vcut] = lax.dot_general(dsc[1], dmix[:, cut], TN, preferred_element_type=f32).astype(bf16)
    outs.append(pltpu.make_async_copy(gsum, gain_out, o_sem.at[1]))
    outs[-1].start()

    for n in range(blocks):
        here = pl.ds(n * block, block)
        t = lax.dot_general(pcot[here, :], wqkv[...], NT, preferred_element_type=f32)
        part[n] = t.astype(bf16).reshape(2, rows, width)
        outs.append(pltpu.make_async_copy(part.at[n], part_ref.at[n], o_sem.at[2 + n]))
        outs[-1].start()
    piece = width // term.shape[0]
    for n in range(term.shape[0]):
        left = normed[:, n * piece:(n + 1) * piece]
        term[n] = lax.dot_general(left, pcot[...], TN, preferred_element_type=f32).astype(bf16)
        outs.append(pltpu.make_async_copy(term.at[n], qkv_out.at[n], o_sem.at[2 + blocks + n]))
        outs[-1].start()
    for c in outs:
        c.wait()
    for j in range(2):
        near(j).wait_send()
        relay(j, chips[j]).wait_send()
    for j in range(4):
        other_core(j).wait_send()


def attention_back(cot, wout, mixed, qkv, pre, turn, segs, gains, normed, wqkv, reps, eps, cid):
    rows, width = cot.shape
    heads_dev = wout.shape[0]
    gr, sw = mixed.shape
    f32, bf16 = jnp.float32, jnp.bfloat16
    S, V, D = jax.ShapeDtypeStruct, pltpu.VMEM, pltpu.SemaphoreType.DMA
    hd = sw // heads_dev
    outs = (S((eps // 2, 2, rows, width), bf16), S((reps, width // reps, 3 * sw), bf16), S(wout.shape, bf16), S((8, hd), f32))
    return pl.pallas_call(
        partial(back_kernel, heads_dev),
        out_shape=outs,
        in_specs=[pl.BlockSpec(memory_space=pl.ANY)] * 10,
        out_specs=[pl.BlockSpec(memory_space=pl.ANY)] * len(outs),
        scratch_shapes=[
            V((eps, rows, width), bf16), *[V(a.shape, a.dtype) for a in (wout, mixed, qkv, pre, turn, segs, gains, normed, wqkv)],
            V((heads_dev, gr, gr), f32), V((2, gr, gr), bf16), V((gr, sw), bf16), V((gr, hd), f32), V((gr, 3 * sw), bf16),
            V(outs[0].shape, bf16), V(outs[1].shape, bf16), V(wout.shape, bf16), V((8, hd), f32),
            D((10,)), D((2 + eps // 2 + reps,)), D((4,)), D((4,)), D((4,)), D((4,)),
        ],
        compiler_params=pltpu.CompilerParams(collective_id=cid, has_side_effects=True, vmem_limit_bytes=58 * 2**20),
    )(cot, wout, mixed, qkv, pre, turn, segs, gains, normed, wqkv)


def last_kernel(reps, eps, part_ref, qkv_ref, out_ref, tok_ref, cot_ref, gain_ref, gains_ref, router_ref,
                input_ref, q_ref, k_ref, v_ref, o_ref, gsum_ref, rsum_ref,
                own, sib_in, relay_in, xin, yin, wo, qall, qup, qdown, wup, wdown, fin, gath, mats, omat, tok, cot, gain,
                gown, gin, gz, gmid, rown, rin, rz, rmid,
                l_sem, ss, sr, hs, hr, qs, qr, ws, wr, us, ur, ds, dr, wus, wur, wds, wdr, ps, pr, gs, gr, gzs, gzr, rs, rr, rzs, rzr):
    f32, bf16 = jnp.float32, jnp.bfloat16
    z = lax.axis_index("rep")
    e = lax.axis_index("ep")
    core = e % 2
    chip = e // 2
    sib, chips = partners(e)
    rows, width = tok_ref.shape
    half = rows // 2
    rows_dev = o_ref.shape[0]
    heads_dev = out_ref.shape[0]
    head_dim = width // (heads_dev * eps)
    slice_width = heads_dev * head_dim

    barrier = pltpu.get_barrier_semaphore()
    for d in range(1, eps):
        pl.semaphore_signal(barrier, inc=1, device_id={"rep": z, "ep": (e + d) % eps}, device_id_type=MESH)
    for d in range(1, reps):
        pl.semaphore_signal(barrier, inc=1, device_id={"rep": (z + d) % reps, "ep": e}, device_id_type=MESH)
    loads = [
        pltpu.make_async_copy(part_ref.at[:, core], own, l_sem.at[0]),
        pltpu.make_async_copy(qkv_ref, qall, l_sem.at[1]),
        pltpu.make_async_copy(out_ref.at[:, core], wo.at[core], l_sem.at[2]),
        pltpu.make_async_copy(tok_ref, tok, l_sem.at[3]),
        pltpu.make_async_copy(cot_ref, cot, l_sem.at[4]),
        pltpu.make_async_copy(gain_ref, gain, l_sem.at[5]),
        pltpu.make_async_copy(gains_ref, gown, l_sem.at[6]),
        pltpu.make_async_copy(router_ref, rown, l_sem.at[7]),
    ]
    for c in loads:
        c.start()
    pl.semaphore_wait(barrier, eps - 1 + reps - 1)

    def to_sib(src, dst, send, recv):
        return pltpu.make_async_remote_copy(src_ref=src, dst_ref=dst, send_sem=send, recv_sem=recv,
                                            device_id={"rep": z, "ep": sib}, device_id_type=MESH)

    def to_chip(src, dst, send, recv, j):
        return pltpu.make_async_remote_copy(src_ref=src, dst_ref=dst, send_sem=send, recv_sem=recv,
                                            device_id={"rep": z, "ep": chips[j]}, device_id_type=MESH)

    def to_plane(src, dst, send, recv, d):
        return pltpu.make_async_remote_copy(src_ref=src, dst_ref=dst, send_sem=send, recv_sem=recv,
                                            device_id={"rep": z, "ep": (e + d) % eps}, device_id_type=MESH)

    def to_rep(src, dst, send, recv, d):
        return pltpu.make_async_remote_copy(src_ref=src, dst_ref=dst, send_sem=send, recv_sem=recv,
                                            device_id={"rep": (z + d) % reps, "ep": e}, device_id_type=MESH)

    def along(src, slot, send, recv, up):
        return pltpu.make_async_remote_copy(src_ref=src, dst_ref=slot, send_sem=send, recv_sem=recv,
                                            device_id={"rep": z + 1 if up else z - 1, "ep": e}, device_id_type=MESH)

    class Sum:
        def __init__(self, mine, up, down, usend, urecv, dsend, drecv, count):
            self.mine, self.up, self.down, self.count = mine, up, down, count
            self.usend, self.urecv, self.dsend, self.drecv = usend, urecv, dsend, drecv

        def hop(self, src, g, up):
            if up:
                return along(src, self.up.at[g], self.usend.at[g], self.urecv.at[g], True)
            return along(src, self.down.at[g], self.dsend.at[g], self.drecv.at[g], False)

        def begin(self):
            @pl.when(z == 0)
            def _():
                for g in range(reps - 1, 0, -1):
                    self.hop(self.mine(g), g, True).start()
            @pl.when(z == reps - 1)
            def _():
                for g in range(reps - 1):
                    self.hop(self.mine(g), g, False).start()

        def forward(self, n):
            g = reps - 1 - n
            @pl.when((z > 0) & (z < g))
            def _():
                self.hop(self.mine(g), g, True).wait_recv()
                add(self.up.at[g], (self.up.at[g], self.mine(g)), self.count)
                self.hop(self.up.at[g], g, True).start()
            @pl.when((z < reps - 1) & (z > n))
            def _():
                self.hop(self.mine(n), n, False).wait_recv()
                add(self.down.at[n], (self.down.at[n], self.mine(n)), self.count)
                self.hop(self.down.at[n], n, False).start()

        def arrived(self):
            @pl.when(z > 0)
            def _():
                self.hop(self.mine(0), z, True).wait_recv()
            @pl.when(z == 0)
            def _():
                self.up[z] = jnp.zeros(self.up.shape[1:], bf16)
            @pl.when(z < reps - 1)
            def _():
                self.hop(self.mine(0), z, False).wait_recv()
            @pl.when(z == reps - 1)
            def _():
                self.down[z] = jnp.zeros(self.down.shape[1:], bf16)

        def sent(self):
            for g in range(reps):
                @pl.when(z < g)
                def _():
                    self.hop(self.mine(g), g, True).wait_send()
                @pl.when(z > g)
                def _():
                    self.hop(self.mine(g), g, False).wait_send()

    step = 16

    def add(out, terms, count):
        @pl.loop(0, count // step)
        def _(i):
            r = pl.ds(pl.multiple_of(i * step, step), step)
            t = terms[0][r, :].astype(f32)
            for other in terms[1:]:
                t = t + other[r, :].astype(f32)
            out[r, :] = t.astype(out.dtype)

    lower, upper = pl.ds(0, half), pl.ds(half, half)
    qkv_sum = Sum(lambda g: qall.at[g], qup, qdown, us, ur, ds, dr, rows_dev * eps)
    out_sum = Sum(lambda g: wo.at[g // heads_dev, g % heads_dev], wup, wdown, wus, wur, wds, wdr, rows_dev)
    wcopy = to_sib(out_ref.at[:, 1 - core], wo.at[core], ws, wr)
    order = (chips[2] // 2, chips[0] // 2, chips[1] // 2, chip)
    scopies = [to_sib(part_ref.at[q, 1 - core], sib_in.at[q], ss.at[n], sr.at[n]) for n, q in enumerate(order)]
    for c in scopies:
        c.start()
    wcopy.start()

    loads[1].wait()
    qkv_sum.begin()
    hcopies = [to_chip(own.at[order[0], (lower, upper)[j]], relay_in.at[j], hs.at[j], hr.at[j], j) for j in range(2)]
    qcopies = [to_chip(own.at[order[1 + j]], (xin, yin)[j], qs.at[j], qr.at[j], j) for j in range(2)]
    loads[0].wait()
    scopies[0].wait_recv()
    d = own.at[order[0]]
    add(d, (d, sib_in.at[order[0]]), rows)
    for c in hcopies:
        c.start()
    for j in range(2):
        mine, other = own.at[order[1 + j]], sib_in.at[order[1 + j]]
        scopies[1 + j].wait_recv()
        direct, through = ((lower, upper), (upper, lower))[j]
        add(mine.at[direct], (mine.at[direct], other.at[direct]), half)
        hcopies[1 - j].wait_recv()
        add(mine.at[through], (mine.at[through], other.at[through], relay_in.at[1 - j]), half)
        qcopies[j].start()
    loads[2].wait()
    wcopy.wait_recv()
    out_sum.begin()
    qkv_sum.forward(0)
    scopies[3].wait_recv()
    for c in loads[3:8]:
        c.wait()
    for c in qcopies:
        c.wait_recv()

    gown[0:1, :] = jnp.zeros((1, width), f32)

    @pl.loop(0, rows // step)
    def _(i):
        r = pl.ds(pl.multiple_of(i * step, step), step)
        nc = (own[chip, r, :].astype(f32) + sib_in[chip, r, :].astype(f32) + xin[r, :].astype(f32) + yin[r, :].astype(f32))
        t = tok[r, :].astype(f32)
        scale = lax.rsqrt(jnp.mean(t * t, axis=-1, keepdims=True) + 1e-6)
        unit = t * scale
        scaled = nc * gain[0:1, :]
        cot[r, :] = cot[r, :] + scale * (scaled - unit * jnp.mean(scaled * unit, axis=-1, keepdims=True))
        gown[0:1, :] += jnp.sum(nc * unit, axis=0, keepdims=True)

    done = [pltpu.make_async_copy(cot, input_ref, l_sem.at[8])]
    done[0].start()

    gcopies = [to_plane(gown, gin.at[d - 1], gs.at[d - 1], gr.at[d - 1], d) for d in range(1, eps)]
    rcopies = [to_plane(rown.at[:, (e + d) % eps], rin.at[d - 1], rs.at[d - 1], rr.at[d - 1], d) for d in range(1, eps)]
    for c in (*gcopies, *rcopies):
        c.start()
    qkv_sum.forward(1)
    out_sum.forward(0)
    for n in range(2, reps - 1):
        qkv_sum.forward(n)
    for n in range(1, reps - 1):
        out_sum.forward(n)
    for c in (*gcopies, *rcopies):
        c.wait_recv()
    t = gown[...]
    for d in range(1, eps):
        t = t + gin[d - 1]
    gmid[...] = t
    t = rown[:, e]
    for d in range(1, eps):
        t = t + rin[d - 1]
    rmid[...] = t
    gzcopies = [to_rep(gmid, gz.at[d - 1], gzs.at[d - 1], gzr.at[d - 1], d) for d in range(1, reps)]
    rzcopies = [to_rep(rmid.at[(z + d) % reps], rz.at[d - 1], rzs.at[d - 1], rzr.at[d - 1], d) for d in range(1, reps)]
    for c in (*gzcopies, *rzcopies):
        c.start()

    qkv_sum.arrived()
    for n in range(eps):
        @pl.loop(0, rows_dev // step)
        def _(i):
            r = pl.ds(pl.multiple_of(i * step, step), step)
            a = pl.ds(pl.multiple_of(n * rows_dev + i * step, step), step)
            t = qall[z, a, :].astype(f32) + qup[z, a, :].astype(f32) + qdown[z, a, :].astype(f32)
            fin[n, r, :] = t.astype(bf16)
    pcopies = [to_plane(fin.at[(e + d) % eps], gath.at[e], ps.at[d - 1], pr.at[d - 1], d) for d in range(1, eps)]
    for c in pcopies:
        c.start()
    mine = pltpu.make_async_copy(fin.at[e], gath.at[e], l_sem.at[9])
    mine.start()
    out_sum.arrived()
    for c in (*gzcopies, *rzcopies):
        c.wait_recv()
    for c in gcopies:
        c.wait_send()
    t = gmid[...]
    for d in range(reps - 1):
        t = t + gz[d]
    gown[...] = t
    t = rmid[z]
    for d in range(reps - 1):
        t = t + rz[d]
    rmid[z] = t
    done.append(pltpu.make_async_copy(gown, gsum_ref, l_sem.at[10]))
    done.append(pltpu.make_async_copy(rmid.at[z], rsum_ref, l_sem.at[11]))
    wmine = wo.at[z // heads_dev, z % heads_dev]

    @pl.loop(0, rows_dev // step)
    def _(i):
        r = pl.ds(pl.multiple_of(i * step, step), step)
        t = wmine[r, :].astype(f32) + wup[z, r, :].astype(f32) + wdown[z, r, :].astype(f32)
        omat[r, :] = t
    done.append(pltpu.make_async_copy(omat, o_ref, l_sem.at[12]))
    for c in rzcopies:
        c.wait_send()
    for c in done[1:]:
        c.start()
    mine.wait()
    for c in pcopies:
        c.wait_recv()
    for src in range(eps):
        for m in range(3):
            for i in range(heads_dev):
                head = ((src % 2) * heads_dev + i) * (eps // 2) + src // 2
                mats[m, :, head * head_dim:(head + 1) * head_dim] = gath[src, :, m * slice_width + i * head_dim:m * slice_width + (i + 1) * head_dim].astype(f32)
    for m, ref in enumerate((q_ref, k_ref, v_ref)):
        done.append(pltpu.make_async_copy(mats.at[m], ref, l_sem.at[13 + m]))
        done[-1].start()
    for c in done:
        c.wait()
    qkv_sum.sent()
    out_sum.sent()
    for c in (*scopies, wcopy, *hcopies, *qcopies, *pcopies, *rcopies, *gzcopies):
        c.wait_send()


def last_sums(part, qkv_term, out_term, tokens, after_cot, gain_in, gains, router, rows_dev, reps, eps, cid):
    rows, width = tokens.shape
    f32, bf16 = jnp.float32, jnp.bfloat16
    heads_dev = out_term.shape[0]
    slices = qkv_term.shape[2]
    q = eps // 2
    half = rows // 2
    D, V = pltpu.SemaphoreType.DMA, pltpu.VMEM
    S = jax.ShapeDtypeStruct
    g8, rt = gains.shape, router.shape[2:]
    outs = (S((rows, width), f32), *[S((rows_dev, width), f32)] * 4, S(g8, f32), S(rt, f32))
    return pl.pallas_call(
        partial(last_kernel, reps, eps),
        out_shape=outs,
        in_specs=[pl.BlockSpec(memory_space=pl.ANY)] * 8,
        out_specs=[pl.BlockSpec(memory_space=pl.ANY)] * len(outs),
        scratch_shapes=[
            V((q, rows, width), bf16), V((q, rows, width), bf16), V((2, half, width), bf16), V((rows, width), bf16), V((rows, width), bf16),
            V((2, heads_dev, rows_dev, width), bf16), *[V((reps, rows_dev * eps, slices), bf16)] * 3, *[V((reps, rows_dev, width), bf16)] * 2,
            V((eps, rows_dev, slices), bf16), V((eps, rows_dev, slices), bf16),
            V((3, rows_dev, width), f32), V((rows_dev, width), f32), V((rows, width), bf16), V((rows, width), f32), V((1, width), f32),
            V(g8, f32), V((eps - 1, *g8), f32), V((reps - 1, *g8), f32), V(g8, f32),
            V(router.shape, f32), V((eps - 1, reps, *rt), f32), V((reps - 1, *rt), f32), V((reps, *rt), f32),
            D((17,)), D((4,)), D((4,)), D((2,)), D((2,)), D((2,)), D((2,)), D, D,
            *[D((reps,))] * 8, D((eps - 1,)), D((eps - 1,)),
            D((eps - 1,)), D((eps - 1,)), D((reps - 1,)), D((reps - 1,)), D((eps - 1,)), D((eps - 1,)), D((reps - 1,)), D((reps - 1,)),
        ],
        compiler_params=pltpu.CompilerParams(collective_id=cid, has_side_effects=True, vmem_limit_bytes=60 * 2**20),
    )(part, qkv_term, out_term, tokens, after_cot, gain_in, gains, router)


def join_kernel(count, *refs):
    z = lax.axis_index("rep")
    cols = refs[0].shape[2]
    down, outs = refs[2 * count], refs[2 * count + 1:]
    outs[2][...] = down[...].astype(outs[2].dtype)
    for n in range(2):
        ins, out = refs[n * count:(n + 1) * count], outs[n]
        for k in range(count):
            place = pl.multiple_of((z + count - k) % count * cols, cols)
            out[:, :, pl.ds(place, cols)] = ins[k][...].astype(out.dtype)


def join_columns(first, first_got, first_even, second, second_got, down):
    count, exp_dev, rows, cols = first.shape
    whole = jax.ShapeDtypeStruct((exp_dev, rows, cols * count), jnp.float32)

    def part(k):
        return pl.BlockSpec((None, 1, rows // 2, cols), lambda j, i: (k, j, i, 0))

    piece = pl.BlockSpec((1, rows // 2, cols), lambda j, i: (j, i, 0))
    tall = pl.BlockSpec((1, down.shape[1] // 2, down.shape[2]), lambda j, i: (j, i, 0))
    return pl.pallas_call(
        partial(join_kernel, count),
        grid=(exp_dev, 2),
        out_shape=(whole, whole, jax.ShapeDtypeStruct(down.shape, jnp.float32)),
        in_specs=[part(0)] + [part(k) if k % 2 else piece for k in range(1, count)] + [part(0)] + [piece] * (count - 1) + [tall],
        out_specs=[pl.BlockSpec((1, rows // 2, cols * count), lambda j, i: (j, i, 0))] * 2 + [tall],
    )(first, *[first_got if k % 2 else first_even[k // 2 - 1] for k in range(1, count)], second, *second_got, down)


def front_kernel(reps, eps, lengths_ref, tok_ref, cot_ref, wq_ref, wk_ref, wv_ref, wo_ref, gains_ref, router_ref, nums_ref, freq_ref,
                 cots_ref, router_all_ref, nums_all_ref, gsum_ref, normed_ref, pre_ref, qkv_ref, mixed_ref, wqkv_ref, wout_ref, turn_ref, attn_ref,
                 toks, normed, wraw, stage, wqkv, wz, wout, proj, qkv, mixed, turn, segs, part, sib_in, relay_in, xin, yin, acc,
                 gown, gz, gmid, gin, gall, nums, freq,
                 l_sem, o_sem, ws, wr, vs, vr, zs, zr, fs, fr, ts, tr, tcs, tcr, cps, cpr, ccs, ccr,
                 gzs, gzr, gps, gpr, rzs, rzr, rps, rpr, ns, nr, ss, sr, hs, hr, qs, qr, os, orr):
    f32, bf16 = jnp.float32, jnp.bfloat16
    z = lax.axis_index("rep")
    e = lax.axis_index("ep")
    core = e % 2
    chip = e // 2
    sib, chips = partners(e)
    rows, width = tok_ref.shape
    half = rows // 2
    rows_dev = wq_ref.shape[0]
    slice_width = mixed.shape[1]
    head_dim = turn.shape[2]
    heads_dev = slice_width // head_dim
    group_rows = eps * rows

    barrier = pltpu.get_barrier_semaphore()
    for d in range(1, eps):
        pl.semaphore_signal(barrier, inc=1, device_id={"rep": z, "ep": (e + d) % eps}, device_id_type=MESH)
    for d in range(1, reps):
        pl.semaphore_signal(barrier, inc=1, device_id={"rep": (z + d) % reps, "ep": e}, device_id_type=MESH)

    def local(src, dst, sem):
        c = pltpu.make_async_copy(src, dst, sem)
        c.start()
        return c

    raw = [local(r, wraw.at[m], l_sem.at[m]) for m, r in enumerate((wq_ref, wk_ref, wv_ref))]
    tok_own = local(tok_ref, toks.at[e], l_sem.at[3])
    wo_own = local(wo_ref, wz.at[z], l_sem.at[4])
    cot_own = local(cot_ref, cots_ref.at[z, e], l_sem.at[5])
    small = [
        local(gains_ref, gown, l_sem.at[6]),
        local(nums_ref, nums.at[e], l_sem.at[7]),
        local(freq_ref, freq, l_sem.at[8]),
        local(router_ref, router_all_ref.at[e, z], l_sem.at[9]),
    ]
    pl.semaphore_wait(barrier, eps - 1 + reps - 1)

    def remote(src, dst, send, recv, rep, ep):
        return pltpu.make_async_remote_copy(src_ref=src, dst_ref=dst, send_sem=send, recv_sem=recv,
                                            device_id={"rep": rep, "ep": ep}, device_id_type=MESH)

    def below(k, fn):
        @pl.when(z - k >= 0)
        def _():
            fn(z - k)

    def above(k, fn):
        @pl.when(z + k < reps)
        def _():
            fn(z + k)

    class Chain:
        def __init__(self, slot, send, recv):
            self.slot, self.send, self.recv = slot, send, recv

        def copy(self, src, g, up):
            d = 0 if up else 1
            return remote(src, self.slot(g), self.send.at[d, g], self.recv.at[g], z + 1 if up else z - 1, e)

        def begin(self, src):
            @pl.when(z < reps - 1)
            def _():
                self.copy(src, z, True).start()
            @pl.when(z > 0)
            def _():
                self.copy(src, z, False).start()

        def take(self, k, then=None):
            def from_below(g):
                self.copy(self.slot(g), g, True).wait_recv()
                if then is not None:
                    then(g)
            def from_above(g):
                self.copy(self.slot(g), g, False).wait_recv()
                if then is not None:
                    then(g)
            below(k, from_below)
            above(k, from_above)

        def forward(self, k):
            @pl.when((z - k >= 0) & (z < reps - 1))
            def _():
                self.copy(self.slot(z - k), z - k, True).start()
            @pl.when((z + k < reps) & (z > 0))
            def _():
                self.copy(self.slot(z + k), z + k, False).start()

        def arrive(self, k):
            self.take(k)
            self.forward(k)

        def sent(self):
            for g in range(reps):
                @pl.when((z < reps - 1) & (z >= g))
                def _():
                    self.copy(self.slot(g), g, True).wait_send()
                @pl.when((z > 0) & (z <= g))
                def _():
                    self.copy(self.slot(g), g, False).wait_send()

    class Spread:
        def __init__(self, slot, send, recv, csend, crecv):
            self.slot, self.send, self.recv, self.csend, self.crecv = slot, send, recv, csend, crecv

        def near(self, src, j):
            return remote(src, self.slot(e), self.send.at[j], self.recv.at[j], z, chips[j])

        def relay(self, j, source):
            p = self.slot(source).at[pl.ds(half * j, half)]
            return remote(p, p, self.send.at[2 + j], self.recv.at[2 + j], z, chips[1 - j])

        def core(self, src, j):
            return remote(src, self.slot(e if j == 0 else chips[j - 1]), self.csend.at[j], self.crecv.at[j], z, sib)

        def begin(self, src):
            self.near(src, 0).start()
            self.near(src, 1).start()
            self.core(src, 0).start()

        def pass_on(self):
            for j in range(2):
                self.near(self.slot(e), j).wait_recv()
                self.relay(j, chips[j]).start()
                self.core(self.slot(chips[j]), j + 1).start()

        def finish(self):
            for j in range(2):
                self.relay(j, chips[2]).wait_recv()
            self.core(self.slot(chips[2]), 3).start()

        def arrived(self):
            for j in range(4):
                self.core(self.slot(e), j).wait_recv()

        def sent(self):
            for j in range(2):
                self.near(self.slot(e), j).wait_send()
                self.relay(j, chips[j]).wait_send()
            for j in range(4):
                self.core(self.slot(e), j).wait_send()

    tok_spread = Spread(lambda who: toks.at[who], ts, tr, tcs, tcr)

    def cot_spread(g):
        return Spread(lambda who: cots_ref.at[g, who], cps.at[g], cpr.at[g], ccs.at[g], ccr.at[g])

    wo_chain = Chain(lambda g: wz.at[g], ws, wr)
    w_chain = Chain(lambda g: wqkv.at[g], vs, vr)
    cot_chain = Chain(lambda g: cots_ref.at[g, e], zs, zr)

    def cot_take(k):
        cot_chain.take(k, lambda g: cot_spread(g).begin(cots_ref.at[g, e]))

    def each(k, fn):
        below(k, lambda g: fn(cot_spread(g)))
        above(k, lambda g: fn(cot_spread(g)))

    gzc = [remote(gains_ref, gz.at[d - 1], gzs.at[d - 1], gzr.at[d - 1], (z + d) % reps, e) for d in range(1, reps)]
    rzc = [remote(router_ref, router_all_ref.at[e, z], rzs.at[d - 1], rzr.at[d - 1], (z + d) % reps, e) for d in range(1, reps)]
    nc = [remote(nums_ref, nums.at[e], ns.at[d - 1], nr.at[d - 1], z, (e + d) % eps) for d in range(1, eps)]
    for c in (*gzc, *rzc, *nc):
        c.start()
    wo_chain.begin(wo_ref)
    for m in range(3):
        raw[m].wait()
        for who in range(eps):
            for i in range(heads_dev):
                head = ((who % 2) * heads_dev + i) * (eps // 2) + who // 2
                at = m * slice_width + i * head_dim
                stage[who, :, at:at + head_dim] = wraw[m, :, head * head_dim:(head + 1) * head_dim]
    vc = [remote(stage.at[(e + d) % eps], wqkv.at[z, e], fs.at[d - 1], fr.at[d - 1], z, (e + d) % eps) for d in range(1, eps)]
    for c in vc:
        c.start()
    v_own = local(stage.at[e], wqkv.at[z, e], l_sem.at[10])
    tok_spread.begin(tok_ref)
    cot_chain.begin(cot_ref)
    cot_spread(z).begin(cot_ref)
    v_own.wait()
    for c in vc:
        c.wait_recv()
    w_chain.begin(wqkv.at[z])
    wo_chain.arrive(1)

    for c in gzc:
        c.wait_recv()
    small[0].wait()
    t = gown[...].astype(f32)
    for d in range(reps - 1):
        t = t + gz[d].astype(f32)
    gmid[...] = t.astype(bf16)
    gpc = [remote(gmid, gin.at[d - 1], gps.at[d - 1], gpr.at[d - 1], z, (e + d) % eps) for d in range(1, eps)]
    for c in gpc:
        c.start()
    small[3].wait()
    for c in rzc:
        c.wait_recv()
    rpc = [remote(router_all_ref.at[e], router_all_ref.at[e], rps.at[d - 1], rpr.at[d - 1], z, (e + d) % eps) for d in range(1, eps)]
    for c in rpc:
        c.start()
    tok_spread.pass_on()
    tok_spread.finish()
    wo_chain.arrive(2)
    cot_take(1)
    for c in gpc:
        c.wait_recv()
    t = gmid[...].astype(f32)
    for d in range(eps - 1):
        t = t + gin[d].astype(f32)
    gall[...] = t
    outs = [local(gall, gsum_ref, o_sem.at[0])]
    w_chain.arrive(1)
    wo_chain.arrive(3)
    cot_chain.forward(1)

    for c in small[1:3]:
        c.wait()
    for c in nc:
        c.wait_recv()
    outs.append(local(nums, nums_all_ref, o_sem.at[1]))
    deal = nums[:, 0, :]
    segment = jnp.zeros(deal.shape, jnp.int32)
    start = jnp.zeros(deal.shape, jnp.int32)
    end = 0
    for n in range(lengths_ref.shape[1]):
        end = end + lengths_ref[0, n]
        after = (deal >= end).astype(jnp.int32)
        segment = segment + after
        start = start + after * lengths_ref[0, n]
    position = (deal - start).astype(f32)
    segs[...] = segment.astype(f32)
    lane = lax.broadcasted_iota(jnp.int32, (rows, head_dim), 1)
    sign = jnp.where(lane < head_dim // 2, -1.0, 1.0)
    for n in range(eps):
        spot = jnp.broadcast_to(position[n:n + 1, :], (rows, rows)).T
        angle = spot * freq[0:1, :]
        here = pl.ds(n * rows, rows)
        turn[0, here, :] = jnp.cos(angle)
        turn[1, here, :] = jnp.sin(angle) * sign
    outs.append(local(turn, turn_ref, o_sem.at[2]))
    cot_spread(z).pass_on()

    tok_own.wait()
    tok_spread.arrived()
    gain_in = jnp.concatenate([gall[n:n + 1, :] for n in range(width // 128)], axis=1)
    step = 16
    for n in range(eps):
        @pl.loop(0, rows // step)
        def _(i):
            r = pl.ds(pl.multiple_of(i * step, step), step)
            t = toks[n, r, :].astype(f32)
            scale = lax.rsqrt(jnp.mean(t * t, axis=-1, keepdims=True) + norm_eps)
            normed[n, r, :] = (t * scale * gain_in).astype(bf16)
    outs.append(local(normed, normed_ref, o_sem.at[3]))
    w_chain.arrive(2)
    cot_take(2)
    cot_chain.forward(2)
    cot_spread(z).finish()

    wo_own.wait()
    wc = [remote(wz.at[(1 - core) * heads_dev + i], wout.at[i, core], os.at[i], orr.at[i], z, sib) for i in range(heads_dev)]
    wl = [local(wz.at[core * heads_dev + i], wout.at[i, core], l_sem.at[11 + i]) for i in range(heads_dev)]
    for c in wc:
        c.start()
    w_chain.arrive(3)
    each(1, lambda s: s.pass_on())


    @pl.loop(0, eps)
    def _(n):
        here = pl.ds(pl.multiple_of(n * rows, rows), rows)
        proj[here, :] = jnp.dot(normed[n], wqkv[...].reshape(width, 3 * slice_width), preferred_element_type=f32)
        for h in range(2 * heads_dev):
            cut = slice(h * head_dim, (h + 1) * head_dim)
            t = proj[here, cut]
            row = 2 * width // 128 + (0 if h < heads_dev else 1)
            t = t * lax.rsqrt(jnp.mean(t * t, axis=-1, keepdims=True) + norm_eps) * gall[row:row + 1, :]
            t = t * turn[0, here, :] + pltpu.roll(t, head_dim // 2, 1) * turn[1, here, :]
            qkv[here, cut] = t.astype(bf16)
        tail = slice(2 * slice_width, 3 * slice_width)
        qkv[here, tail] = proj[here, tail].astype(bf16)

    outs.append(local(proj.at[:, pl.ds(0, 2 * slice_width)], pre_ref, o_sem.at[4]))
    outs.append(local(qkv, qkv_ref, o_sem.at[5]))
    outs.append(local(wqkv, wqkv_ref, o_sem.at[6]))

    seg_row = jnp.concatenate([segs[n:n + 1, :] for n in range(eps)], axis=1)
    block = 2 * rows

    def attend(h):
        cut = slice(h * head_dim, (h + 1) * head_dim)
        kcut = slice(slice_width + h * head_dim, slice_width + (h + 1) * head_dim)
        vcut = slice(2 * slice_width + h * head_dim, 2 * slice_width + (h + 1) * head_dim)
        for n in range(eps // 2):
            here = pl.ds(n * block, block)
            s = lax.dot_general(qkv[here, cut], qkv[:, kcut], NT, preferred_element_type=f32) * (head_dim ** -0.5)
            seg_col = jnp.concatenate(
                [jnp.broadcast_to(segs[2 * n + j:2 * n + j + 1, :], (rows, rows)).T[:, 0:1] for j in range(2)], axis=0)
            s = jnp.where(seg_col == seg_row, s, masked_score)
            p = jnp.exp(s - jnp.max(s, axis=-1, keepdims=True))
            p = (p / jnp.sum(p, axis=-1, keepdims=True)).astype(bf16)
            mixed[here, cut] = jnp.dot(p, qkv[:, vcut], preferred_element_type=f32).astype(bf16)

    each(1, lambda s: s.finish())
    attend(0)
    each(2, lambda s: s.pass_on())
    for h in range(1, heads_dev):
        attend(h)
    outs.append(local(mixed, mixed_ref, o_sem.at[7]))
    for c in wl:
        c.wait()
    for c in wc:
        c.wait_recv()
    outs.append(local(wout, wout_ref, o_sem.at[8]))

    order = (chips[2] // 2, chips[0] // 2, chips[1] // 2, chip)
    scopies = [remote(part.at[q, 1 - core], sib_in.at[q], ss.at[n], sr.at[n], z, sib) for n, q in enumerate(order)]
    for n in range(eps // 2):
        q = order[n]
        here = pl.ds(pl.multiple_of(q * block, block), block)
        t = jnp.dot(mixed[here, :], wout[...].reshape(slice_width, width), preferred_element_type=f32)
        part[q] = t.astype(bf16).reshape(2, rows, width)
        scopies[n].start()

    cot_take(3)

    def add(out, terms, count):
        @pl.loop(0, count // step)
        def _(i):
            r = pl.ds(pl.multiple_of(i * step, step), step)
            t = terms[0][r, :].astype(f32)
            for other in terms[1:]:
                t = t + other[r, :].astype(f32)
            out[r, :] = t.astype(out.dtype)

    lower, upper = pl.ds(0, half), pl.ds(half, half)
    first = part.at[order[0], core]
    hcopies = [remote(first.at[(lower, upper)[j]], relay_in.at[j], hs.at[j], hr.at[j], z, chips[j]) for j in range(2)]
    qcopies = [remote(part.at[order[1 + j], core], (xin, yin)[j], qs.at[j], qr.at[j], z, chips[j]) for j in range(2)]
    scopies[0].wait_recv()
    add(first, (first, sib_in.at[order[0]]), rows)
    for c in hcopies:
        c.start()
    for j in range(2):
        mine, other = part.at[order[1 + j], core], sib_in.at[order[1 + j]]
        scopies[1 + j].wait_recv()
        direct, through = ((lower, upper), (upper, lower))[j]
        add(mine.at[direct], (mine.at[direct], other.at[direct]), half)
        hcopies[1 - j].wait_recv()
        add(mine.at[through], (mine.at[through], other.at[through], relay_in.at[1 - j]), half)
        qcopies[j].start()
    scopies[3].wait_recv()
    each(3, lambda s: s.pass_on())
    each(2, lambda s: s.finish())
    for c in qcopies:
        c.wait_recv()
    add(acc, (part.at[chip, core], sib_in.at[chip], xin, yin, toks.at[e]), rows)
    outs.append(local(acc, attn_ref, o_sem.at[9]))
    each(3, lambda s: s.finish())
    cot_own.wait()
    for g in range(reps):
        cot_spread(g).arrived()
        cot_spread(g).sent()
    for chain in (wo_chain, w_chain, cot_chain):
        chain.sent()
    tok_spread.sent()
    for c in rpc:
        c.wait_recv()
    for c in (*gzc, *rzc, *nc, *vc, *gpc, *rpc, *wc, *scopies, *hcopies, *qcopies):
        c.wait_send()
    for c in outs:
        c.wait()


def front(lengths, tokens, cot, wq, wk, wv, wo, gains, router, nums, freq, heads_dev, reps, eps, cid):
    rows, width = tokens.shape
    rows_dev = wq.shape[0]
    f32, bf16, i32 = jnp.float32, jnp.bfloat16, jnp.int32
    head_dim = freq.shape[1]
    sw = heads_dev * head_dim
    gr = eps * rows
    half = rows // 2
    q = eps // 2
    S, V, D = jax.ShapeDtypeStruct, pltpu.VMEM, pltpu.SemaphoreType.DMA
    outs = (
        S((reps, eps, rows, width), bf16), S((eps, reps, *router.shape), bf16), S((eps, *nums.shape), i32), S(gains.shape, f32),
        S((eps, rows, width), bf16), S((gr, 2 * sw), f32), S((gr, 3 * sw), bf16), S((gr, sw), bf16),
        S((reps, eps, rows_dev, 3 * sw), bf16), S((heads_dev, 2, rows_dev, width), bf16), S((2, gr, head_dim), f32), S((rows, width), f32),
    )
    return pl.pallas_call(
        partial(front_kernel, reps, eps),
        out_shape=outs,
        in_specs=[pl.BlockSpec(memory_space=pltpu.SMEM)] + [pl.BlockSpec(memory_space=pl.ANY)] * 10,
        out_specs=[pl.BlockSpec(memory_space=pl.ANY)] * len(outs),
        scratch_shapes=[
            V((eps, rows, width), bf16), V((eps, rows, width), bf16), V((3, rows_dev, width), bf16), V((eps, rows_dev, 3 * sw), bf16),
            V((reps, eps, rows_dev, 3 * sw), bf16), V((reps, rows_dev, width), bf16), V((heads_dev, 2, rows_dev, width), bf16),
            V((gr, 3 * sw), f32), V((gr, 3 * sw), bf16), V((gr, sw), bf16), V((2, gr, head_dim), f32), V((eps, rows), f32),
            V((q, 2, rows, width), bf16), V((q, rows, width), bf16), V((2, half, width), bf16), V((rows, width), bf16), V((rows, width), bf16),
            V((rows, width), f32),
            V(gains.shape, bf16), V((reps - 1, *gains.shape), bf16), V(gains.shape, bf16), V((eps - 1, *gains.shape), bf16), V(gains.shape, f32),
            V((eps, *nums.shape), i32), V(freq.shape, f32),
            D((16,)), D((16,)), D((2, reps)), D((reps,)), D((2, reps)), D((reps,)), D((2, reps)), D((reps,)), D((eps - 1,)), D((eps - 1,)),
            D((4,)), D((4,)), D((4,)), D((4,)), D((reps, 4)), D((reps, 4)), D((reps, 4)), D((reps, 4)),
            D((reps - 1,)), D((reps - 1,)), D((eps - 1,)), D((eps - 1,)), D((reps - 1,)), D((reps - 1,)), D((eps - 1,)), D((eps - 1,)),
            D((eps - 1,)), D((eps - 1,)), D((4,)), D((4,)), D((2,)), D((2,)), D((2,)), D((2,)), D((2,)), D((2,)),
        ],
        compiler_params=pltpu.CompilerParams(collective_id=cid, has_side_effects=True, vmem_limit_bytes=56 * 2**20),
    )(lengths, tokens, cot, wq, wk, wv, wo, gains, router, nums, freq)


def on_device_split(
    tokens,
    cotangent,
    query_weight,
    key_weight,
    value_weight,
    output_weight,
    router_weight,
    gains,
    expert_gate,
    expert_up,
    expert_down,
    lengths,
    deal,
    routes,
    priority,
):
    bf16, f32 = jnp.bfloat16, jnp.float32
    tok_dev, width = tokens.shape
    ep_count, rep_count = lax.axis_size("ep"), lax.axis_size("rep")
    ep_index, rep_index = lax.axis_index("ep"), lax.axis_index("rep")
    exp_dev, _, ff_width = expert_gate.shape
    top_count = routes.shape[1]
    experts_all = exp_dev * ep_count
    group_rows = tok_dev * ep_count
    capacity = 5 * tok_dev * top_count // (4 * exp_dev)
    head_dim = HD
    heads_dev = width // head_dim // ep_count
    slice_width = heads_dev * head_dim
    rows_dev = query_weight.shape[0]

    gains_dev = gains.shape[0]
    gain_rows = -(-gains_dev * rep_count * ep_count // 2048) * 16
    gains_placed = lax.dynamic_update_slice_in_dim(
        jnp.zeros((gain_rows * 128,), bf16),
        gains,
        (rep_index * ep_count + ep_index) * gains_dev,
        axis=0,
    ).reshape(gain_rows, 128)
    router_rows = router_weight.size // 128
    router_placed = jnp.pad(router_weight.reshape(router_rows, 128), ((0, -router_rows % 16), (0, 0)))
    numbers = jnp.concatenate([deal[None], priority[None], routes.T])
    numbers = jnp.pad(numbers, ((0, -numbers.shape[0] % 8), (0, 0)))
    frequency = rope_base ** (
        -2.0 * jnp.arange(head_dim // 2, dtype=jnp.float32) / head_dim
    )
    (
        cot_all,
        router_all,
        numbers_all,
        gains_all,
        normed_group,
        pre,
        qkv_low,
        mixed_low,
        qkv_slice,
        out_slice,
        turn,
        after_attn,
    ) = front(
        lengths,
        tokens,
        cotangent,
        query_weight,
        key_weight,
        value_weight,
        output_weight,
        gains_placed,
        router_placed,
        numbers,
        jnp.concatenate([frequency, frequency]).reshape(1, head_dim),
        heads_dev,
        rep_count,
        ep_count,
        0,
    )
    gains_float = gains_all.reshape(-1)
    gain_in = gains_float[:width]
    gain_mid = gains_float[width : 2 * width]
    router_full = (
        router_all[:, :, :router_rows].transpose(1, 0, 2, 3).reshape(width, experts_all)
    )
    deal_all = numbers_all[:, 0].reshape(-1)
    priority_all = numbers_all[:, 1].reshape(-1)
    routes_all = numbers_all[:, 2 : 2 + top_count].transpose(0, 2, 1).reshape(group_rows, top_count)
    segment_all, _ = placement(deal_all, lengths[0])
    normed_group = normed_group.reshape(group_rows, width)
    qkv_slice = qkv_slice.reshape(width, 3 * slice_width)
    mid_low = rms_scale(after_attn, gain_mid).astype(bf16)

    logits = jnp.dot(mid_low, router_full, preferred_element_type=f32)
    expert_ids = jnp.arange(experts_all, dtype=jnp.int32)
    member = (routes[:, :, None] == expert_ids[None, None, :]).astype(f32)
    named = jnp.sum(member, axis=1)
    lifted = jnp.where(named > 0, logits, masked_score)
    lifted = jnp.exp(lifted - jnp.max(lifted, axis=-1, keepdims=True)) * named
    gate_dense = lifted / jnp.sum(lifted, axis=-1, keepdims=True)
    onehot_all = jnp.sum(
        (routes_all[:, :, None] == expert_ids[None, None, :]).astype(bf16), axis=1
    )
    earlier = (priority_all[None, :] < priority[:, None]).astype(bf16)
    slots = jnp.dot(earlier, onehot_all, preferred_element_type=f32)
    kept_dense = named * (slots < capacity).astype(f32)
    pair_weight = gate_dense * kept_dense

    weight_high = pair_weight.astype(bf16)
    weight_low = (pair_weight - weight_high.astype(f32)).astype(bf16)
    side = jnp.concatenate(
        [weight_high, weight_low, jnp.zeros((tok_dev, 128 - 2 * experts_all), bf16)], axis=1
    )
    row_sum, moe_sum, gate_term, up_term, down_term, gate_got = moe(
        jnp.concatenate([mid_low, side], axis=1),
        cot_all,
        expert_gate,
        expert_up,
        expert_down,
        experts_all,
        3,
    )
    moe_out = moe_sum.astype(f32)
    block_out = (after_attn + moe_out).astype(bf16)

    def from_below(part, k):
        return lax.ppermute(part, "rep", [(i, (i + k) % rep_count) for i in range(rep_count)])

    gate_pieces = [from_below(gate_term[k], k) for k in range(2, rep_count, 2)]
    up_pieces = [from_below(up_term[k], k) for k in range(1, rep_count)]

    out_grad = cotangent.astype(f32)
    gate_cot = row_sum[:, width : width + experts_all].astype(f32) * kept_dense
    chosen_cot = gate_dense * (gate_cot - jnp.sum(gate_dense * gate_cot, axis=-1, keepdims=True))
    logit_cot = chosen_cot.astype(bf16)
    mid_cot = row_sum[:, :width].astype(f32) + jnp.dot(
        logit_cot, router_full.T, preferred_element_type=f32
    )
    router_term = jnp.dot(mid_low.T, logit_cot, preferred_element_type=f32)
    _, mid_pull = jax.vjp(rms_scale, after_attn, gain_mid)
    after_extra, gain_mid_cot = mid_pull(mid_cot)
    after_cot = out_grad + after_extra
    normed_part, qkv_term, output_term, head_gains = attention_back(
        after_cot.astype(bf16),
        out_slice,
        mixed_low,
        qkv_low,
        pre,
        turn,
        segment_all.astype(f32).reshape(ep_count, tok_dev),
        gains_all,
        normed_group,
        qkv_slice,
        rep_count,
        ep_count,
        1,
    )
    gains_term = jnp.concatenate(
        [
            jnp.zeros((width,), f32),
            gain_mid_cot,
            head_gains[:2].reshape(-1),
            jnp.zeros((6 * width - 2 * head_dim,), f32),
        ]
    ).reshape(8, width)
    router_parts = jnp.pad(
        router_term.reshape(rep_count, ep_count, router_rows, 128),
        ((0, 0), (0, 0), (0, -router_rows % 8), (0, 0)),
    )
    input_grad, query_sum, key_sum, value_sum, output_sum, gains_all, router_own = last_sums(
        normed_part,
        qkv_term,
        output_term,
        tokens,
        after_cot,
        gain_in.reshape(1, width),
        gains_term,
        router_parts,
        rows_dev,
        rep_count,
        ep_count,
        4,
    )
    gains_sum = lax.dynamic_slice_in_dim(
        gains_all.reshape(-1), (rep_index * ep_count + ep_index) * gains_dev, gains_dev
    )
    router_sum = router_own[:router_rows].reshape(rows_dev, experts_all)
    gate_w_grad, up_w_grad, down_w_grad = join_columns(
        gate_term, gate_got, gate_pieces, up_term, up_pieces, down_term
    )
    return (
        block_out,
        input_grad,
        query_sum,
        key_sum,
        value_sum,
        output_sum,
        router_sum,
        gains_sum,
        gate_w_grad,
        up_w_grad,
        down_w_grad,
    )


def solution(mesh):
    placed = (
        P(("rep", "ep"), None),
        P(("rep", "ep"), None),
        P(("rep", "ep"), None),
        P(("rep", "ep"), None),
        P(("rep", "ep"), None),
        P(("rep", "ep"), None),
        P(("rep", "ep"), None),
        P(("rep", "ep")),
        P("ep", None, None),
        P("ep", None, None),
        P("ep", None, None),
        P("rep", None),
        P(("rep", "ep")),
        P(("rep", "ep"), None),
        P(("rep", "ep")),
    )
    return jax.shard_map(
        on_device_split if mesh.shape["rep"] == 4 else on_device_general,
        mesh=mesh,
        in_specs=placed,
        out_specs=(
            P(("rep", "ep"), None),
            P(("rep", "ep"), None),
            P(("rep", "ep"), None),
            P(("rep", "ep"), None),
            P(("rep", "ep"), None),
            P(("rep", "ep"), None),
            P(("rep", "ep"), None),
            P(("rep", "ep")),
            P("ep", "rep", None),
            P("ep", "rep", None),
            P("ep", "rep", None),
        ),
        check_vma=False,
    )
```

```python
from functools import partial

import jax
import jax.numpy as jnp
from jax import lax
from jax.experimental import pallas as pl
from jax.experimental.pallas import tpu as pltpu
from jax.sharding import PartitionSpec as P

HD = 128


norm_eps = 1e-06
rope_base = 10000.0
masked_score = -1e30
highest = lax.Precision.HIGHEST


def rms_scale(values, gain_vec):
    return (
        values * lax.rsqrt(jnp.mean(values * values, axis=-1, keepdims=True) + norm_eps) * gain_vec
    )


def rotate(values, positions):
    half_width = values.shape[-1] // 2
    frequency = rope_base ** (-2.0 * jnp.arange(half_width, dtype=jnp.float32) / values.shape[-1])
    angles = positions.astype(jnp.float32)[:, None] * frequency[None, :]
    cosine = jnp.cos(angles)[:, None, :]
    sine_part = jnp.sin(angles)[:, None, :]
    low_half = values[..., :half_width]
    high_half = values[..., half_width:]
    return jnp.concatenate(
        [low_half * cosine - high_half * sine_part, high_half * cosine + low_half * sine_part],
        axis=-1,
    )


def placement(deal_rows, lengths_row):
    seq_ends = jnp.cumsum(lengths_row)
    is_after = (seq_ends[None, :] <= deal_rows[:, None]).astype(jnp.int32)
    segment = jnp.sum(is_after, axis=1)
    seq_start = jnp.sum(is_after * lengths_row[None, :], axis=1)
    return (segment, deal_rows - seq_start)


def rope_norm(projected, gain_vec, positions):
    return rotate(rms_scale(projected, gain_vec), positions)


def attend_forward(parts, same_seq, score_scale):
    head_query, head_key, head_value = parts
    scores = (
        jnp.einsum("thd,shd->hts", head_query, head_key, preferred_element_type=jnp.float32)
        * score_scale
    )
    scores = jnp.where(same_seq[None], scores, masked_score)
    top_score = jnp.max(scores, axis=-1, keepdims=True)
    lifted = jnp.exp(scores - top_score)
    total_sum = jnp.sum(lifted, axis=-1, keepdims=True)
    prob_low = (lifted / total_sum).astype(jnp.bfloat16)
    mixed_out = jnp.einsum("hts,shd->thd", prob_low, head_value, preferred_element_type=jnp.float32)
    return (mixed_out, top_score, total_sum)


def attend_backward(parts, same_seq, score_scale):
    head_query, head_key, head_value, head_grad, top_score, total_sum = parts
    scores = (
        jnp.einsum("thd,shd->hts", head_query, head_key, preferred_element_type=jnp.float32)
        * score_scale
    )
    scores = jnp.where(same_seq[None], scores, masked_score)
    prob_full = jnp.exp(scores - top_score) / total_sum
    prob_low = prob_full.astype(jnp.bfloat16)
    prob_grad = jnp.einsum(
        "thd,shd->hts", head_grad, head_value, preferred_element_type=jnp.float32
    )
    row_dot = jnp.sum(prob_full * prob_grad, axis=-1, keepdims=True)
    score_grad = (prob_full * (prob_grad - row_dot)).astype(jnp.bfloat16)
    query_grad = (
        jnp.einsum("hts,shd->thd", score_grad, head_key, preferred_element_type=jnp.float32)
        * score_scale
    )
    key_grad = (
        jnp.einsum("hts,thd->shd", score_grad, head_query, preferred_element_type=jnp.float32)
        * score_scale
    )
    value_grad = jnp.einsum("hts,thd->shd", prob_low, head_grad, preferred_element_type=jnp.float32)
    return (query_grad, key_grad, value_grad)


def on_device_general(
    tokens,
    cotangent,
    query_weight,
    key_weight,
    value_weight,
    output_weight,
    router_weight,
    gains,
    expert_gate,
    expert_up,
    expert_down,
    lengths,
    deal,
    routes,
    priority,
):
    tok_dev, width = tokens.shape
    ep_count = lax.axis_size("ep")
    ep_index = lax.axis_index("ep")
    exp_dev = expert_gate.shape[0]
    top_count = routes.shape[1]
    experts_all = exp_dev * ep_count
    group_rows = tok_dev * ep_count
    send_most = min(tok_dev, 3 * tok_dev * top_count // (2 * experts_all))
    capacity = 5 * tok_dev * top_count // (4 * exp_dev)
    head_dim = HD
    head_count = width // head_dim
    per_group = min(head_count, 4)
    group_count = head_count // per_group
    score_scale = head_dim ** (-0.5)
    query_full, key_full, value_full, output_full, router_full, gains_full = (
        lax.all_gather(query_weight, ("rep", "ep"), axis=0, tiled=True),
        lax.all_gather(key_weight, ("rep", "ep"), axis=0, tiled=True),
        lax.all_gather(value_weight, ("rep", "ep"), axis=0, tiled=True),
        lax.all_gather(output_weight, ("rep", "ep"), axis=0, tiled=True),
        lax.all_gather(router_weight, ("rep", "ep"), axis=0, tiled=True),
        lax.all_gather(gains, ("rep", "ep"), axis=0, tiled=True),
    )
    gains_float = gains_full.astype(jnp.float32)
    gain_in = gains_float[:width]
    gain_mid = gains_float[width : 2 * width]
    gain_query = gains_float[2 * width : 2 * width + head_dim]
    gain_key = gains_float[2 * width + head_dim :]
    deal_all, priority_all, routes_all = (
        lax.all_gather(deal, "ep", axis=0, tiled=True),
        lax.all_gather(priority, "ep", axis=0, tiled=True),
        lax.all_gather(routes, "ep", axis=0, tiled=True),
    )
    segment_all, position_all = placement(deal_all, lengths[0])
    segment_own = lax.dynamic_slice_in_dim(segment_all, ep_index * tok_dev, tok_dev)
    position_own = lax.dynamic_slice_in_dim(position_all, ep_index * tok_dev, tok_dev)
    residual = tokens.astype(jnp.float32)
    normed_low = rms_scale(residual, gain_in).astype(jnp.bfloat16)
    query_pre = jnp.dot(normed_low, query_full, preferred_element_type=jnp.float32).reshape(
        tok_dev, head_count, head_dim
    )
    key_pre = jnp.dot(normed_low, key_full, preferred_element_type=jnp.float32).reshape(
        tok_dev, head_count, head_dim
    )
    value_low = jnp.dot(normed_low, value_full, preferred_element_type=jnp.float32).astype(
        jnp.bfloat16
    )
    query_low = rope_norm(query_pre, gain_query, position_own).astype(jnp.bfloat16)
    key_low = (
        rope_norm(key_pre, gain_key, position_own).astype(jnp.bfloat16).reshape(tok_dev, width)
    )
    key_group, value_group = (
        lax.all_gather(key_low, "ep", axis=0, tiled=True),
        lax.all_gather(value_low, "ep", axis=0, tiled=True),
    )
    same_seq = segment_own[:, None] == segment_all[None, :]
    query_heads = query_low.reshape(tok_dev, group_count, per_group, head_dim).transpose(1, 0, 2, 3)
    key_heads = key_group.reshape(group_rows, group_count, per_group, head_dim).transpose(
        1, 0, 2, 3
    )
    value_heads = value_group.reshape(group_rows, group_count, per_group, head_dim).transpose(
        1, 0, 2, 3
    )
    mixed_heads, top_heads, total_heads = lax.map(
        partial(attend_forward, same_seq=same_seq, score_scale=score_scale),
        (query_heads, key_heads, value_heads),
    )
    mixed_low = mixed_heads.transpose(1, 0, 2, 3).reshape(tok_dev, width).astype(jnp.bfloat16)
    after_attn = residual + jnp.dot(mixed_low, output_full, preferred_element_type=jnp.float32)
    mid_low = rms_scale(after_attn, gain_mid).astype(jnp.bfloat16)
    logits = jnp.dot(mid_low, router_full, preferred_element_type=jnp.float32)
    chosen = jnp.take_along_axis(logits, routes, axis=1)
    gate_prob = jax.nn.softmax(chosen, axis=-1)
    expert_ids = jnp.arange(experts_all, dtype=jnp.int32)
    onehot_all = jnp.sum(
        (routes_all[:, :, None] == expert_ids[None, None, :]).astype(jnp.float32), axis=1
    )
    earlier = (priority_all[None, :] < priority_all[:, None]).astype(jnp.float32)
    slot_all = jnp.take_along_axis(
        jnp.dot(earlier, onehot_all, precision=highest), routes_all, axis=1
    ).astype(jnp.int32)
    row_ids = jnp.arange(tok_dev, dtype=jnp.int32)
    lower_tri = (row_ids[:, None] > row_ids[None, :]).astype(jnp.float32)
    before = jnp.einsum(
        "ij,dje->die",
        lower_tri,
        onehot_all.reshape(ep_count, tok_dev, experts_all),
        precision=highest,
    ).reshape(group_rows, experts_all)
    place_all = jnp.take_along_axis(before, routes_all, axis=1).astype(jnp.int32)
    kept_all = slot_all < capacity
    kept_own = lax.dynamic_slice_in_dim(kept_all, ep_index * tok_dev, tok_dev)
    place_own = lax.dynamic_slice_in_dim(place_all, ep_index * tok_dev, tok_dev)
    buffer_index = (routes * send_most + place_own).reshape(-1)
    rows_out = jnp.where(
        kept_own[:, :, None], mid_low[:, None, :], jnp.zeros((), jnp.bfloat16)
    ).reshape(tok_dev * top_count, width)
    send_rows = (
        jnp.zeros((experts_all * send_most, width), jnp.bfloat16)
        .at[buffer_index]
        .set(rows_out)
        .reshape(experts_all, send_most, width)
    )
    received = lax.all_to_all(send_rows, "ep", split_axis=0, concat_axis=1, tiled=True)
    gate_part = jnp.einsum(
        "erd,edf->erf", received, expert_gate, preferred_element_type=jnp.float32
    )
    up_part = jnp.einsum("erd,edf->erf", received, expert_up, preferred_element_type=jnp.float32)
    hidden = (jax.nn.silu(gate_part) * up_part).astype(jnp.bfloat16)
    result = jnp.einsum(
        "erf,efd->erd", hidden, expert_down, preferred_element_type=jnp.float32
    ).astype(jnp.bfloat16)
    returned = lax.all_to_all(result, "ep", split_axis=1, concat_axis=0, tiled=True)
    pair_out = returned.reshape(experts_all * send_most, width)[buffer_index].reshape(
        tok_dev, top_count, width
    )
    pair_weight = gate_prob * kept_own.astype(jnp.float32)
    moe_out = jnp.einsum("tk,tkd->td", pair_weight, pair_out, preferred_element_type=jnp.float32)
    block_out = (after_attn + moe_out).astype(jnp.bfloat16)
    out_grad = cotangent.astype(jnp.float32)
    pair_gate_grad = kept_own.astype(jnp.float32) * jnp.einsum(
        "tkd,td->tk", pair_out, out_grad, preferred_element_type=jnp.float32
    )
    pair_grad = (
        (pair_weight[:, :, None] * out_grad[:, None, :])
        .astype(jnp.bfloat16)
        .reshape(tok_dev * top_count, width)
    )
    grad_send = (
        jnp.zeros((experts_all * send_most, width), jnp.bfloat16)
        .at[buffer_index]
        .set(pair_grad)
        .reshape(experts_all, send_most, width)
    )
    grad_received = lax.all_to_all(grad_send, "ep", split_axis=0, concat_axis=1, tiled=True)
    hidden_grad = jnp.einsum(
        "erd,efd->erf", grad_received, expert_down, preferred_element_type=jnp.float32
    )
    _, silu_pull = jax.vjp(lambda gate_in, up_in: jax.nn.silu(gate_in) * up_in, gate_part, up_part)
    gate_part_grad, up_part_grad = silu_pull(hidden_grad)
    gate_low_grad = gate_part_grad.astype(jnp.bfloat16)
    up_low_grad = up_part_grad.astype(jnp.bfloat16)
    down_term = jnp.einsum(
        "erf,erd->efd", hidden, grad_received, preferred_element_type=jnp.float32
    )
    gate_term = jnp.einsum(
        "erd,erf->edf", received, gate_low_grad, preferred_element_type=jnp.float32
    )
    up_term = jnp.einsum("erd,erf->edf", received, up_low_grad, preferred_element_type=jnp.float32)
    rows_grad = (
        jnp.einsum("erf,edf->erd", gate_low_grad, expert_gate, preferred_element_type=jnp.float32)
        + jnp.einsum("erf,edf->erd", up_low_grad, expert_up, preferred_element_type=jnp.float32)
    ).astype(jnp.bfloat16)
    back_rows = lax.all_to_all(rows_grad, "ep", split_axis=1, concat_axis=0, tiled=True)
    mid_grad = jnp.sum(
        back_rows.reshape(experts_all * send_most, width)[buffer_index]
        .reshape(tok_dev, top_count, width)
        .astype(jnp.float32),
        axis=1,
    )
    gate_w_grad, up_w_grad, down_w_grad = (
        lax.psum_scatter(
            gate_term.astype(jnp.bfloat16), "rep", scatter_dimension=1, tiled=True
        ).astype(jnp.float32),
        lax.psum_scatter(
            up_term.astype(jnp.bfloat16), "rep", scatter_dimension=1, tiled=True
        ).astype(jnp.float32),
        lax.psum_scatter(
            down_term.astype(jnp.bfloat16), "rep", scatter_dimension=1, tiled=True
        ).astype(jnp.float32),
    )
    _, soft_pull = jax.vjp(lambda values: jax.nn.softmax(values, axis=-1), chosen)
    (chosen_grad,) = soft_pull(pair_gate_grad)
    onehot_own = (routes[:, :, None] == expert_ids[None, None, :]).astype(jnp.float32)
    logit_grad = jnp.einsum("tk,tke->te", chosen_grad, onehot_own).astype(jnp.bfloat16)
    mid_grad = mid_grad + jnp.dot(logit_grad, router_full.T, preferred_element_type=jnp.float32)
    router_term = jnp.dot(mid_low.T, logit_grad, preferred_element_type=jnp.float32)
    _, mid_pull = jax.vjp(rms_scale, after_attn, gain_mid)
    after_extra, gain_mid_grad = mid_pull(mid_grad)
    after_grad = out_grad + after_extra
    attn_low_grad = after_grad.astype(jnp.bfloat16)
    output_term = jnp.dot(mixed_low.T, attn_low_grad, preferred_element_type=jnp.float32)
    mixed_grad = jnp.dot(attn_low_grad, output_full.T, preferred_element_type=jnp.float32).astype(
        jnp.bfloat16
    )
    mixed_grad_heads = mixed_grad.reshape(tok_dev, group_count, per_group, head_dim).transpose(
        1, 0, 2, 3
    )
    query_grad_h, key_grad_h, value_grad_h = lax.map(
        partial(attend_backward, same_seq=same_seq, score_scale=score_scale),
        (query_heads, key_heads, value_heads, mixed_grad_heads, top_heads, total_heads),
    )
    query_grad_own = query_grad_h.transpose(1, 0, 2, 3).reshape(tok_dev, head_count, head_dim)
    key_grad_group = key_grad_h.transpose(1, 0, 2, 3).reshape(group_rows, width)
    value_grad_group = value_grad_h.transpose(1, 0, 2, 3).reshape(group_rows, width)
    key_sum, value_sum = (
        lax.psum_scatter(
            key_grad_group.astype(jnp.bfloat16), "ep", scatter_dimension=0, tiled=True
        ).astype(jnp.float32),
        lax.psum_scatter(
            value_grad_group.astype(jnp.bfloat16), "ep", scatter_dimension=0, tiled=True
        ).astype(jnp.float32),
    )
    value_low_grad = value_sum.astype(jnp.bfloat16)
    _, query_pull = jax.vjp(
        lambda projected, gain_vec: rope_norm(projected, gain_vec, position_own),
        query_pre,
        gain_query,
    )
    query_pre_grad, gain_query_grad = query_pull(query_grad_own)
    _, key_pull = jax.vjp(
        lambda projected, gain_vec: rope_norm(projected, gain_vec, position_own), key_pre, gain_key
    )
    key_pre_grad, gain_key_grad = key_pull(key_sum.reshape(tok_dev, head_count, head_dim))
    query_low_grad = query_pre_grad.reshape(tok_dev, width).astype(jnp.bfloat16)
    key_low_grad = key_pre_grad.reshape(tok_dev, width).astype(jnp.bfloat16)
    normed_grad = jnp.dot(query_low_grad, query_full.T, preferred_element_type=jnp.float32)
    normed_grad = normed_grad + jnp.dot(
        key_low_grad, key_full.T, preferred_element_type=jnp.float32
    )
    normed_grad = normed_grad + jnp.dot(
        value_low_grad, value_full.T, preferred_element_type=jnp.float32
    )
    query_term = jnp.dot(normed_low.T, query_low_grad, preferred_element_type=jnp.float32)
    key_term = jnp.dot(normed_low.T, key_low_grad, preferred_element_type=jnp.float32)
    value_term = jnp.dot(normed_low.T, value_low_grad, preferred_element_type=jnp.float32)
    _, input_pull = jax.vjp(rms_scale, residual, gain_in)
    input_extra, gain_in_grad = input_pull(normed_grad)
    input_grad = after_grad + input_extra
    gains_term = jnp.concatenate([gain_in_grad, gain_mid_grad, gain_query_grad, gain_key_grad])
    query_sum, key_total, value_total, output_sum, router_sum, gains_sum = (
        lax.psum_scatter(query_term, ("rep", "ep"), scatter_dimension=0, tiled=True),
        lax.psum_scatter(key_term, ("rep", "ep"), scatter_dimension=0, tiled=True),
        lax.psum_scatter(value_term, ("rep", "ep"), scatter_dimension=0, tiled=True),
        lax.psum_scatter(output_term, ("rep", "ep"), scatter_dimension=0, tiled=True),
        lax.psum_scatter(router_term, ("rep", "ep"), scatter_dimension=0, tiled=True),
        lax.psum_scatter(gains_term, ("rep", "ep"), scatter_dimension=0, tiled=True),
    )
    return (
        block_out,
        input_grad,
        query_sum,
        key_total,
        value_total,
        output_sum,
        router_sum,
        gains_sum,
        gate_w_grad,
        up_w_grad,
        down_w_grad,
    )


MESH = pl.DeviceIdType.MESH


def partners(e):
    sib = e + 1 - 2 * (e % 2)
    xn = e + 2 - 4 * ((e // 2) % 2)
    yn = e + 4 - 8 * ((e // 4) % 2)
    dg = xn + 4 - 8 * ((e // 4) % 2)
    return sib, (xn, yn, dg)


NT = (((1,), (1,)), ((), ()))
TN = (((0,), (0,)), ((), ()))


def visit_order(reps):
    if reps != 4:
        return [sorted((g for g in range(reps) if g != z), key=lambda g: (abs(g - z), g)) + [z] for z in range(reps)]
    return [[2, 3, 1, 0], [2, 3, 0, 1], [1, 0, 3, 2], [1, 0, 2, 3]]


def moe_kernel(reps, side_lanes, experts_all, x_ref, cot_ref, eg_ref, eu_ref, ed_ref,
               row_ref, moe_ref, gout_ref, uout_ref, dout_ref, gin_ref,
               mid_ref, a_ref, b_ref, h_ref,
               wgu, wd, xbuf, cbuf, abuf, pbuf, sib_in, relay_in, sendbuf, ownbuf, rbuf, xin, yin, zin, colbuf, gst, dst,
               own_sem, w_sem, x_sem, c_sem, ab_sem, col_sem, g_sem, o_sem,
               zs, zr, ps, pr, cs, cr, ss, sr, hs, hr, qs, qr, fs, fr, xs, xr):
    f32, bf16 = jnp.float32, jnp.bfloat16
    z = lax.axis_index("rep")
    e = lax.axis_index("ep")
    core = e % 2
    chip = e // 2
    sib, chips = partners(e)
    rows = x_ref.shape[0]
    half = rows // 2
    width = cot_ref.shape[-1]
    W1 = x_ref.shape[1]
    WP = pbuf.shape[-1]
    exp_dev = eg_ref.shape[0]
    F = wgu.shape[2] // exp_dev
    EF = exp_dev * F
    steps = 4 * reps
    table = visit_order(reps)

    def group_of(s):
        g = 0
        for zi in range(reps):
            for si in range(reps):
                g = g + jnp.where((z == zi) & (s == si), table[zi][si], 0)
        return g

    def chip_of(k):
        return jnp.where(k == 0, chips[2] // 2, jnp.where(k == 1, chip, jnp.where(k == 2, chips[0] // 2, chips[1] // 2)))

    barrier = pltpu.get_barrier_semaphore()
    for other in (sib, *chips):
        pl.semaphore_signal(barrier, inc=1, device_id={"rep": z, "ep": other}, device_id_type=MESH)
    for d in range(1, reps):
        pl.semaphore_signal(barrier, inc=1, device_id={"rep": (z + d) % reps, "ep": e}, device_id_type=MESH)
    weights = []
    for j in range(exp_dev):
        cut = pl.ds(pl.multiple_of(z * F, F), F)
        weights.append(pltpu.make_async_copy(eg_ref.at[j, :, cut], wgu.at[0, :, pl.ds(j * F, F)], w_sem.at[j]))
        weights.append(pltpu.make_async_copy(eu_ref.at[j, :, cut], wgu.at[1, :, pl.ds(j * F, F)], w_sem.at[exp_dev + j]))
        weights.append(pltpu.make_async_copy(ed_ref.at[j, cut, :], wd.at[pl.ds(j * F, F), :], w_sem.at[2 * exp_dev + j]))
    for w in weights:
        w.start()
    local = pltpu.make_async_copy(x_ref, mid_ref.at[z, e], own_sem)
    local.start()
    pl.semaphore_wait(barrier, 4 + reps - 1)

    def zcopy(src, g, up):
        d = 0 if up else 1
        return pltpu.make_async_remote_copy(
            src_ref=src, dst_ref=mid_ref.at[g, e], send_sem=zs.at[d, g], recv_sem=zr.at[g],
            device_id={"rep": z + 1 if up else z - 1, "ep": e}, device_id_type=MESH)

    def pcopy(src, g, j):
        return pltpu.make_async_remote_copy(
            src_ref=src, dst_ref=mid_ref.at[g, e], send_sem=ps.at[g, j], recv_sem=pr.at[g, j],
            device_id={"rep": z, "ep": chips[j]}, device_id_type=MESH)

    def relay(g, j, source):
        part = mid_ref.at[g, source, pl.ds(half * j, half)]
        return pltpu.make_async_remote_copy(
            src_ref=part, dst_ref=part, send_sem=ps.at[g, 2 + j], recv_sem=pr.at[g, 2 + j],
            device_id={"rep": z, "ep": chips[1 - j]}, device_id_type=MESH)

    def ccopy(src, g, j):
        who = e if j == 0 else chips[j - 1]
        return pltpu.make_async_remote_copy(
            src_ref=src, dst_ref=mid_ref.at[g, who], send_sem=cs.at[g, j], recv_sem=cr.at[g, j],
            device_id={"rep": z, "ep": sib}, device_id_type=MESH)

    def spread(src, g):
        pcopy(src, g, 0).start()
        pcopy(src, g, 1).start()
        ccopy(src, g, 0).start()

    def pass_on(g):
        for j in range(2):
            pcopy(x_ref, g, j).wait_recv()
            relay(g, j, chips[j]).start()
            ccopy(mid_ref.at[g, chips[j]], g, j + 1).start()

    def finish_in(g):
        for j in range(2):
            relay(g, j, chips[2]).wait_recv()
        ccopy(mid_ref.at[g, chips[2]], g, 3).start()

    def at(k, fn):
        if k == 0:
            fn(z)
            return
        @pl.when(z - k >= 0)
        def _():
            fn(z - k)
        @pl.when(z + k < reps)
        def _():
            fn(z + k)

    def arrive(k):
        @pl.when(z - k >= 0)
        def _():
            g = z - k
            zcopy(x_ref, g, True).wait_recv()
            @pl.when(z < reps - 1)
            def _():
                zcopy(mid_ref.at[g, e], g, True).start()
            spread(mid_ref.at[g, e], g)
        @pl.when(z + k < reps)
        def _():
            g = z + k
            zcopy(x_ref, g, False).wait_recv()
            @pl.when(z > 0)
            def _():
                zcopy(mid_ref.at[g, e], g, False).start()
            spread(mid_ref.at[g, e], g)

    def ready(g):
        for j in range(4):
            ccopy(x_ref, g, j).wait_recv()

    def load_x(i):
        g, q = group_of(i // 4), chip_of(i % 4)
        return pltpu.make_async_copy(mid_ref.at[g, pl.ds(2 * q, 2)], xbuf.at[i % 2], x_sem.at[i % 2])

    def load_c(i):
        g, q = group_of(i // 4), chip_of(i % 4)
        return pltpu.make_async_copy(cot_ref.at[g, pl.ds(2 * q, 2)], cbuf.at[i % 2], c_sem.at[i % 2])

    def keep(i, m):
        g, q = group_of(i // 4), chip_of(i % 4)
        place = pl.ds(pl.multiple_of((g * 4 + q) * 2 * rows, 2 * rows), 2 * rows)
        return pltpu.make_async_copy(abuf.at[i % 2, m], (a_ref, b_ref, h_ref)[m].at[place], ab_sem.at[i % 2, m])

    def compute(i):
        slot = i % 2
        lane = lax.broadcasted_iota(jnp.int32, (2 * rows, side_lanes), 1)
        side = xbuf[slot, :, :, pl.ds(width, side_lanes)].reshape(2 * rows, side_lanes).astype(f32)

        def one(j, cots):
            cols = pl.ds(pl.multiple_of(j * F, F), F)
            x = xbuf[slot, :, :, pl.ds(0, width)].reshape(2 * rows, width)
            c = cbuf[slot].reshape(2 * rows, width)
            index = e * exp_dev + j
            w = jnp.sum(jnp.where((lane == index) | (lane == index + experts_all), side, 0.0), axis=1, keepdims=True)
            ga = jnp.dot(x, wgu[0, :, cols], preferred_element_type=f32)
            up = jnp.dot(x, wgu[1, :, cols], preferred_element_type=f32)
            hc = lax.dot_general(c, wd[cols, :], NT, preferred_element_type=f32)
            sigma = 1.0 / (1.0 + jnp.exp(-ga))
            silu = ga * sigma
            hid = (silu * up).astype(bf16).astype(f32)
            hcw = hc * w
            abuf[slot, 0, :, cols] = (hcw * up * (sigma * (1.0 + ga * (1.0 - sigma)))).astype(bf16)
            abuf[slot, 1, :, cols] = (hcw * silu).astype(bf16)
            abuf[slot, 2, :, cols] = (hid * w).astype(bf16)
            dots = jnp.sum(hid * hc, axis=1, keepdims=True)
            return cots + jnp.where(lane == index, dots, 0.0)

        cots = lax.fori_loop(0, exp_dev, one, jnp.zeros((2 * rows, side_lanes), f32), unroll=True)
        pbuf[slot, :, :, pl.ds(width, side_lanes)] = cots.astype(bf16).reshape(2, rows, side_lanes)
        t = lax.dot_general(abuf[slot, 0], wgu[0], NT, preferred_element_type=f32)
        t = t + lax.dot_general(abuf[slot, 1], wgu[1], NT, preferred_element_type=f32)
        pbuf[slot, :, :, pl.ds(0, width)] = t.astype(bf16).reshape(2, rows, width)
        t = jnp.dot(abuf[slot, 2], wd[...], preferred_element_type=f32)
        pbuf[slot, :, :, pl.ds(W1, width)] = t.astype(bf16).reshape(2, rows, width)

    def sibcopy(i):
        return pltpu.make_async_remote_copy(
            src_ref=pbuf.at[i % 2, 1 - core], dst_ref=sib_in.at[i % 4], send_sem=ss.at[i], recv_sem=sr.at[i],
            device_id={"rep": z, "ep": sib}, device_id_type=MESH)

    def hcopy(s, j):
        part = pl.ds(half * j, half)
        return pltpu.make_async_remote_copy(
            src_ref=sendbuf.at[0, part], dst_ref=relay_in.at[s, j], send_sem=hs.at[s, j], recv_sem=hr.at[s, j],
            device_id={"rep": z, "ep": chips[j]}, device_id_type=MESH)

    def qcopy(s, j):
        return pltpu.make_async_remote_copy(
            src_ref=sendbuf.at[1 + j], dst_ref=(xin, yin)[j].at[s], send_sem=qs.at[s, j], recv_sem=qr.at[s, j],
            device_id={"rep": z, "ep": chips[j]}, device_id_type=MESH)

    def fcopy(s, g):
        return pltpu.make_async_remote_copy(
            src_ref=rbuf.at[s % 2], dst_ref=zin.at[z], send_sem=fs.at[s], recv_sem=fr.at[z],
            device_id={"rep": g, "ep": e}, device_id_type=MESH)

    step = 16

    def add(out, terms, count=rows):
        @pl.loop(0, count // step)
        def _(i):
            r = pl.ds(pl.multiple_of(i * step, step), step)
            t = terms[0][r, :].astype(f32)
            for other in terms[1:]:
                t = t + other[r, :].astype(f32)
            out[r, :] = t.astype(out.dtype)

    def finish(i):
        s, k = i // 4, i % 4
        sibcopy(i).wait_recv()
        mine, other = pbuf.at[i % 2, core], sib_in.at[i % 4]
        lower, upper = pl.ds(0, half), pl.ds(half, half)
        @pl.when(k == 1)
        def _():
            add(ownbuf.at[s % 2], (mine, other))
        @pl.when(k == 0)
        def _():
            @pl.when(s > 0)
            def _():
                hcopy(s - 1, 0).wait_send()
                hcopy(s - 1, 1).wait_send()
            add(sendbuf.at[0], (mine, other))
            hcopy(s, 0).start()
            hcopy(s, 1).start()
        @pl.when(k == 2)
        def _():
            @pl.when(s > 0)
            def _():
                qcopy(s - 1, 0).wait_send()
            add(sendbuf.at[1, lower], (mine.at[lower], other.at[lower]), half)
            hcopy(s, 1).wait_recv()
            add(sendbuf.at[1, upper], (mine.at[upper], other.at[upper], relay_in.at[s, 1]), half)
            qcopy(s, 0).start()
        @pl.when(k == 3)
        def _():
            @pl.when(s > 0)
            def _():
                qcopy(s - 1, 1).wait_send()
            add(sendbuf.at[2, upper], (mine.at[upper], other.at[upper]), half)
            hcopy(s, 0).wait_recv()
            add(sendbuf.at[2, lower], (mine.at[lower], other.at[lower], relay_in.at[s, 0]), half)
            qcopy(s, 1).start()

    def total(s):
        for j in range(2):
            qcopy(s, j).wait_recv()

    def plane_sum(s):
        total(s)
        @pl.when(s >= 2)
        def _():
            fcopy(s - 2, group_of(s - 2)).wait_send()
        add(rbuf.at[s % 2], (ownbuf.at[s % 2], xin.at[s], yin.at[s]))
        fcopy(s, group_of(s)).start()

    @pl.when(z < reps - 1)
    def _():
        zcopy(x_ref, z, True).start()
    @pl.when(z > 0)
    def _():
        zcopy(x_ref, z, False).start()
    spread(x_ref, z)
    arrive(1)
    pass_on(z)
    arrive(2)
    at(1, pass_on)
    finish_in(z)
    arrive(3)
    at(2, pass_on)
    at(1, finish_in)
    end = (z == 0) | (z == reps - 1)

    @pl.when(end)
    def _():
        at(2, finish_in)
    for w in weights:
        w.wait()
    ready(group_of(0))
    load_x(0).start()
    load_c(0).start()

    @pl.loop(0, steps)
    def _(i):
        load_x(i).wait()
        load_c(i).wait()
        @pl.when(i == 1)
        def _():
            at(3, pass_on)
        @pl.when(i == 3)
        def _():
            at(3, finish_in)

            @pl.when(jnp.logical_not(end))
            def _():
                at(2, finish_in)
        @pl.when(i == steps - 5)
        def _():
            local.wait()
        @pl.when(i < steps - 1)
        def _():
            @pl.when(i % 4 == 3)
            def _():
                ready(group_of(i // 4 + 1))
            load_x(i + 1).start()
            load_c(i + 1).start()
        @pl.when(i >= 2)
        def _():
            sibcopy(i - 2).wait_send()
            for m in range(3):
                keep(i - 2, m).wait()
        compute(i)
        sibcopy(i).start()
        for m in range(3):
            keep(i, m).start()
        @pl.when(i >= 1)
        def _():
            finish(i - 1)
        @pl.when((i % 4 == 3) & (i >= 7) & (i < steps - 1))
        def _():
            plane_sum(i // 4 - 1)

    for i in (steps - 2, steps - 1):
        sibcopy(i).wait_send()
        for m in range(3):
            keep(i, m).wait()
    finish(steps - 1)
    plane_sum(reps - 2)

    blocks = width // 256
    halves = wgu.shape[1]

    def resident(src, m):
        return pltpu.make_async_copy(src.at[pl.ds(m * halves, halves)], wgu.at[m], w_sem.at[m])

    def load_col(src, n):
        return pltpu.make_async_copy(src.at[:, :, :, pl.ds(pl.multiple_of(n * 256, 256), 256)], colbuf.at[n % 2], col_sem.at[n % 2])

    def product(n, m):
        left = colbuf[n % 2, pl.ds(m * (reps // 2), reps // 2)].reshape(halves, 256)
        return left, wgu[m]

    def hand_over(k):
        return pltpu.make_async_remote_copy(
            src_ref=gout_ref.at[k], dst_ref=gin_ref.at[k], send_sem=xs.at[k], recv_sem=xr.at[k],
            device_id={"rep": (z + k) % reps, "ep": e}, device_id_type=MESH)

    per_piece = width // reps // 256

    def piece_done(n):
        k = (n // per_piece + reps - z) % reps
        @pl.when((n % per_piece == per_piece - 1) & (k % 2 == 1))
        def _():
            hand_over(k).start()

    def grad_rows(src, out, send):
        def store(n, j):
            per = width // reps
            place = pl.ds(pl.multiple_of((n * 256) % per, 256), 256)
            return pltpu.make_async_copy(gst.at[n % 2, j], out.at[((n * 256) // per + reps - z) % reps, j, place], g_sem.at[n % 2, j])
        for m in range(2):
            resident(src, m).start()
        load_col(mid_ref, 0).start()
        for m in range(2):
            resident(src, m).wait()
        @pl.loop(0, blocks)
        def _(n):
            load_col(mid_ref, n).wait()
            @pl.when(n < blocks - 1)
            def _():
                load_col(mid_ref, n + 1).start()
            @pl.when(n >= 2)
            def _():
                for j in range(exp_dev):
                    store(n - 2, j).wait()
                if send:
                    piece_done(n - 2)
            t = jnp.zeros((256, EF), f32)
            for m in range(2):
                left, right = product(n, m)
                t = t + lax.dot_general(left, right, TN, preferred_element_type=f32)
            for j in range(exp_dev):
                gst[n % 2, j] = t[:, j * F:(j + 1) * F].astype(bf16)
                store(n, j).start()
        for n in (blocks - 2, blocks - 1):
            for j in range(exp_dev):
                store(n, j).wait()
            if send:
                piece_done(n)

    def grad_down():
        def store(n):
            return pltpu.make_async_copy(dst.at[n % 2], dout_ref.at[:, :, pl.ds(pl.multiple_of(n * 256, 256), 256)], g_sem.at[n % 2, 0])
        for m in range(2):
            resident(h_ref, m).start()
        load_col(cot_ref, 0).start()
        for m in range(2):
            resident(h_ref, m).wait()
        @pl.loop(0, blocks)
        def _(n):
            load_col(cot_ref, n).wait()
            @pl.when(n < blocks - 1)
            def _():
                load_col(cot_ref, n + 1).start()
            @pl.when(n >= 2)
            def _():
                store(n - 2).wait()
            t = jnp.zeros((EF, 256), f32)
            for m in range(2):
                left, right = product(n, m)
                t = t + lax.dot_general(right, left, TN, preferred_element_type=f32)
            dst[n % 2] = t.reshape(exp_dev, F, 256).astype(bf16)
            store(n).start()
        for n in (blocks - 2, blocks - 1):
            store(n).wait()

    grad_rows(a_ref, gout_ref, True)
    grad_rows(b_ref, uout_ref, False)
    grad_down()

    last = reps - 1
    total(last)
    for d in range(1, reps):
        src = (z + d) % reps
        pltpu.make_async_remote_copy(
            src_ref=rbuf.at[0], dst_ref=zin.at[src], send_sem=fs.at[last], recv_sem=fr.at[src],
            device_id={"rep": src, "ep": e}, device_id_type=MESH).wait_recv()
    fcopy(reps - 3, group_of(reps - 3)).wait_send()
    add(rbuf.at[(reps - 3) % 2], (ownbuf.at[last % 2], xin.at[last], yin.at[last], *(zin.at[(z + d) % reps] for d in range(1, reps))))
    outs = (
        pltpu.make_async_copy(rbuf.at[(reps - 3) % 2, :, pl.ds(0, W1)], row_ref, o_sem.at[0]),
        pltpu.make_async_copy(rbuf.at[(reps - 3) % 2, :, pl.ds(W1, width)], moe_ref, o_sem.at[1]),
    )
    for o in outs:
        o.start()
    for o in outs:
        o.wait()
    fcopy(reps - 2, group_of(reps - 2)).wait_send()
    for k in range(1, reps, 2):
        hand_over(k).wait()
    for j in range(2):
        hcopy(last, j).wait_send()
        qcopy(last, j).wait_send()
    for g in range(reps):
        for j in range(4):
            ccopy(x_ref, g, j).wait_send()
        for j in range(2):
            pcopy(x_ref, g, j).wait_send()
            relay(g, j, chips[j]).wait_send()
        @pl.when((z < reps - 1) & (z >= g))
        def _():
            zcopy(x_ref, g, True).wait_send()
        @pl.when((z > 0) & (z <= g))
        def _():
            zcopy(x_ref, g, False).wait_send()


def moe(x, cot_all, eg, eu, ed, experts_all, cid):
    reps, eps, rows, width = cot_all.shape
    W1 = x.shape[1]
    side = W1 - width
    WP = W1 + width
    exp_dev, _, ff = eg.shape
    F = ff // reps
    EF = exp_dev * F
    f32, bf16 = jnp.float32, jnp.bfloat16
    D, V = pltpu.SemaphoreType.DMA, pltpu.VMEM
    S = jax.ShapeDtypeStruct
    tokens = reps * eps * rows
    steps = 4 * reps
    outs = (
        S((rows, W1), bf16), S((rows, width), bf16),
        S((reps, exp_dev, width // reps, F), bf16), S((reps, exp_dev, width // reps, F), bf16), S((exp_dev, F, width), bf16),
        S((reps, exp_dev, width // reps, F), bf16),
        S((reps, eps, rows, W1), bf16), S((tokens, EF), bf16), S((tokens, EF), bf16), S((tokens, EF), bf16),
    )
    return pl.pallas_call(
        partial(moe_kernel, reps, side, experts_all),
        out_shape=outs,
        in_specs=[pl.BlockSpec(memory_space=pl.ANY)] * 5,
        out_specs=[pl.BlockSpec(memory_space=pl.ANY)] * len(outs),
        scratch_shapes=[
            V((2, width, EF), bf16), V((EF, width), bf16),
            V((2, 2, rows, W1), bf16), V((2, 2, rows, width), bf16),
            V((2, 3, 2 * rows, EF), bf16), V((2, 2, rows, WP), bf16), V((4, rows, WP), bf16),
            V((reps, 2, rows // 2, WP), bf16), V((3, rows, WP), bf16), V((2, rows, WP), bf16), V((2, rows, WP), bf16),
            *[V((reps, rows, WP), bf16)] * 3, V((2, reps, eps, rows, 256), bf16),
            V((2, exp_dev, 256, F), bf16), V((2, exp_dev, F, 256), bf16),
            D, D((3 * exp_dev,)), D((2,)), D((2,)), D((2, 3)), D((2,)), D((2, exp_dev)), D((2,)),
            D((2, reps)), D((reps,)), D((reps, 4)), D((reps, 4)), D((reps, 4)), D((reps, 4)),
            D((steps,)), D((steps,)), D((reps, 2)), D((reps, 2)), D((reps, 2)), D((reps, 2)), D((reps,)), D((reps,)), D((reps,)), D((reps,)),
        ],
        compiler_params=pltpu.CompilerParams(collective_id=cid, has_side_effects=True, vmem_limit_bytes=63 * 2**20),
    )(x, cot_all, eg, eu, ed)[:6]


def back_kernel(heads_dev, cot_ref, wout_ref, mixed_ref, qkv_ref, pre_ref, turn_ref, segs_ref, gains_ref, normed_ref, wqkv_ref,
                part_ref, qkv_out, out_out, gain_out,
                cots, wout, mixed, qkv, pre, turn, segs, gains, normed, wqkv, probs, dsc, dmix, dkey, pcot, part, term, oterm, gsum,
                l_sem, o_sem, ts, tr, tcs, tcr):
    f32, bf16 = jnp.float32, jnp.bfloat16
    z = lax.axis_index("rep")
    e = lax.axis_index("ep")
    sib, chips = partners(e)
    eps, rows, width = cots.shape
    half = rows // 2
    group_rows = eps * rows
    slice_width = mixed.shape[1]
    head_dim = slice_width // heads_dev
    scale = head_dim ** -0.5

    barrier = pltpu.get_barrier_semaphore()
    for other in (sib, *chips):
        pl.semaphore_signal(barrier, inc=1, device_id={"rep": z, "ep": other}, device_id_type=MESH)
    pairs = ((qkv_ref, qkv), (segs_ref, segs), (wout_ref, wout), (mixed_ref, mixed), (pre_ref, pre), (turn_ref, turn),
             (gains_ref, gains), (normed_ref, normed), (wqkv_ref, wqkv), (cot_ref, cots.at[e]))
    loads = [pltpu.make_async_copy(a, b, l_sem.at[n]) for n, (a, b) in enumerate(pairs)]
    for c in loads:
        c.start()
    pl.semaphore_wait(barrier, 4)

    def remote(src, dst, send, recv, ep):
        return pltpu.make_async_remote_copy(src_ref=src, dst_ref=dst, send_sem=send, recv_sem=recv,
                                            device_id={"rep": z, "ep": ep}, device_id_type=MESH)

    def near(j):
        return remote(cot_ref, cots.at[e], ts.at[j], tr.at[j], chips[j])

    def relay(j, source):
        p = cots.at[source, pl.ds(half * j, half)]
        return remote(p, p, ts.at[2 + j], tr.at[2 + j], chips[1 - j])

    def other_core(j):
        if j == 0:
            return remote(cot_ref, cots.at[e], tcs.at[0], tcr.at[0], sib)
        p = cots.at[chips[j - 1]]
        return remote(p, p, tcs.at[j], tcr.at[j], sib)

    near(0).start()
    near(1).start()
    other_core(0).start()

    block = 2 * rows
    blocks = group_rows // block
    loads[0].wait()
    loads[1].wait()
    seg_row = jnp.concatenate([segs[n:n + 1, :] for n in range(eps)], axis=1)

    def softmax(h, n):
        here = pl.ds(n * block, block)
        cut = slice(h * head_dim, (h + 1) * head_dim)
        kcut = slice(slice_width + h * head_dim, slice_width + (h + 1) * head_dim)
        s = lax.dot_general(qkv[here, cut], qkv[:, kcut], NT, preferred_element_type=f32) * scale
        seg_col = jnp.concatenate(
            [jnp.broadcast_to(segs[2 * n + j:2 * n + j + 1, :], (rows, rows)).T[:, 0:1] for j in range(2)], axis=0)
        s = jnp.where(seg_col == seg_row, s, masked_score)
        p = jnp.exp(s - jnp.max(s, axis=-1, keepdims=True))
        probs[h, here, :] = p / jnp.sum(p, axis=-1, keepdims=True)

    for n in range(blocks):
        softmax(0, n)
    for j in range(2):
        near(j).wait_recv()
        relay(j, chips[j]).start()
        other_core(j + 1).start()
    for h in range(1, heads_dev):
        for n in range(blocks):
            softmax(h, n)
    for j in range(2):
        relay(j, chips[2]).wait_recv()
    other_core(3).start()
    for c in loads[2:]:
        c.wait()
    for j in range(4):
        other_core(j).wait_recv()

    flat = cots[...].reshape(group_rows, width)
    weight = wout[...].reshape(slice_width, width)
    for n in range(blocks):
        here = pl.ds(n * block, block)
        left = cots[pl.ds(2 * n, 2)].reshape(block, width)
        dmix[here, :] = lax.dot_general(left, weight, NT, preferred_element_type=f32).astype(bf16)
    oterm[...] = lax.dot_general(mixed[...], flat, TN, preferred_element_type=f32).astype(bf16).reshape(oterm.shape)
    outs = [pltpu.make_async_copy(oterm, out_out, o_sem.at[0])]
    outs[0].start()

    def through_norm(index, dy, here, gain_row):
        cut = slice(index * head_dim, (index + 1) * head_dim)
        x = pre[here, cut]
        dn = dy * turn[0, here, :] + pltpu.roll(dy * turn[1, here, :], head_dim // 2, 1)
        r = lax.rsqrt(jnp.mean(x * x, axis=-1, keepdims=True) + norm_eps)
        unit = x * r
        gsum[gain_row:gain_row + 1, :] += jnp.sum(dn * unit, axis=0, keepdims=True)
        base = 2 * width // 128 + gain_row
        w = dn * gains[base:base + 1, :]
        pcot[here, cut] = (r * (w - unit * jnp.mean(w * unit, axis=-1, keepdims=True))).astype(bf16)

    gsum[...] = jnp.zeros_like(gsum)
    for h in range(heads_dev):
        cut = slice(h * head_dim, (h + 1) * head_dim)
        kcut = slice(slice_width + h * head_dim, slice_width + (h + 1) * head_dim)
        vcut = slice(2 * slice_width + h * head_dim, 2 * slice_width + (h + 1) * head_dim)
        for n in range(blocks):
            here = pl.ds(n * block, block)
            p = probs[h, here, :]
            dp = lax.dot_general(dmix[here, cut], qkv[:, vcut], NT, preferred_element_type=f32)
            ds = (p * (dp - jnp.sum(p * dp, axis=-1, keepdims=True))).astype(bf16)
            dsc[0, here, :] = ds
            dsc[1, here, :] = p.astype(bf16)
            through_norm(h, jnp.dot(ds, qkv[:, kcut], preferred_element_type=f32) * scale, here, 0)
        dkey[...] = lax.dot_general(dsc[0], qkv[:, cut], TN, preferred_element_type=f32) * scale
        for n in range(blocks):
            here = pl.ds(n * block, block)
            through_norm(heads_dev + h, dkey[here, :], here, 1)
        pcot[:, vcut] = lax.dot_general(dsc[1], dmix[:, cut], TN, preferred_element_type=f32).astype(bf16)
    outs.append(pltpu.make_async_copy(gsum, gain_out, o_sem.at[1]))
    outs[-1].start()

    for n in range(blocks):
        here = pl.ds(n * block, block)
        t = lax.dot_general(pcot[here, :], wqkv[...], NT, preferred_element_type=f32)
        part[n] = t.astype(bf16).reshape(2, rows, width)
        outs.append(pltpu.make_async_copy(part.at[n], part_ref.at[n], o_sem.at[2 + n]))
        outs[-1].start()
    piece = width // term.shape[0]
    for n in range(term.shape[0]):
        left = normed[:, n * piece:(n + 1) * piece]
        term[n] = lax.dot_general(left, pcot[...], TN, preferred_element_type=f32).astype(bf16)
        outs.append(pltpu.make_async_copy(term.at[n], qkv_out.at[n], o_sem.at[2 + blocks + n]))
        outs[-1].start()
    for c in outs:
        c.wait()
    for j in range(2):
        near(j).wait_send()
        relay(j, chips[j]).wait_send()
    for j in range(4):
        other_core(j).wait_send()


def attention_back(cot, wout, mixed, qkv, pre, turn, segs, gains, normed, wqkv, reps, eps, cid):
    rows, width = cot.shape
    heads_dev = wout.shape[0]
    gr, sw = mixed.shape
    f32, bf16 = jnp.float32, jnp.bfloat16
    S, V, D = jax.ShapeDtypeStruct, pltpu.VMEM, pltpu.SemaphoreType.DMA
    hd = sw // heads_dev
    outs = (S((eps // 2, 2, rows, width), bf16), S((reps, width // reps, 3 * sw), bf16), S(wout.shape, bf16), S((8, hd), f32))
    return pl.pallas_call(
        partial(back_kernel, heads_dev),
        out_shape=outs,
        in_specs=[pl.BlockSpec(memory_space=pl.ANY)] * 10,
        out_specs=[pl.BlockSpec(memory_space=pl.ANY)] * len(outs),
        scratch_shapes=[
            V((eps, rows, width), bf16), *[V(a.shape, a.dtype) for a in (wout, mixed, qkv, pre, turn, segs, gains, normed, wqkv)],
            V((heads_dev, gr, gr), f32), V((2, gr, gr), bf16), V((gr, sw), bf16), V((gr, hd), f32), V((gr, 3 * sw), bf16),
            V(outs[0].shape, bf16), V(outs[1].shape, bf16), V(wout.shape, bf16), V((8, hd), f32),
            D((10,)), D((2 + eps // 2 + reps,)), D((4,)), D((4,)), D((4,)), D((4,)),
        ],
        compiler_params=pltpu.CompilerParams(collective_id=cid, has_side_effects=True, vmem_limit_bytes=58 * 2**20),
    )(cot, wout, mixed, qkv, pre, turn, segs, gains, normed, wqkv)


def last_kernel(reps, eps, part_ref, qkv_ref, out_ref, tok_ref, cot_ref, gain_ref, gains_ref, router_ref,
                input_ref, q_ref, k_ref, v_ref, o_ref, gsum_ref, rsum_ref,
                own, sib_in, relay_in, xin, yin, wo, qall, qup, qdown, wup, wdown, fin, gath, mats, omat, tok, cot, gain,
                gown, gin, gz, gmid, rown, rin, rz, rmid,
                l_sem, ss, sr, hs, hr, qs, qr, ws, wr, us, ur, ds, dr, wus, wur, wds, wdr, ps, pr, gs, gr, gzs, gzr, rs, rr, rzs, rzr):
    f32, bf16 = jnp.float32, jnp.bfloat16
    z = lax.axis_index("rep")
    e = lax.axis_index("ep")
    core = e % 2
    chip = e // 2
    sib, chips = partners(e)
    rows, width = tok_ref.shape
    half = rows // 2
    rows_dev = o_ref.shape[0]
    heads_dev = out_ref.shape[0]
    head_dim = width // (heads_dev * eps)
    slice_width = heads_dev * head_dim

    barrier = pltpu.get_barrier_semaphore()
    for d in range(1, eps):
        pl.semaphore_signal(barrier, inc=1, device_id={"rep": z, "ep": (e + d) % eps}, device_id_type=MESH)
    for d in range(1, reps):
        pl.semaphore_signal(barrier, inc=1, device_id={"rep": (z + d) % reps, "ep": e}, device_id_type=MESH)
    loads = [
        pltpu.make_async_copy(part_ref.at[:, core], own, l_sem.at[0]),
        pltpu.make_async_copy(qkv_ref, qall, l_sem.at[1]),
        pltpu.make_async_copy(out_ref.at[:, core], wo.at[core], l_sem.at[2]),
        pltpu.make_async_copy(tok_ref, tok, l_sem.at[3]),
        pltpu.make_async_copy(cot_ref, cot, l_sem.at[4]),
        pltpu.make_async_copy(gain_ref, gain, l_sem.at[5]),
        pltpu.make_async_copy(gains_ref, gown, l_sem.at[6]),
        pltpu.make_async_copy(router_ref, rown, l_sem.at[7]),
    ]
    for c in loads:
        c.start()
    pl.semaphore_wait(barrier, eps - 1 + reps - 1)

    def to_sib(src, dst, send, recv):
        return pltpu.make_async_remote_copy(src_ref=src, dst_ref=dst, send_sem=send, recv_sem=recv,
                                            device_id={"rep": z, "ep": sib}, device_id_type=MESH)

    def to_chip(src, dst, send, recv, j):
        return pltpu.make_async_remote_copy(src_ref=src, dst_ref=dst, send_sem=send, recv_sem=recv,
                                            device_id={"rep": z, "ep": chips[j]}, device_id_type=MESH)

    def to_plane(src, dst, send, recv, d):
        return pltpu.make_async_remote_copy(src_ref=src, dst_ref=dst, send_sem=send, recv_sem=recv,
                                            device_id={"rep": z, "ep": (e + d) % eps}, device_id_type=MESH)

    def to_rep(src, dst, send, recv, d):
        return pltpu.make_async_remote_copy(src_ref=src, dst_ref=dst, send_sem=send, recv_sem=recv,
                                            device_id={"rep": (z + d) % reps, "ep": e}, device_id_type=MESH)

    def along(src, slot, send, recv, up):
        return pltpu.make_async_remote_copy(src_ref=src, dst_ref=slot, send_sem=send, recv_sem=recv,
                                            device_id={"rep": z + 1 if up else z - 1, "ep": e}, device_id_type=MESH)

    class Sum:
        def __init__(self, mine, up, down, usend, urecv, dsend, drecv, count):
            self.mine, self.up, self.down, self.count = mine, up, down, count
            self.usend, self.urecv, self.dsend, self.drecv = usend, urecv, dsend, drecv

        def hop(self, src, g, up):
            if up:
                return along(src, self.up.at[g], self.usend.at[g], self.urecv.at[g], True)
            return along(src, self.down.at[g], self.dsend.at[g], self.drecv.at[g], False)

        def begin(self, source):
            @pl.when(z == 0)
            def _():
                for g in range(reps - 1, 0, -1):
                    self.hop(source(g), g, True).start()
            @pl.when(z == reps - 1)
            def _():
                for g in range(reps - 1):
                    self.hop(source(g), g, False).start()

        def forward(self, n):
            g = reps - 1 - n
            @pl.when((z > 0) & (z < g))
            def _():
                self.hop(self.mine(g), g, True).wait_recv()
                add(self.up.at[g], (self.up.at[g], self.mine(g)), self.count)
                self.hop(self.up.at[g], g, True).start()
            @pl.when((z < reps - 1) & (z > n))
            def _():
                self.hop(self.mine(n), n, False).wait_recv()
                add(self.down.at[n], (self.down.at[n], self.mine(n)), self.count)
                self.hop(self.down.at[n], n, False).start()

        def arrived(self):
            @pl.when(z > 0)
            def _():
                self.hop(self.mine(0), z, True).wait_recv()
            @pl.when(z == 0)
            def _():
                self.up[z] = jnp.zeros(self.up.shape[1:], bf16)
            @pl.when(z < reps - 1)
            def _():
                self.hop(self.mine(0), z, False).wait_recv()
            @pl.when(z == reps - 1)
            def _():
                self.down[z] = jnp.zeros(self.down.shape[1:], bf16)

        def sent(self):
            for g in range(reps):
                @pl.when(z < g)
                def _():
                    self.hop(self.mine(g), g, True).wait_send()
                @pl.when(z > g)
                def _():
                    self.hop(self.mine(g), g, False).wait_send()

    step = 16

    def add(out, terms, count):
        @pl.loop(0, count // step)
        def _(i):
            r = pl.ds(pl.multiple_of(i * step, step), step)
            t = terms[0][r, :].astype(f32)
            for other in terms[1:]:
                t = t + other[r, :].astype(f32)
            out[r, :] = t.astype(out.dtype)

    lower, upper = pl.ds(0, half), pl.ds(half, half)
    qkv_sum = Sum(lambda g: qall.at[g], qup, qdown, us, ur, ds, dr, rows_dev * eps)
    out_sum = Sum(lambda g: wo.at[g // heads_dev, g % heads_dev], wup, wdown, wus, wur, wds, wdr, rows_dev)
    wcopy = to_sib(out_ref.at[:, 1 - core], wo.at[core], ws, wr)
    order = (chips[2] // 2, chips[0] // 2, chips[1] // 2, chip)
    scopies = [to_sib(part_ref.at[q, 1 - core], sib_in.at[q], ss.at[n], sr.at[n]) for n, q in enumerate(order)]
    qkv_sum.begin(lambda g: qkv_ref.at[g])
    for c in scopies:
        c.start()
    wcopy.start()

    hcopies = [to_chip(own.at[order[0], (lower, upper)[j]], relay_in.at[j], hs.at[j], hr.at[j], j) for j in range(2)]
    qcopies = [to_chip(own.at[order[1 + j]], (xin, yin)[j], qs.at[j], qr.at[j], j) for j in range(2)]
    loads[0].wait()
    scopies[0].wait_recv()
    d = own.at[order[0]]
    add(d, (d, sib_in.at[order[0]]), rows)
    for c in hcopies:
        c.start()
    for j in range(2):
        mine, other = own.at[order[1 + j]], sib_in.at[order[1 + j]]
        scopies[1 + j].wait_recv()
        direct, through = ((lower, upper), (upper, lower))[j]
        add(mine.at[direct], (mine.at[direct], other.at[direct]), half)
        hcopies[1 - j].wait_recv()
        add(mine.at[through], (mine.at[through], other.at[through], relay_in.at[1 - j]), half)
        qcopies[j].start()
    loads[2].wait()
    wcopy.wait_recv()
    out_sum.begin(out_sum.mine)
    loads[1].wait()
    qkv_sum.forward(0)
    scopies[3].wait_recv()
    for c in loads[3:8]:
        c.wait()
    for c in qcopies:
        c.wait_recv()

    gown[0:1, :] = jnp.zeros((1, width), f32)

    @pl.loop(0, rows // step)
    def _(i):
        r = pl.ds(pl.multiple_of(i * step, step), step)
        nc = (own[chip, r, :].astype(f32) + sib_in[chip, r, :].astype(f32) + xin[r, :].astype(f32) + yin[r, :].astype(f32))
        t = tok[r, :].astype(f32)
        scale = lax.rsqrt(jnp.mean(t * t, axis=-1, keepdims=True) + 1e-6)
        unit = t * scale
        scaled = nc * gain[0:1, :]
        cot[r, :] = cot[r, :] + scale * (scaled - unit * jnp.mean(scaled * unit, axis=-1, keepdims=True))
        gown[0:1, :] += jnp.sum(nc * unit, axis=0, keepdims=True)

    done = [pltpu.make_async_copy(cot, input_ref, l_sem.at[8])]
    done[0].start()

    gcopies = [to_plane(gown, gin.at[d - 1], gs.at[d - 1], gr.at[d - 1], d) for d in range(1, eps)]
    rcopies = [to_plane(rown.at[:, (e + d) % eps], rin.at[d - 1], rs.at[d - 1], rr.at[d - 1], d) for d in range(1, eps)]
    for c in (*gcopies, *rcopies):
        c.start()
    qkv_sum.forward(1)
    out_sum.forward(0)
    for n in range(2, reps - 1):
        qkv_sum.forward(n)
    for n in range(1, reps - 1):
        out_sum.forward(n)
    for c in (*gcopies, *rcopies):
        c.wait_recv()
    t = gown[...]
    for d in range(1, eps):
        t = t + gin[d - 1]
    gmid[...] = t
    t = rown[:, e]
    for d in range(1, eps):
        t = t + rin[d - 1]
    rmid[...] = t
    gzcopies = [to_rep(gmid, gz.at[d - 1], gzs.at[d - 1], gzr.at[d - 1], d) for d in range(1, reps)]
    rzcopies = [to_rep(rmid.at[(z + d) % reps], rz.at[d - 1], rzs.at[d - 1], rzr.at[d - 1], d) for d in range(1, reps)]
    for c in (*gzcopies, *rzcopies):
        c.start()

    qkv_sum.arrived()
    for n in range(eps):
        @pl.loop(0, rows_dev // step)
        def _(i):
            r = pl.ds(pl.multiple_of(i * step, step), step)
            a = pl.ds(pl.multiple_of(n * rows_dev + i * step, step), step)
            t = qall[z, a, :].astype(f32) + qup[z, a, :].astype(f32) + qdown[z, a, :].astype(f32)
            fin[n, r, :] = t.astype(bf16)
    pcopies = [to_plane(fin.at[(e + d) % eps], gath.at[e], ps.at[d - 1], pr.at[d - 1], d) for d in range(1, eps)]
    for c in pcopies:
        c.start()
    mine = pltpu.make_async_copy(fin.at[e], gath.at[e], l_sem.at[9])
    mine.start()
    out_sum.arrived()
    for c in (*gzcopies, *rzcopies):
        c.wait_recv()
    for c in gcopies:
        c.wait_send()
    t = gmid[...]
    for d in range(reps - 1):
        t = t + gz[d]
    gown[...] = t
    t = rmid[z]
    for d in range(reps - 1):
        t = t + rz[d]
    rmid[z] = t
    done.append(pltpu.make_async_copy(gown, gsum_ref, l_sem.at[10]))
    done.append(pltpu.make_async_copy(rmid.at[z], rsum_ref, l_sem.at[11]))
    wmine = wo.at[z // heads_dev, z % heads_dev]

    @pl.loop(0, rows_dev // step)
    def _(i):
        r = pl.ds(pl.multiple_of(i * step, step), step)
        t = wmine[r, :].astype(f32) + wup[z, r, :].astype(f32) + wdown[z, r, :].astype(f32)
        omat[r, :] = t
    done.append(pltpu.make_async_copy(omat, o_ref, l_sem.at[12]))
    for c in rzcopies:
        c.wait_send()
    for c in done[1:]:
        c.start()
    mine.wait()
    for c in pcopies:
        c.wait_recv()
    for src in range(eps):
        for m in range(3):
            for i in range(heads_dev):
                head = ((src % 2) * heads_dev + i) * (eps // 2) + src // 2
                mats[m, :, head * head_dim:(head + 1) * head_dim] = gath[src, :, m * slice_width + i * head_dim:m * slice_width + (i + 1) * head_dim].astype(f32)
    for m, ref in enumerate((q_ref, k_ref, v_ref)):
        done.append(pltpu.make_async_copy(mats.at[m], ref, l_sem.at[13 + m]))
        done[-1].start()
    for c in done:
        c.wait()
    qkv_sum.sent()
    out_sum.sent()
    for c in (*scopies, wcopy, *hcopies, *qcopies, *pcopies, *rcopies, *gzcopies):
        c.wait_send()


def last_sums(part, qkv_term, out_term, tokens, after_cot, gain_in, gains, router, rows_dev, reps, eps, cid):
    rows, width = tokens.shape
    f32, bf16 = jnp.float32, jnp.bfloat16
    heads_dev = out_term.shape[0]
    slices = qkv_term.shape[2]
    q = eps // 2
    half = rows // 2
    D, V = pltpu.SemaphoreType.DMA, pltpu.VMEM
    S = jax.ShapeDtypeStruct
    g8, rt = gains.shape, router.shape[2:]
    outs = (S((rows, width), f32), *[S((rows_dev, width), f32)] * 4, S(g8, f32), S(rt, f32))
    return pl.pallas_call(
        partial(last_kernel, reps, eps),
        out_shape=outs,
        in_specs=[pl.BlockSpec(memory_space=pl.ANY)] * 8,
        out_specs=[pl.BlockSpec(memory_space=pl.ANY)] * len(outs),
        scratch_shapes=[
            V((q, rows, width), bf16), V((q, rows, width), bf16), V((2, half, width), bf16), V((rows, width), bf16), V((rows, width), bf16),
            V((2, heads_dev, rows_dev, width), bf16), *[V((reps, rows_dev * eps, slices), bf16)] * 3, *[V((reps, rows_dev, width), bf16)] * 2,
            V((eps, rows_dev, slices), bf16), V((eps, rows_dev, slices), bf16),
            V((3, rows_dev, width), f32), V((rows_dev, width), f32), V((rows, width), bf16), V((rows, width), f32), V((1, width), f32),
            V(g8, f32), V((eps - 1, *g8), f32), V((reps - 1, *g8), f32), V(g8, f32),
            V(router.shape, f32), V((eps - 1, reps, *rt), f32), V((reps - 1, *rt), f32), V((reps, *rt), f32),
            D((17,)), D((4,)), D((4,)), D((2,)), D((2,)), D((2,)), D((2,)), D, D,
            *[D((reps,))] * 8, D((eps - 1,)), D((eps - 1,)),
            D((eps - 1,)), D((eps - 1,)), D((reps - 1,)), D((reps - 1,)), D((eps - 1,)), D((eps - 1,)), D((reps - 1,)), D((reps - 1,)),
        ],
        compiler_params=pltpu.CompilerParams(collective_id=cid, has_side_effects=True, vmem_limit_bytes=60 * 2**20),
    )(part, qkv_term, out_term, tokens, after_cot, gain_in, gains, router)


def join_kernel(count, *refs):
    z = lax.axis_index("rep")
    cols = refs[0].shape[2]
    down, outs = refs[2 * count], refs[2 * count + 1:]
    outs[2][...] = down[...].astype(outs[2].dtype)
    for n in range(2):
        ins, out = refs[n * count:(n + 1) * count], outs[n]
        for k in range(count):
            place = pl.multiple_of((z + count - k) % count * cols, cols)
            out[:, :, pl.ds(place, cols)] = ins[k][...].astype(out.dtype)


def join_columns(first, first_got, first_even, second, second_got, down):
    count, exp_dev, rows, cols = first.shape
    whole = jax.ShapeDtypeStruct((exp_dev, rows, cols * count), jnp.float32)

    def part(k):
        return pl.BlockSpec((None, 1, rows // 2, cols), lambda j, i: (k, j, i, 0))

    piece = pl.BlockSpec((1, rows // 2, cols), lambda j, i: (j, i, 0))
    tall = pl.BlockSpec((1, down.shape[1] // 2, down.shape[2]), lambda j, i: (j, i, 0))
    return pl.pallas_call(
        partial(join_kernel, count),
        grid=(exp_dev, 2),
        out_shape=(whole, whole, jax.ShapeDtypeStruct(down.shape, jnp.float32)),
        in_specs=[part(0)] + [part(k) if k % 2 else piece for k in range(1, count)] + [part(0)] + [piece] * (count - 1) + [tall],
        out_specs=[pl.BlockSpec((1, rows // 2, cols * count), lambda j, i: (j, i, 0))] * 2 + [tall],
    )(first, *[first_got if k % 2 else first_even[k // 2 - 1] for k in range(1, count)], second, *second_got, down)


def front_kernel(reps, eps, lengths_ref, tok_ref, cot_ref, wq_ref, wk_ref, wv_ref, wo_ref, gains_ref, router_ref, nums_ref, freq_ref,
                 cots_ref, router_all_ref, nums_all_ref, gsum_ref, normed_ref, pre_ref, qkv_ref, mixed_ref, wqkv_ref, wout_ref, turn_ref, attn_ref,
                 toks, normed, wraw, stage, wqkv, wz, wout, proj, qkv, mixed, turn, segs, part, sib_in, relay_in, xin, yin, acc,
                 gown, gz, gmid, gin, gall, nums, freq,
                 l_sem, o_sem, ws, wr, vs, vr, zs, zr, fs, fr, ts, tr, tcs, tcr, cps, cpr, ccs, ccr,
                 gzs, gzr, gps, gpr, rzs, rzr, rps, rpr, ns, nr, ss, sr, hs, hr, qs, qr, os, orr):
    f32, bf16 = jnp.float32, jnp.bfloat16
    z = lax.axis_index("rep")
    e = lax.axis_index("ep")
    core = e % 2
    chip = e // 2
    sib, chips = partners(e)
    rows, width = tok_ref.shape
    half = rows // 2
    rows_dev = wq_ref.shape[0]
    slice_width = mixed.shape[1]
    head_dim = turn.shape[2]
    heads_dev = slice_width // head_dim
    group_rows = eps * rows

    barrier = pltpu.get_barrier_semaphore()
    for d in range(1, eps):
        pl.semaphore_signal(barrier, inc=1, device_id={"rep": z, "ep": (e + d) % eps}, device_id_type=MESH)
    for d in range(1, reps):
        pl.semaphore_signal(barrier, inc=1, device_id={"rep": (z + d) % reps, "ep": e}, device_id_type=MESH)

    def local(src, dst, sem):
        c = pltpu.make_async_copy(src, dst, sem)
        c.start()
        return c

    raw = [local(r, wraw.at[m], l_sem.at[m]) for m, r in enumerate((wq_ref, wk_ref, wv_ref))]
    tok_own = local(tok_ref, toks.at[e], l_sem.at[3])
    wo_own = local(wo_ref, wz.at[z], l_sem.at[4])
    cot_own = local(cot_ref, cots_ref.at[z, e], l_sem.at[5])
    small = [
        local(gains_ref, gown, l_sem.at[6]),
        local(nums_ref, nums.at[e], l_sem.at[7]),
        local(freq_ref, freq, l_sem.at[8]),
        local(router_ref, router_all_ref.at[e, z], l_sem.at[9]),
    ]
    pl.semaphore_wait(barrier, eps - 1 + reps - 1)

    def remote(src, dst, send, recv, rep, ep):
        return pltpu.make_async_remote_copy(src_ref=src, dst_ref=dst, send_sem=send, recv_sem=recv,
                                            device_id={"rep": rep, "ep": ep}, device_id_type=MESH)

    def below(k, fn):
        @pl.when(z - k >= 0)
        def _():
            fn(z - k)

    def above(k, fn):
        @pl.when(z + k < reps)
        def _():
            fn(z + k)

    class Chain:
        def __init__(self, slot, send, recv):
            self.slot, self.send, self.recv = slot, send, recv

        def copy(self, src, g, up):
            d = 0 if up else 1
            return remote(src, self.slot(g), self.send.at[d, g], self.recv.at[g], z + 1 if up else z - 1, e)

        def begin(self, src):
            @pl.when(z < reps - 1)
            def _():
                self.copy(src, z, True).start()
            @pl.when(z > 0)
            def _():
                self.copy(src, z, False).start()

        def take(self, k, then=None):
            def from_below(g):
                self.copy(self.slot(g), g, True).wait_recv()
                if then is not None:
                    then(g)
            def from_above(g):
                self.copy(self.slot(g), g, False).wait_recv()
                if then is not None:
                    then(g)
            below(k, from_below)
            above(k, from_above)

        def forward(self, k):
            @pl.when((z - k >= 0) & (z < reps - 1))
            def _():
                self.copy(self.slot(z - k), z - k, True).start()
            @pl.when((z + k < reps) & (z > 0))
            def _():
                self.copy(self.slot(z + k), z + k, False).start()

        def arrive(self, k):
            self.take(k)
            self.forward(k)

        def sent(self):
            for g in range(reps):
                @pl.when((z < reps - 1) & (z >= g))
                def _():
                    self.copy(self.slot(g), g, True).wait_send()
                @pl.when((z > 0) & (z <= g))
                def _():
                    self.copy(self.slot(g), g, False).wait_send()

    class Spread:
        def __init__(self, slot, send, recv, csend, crecv):
            self.slot, self.send, self.recv, self.csend, self.crecv = slot, send, recv, csend, crecv

        def near(self, src, j):
            return remote(src, self.slot(e), self.send.at[j], self.recv.at[j], z, chips[j])

        def relay(self, j, source):
            p = self.slot(source).at[pl.ds(half * j, half)]
            return remote(p, p, self.send.at[2 + j], self.recv.at[2 + j], z, chips[1 - j])

        def core(self, src, j):
            return remote(src, self.slot(e if j == 0 else chips[j - 1]), self.csend.at[j], self.crecv.at[j], z, sib)

        def begin(self, src):
            self.near(src, 0).start()
            self.near(src, 1).start()
            self.core(src, 0).start()

        def pass_on(self):
            for j in range(2):
                self.near(self.slot(e), j).wait_recv()
                self.relay(j, chips[j]).start()
                self.core(self.slot(chips[j]), j + 1).start()

        def finish(self):
            for j in range(2):
                self.relay(j, chips[2]).wait_recv()
            self.core(self.slot(chips[2]), 3).start()

        def arrived(self):
            for j in range(4):
                self.core(self.slot(e), j).wait_recv()

        def sent(self):
            for j in range(2):
                self.near(self.slot(e), j).wait_send()
                self.relay(j, chips[j]).wait_send()
            for j in range(4):
                self.core(self.slot(e), j).wait_send()

    tok_spread = Spread(lambda who: toks.at[who], ts, tr, tcs, tcr)

    def cot_spread(g):
        return Spread(lambda who: cots_ref.at[g, who], cps.at[g], cpr.at[g], ccs.at[g], ccr.at[g])

    wo_chain = Chain(lambda g: wz.at[g], ws, wr)
    w_chain = Chain(lambda g: wqkv.at[g], vs, vr)
    cot_chain = Chain(lambda g: cots_ref.at[g, e], zs, zr)

    def cot_take(k):
        cot_chain.take(k, lambda g: cot_spread(g).begin(cots_ref.at[g, e]))

    def each(k, fn):
        below(k, lambda g: fn(cot_spread(g)))
        above(k, lambda g: fn(cot_spread(g)))

    gzc = [remote(gains_ref, gz.at[d - 1], gzs.at[d - 1], gzr.at[d - 1], (z + d) % reps, e) for d in range(1, reps)]
    rzc = [remote(router_ref, router_all_ref.at[e, z], rzs.at[d - 1], rzr.at[d - 1], (z + d) % reps, e) for d in range(1, reps)]
    nc = [remote(nums_ref, nums.at[e], ns.at[d - 1], nr.at[d - 1], z, (e + d) % eps) for d in range(1, eps)]
    for c in (*gzc, *rzc, *nc):
        c.start()
    wo_chain.begin(wo_ref)
    for m in range(3):
        raw[m].wait()
        for who in range(eps):
            for i in range(heads_dev):
                head = ((who % 2) * heads_dev + i) * (eps // 2) + who // 2
                at = m * slice_width + i * head_dim
                stage[who, :, at:at + head_dim] = wraw[m, :, head * head_dim:(head + 1) * head_dim]
    vc = [remote(stage.at[(e + d) % eps], wqkv.at[z, e], fs.at[d - 1], fr.at[d - 1], z, (e + d) % eps) for d in range(1, eps)]
    for c in vc:
        c.start()
    v_own = local(stage.at[e], wqkv.at[z, e], l_sem.at[10])
    tok_spread.begin(tok_ref)
    cot_chain.begin(cot_ref)
    cot_spread(z).begin(cot_ref)
    v_own.wait()
    for c in vc:
        c.wait_recv()
    w_chain.begin(wqkv.at[z])
    wo_chain.arrive(1)

    for c in gzc:
        c.wait_recv()
    small[0].wait()
    t = gown[...].astype(f32)
    for d in range(reps - 1):
        t = t + gz[d].astype(f32)
    gmid[...] = t.astype(bf16)
    gpc = [remote(gmid, gin.at[d - 1], gps.at[d - 1], gpr.at[d - 1], z, (e + d) % eps) for d in range(1, eps)]
    for c in gpc:
        c.start()
    small[3].wait()
    for c in rzc:
        c.wait_recv()
    rpc = [remote(router_all_ref.at[e], router_all_ref.at[e], rps.at[d - 1], rpr.at[d - 1], z, (e + d) % eps) for d in range(1, eps)]
    for c in rpc:
        c.start()
    tok_spread.pass_on()
    tok_spread.finish()
    cot_take(1)
    for c in gpc:
        c.wait_recv()
    t = gmid[...].astype(f32)
    for d in range(eps - 1):
        t = t + gin[d].astype(f32)
    gall[...] = t
    outs = [local(gall, gsum_ref, o_sem.at[0])]
    w_chain.arrive(1)
    wo_chain.arrive(2)
    cot_chain.forward(1)

    for c in small[1:3]:
        c.wait()
    for c in nc:
        c.wait_recv()
    outs.append(local(nums, nums_all_ref, o_sem.at[1]))
    deal = nums[:, 0, :]
    segment = jnp.zeros(deal.shape, jnp.int32)
    start = jnp.zeros(deal.shape, jnp.int32)
    end = 0
    for n in range(lengths_ref.shape[1]):
        end = end + lengths_ref[0, n]
        after = (deal >= end).astype(jnp.int32)
        segment = segment + after
        start = start + after * lengths_ref[0, n]
    position = (deal - start).astype(f32)
    segs[...] = segment.astype(f32)
    lane = lax.broadcasted_iota(jnp.int32, (rows, head_dim), 1)
    sign = jnp.where(lane < head_dim // 2, -1.0, 1.0)
    for n in range(eps):
        spot = jnp.broadcast_to(position[n:n + 1, :], (rows, rows)).T
        angle = spot * freq[0:1, :]
        here = pl.ds(n * rows, rows)
        turn[0, here, :] = jnp.cos(angle)
        turn[1, here, :] = jnp.sin(angle) * sign
    outs.append(local(turn, turn_ref, o_sem.at[2]))
    cot_spread(z).pass_on()

    tok_own.wait()
    tok_spread.arrived()
    gain_in = jnp.concatenate([gall[n:n + 1, :] for n in range(width // 128)], axis=1)
    step = 16
    for n in range(eps):
        @pl.loop(0, rows // step)
        def _(i):
            r = pl.ds(pl.multiple_of(i * step, step), step)
            t = toks[n, r, :].astype(f32)
            scale = lax.rsqrt(jnp.mean(t * t, axis=-1, keepdims=True) + norm_eps)
            normed[n, r, :] = (t * scale * gain_in).astype(bf16)
    outs.append(local(normed, normed_ref, o_sem.at[3]))
    w_chain.arrive(2)
    wo_chain.arrive(3)
    cot_take(2)
    cot_chain.forward(2)
    cot_spread(z).finish()

    wo_own.wait()
    wc = [remote(wz.at[(1 - core) * heads_dev + i], wout.at[i, core], os.at[i], orr.at[i], z, sib) for i in range(heads_dev)]
    wl = [local(wz.at[core * heads_dev + i], wout.at[i, core], l_sem.at[11 + i]) for i in range(heads_dev)]
    for c in wc:
        c.start()
    w_chain.arrive(3)
    each(1, lambda s: s.pass_on())


    @pl.loop(0, eps)
    def _(n):
        here = pl.ds(pl.multiple_of(n * rows, rows), rows)
        proj[here, :] = jnp.dot(normed[n], wqkv[...].reshape(width, 3 * slice_width), preferred_element_type=f32)
        for h in range(2 * heads_dev):
            cut = slice(h * head_dim, (h + 1) * head_dim)
            t = proj[here, cut]
            row = 2 * width // 128 + (0 if h < heads_dev else 1)
            t = t * lax.rsqrt(jnp.mean(t * t, axis=-1, keepdims=True) + norm_eps) * gall[row:row + 1, :]
            t = t * turn[0, here, :] + pltpu.roll(t, head_dim // 2, 1) * turn[1, here, :]
            qkv[here, cut] = t.astype(bf16)
        tail = slice(2 * slice_width, 3 * slice_width)
        qkv[here, tail] = proj[here, tail].astype(bf16)

    outs.append(local(proj.at[:, pl.ds(0, 2 * slice_width)], pre_ref, o_sem.at[4]))
    outs.append(local(qkv, qkv_ref, o_sem.at[5]))
    outs.append(local(wqkv, wqkv_ref, o_sem.at[6]))

    seg_row = jnp.concatenate([segs[n:n + 1, :] for n in range(eps)], axis=1)
    block = 2 * rows

    def attend(h):
        cut = slice(h * head_dim, (h + 1) * head_dim)
        kcut = slice(slice_width + h * head_dim, slice_width + (h + 1) * head_dim)
        vcut = slice(2 * slice_width + h * head_dim, 2 * slice_width + (h + 1) * head_dim)
        for n in range(eps // 2):
            here = pl.ds(n * block, block)
            s = lax.dot_general(qkv[here, cut], qkv[:, kcut], NT, preferred_element_type=f32) * (head_dim ** -0.5)
            seg_col = jnp.concatenate(
                [jnp.broadcast_to(segs[2 * n + j:2 * n + j + 1, :], (rows, rows)).T[:, 0:1] for j in range(2)], axis=0)
            s = jnp.where(seg_col == seg_row, s, masked_score)
            p = jnp.exp(s - jnp.max(s, axis=-1, keepdims=True))
            p = (p / jnp.sum(p, axis=-1, keepdims=True)).astype(bf16)
            mixed[here, cut] = jnp.dot(p, qkv[:, vcut], preferred_element_type=f32).astype(bf16)

    each(1, lambda s: s.finish())
    attend(0)
    each(2, lambda s: s.pass_on())
    for h in range(1, heads_dev):
        attend(h)
    outs.append(local(mixed, mixed_ref, o_sem.at[7]))
    for c in wl:
        c.wait()
    for c in wc:
        c.wait_recv()
    outs.append(local(wout, wout_ref, o_sem.at[8]))

    order = (chips[2] // 2, chips[0] // 2, chips[1] // 2, chip)
    scopies = [remote(part.at[q, 1 - core], sib_in.at[q], ss.at[n], sr.at[n], z, sib) for n, q in enumerate(order)]
    for n in range(eps // 2):
        q = order[n]
        here = pl.ds(pl.multiple_of(q * block, block), block)
        t = jnp.dot(mixed[here, :], wout[...].reshape(slice_width, width), preferred_element_type=f32)
        part[q] = t.astype(bf16).reshape(2, rows, width)
        scopies[n].start()

    cot_take(3)

    def add(out, terms, count):
        @pl.loop(0, count // step)
        def _(i):
            r = pl.ds(pl.multiple_of(i * step, step), step)
            t = terms[0][r, :].astype(f32)
            for other in terms[1:]:
                t = t + other[r, :].astype(f32)
            out[r, :] = t.astype(out.dtype)

    lower, upper = pl.ds(0, half), pl.ds(half, half)
    first = part.at[order[0], core]
    hcopies = [remote(first.at[(lower, upper)[j]], relay_in.at[j], hs.at[j], hr.at[j], z, chips[j]) for j in range(2)]
    qcopies = [remote(part.at[order[1 + j], core], (xin, yin)[j], qs.at[j], qr.at[j], z, chips[j]) for j in range(2)]
    scopies[0].wait_recv()
    add(first, (first, sib_in.at[order[0]]), rows)
    for c in hcopies:
        c.start()
    for j in range(2):
        mine, other = part.at[order[1 + j], core], sib_in.at[order[1 + j]]
        scopies[1 + j].wait_recv()
        direct, through = ((lower, upper), (upper, lower))[j]
        add(mine.at[direct], (mine.at[direct], other.at[direct]), half)
        hcopies[1 - j].wait_recv()
        add(mine.at[through], (mine.at[through], other.at[through], relay_in.at[1 - j]), half)
        qcopies[j].start()
    scopies[3].wait_recv()
    each(3, lambda s: s.pass_on())
    each(2, lambda s: s.finish())
    for c in qcopies:
        c.wait_recv()
    add(acc, (part.at[chip, core], sib_in.at[chip], xin, yin, toks.at[e]), rows)
    outs.append(local(acc, attn_ref, o_sem.at[9]))
    each(3, lambda s: s.finish())
    cot_own.wait()
    for g in range(reps):
        cot_spread(g).arrived()
        cot_spread(g).sent()
    for chain in (wo_chain, w_chain, cot_chain):
        chain.sent()
    tok_spread.sent()
    for c in rpc:
        c.wait_recv()
    for c in (*gzc, *rzc, *nc, *vc, *gpc, *rpc, *wc, *scopies, *hcopies, *qcopies):
        c.wait_send()
    for c in outs:
        c.wait()


def front(lengths, tokens, cot, wq, wk, wv, wo, gains, router, nums, freq, heads_dev, reps, eps, cid):
    rows, width = tokens.shape
    rows_dev = wq.shape[0]
    f32, bf16, i32 = jnp.float32, jnp.bfloat16, jnp.int32
    head_dim = freq.shape[1]
    sw = heads_dev * head_dim
    gr = eps * rows
    half = rows // 2
    q = eps // 2
    S, V, D = jax.ShapeDtypeStruct, pltpu.VMEM, pltpu.SemaphoreType.DMA
    outs = (
        S((reps, eps, rows, width), bf16), S((eps, reps, *router.shape), bf16), S((eps, *nums.shape), i32), S(gains.shape, f32),
        S((eps, rows, width), bf16), S((gr, 2 * sw), f32), S((gr, 3 * sw), bf16), S((gr, sw), bf16),
        S((reps, eps, rows_dev, 3 * sw), bf16), S((heads_dev, 2, rows_dev, width), bf16), S((2, gr, head_dim), f32), S((rows, width), f32),
    )
    return pl.pallas_call(
        partial(front_kernel, reps, eps),
        out_shape=outs,
        in_specs=[pl.BlockSpec(memory_space=pltpu.SMEM)] + [pl.BlockSpec(memory_space=pl.ANY)] * 10,
        out_specs=[pl.BlockSpec(memory_space=pl.ANY)] * len(outs),
        scratch_shapes=[
            V((eps, rows, width), bf16), V((eps, rows, width), bf16), V((3, rows_dev, width), bf16), V((eps, rows_dev, 3 * sw), bf16),
            V((reps, eps, rows_dev, 3 * sw), bf16), V((reps, rows_dev, width), bf16), V((heads_dev, 2, rows_dev, width), bf16),
            V((gr, 3 * sw), f32), V((gr, 3 * sw), bf16), V((gr, sw), bf16), V((2, gr, head_dim), f32), V((eps, rows), f32),
            V((q, 2, rows, width), bf16), V((q, rows, width), bf16), V((2, half, width), bf16), V((rows, width), bf16), V((rows, width), bf16),
            V((rows, width), f32),
            V(gains.shape, bf16), V((reps - 1, *gains.shape), bf16), V(gains.shape, bf16), V((eps - 1, *gains.shape), bf16), V(gains.shape, f32),
            V((eps, *nums.shape), i32), V(freq.shape, f32),
            D((16,)), D((16,)), D((2, reps)), D((reps,)), D((2, reps)), D((reps,)), D((2, reps)), D((reps,)), D((eps - 1,)), D((eps - 1,)),
            D((4,)), D((4,)), D((4,)), D((4,)), D((reps, 4)), D((reps, 4)), D((reps, 4)), D((reps, 4)),
            D((reps - 1,)), D((reps - 1,)), D((eps - 1,)), D((eps - 1,)), D((reps - 1,)), D((reps - 1,)), D((eps - 1,)), D((eps - 1,)),
            D((eps - 1,)), D((eps - 1,)), D((4,)), D((4,)), D((2,)), D((2,)), D((2,)), D((2,)), D((2,)), D((2,)),
        ],
        compiler_params=pltpu.CompilerParams(collective_id=cid, has_side_effects=True, vmem_limit_bytes=56 * 2**20),
    )(lengths, tokens, cot, wq, wk, wv, wo, gains, router, nums, freq)


def on_device_split(
    tokens,
    cotangent,
    query_weight,
    key_weight,
    value_weight,
    output_weight,
    router_weight,
    gains,
    expert_gate,
    expert_up,
    expert_down,
    lengths,
    deal,
    routes,
    priority,
):
    bf16, f32 = jnp.bfloat16, jnp.float32
    tok_dev, width = tokens.shape
    ep_count, rep_count = lax.axis_size("ep"), lax.axis_size("rep")
    ep_index, rep_index = lax.axis_index("ep"), lax.axis_index("rep")
    exp_dev, _, ff_width = expert_gate.shape
    top_count = routes.shape[1]
    experts_all = exp_dev * ep_count
    group_rows = tok_dev * ep_count
    capacity = 5 * tok_dev * top_count // (4 * exp_dev)
    head_dim = HD
    heads_dev = width // head_dim // ep_count
    slice_width = heads_dev * head_dim
    rows_dev = query_weight.shape[0]

    gains_dev = gains.shape[0]
    gain_rows = -(-gains_dev * rep_count * ep_count // 2048) * 16
    gains_placed = lax.dynamic_update_slice_in_dim(
        jnp.zeros((gain_rows * 128,), bf16),
        gains,
        (rep_index * ep_count + ep_index) * gains_dev,
        axis=0,
    ).reshape(gain_rows, 128)
    router_rows = router_weight.size // 128
    router_placed = jnp.pad(router_weight.reshape(router_rows, 128), ((0, -router_rows % 16), (0, 0)))
    numbers = jnp.concatenate([deal[None], priority[None], routes.T])
    numbers = jnp.pad(numbers, ((0, -numbers.shape[0] % 8), (0, 0)))
    frequency = rope_base ** (
        -2.0 * jnp.arange(head_dim // 2, dtype=jnp.float32) / head_dim
    )
    (
        cot_all,
        router_all,
        numbers_all,
        gains_all,
        normed_group,
        pre,
        qkv_low,
        mixed_low,
        qkv_slice,
        out_slice,
        turn,
        after_attn,
    ) = front(
        lengths,
        tokens,
        cotangent,
        query_weight,
        key_weight,
        value_weight,
        output_weight,
        gains_placed,
        router_placed,
        numbers,
        jnp.concatenate([frequency, frequency]).reshape(1, head_dim),
        heads_dev,
        rep_count,
        ep_count,
        0,
    )
    gains_float = gains_all.reshape(-1)
    gain_in = gains_float[:width]
    gain_mid = gains_float[width : 2 * width]
    router_full = (
        router_all[:, :, :router_rows].transpose(1, 0, 2, 3).reshape(width, experts_all)
    )
    deal_all = numbers_all[:, 0].reshape(-1)
    priority_all = numbers_all[:, 1].reshape(-1)
    routes_all = numbers_all[:, 2 : 2 + top_count].transpose(0, 2, 1).reshape(group_rows, top_count)
    segment_all, _ = placement(deal_all, lengths[0])
    normed_group = normed_group.reshape(group_rows, width)
    qkv_slice = qkv_slice.reshape(width, 3 * slice_width)
    mid_low = rms_scale(after_attn, gain_mid).astype(bf16)

    logits = jnp.dot(mid_low, router_full, preferred_element_type=f32)
    expert_ids = jnp.arange(experts_all, dtype=jnp.int32)
    member = (routes[:, :, None] == expert_ids[None, None, :]).astype(f32)
    named = jnp.sum(member, axis=1)
    lifted = jnp.where(named > 0, logits, masked_score)
    lifted = jnp.exp(lifted - jnp.max(lifted, axis=-1, keepdims=True)) * named
    gate_dense = lifted / jnp.sum(lifted, axis=-1, keepdims=True)
    onehot_all = jnp.sum(
        (routes_all[:, :, None] == expert_ids[None, None, :]).astype(bf16), axis=1
    )
    earlier = (priority_all[None, :] < priority[:, None]).astype(bf16)
    slots = jnp.dot(earlier, onehot_all, preferred_element_type=f32)
    kept_dense = named * (slots < capacity).astype(f32)
    pair_weight = gate_dense * kept_dense

    weight_high = pair_weight.astype(bf16)
    weight_low = (pair_weight - weight_high.astype(f32)).astype(bf16)
    side = jnp.concatenate(
        [weight_high, weight_low, jnp.zeros((tok_dev, 128 - 2 * experts_all), bf16)], axis=1
    )
    row_sum, moe_sum, gate_term, up_term, down_term, gate_got = moe(
        jnp.concatenate([mid_low, side], axis=1),
        cot_all,
        expert_gate,
        expert_up,
        expert_down,
        experts_all,
        3,
    )
    moe_out = moe_sum.astype(f32)
    block_out = (after_attn + moe_out).astype(bf16)

    def from_below(part, k):
        return lax.ppermute(part, "rep", [(i, (i + k) % rep_count) for i in range(rep_count)])

    gate_pieces = [from_below(gate_term[k], k) for k in range(2, rep_count, 2)]
    up_pieces = [from_below(up_term[k], k) for k in range(1, rep_count)]

    out_grad = cotangent.astype(f32)
    gate_cot = row_sum[:, width : width + experts_all].astype(f32) * kept_dense
    chosen_cot = gate_dense * (gate_cot - jnp.sum(gate_dense * gate_cot, axis=-1, keepdims=True))
    logit_cot = chosen_cot.astype(bf16)
    mid_cot = row_sum[:, :width].astype(f32) + jnp.dot(
        logit_cot, router_full.T, preferred_element_type=f32
    )
    router_term = jnp.dot(mid_low.T, logit_cot, preferred_element_type=f32)
    _, mid_pull = jax.vjp(rms_scale, after_attn, gain_mid)
    after_extra, gain_mid_cot = mid_pull(mid_cot)
    after_cot = out_grad + after_extra
    normed_part, qkv_term, output_term, head_gains = attention_back(
        after_cot.astype(bf16),
        out_slice,
        mixed_low,
        qkv_low,
        pre,
        turn,
        segment_all.astype(f32).reshape(ep_count, tok_dev),
        gains_all,
        normed_group,
        qkv_slice,
        rep_count,
        ep_count,
        1,
    )
    gains_term = jnp.concatenate(
        [
            jnp.zeros((width,), f32),
            gain_mid_cot,
            head_gains[:2].reshape(-1),
            jnp.zeros((6 * width - 2 * head_dim,), f32),
        ]
    ).reshape(8, width)
    router_parts = jnp.pad(
        router_term.reshape(rep_count, ep_count, router_rows, 128),
        ((0, 0), (0, 0), (0, -router_rows % 8), (0, 0)),
    )
    input_grad, query_sum, key_sum, value_sum, output_sum, gains_all, router_own = last_sums(
        normed_part,
        qkv_term,
        output_term,
        tokens,
        after_cot,
        gain_in.reshape(1, width),
        gains_term,
        router_parts,
        rows_dev,
        rep_count,
        ep_count,
        4,
    )
    gains_sum = lax.dynamic_slice_in_dim(
        gains_all.reshape(-1), (rep_index * ep_count + ep_index) * gains_dev, gains_dev
    )
    router_sum = router_own[:router_rows].reshape(rows_dev, experts_all)
    gate_w_grad, up_w_grad, down_w_grad = join_columns(
        gate_term, gate_got, gate_pieces, up_term, up_pieces, down_term
    )
    return (
        block_out,
        input_grad,
        query_sum,
        key_sum,
        value_sum,
        output_sum,
        router_sum,
        gains_sum,
        gate_w_grad,
        up_w_grad,
        down_w_grad,
    )


def solution(mesh):
    placed = (
        P(("rep", "ep"), None),
        P(("rep", "ep"), None),
        P(("rep", "ep"), None),
        P(("rep", "ep"), None),
        P(("rep", "ep"), None),
        P(("rep", "ep"), None),
        P(("rep", "ep"), None),
        P(("rep", "ep")),
        P("ep", None, None),
        P("ep", None, None),
        P("ep", None, None),
        P("rep", None),
        P(("rep", "ep")),
        P(("rep", "ep"), None),
        P(("rep", "ep")),
    )
    return jax.shard_map(
        on_device_split if mesh.shape["rep"] == 4 else on_device_general,
        mesh=mesh,
        in_specs=placed,
        out_specs=(
            P(("rep", "ep"), None),
            P(("rep", "ep"), None),
            P(("rep", "ep"), None),
            P(("rep", "ep"), None),
            P(("rep", "ep"), None),
            P(("rep", "ep"), None),
            P(("rep", "ep"), None),
            P(("rep", "ep")),
            P("ep", "rep", None),
            P("ep", "rep", None),
            P("ep", "rep", None),
        ),
        check_vma=False,
    )
```
